32 devices in a mesh: dp: 2 (over y), ctx: 4 (over x, core), tp: 4 (over z).
Axes of the slice: x: 2, y: 2, z: 4, core: 2. Of those that a mesh axis runs over, the one named last changes fastest.
Arguments:
- tokens: bfloat16 [2, 2, 2, 2048, 1152], P(None, 'dp', None, 'ctx'), may hold values from -6 to 6
- segments: int32 [2, 2, 2, 2048], P(None, 'dp', None, 'ctx'), may hold values from 0 to 66, as said below
- cotangent: bfloat16 [2, 2, 2, 2048, 1152], P(None, 'dp', None, 'ctx'), may hold values from -6 to 6
- w_query: bfloat16 [1152, 1024], P(('dp', 'ctx'), 'tp'), may hold values from -0.1875 to 0.1875
- w_key: bfloat16 [1152, 256], P(('dp', 'ctx')), may hold values from -0.1875 to 0.1875
- w_value: bfloat16 [1152, 256], P(('dp', 'ctx')), may hold values from -0.1875 to 0.1875
- w_out: bfloat16 [1024, 1152], P('tp', ('dp', 'ctx')), may hold values from -0.375 to 0.375
- w_gate: bfloat16 [1152, 6912], P(('dp', 'ctx'), 'tp'), may hold values from -0.1875 to 0.1875
- w_up: bfloat16 [1152, 6912], P(('dp', 'ctx'), 'tp'), may hold values from -0.1875 to 0.1875
- w_down: bfloat16 [6912, 1152], P('tp', ('dp', 'ctx')), may hold values from -0.078125 to 0.078125
- g_input: bfloat16 [1152], P(('dp', 'ctx')), may hold values from -0.59765625 to 0.59765625
- g_post_attn: bfloat16 [1152], P(('dp', 'ctx')), may hold values from -0.59765625 to 0.59765625
- g_pre_ffn: bfloat16 [1152], P(('dp', 'ctx')), may hold values from -0.59765625 to 0.59765625
- g_post_ffn: bfloat16 [1152], P(('dp', 'ctx')), may hold values from -0.59765625 to 0.59765625
- g_query: bfloat16 [256], P(('dp', 'ctx')), may hold values from -0.59765625 to 0.59765625
- g_key: bfloat16 [256], P(('dp', 'ctx')), may hold values from -0.59765625 to 0.59765625
Outputs:
- output: bfloat16 [2, 2, 2, 2048, 1152], P(None, 'dp', None, 'ctx')
- d_tokens: float32 [2, 2, 2, 2048, 1152], P(None, 'dp', None, 'ctx')
- grad_w_query: float32 [1152, 1024], P(('dp', 'ctx'), 'tp')
- grad_w_key: float32 [1152, 256], P(('dp', 'ctx'))
- grad_w_value: float32 [1152, 256], P(('dp', 'ctx'))
- grad_w_out: float32 [1024, 1152], P('tp', ('dp', 'ctx'))
- grad_w_gate: float32 [1152, 6912], P(('dp', 'ctx'), 'tp')
- grad_w_up: float32 [1152, 6912], P(('dp', 'ctx'), 'tp')
- grad_w_down: float32 [6912, 1152], P('tp', ('dp', 'ctx'))
- grad_g_input: float32 [1152], P(('dp', 'ctx'))
- grad_g_post_attn: float32 [1152], P(('dp', 'ctx'))
- grad_g_pre_ffn: float32 [1152], P(('dp', 'ctx'))
- grad_g_post_ffn: float32 [1152], P(('dp', 'ctx'))
- grad_g_query: float32 [256], P(('dp', 'ctx'))
- grad_g_key: float32 [256], P(('dp', 'ctx'))
The draws below stay inside these ranges and needn't reach their ends.
Inputs may be any that keep to these rules, and one draw needn't show every extreme that they name: `segments`: read in each sequence's true order, ids never fall before the padding; id 0 marks padding, which fills the last positions of every sequence; the last token before the padding has the largest id.
All inputs are finite; a program needn't handle non-finite values.
Results may differ from the reference program's by a relative error of at most 0.025.
Values may be sent and summed in bfloat16 or wider, within the bound.
A program may use at most 320 MiB of HBM per device.

```python
import math
import jax
import jax.numpy as jnp
from jax import lax

D = 1152
H = 4
HD = 256
FF = 6912
SEQ_LEN = 4096
MB = 2
SEQS = 2


TOP_ID = 66


def one_sequence(seq_key):
    pad_key, first_key, power_key, length_key = jax.random.split(seq_key, 4)
    padding = jax.random.randint(pad_key, (), 1, SEQ_LEN // 8 + 1, dtype=jnp.int32)
    first_doc = jax.random.randint(first_key, (), 5 * SEQ_LEN // 8, 3 * SEQ_LEN // 4 + 1, dtype=jnp.int32)
    top_power = max(1, int(math.log2(SEQ_LEN)) - 3)
    powers = jax.random.randint(power_key, (64,), 1, top_power + 1, dtype=jnp.int32)
    longest = jnp.left_shift(jnp.ones((64,), jnp.int32), powers)
    doc_lengths = jax.random.randint(length_key, (64,), 1, longest + 1, dtype=jnp.int32)
    doc_ends = first_doc + jnp.cumsum(doc_lengths)
    position = jnp.arange(SEQ_LEN, dtype=jnp.int32)
    later = 2 + jnp.sum((position[:, None] >= doc_ends[None, :]).astype(jnp.int32), axis=1)
    seg_ids = jnp.where(position < first_doc, 1, later)
    seg_ids = jnp.where(position == SEQ_LEN - padding - 1, TOP_ID, seg_ids)
    seg_ids = jnp.where(position >= SEQ_LEN - padding, 0, seg_ids)
    half_len = SEQ_LEN // 2
    return jnp.stack([seg_ids[:half_len], jnp.flip(seg_ids[half_len:])], axis=0)


def draw_segments(key, part):
    seq_keys = jax.random.split(jax.random.fold_in(key, 17), MB * SEQS)
    return jax.vmap(one_sequence)(seq_keys).reshape(MB, SEQS, 2, SEQ_LEN // 2).astype(jnp.int32)


def block_scale(stream_key, shape, shards, smallest, high):
    factor_of, own = 1.0, jax.random.fold_in(stream_key, 6)
    for dim, blocks in shards:
        heights = jnp.exp(jax.random.uniform(jax.random.fold_in(own, dim), (blocks,), jnp.float32, smallest / len(shards), high / len(shards)))
        factor_of = factor_of * jnp.repeat(heights, shape[dim] // blocks).reshape([-1 if axis == dim else 1 for axis in range(len(shape))])
    return factor_of


def noise(key, shape, spread, limit, cuts=(), kind=jnp.bfloat16):
    drawn = jax.random.normal(key, shape, jnp.float32) * spread
    if len(cuts) > 0:
        drawn = block_scale(key, shape, cuts, -0.22, 0.18) * drawn
    return jnp.clip(drawn, min=-limit, max=limit).astype(kind)


def setup_inputs(seed: int = 0) -> dict:
    key_list = jax.random.split(jax.random.key(seed), 17)
    tokens = noise(key_list[0], (MB, SEQS, 2, SEQ_LEN // 2, D), 1.0, 6.0, ((1, 2), (3, 4)))
    segments = draw_segments(jax.random.fold_in(key_list[16], 71), 0)
    cotangent = noise(key_list[2], (MB, SEQS, 2, SEQ_LEN // 2, D), 1.0, 6.0, ((1, 2), (3, 4)))
    w_query = noise(key_list[3], (D, H * HD), D ** -0.5, 0.1875, ((0, 8), (1, 4)))
    w_key = noise(key_list[4], (D, HD), D ** -0.5, 0.1875, ((0, 8),))
    w_value = noise(key_list[5], (D, HD), D ** -0.5, 0.1875, ((0, 8),))
    w_out = noise(key_list[6], (H * HD, D), HD ** -0.5, 0.375, ((0, 4), (1, 8)))
    w_gate = noise(key_list[7], (D, FF), D ** -0.5, 0.1875, ((0, 8), (1, 4)))
    w_up = noise(key_list[8], (D, FF), D ** -0.5, 0.1875, ((0, 8), (1, 4)))
    w_down = noise(key_list[9], (FF, D), FF ** -0.5, 0.078125, ((0, 4), (1, 8)))
    g_input = jnp.clip(jax.random.uniform(key_list[10], (D,), jnp.float32, -0.59765625, 0.59765625) * block_scale(key_list[10], (D,), ((0, 8),), -0.4, 0.0), -0.59765625, 0.59765625).astype(jnp.bfloat16)
    g_post_attn = jnp.clip(jax.random.uniform(key_list[11], (D,), jnp.float32, -0.59765625, 0.59765625) * block_scale(key_list[11], (D,), ((0, 8),), -0.4, 0.0), -0.59765625, 0.59765625).astype(jnp.bfloat16)
    g_pre_ffn = jnp.clip(jax.random.uniform(key_list[12], (D,), jnp.float32, -0.59765625, 0.59765625) * block_scale(key_list[12], (D,), ((0, 8),), -0.4, 0.0), -0.59765625, 0.59765625).astype(jnp.bfloat16)
    g_post_ffn = jnp.clip(jax.random.uniform(key_list[13], (D,), jnp.float32, -0.59765625, 0.59765625) * block_scale(key_list[13], (D,), ((0, 8),), -0.4, 0.0), -0.59765625, 0.59765625).astype(jnp.bfloat16)
    g_query = jnp.clip(jax.random.uniform(key_list[14], (HD,), jnp.float32, -0.59765625, 0.59765625) * block_scale(key_list[14], (HD,), ((0, 8),), -0.4, 0.0), -0.59765625, 0.59765625).astype(jnp.bfloat16)
    g_key = jnp.clip(jax.random.uniform(key_list[15], (HD,), jnp.float32, -0.59765625, 0.59765625) * block_scale(key_list[15], (HD,), ((0, 8),), -0.4, 0.0), -0.59765625, 0.59765625).astype(jnp.bfloat16)
    return dict(tokens=tokens, segments=segments, cotangent=cotangent, w_query=w_query, w_key=w_key, w_value=w_value, w_out=w_out, w_gate=w_gate, w_up=w_up, w_down=w_down, g_input=g_input, g_post_attn=g_post_attn, g_pre_ffn=g_pre_ffn, g_post_ffn=g_post_ffn, g_query=g_query, g_key=g_key)


EPS = 1e-06
THETA = 1000000.0
SCALE = 0.0625
NEGATIVE = -1e+30
HIGHEST = lax.Precision.HIGHEST

@jax.custom_vjp
def low(v):
    return lax.optimization_barrier(v.astype(jnp.bfloat16)).astype(jnp.float32)

@jax.custom_vjp
def low_back(v):
    return v

def low_keep(v):
    return (low(v), None)

def low_pass(kept, grad):
    return (grad,)

def back_keep(v):
    return (v, None)

def back_low(kept, grad):
    return (low(grad),)
low.defvjp(low_keep, low_pass)
low_back.defvjp(back_keep, back_low)

def normed(values, gain_vec):
    return values * lax.rsqrt(lax.optimization_barrier(jnp.mean(values * values, axis=-1, keepdims=True)) + EPS) * (1.0 + gain_vec)

def angles(position, half_size, full_size):
    frequency = THETA ** (-2.0 * jnp.arange(half_size, dtype=jnp.float32) / full_size)
    turned = position[:, None] * frequency[None, :]
    return (jnp.cos(turned), jnp.sin(turned))

def rotate(tensor, cosine, sine_table):
    half_size = tensor.shape[-1] // 2
    first_half = tensor[..., :half_size]
    second_half = tensor[..., half_size:]
    return jnp.concatenate([first_half * cosine - second_half * sine_table, second_half * cosine + first_half * sine_table], axis=-1)

def product(left_side, right_side):
    return jnp.dot(left_side, right_side, precision=HIGHEST)

def attend(begin_row, queries, key_rows, value_rows, seg_ids, token_index):
    block_rows = min(512, key_rows.shape[0])
    q_block = lax.dynamic_slice_in_dim(queries, begin_row, block_rows, 0)
    q_index = lax.dynamic_slice_in_dim(token_index, begin_row, block_rows, 0)
    q_seg = lax.dynamic_slice_in_dim(seg_ids, begin_row, block_rows, 0)
    scores = low_back(SCALE * jnp.einsum('qhd,kd->hqk', q_block, key_rows, precision=HIGHEST))
    allowed = (seg_ids[None, :] == q_seg[:, None]) & (seg_ids[None, :] != 0) & (token_index[None, :] <= q_index[:, None]) | (token_index[None, :] == q_index[:, None])
    masked = jnp.where(allowed[None], scores, NEGATIVE)
    shifted = jnp.exp(masked - lax.optimization_barrier(jnp.max(masked, axis=-1, keepdims=True)))
    probabilities = shifted / lax.optimization_barrier(jnp.sum(shifted, axis=-1, keepdims=True))
    return jnp.einsum('hqk,kd->qhd', low(probabilities), value_rows, precision=HIGHEST)

def block_layer(inputs, seg_ids, weight_set):
    w_query, w_key, w_value, w_out, w_gate, w_up, w_down, g_input, g_post_attn, g_pre_ffn, g_post_ffn, g_query, g_key = weight_set
    length = inputs.shape[0]
    position = jnp.arange(length, dtype=jnp.float32)
    token_index = jnp.arange(length, dtype=jnp.int32)
    cosine, sine_table = angles(position, HD // 2, HD)
    hidden_one = low(normed(inputs, g_input))
    q_raw = low_back(product(hidden_one, w_query)).reshape(length, H, HD)
    k_raw = low_back(product(hidden_one, w_key))
    v_raw = low_back(product(hidden_one, w_value))
    queries = low(rotate(normed(q_raw, g_query), cosine[:, None, :], sine_table[:, None, :]))
    key_rows = low(rotate(normed(k_raw, g_key), cosine, sine_table))
    value_rows = low(v_raw)
    block_rows = min(512, length)
    block_starts = jnp.arange(0, length, block_rows, dtype=jnp.int32)
    head_out = lax.map(lambda begin_row: jax.checkpoint(attend)(begin_row, queries, key_rows, value_rows, seg_ids, token_index), block_starts)
    head_out = low_back(low(head_out.reshape(length, H * HD)))
    attn_out = low_back(product(head_out, w_out))
    middle = inputs + normed(attn_out, g_post_attn)
    hidden_two = low(normed(middle, g_pre_ffn))
    gate_proj = low_back(product(hidden_two, w_gate))
    up_proj = low_back(product(hidden_two, w_up))
    hidden_ffn = low(jax.nn.gelu(gate_proj, approximate=True) * up_proj)
    ffn_out = low_back(product(hidden_ffn, w_down))
    return middle + normed(ffn_out, g_post_ffn)

def true_order(stored):
    return jnp.concatenate([stored[:, :, 0], jnp.flip(stored[:, :, 1], axis=2)], axis=2)

def to_stored(ordered):
    half_len = ordered.shape[2] // 2
    return jnp.stack([ordered[:, :, :half_len], jnp.flip(ordered[:, :, half_len:], axis=2)], axis=2)

def reference(tokens, segments, cotangent, w_query, w_key, w_value, w_out, w_gate, w_up, w_down, g_input, g_post_attn, g_pre_ffn, g_post_ffn, g_query, g_key):
    seq_total = MB * SEQS
    inputs = true_order(tokens.astype(jnp.float32)).reshape(seq_total, SEQ_LEN, D)
    seg_all = true_order(segments).reshape(seq_total, SEQ_LEN)
    upstream = true_order(cotangent.astype(jnp.float32)).reshape(seq_total, SEQ_LEN, D)
    weight_set = (w_query.astype(jnp.float32), w_key.astype(jnp.float32), w_value.astype(jnp.float32), w_out.astype(jnp.float32), w_gate.astype(jnp.float32), w_up.astype(jnp.float32), w_down.astype(jnp.float32), g_input.astype(jnp.float32), g_post_attn.astype(jnp.float32), g_pre_ffn.astype(jnp.float32), g_post_ffn.astype(jnp.float32), g_query.astype(jnp.float32), g_key.astype(jnp.float32))

    def forward(all_inputs, all_weights):

        def per_sequence(seq_pair):
            return jax.checkpoint(block_layer)(seq_pair[0], seq_pair[1], all_weights)
        return lax.map(per_sequence, (all_inputs, seg_all))
    outputs, pull_back = jax.vjp(forward, inputs, weight_set)
    d_inputs, d_weights = pull_back(upstream)
    output = to_stored(outputs.reshape(MB, SEQS, SEQ_LEN, D)).astype(jnp.bfloat16)
    d_tokens = to_stored(d_inputs.reshape(MB, SEQS, SEQ_LEN, D))
    return (output, d_tokens, d_weights[0], d_weights[1], d_weights[2], d_weights[3], d_weights[4], d_weights[5], d_weights[6], d_weights[7], d_weights[8], d_weights[9], d_weights[10], d_weights[11], d_weights[12])
```

```python
import functools

import jax
import jax.numpy as jnp
from jax import lax
from jax.experimental import pallas as pl
from jax.experimental.pallas import tpu as pltpu
from jax.sharding import PartitionSpec as P

EPS = 1e-06
THETA = 1000000.0
SCALE = 0.0625
NEGATIVE = -1e30
BF16 = jnp.bfloat16
F32 = jnp.float32
MESH = pl.DeviceIdType.MESH
NN = (((1,), (0,)), ((), ()))
NT = (((1,), (1,)), ((), ()))
TN = (((0,), (0,)), ((), ()))


def dot(a, b, dims=NN):
    return lax.dot_general(a, b, dims, preferred_element_type=F32)


def barrier_line(z):
    bar = pltpu.get_barrier_semaphore()

    @pl.when(z > 0)
    def _():
        pl.semaphore_signal(bar, inc=1, device_id={"tp": z - 1}, device_id_type=MESH)

    @pl.when(z < 3)
    def _():
        pl.semaphore_signal(bar, inc=1, device_id={"tp": z + 1}, device_id_type=MESH)

    pl.semaphore_wait(bar, jnp.where((z == 0) | (z == 3), 1, 2))


def sum_kernel(n, tile, x_ref, o_ref, own, got, pair, other, *sems):
    lsem, ssem1, rsem1, ssem2, rsem2, ssem3, rsem3, osem = sems
    z = lax.axis_index("tp")
    hub = (z == 1) | (z == 2)
    leaf = jnp.logical_not(hub)
    other_hub = jnp.where(z == 1, 2, 1)
    my_hub = jnp.where(z == 0, 1, 2)
    my_leaf = jnp.where(z == 1, 0, 3)
    barrier_line(z)

    def rows(t):
        return pl.ds(t * tile, tile)

    def up(t):
        return pltpu.make_async_remote_copy(
            x_ref.at[rows(t)], got.at[rows(t)], ssem1.at[t], rsem1.at[t],
            device_id={"tp": my_hub}, device_id_type=MESH)

    def across(t):
        return pltpu.make_async_remote_copy(
            pair.at[rows(t)], other.at[rows(t)], ssem2.at[t], rsem2.at[t],
            device_id={"tp": other_hub}, device_id_type=MESH)

    def back(t):
        return pltpu.make_async_remote_copy(
            own.at[rows(t)], o_ref.at[rows(t)], ssem3.at[t], rsem3.at[t],
            device_id={"tp": my_leaf}, device_id_type=MESH)

    def load(t):
        return pltpu.make_async_copy(x_ref.at[rows(t)], own.at[rows(t)], lsem.at[t])

    def store(t):
        return pltpu.make_async_copy(own.at[rows(t)], o_ref.at[rows(t)], osem.at[t])

    @pl.when(leaf)
    def _():
        for t in range(n):
            up(t).start()
        for t in range(n):
            back(t).wait_recv()
        for t in range(n):
            up(t).wait_send()

    @pl.when(hub)
    def _():
        for t in range(n):
            load(t).start()

        def finish(t):
            across(t).wait_recv()
            own[rows(t), :] = (pair[rows(t), :].astype(F32) + other[rows(t), :].astype(F32)).astype(BF16)
            back(t).start()
            store(t).start()

        for t in range(n):
            load(t).wait()
            up(t).wait_recv()
            pair[rows(t), :] = (own[rows(t), :].astype(F32) + got[rows(t), :].astype(F32)).astype(BF16)
            across(t).start()
            if t > 0:
                finish(t - 1)
        finish(n - 1)
        for t in range(n):
            across(t).wait_send()
            back(t).wait_send()
            store(t).wait()


def sum_tp(x, ident):
    rows, cols = x.shape
    tile = 128 if rows % 128 == 0 else rows
    n = rows // tile
    dma = pltpu.SemaphoreType.DMA((n,))
    return pl.pallas_call(
        functools.partial(sum_kernel, n, tile),
        out_shape=jax.ShapeDtypeStruct((rows, cols), BF16),
        in_specs=[pl.BlockSpec(memory_space=pl.ANY)],
        out_specs=pl.BlockSpec(memory_space=pl.ANY),
        scratch_shapes=[pltpu.VMEM((rows, cols), BF16)] * 4 + [dma] * 8,
        compiler_params=pltpu.CompilerParams(
            collective_id=ident, has_side_effects=True, vmem_limit_bytes=40 * 2**20),
        name=f"sum_tp_{ident}",
    )(x)


def gather_kernel(n, tile, width, x_ref, o_ref, lsem, *sems):
    su, ru, sd, rd = sems
    z = lax.axis_index("tp")
    barrier_line(z)

    def place(src, t):
        return o_ref.at[pl.ds(t * tile, tile), pl.ds(pl.multiple_of(src * width, width), width)]

    def send(src, t, k, way):
        ss, rs = (su, ru) if way > 0 else (sd, rd)
        here = x_ref.at[pl.ds(t * tile, tile)] if k == 0 else place(src, t)
        return pltpu.make_async_remote_copy(
            here, place(src, t), ss.at[k, t], rs.at[k, t],
            device_id={"tp": z + way}, device_id_type=MESH)

    own = pltpu.make_async_copy(x_ref, o_ref.at[:, pl.ds(pl.multiple_of(z * width, width), width)], lsem)
    own.start()
    for k in range(3):
        for t in range(n):
            for way in (1, -1):
                src = z - way * k
                ok = (z + way >= 0) & (z + way <= 3) & (src >= 0) & (src <= 3)
                if k > 0:
                    came = (src >= 0) & (src <= 3)

                    @pl.when(came)
                    def _():
                        send(src, t, k - 1, way).wait_recv()

                @pl.when(ok)
                def _():
                    send(src, t, k, way).start()
    for way in (1, -1):
        src = z - way * 3
        came = (src >= 0) & (src <= 3)

        @pl.when(came)
        def _():
            for t in range(n):
                send(src, t, 2, way).wait_recv()

    for k in range(3):
        for way in (1, -1):
            src = z - way * k
            ok = (z + way >= 0) & (z + way <= 3) & (src >= 0) & (src <= 3)

            @pl.when(ok)
            def _():
                for t in range(n):
                    send(src, t, k, way).wait_send()
    own.wait()


def gather_tp(x, ident):
    rows, width = x.shape
    tile = 256 if rows % 256 == 0 else rows
    n = rows // tile
    dma = pltpu.SemaphoreType.DMA((3, n))
    return pl.pallas_call(
        functools.partial(gather_kernel, n, tile, width),
        out_shape=jax.ShapeDtypeStruct((rows, 4 * width), x.dtype),
        in_specs=[pl.BlockSpec(memory_space=pl.ANY)],
        out_specs=pl.BlockSpec(memory_space=pl.ANY),
        scratch_shapes=[pltpu.SemaphoreType.DMA] + [dma] * 4,
        compiler_params=pltpu.CompilerParams(collective_id=ident, has_side_effects=True),
        name=f"gather_tp_{ident}",
    )(x)


def block_starts(half, t, blocks, rank):
    if half == 0:
        return t
    return jnp.where(t < blocks, t, t + rank + 1)


def attend_kernel(blocks, q_ref, k_ref, v_ref, qs_ref, ks_ref, o_ref, l_ref):
    rank = lax.axis_index("ctx")
    size = q_ref.shape[2]
    row = lax.broadcasted_iota(jnp.int32, (size, size), 0)
    col = lax.broadcasted_iota(jnp.int32, (size, size), 1)
    for half in range(2):
        q = q_ref[0, half] * jnp.asarray(SCALE, BF16)
        qseg = qs_ref[0, half]

        def part(block):
            start = pl.multiple_of(block * size, size)
            k = k_ref[0, pl.ds(start, size), :]
            v = v_ref[0, pl.ds(start, size), :]
            same = qseg == ks_ref[0, :, pl.ds(start, size)]
            return dot(q, k, NT), v, same

        s, v, same = part(rank + half * blocks)
        order = (col <= row) if half == 0 else (col >= row)
        s = jnp.where((same & order) | (col == row), s, NEGATIVE)
        top = jnp.max(s, axis=1, keepdims=True)
        p = jnp.exp(s - top)
        mass = jnp.sum(p, axis=1, keepdims=True)
        acc = dot(p.astype(BF16), v)

        def step(t, carry):
            top, mass, acc = carry
            s, v, same = part(block_starts(half, t, blocks, rank))
            s = jnp.where(same, s, NEGATIVE)
            new = jnp.maximum(top, jnp.max(s, axis=1, keepdims=True))
            keep = jnp.exp(top - new)
            p = jnp.exp(s - new)
            mass = mass * keep + jnp.sum(p, axis=1, keepdims=True)
            acc = acc * keep + dot(p.astype(BF16), v)
            return new, mass, acc

        count = rank if half == 0 else 2 * blocks - 1 - rank
        top, mass, acc = lax.fori_loop(0, count, step, (top, mass, acc))
        o_ref[0, half] = (acc / mass).astype(BF16)
        l_ref[0, half] = top + jnp.log(mass)


def attend(q, k, v, qseg, kseg):
    groups, _, size, head = q.shape
    length = k.shape[1]
    blocks = length // (2 * size)
    return pl.pallas_call(
        functools.partial(attend_kernel, blocks),
        grid=(groups,),
        out_shape=(
            jax.ShapeDtypeStruct(q.shape, BF16),
            jax.ShapeDtypeStruct((groups, 2, size, 1), F32),
        ),
        in_specs=[
            pl.BlockSpec((1, 2, size, head), lambda g: (g, 0, 0, 0)),
            pl.BlockSpec((1, length, head), lambda g: (g, 0, 0)),
            pl.BlockSpec((1, length, head), lambda g: (g, 0, 0)),
            pl.BlockSpec((1, 2, size, 1), lambda g: (g, 0, 0, 0)),
            pl.BlockSpec((1, 1, length), lambda g: (g, 0, 0)),
        ],
        out_specs=(
            pl.BlockSpec((1, 2, size, head), lambda g: (g, 0, 0, 0)),
            pl.BlockSpec((1, 2, size, 1), lambda g: (g, 0, 0, 0)),
        ),
        compiler_params=pltpu.CompilerParams(vmem_limit_bytes=48 * 2**20),
        name="attend",
    )(q, k, v, qseg, kseg)


def attend_back_kernel(blocks, q_ref, k_ref, v_ref, do_ref, l_ref, d_ref, qs_ref, ks_ref,
                       dq_ref, dkv_ref, dk_acc, dv_acc):
    rank = lax.axis_index("ctx")
    size = q_ref.shape[2]
    head = q_ref.shape[3]
    row = lax.broadcasted_iota(jnp.int32, (size, size), 0)
    col = lax.broadcasted_iota(jnp.int32, (size, size), 1)
    dk_acc[...] = jnp.zeros_like(dk_acc)
    dv_acc[...] = jnp.zeros_like(dv_acc)
    for half in range(2):
        q = q_ref[0, half] * jnp.asarray(SCALE, BF16)
        do = do_ref[0, half]
        qseg = qs_ref[0, half]
        log_mass = l_ref[0, half]
        delta = d_ref[0, half]

        def part(block, own):
            rows = pl.ds(pl.multiple_of(block * size, size), size)
            k = k_ref[0, rows, :]
            v = v_ref[0, rows, :]
            allowed = ks_ref[0, rows, :] == qseg
            if own:
                order = (row <= col) if half == 0 else (row >= col)
                allowed = (allowed & order) | (col == row)
            s = jnp.where(allowed, dot(k, q, NT), NEGATIVE)
            p = jnp.exp(s - log_mass)
            ds = (p * (dot(v, do, NT) - delta)).astype(BF16)
            dv_acc[rows, :] += dot(p.astype(BF16), do)
            dk_acc[rows, :] += dot(ds, q)
            return dot(ds, k, TN)

        def step(t, dq):
            return dq + part(block_starts(half, t, blocks, rank), False)

        dq = part(rank + half * blocks, True)
        count = rank if half == 0 else 2 * blocks - 1 - rank
        dq_ref[0, half] = SCALE * lax.fori_loop(0, count, step, dq)
    dkv_ref[0, :, :head] = dk_acc[...].astype(BF16)
    dkv_ref[0, :, head:] = dv_acc[...].astype(BF16)


def attend_back(q, k, v, do, log_mass, delta, qseg, kseg):
    groups, _, size, head = q.shape
    length = k.shape[1]
    blocks = length // (2 * size)
    halves = pl.BlockSpec((1, 2, size, head), lambda g: (g, 0, 0, 0))
    whole = pl.BlockSpec((1, length, head), lambda g: (g, 0, 0))
    line = pl.BlockSpec((1, 2, 1, size), lambda g: (g, 0, 0, 0))
    return pl.pallas_call(
        functools.partial(attend_back_kernel, blocks),
        grid=(groups,),
        out_shape=(
            jax.ShapeDtypeStruct(q.shape, F32),
            jax.ShapeDtypeStruct((groups, length, 2 * head), BF16),
        ),
        in_specs=[halves, whole, whole, halves, line, line, line,
                  pl.BlockSpec((1, length, 1), lambda g: (g, 0, 0))],
        out_specs=(halves, pl.BlockSpec((1, length, 2 * head), lambda g: (g, 0, 0))),
        scratch_shapes=[pltpu.VMEM((length, head), F32)] * 2,
        compiler_params=pltpu.CompilerParams(vmem_limit_bytes=56 * 2**20),
        name="attend_back",
    )(q, k, v, do, log_mass, delta, qseg, kseg)


def angles(position, half_size, full_size):
    frequency = THETA ** (-2.0 * jnp.arange(half_size, dtype=F32) / full_size)
    turned = position[:, None] * frequency[None, :]
    return (jnp.cos(turned), jnp.sin(turned))


def rotate(tensor, cosine, sine):
    half_size = tensor.shape[-1] // 2
    a = tensor[..., :half_size]
    b = tensor[..., half_size:]
    return jnp.concatenate([a * cosine - b * sine, b * cosine + a * sine], axis=-1)


def norm_parts(values):
    inv = lax.rsqrt(jnp.mean(values * values, axis=-1, keepdims=True) + EPS)
    return (values * inv, inv)


def norm_back(upstream, normalized, inv, gain):
    d_norm = upstream * (1.0 + gain)
    d_values = inv * (d_norm - normalized * jnp.mean(d_norm * normalized, axis=-1, keepdims=True))
    return (d_values, jnp.sum(upstream * normalized, axis=0))


def gelu_tanh(values):
    return jax.nn.gelu(values, approximate=True)


def shards(tokens, segments, cotangent, w_query, w_key, w_value, w_out, w_gate, w_up, w_down,
           g_input, g_post_attn, g_pre_ffn, g_post_ffn, g_query, g_key):
    batches, seq_local, _, size, width = tokens.shape
    head = w_key.shape[1]
    groups = batches * seq_local
    per_group = 2 * size
    rows = groups * per_group
    ctx = lax.axis_size("ctx")
    length = per_group * ctx
    rank = lax.axis_index("ctx")
    shared = ("dp", "ctx")
    own_rows = g_input.shape[0]
    hidden = w_gate.shape[1]

    def column(gain):
        return jnp.pad(gain, (0, own_rows - gain.shape[0]))[:, None]

    gains = jnp.concatenate([column(g) for g in (g_input, g_post_attn, g_pre_ffn, g_post_ffn, g_query, g_key)], axis=1)
    gains = jnp.pad(gains, ((0, 0), (0, 128 - gains.shape[1])))
    first = lax.all_gather(
        jnp.concatenate([w_query, w_key, w_value, gains], axis=1), shared, axis=0, tiled=True)
    key_ids = lax.all_gather(segments, "ctx", axis=3, tiled=True).reshape(groups, length)
    both = lax.all_gather(
        jnp.concatenate([w_query, w_out.T], axis=1), ("dp", "ctx", "tp"), axis=0, tiled=True)
    both = both.reshape(width // own_rows, 4, own_rows, 2 * head)
    both = both.transpose(0, 2, 3, 1).reshape(width, 2, head, 4).transpose(0, 1, 3, 2)
    query_full = both[:, 0].reshape(width, 4 * head)
    out_full = both[:, 1].reshape(width, 4 * head)
    ffn = lax.all_gather(
        jnp.concatenate([w_gate, w_up, w_down.T], axis=1), shared, axis=0, tiled=True)
    mat_qkv = first[:, : 3 * head]
    gain_cols = first[:, 3 * head :].astype(F32)
    gain_input, gain_post_attn, gain_pre_ffn, gain_post_ffn = (gain_cols[:, i] for i in range(4))
    short = g_query.shape[0]
    gain_query, gain_key = (
        gain_cols[:, i].reshape(-1, own_rows)[:, :short].reshape(-1) for i in (4, 5))
    mat_gate, mat_up, mat_down_t = ffn[:, :hidden], ffn[:, hidden : 2 * hidden], ffn[:, 2 * hidden :]
    tp_rank = lax.axis_index("tp")
    mat_out_t = lax.dynamic_slice_in_dim(out_full, tp_rank * head, head, axis=1)

    offsets = rank * size + jnp.arange(size, dtype=jnp.int32)
    position = jnp.concatenate([offsets, length - 1 - offsets]).astype(F32)
    cosine, sine = angles(position, head // 2, head)
    cosine = jnp.broadcast_to(cosine, (groups, per_group, head // 2)).reshape(rows, head // 2)
    sine = jnp.broadcast_to(sine, (groups, per_group, head // 2)).reshape(rows, head // 2)
    key_ids = jnp.where(key_ids == 0, -1, key_ids)
    own_ids = segments.reshape(groups, 2, size)

    inputs = tokens.reshape(rows, width).astype(F32)
    upstream = cotangent.reshape(rows, width).astype(F32)

    norm_one, scale_one = norm_parts(inputs)
    hidden_one = (norm_one * (1.0 + gain_input)).astype(BF16)
    raw = dot(hidden_one, mat_qkv)
    q_hat, q_scale = norm_parts(raw[:, :head])
    k_hat, k_scale = norm_parts(raw[:, head : 2 * head])
    queries = rotate(q_hat * (1.0 + gain_query), cosine, sine).astype(BF16)
    keys = rotate(k_hat * (1.0 + gain_key), cosine, sine).astype(BF16)
    values = raw[:, 2 * head :].astype(BF16)
    queries = queries.reshape(groups, 2, size, head)
    key_all = lax.all_gather(keys.reshape(groups, 2, size, head), "ctx", axis=2, tiled=True)
    value_all = lax.all_gather(values.reshape(groups, 2, size, head), "ctx", axis=2, tiled=True)
    key_all = key_all.reshape(groups, length, head)
    value_all = value_all.reshape(groups, length, head)
    heads, log_mass = attend(queries, key_all, value_all, own_ids[..., None], key_ids[:, None, :])
    heads_own = heads.reshape(rows, head)
    heads_all = gather_tp(heads_own, 0)
    attn = dot(heads_all, out_full, NT)
    norm_attn, scale_attn = norm_parts(attn)
    middle = inputs + norm_attn * (1.0 + gain_post_attn)
    norm_two, scale_two = norm_parts(middle)
    hidden_two = (norm_two * (1.0 + gain_pre_ffn)).astype(BF16)

    gate = dot(hidden_two, mat_gate)
    up = dot(hidden_two, mat_up)
    activated, gelu_pull = jax.vjp(gelu_tanh, gate)
    hidden_ffn = (activated * up).astype(BF16)
    ffn_out = sum_tp(dot(hidden_ffn, mat_down_t, NT).astype(BF16), 1).astype(F32)
    norm_ffn, scale_ffn = norm_parts(ffn_out)
    output = (middle + norm_ffn * (1.0 + gain_post_ffn)).astype(BF16)
    d_ffn, d_gain_post_ffn = norm_back(upstream, norm_ffn, scale_ffn, gain_post_ffn)
    d_ffn = d_ffn.astype(BF16)
    d_hidden = dot(d_ffn, mat_down_t)
    (d_gate,) = gelu_pull(d_hidden * up)
    d_gate = d_gate.astype(BF16)
    d_up = (d_hidden * activated).astype(BF16)
    d_two = sum_tp((dot(d_gate, mat_gate, NT) + dot(d_up, mat_up, NT)).astype(BF16), 2).astype(F32)
    grad_ffn = jnp.concatenate(
        [dot(hidden_two, d_gate, TN).astype(BF16), dot(hidden_two, d_up, TN).astype(BF16),
         dot(d_ffn, hidden_ffn, TN).astype(BF16)], axis=1)
    grad_ffn = lax.psum_scatter(grad_ffn, shared, scatter_dimension=0, tiled=True).astype(F32)
    d_part, d_gain_pre_ffn = norm_back(d_two, norm_two, scale_two, gain_pre_ffn)
    d_middle = upstream + d_part
    d_attn, d_gain_post_attn = norm_back(d_middle, norm_attn, scale_attn, gain_post_attn)
    d_attn = d_attn.astype(BF16)

    grad_out_t = dot(d_attn, heads_own, TN)
    d_heads = dot(d_attn, mat_out_t).astype(BF16)
    delta = jnp.sum(d_heads.astype(F32) * heads_own.astype(F32), axis=-1)
    d_query, d_kv = attend_back(
        queries, key_all, value_all, d_heads.reshape(groups, 2, size, head),
        log_mass.reshape(groups, 2, 1, size), delta.reshape(groups, 2, 1, size),
        own_ids[:, :, None, :], key_ids[:, :, None])
    d_kv = lax.psum_scatter(
        d_kv.reshape(groups, 2, length // 2, 2 * head), "ctx", scatter_dimension=2, tiled=True)
    d_kv = sum_tp(d_kv.reshape(rows, 2 * head), 3).astype(F32)
    d_q_rot = rotate(d_query.reshape(rows, head), cosine, -sine)
    d_q_raw, d_gain_query = norm_back(d_q_rot, q_hat, q_scale, gain_query)
    d_q_raw = d_q_raw.astype(BF16)
    d_q_all = gather_tp(d_q_raw, 4)
    d_k_rot = rotate(d_kv[:, :head], cosine, -sine)
    d_k_raw, d_gain_key = norm_back(d_k_rot, k_hat, k_scale, gain_key)
    d_kv_raw = jnp.concatenate([d_k_raw.astype(BF16), d_kv[:, head:].astype(BF16)], axis=1)
    d_one = dot(d_q_all, query_full, NT) + dot(d_kv_raw, mat_qkv[:, head:], NT)
    d_part, d_gain_input = norm_back(d_one, norm_one, scale_one, gain_input)
    d_tokens = d_middle + d_part
    d_gain_query = lax.psum(d_gain_query, "tp")

    def spread(vector):
        return jnp.pad(vector.reshape(-1, short), ((0, 0), (0, own_rows - short))).reshape(-1)

    d_gains = jnp.stack(
        [d_gain_input, d_gain_post_attn, d_gain_pre_ffn, d_gain_post_ffn, spread(d_gain_query), spread(d_gain_key)], axis=1)
    d_gains = jnp.pad(d_gains, ((0, 0), (0, 128 - d_gains.shape[1]))).astype(BF16)
    last = jnp.concatenate(
        [dot(hidden_one, d_q_raw, TN).astype(BF16), dot(hidden_one, d_kv_raw, TN).astype(BF16),
         grad_out_t.astype(BF16), d_gains], axis=1)
    last = lax.psum_scatter(last, shared, scatter_dimension=0, tiled=True).astype(F32)
    g = last[:, 4 * head :]
    return (
        output.reshape(tokens.shape),
        d_tokens.reshape(tokens.shape),
        last[:, :head],
        last[:, head : 2 * head],
        last[:, 2 * head : 3 * head],
        last[:, 3 * head : 4 * head].T,
        grad_ffn[:, :hidden],
        grad_ffn[:, hidden : 2 * hidden],
        grad_ffn[:, 2 * hidden :].T,
        g[:, 0],
        g[:, 1],
        g[:, 2],
        g[:, 3],
        g[:short, 4],
        g[:short, 5],
    )


def solution(mesh):
    shared = ("dp", "ctx")
    rows = P(None, "dp", None, "ctx", None)
    weights = (
        P(shared, "tp"), P(shared, None), P(shared, None), P("tp", shared),
        P(shared, "tp"), P(shared, "tp"), P("tp", shared),
    )
    gains = (P(shared),) * 6
    return jax.shard_map(
        shards,
        mesh=mesh,
        in_specs=(rows, P(None, "dp", None, "ctx"), rows) + weights + gains,
        out_specs=(rows, rows) + weights + gains,
        check_vma=False,
    )
```

```python
import functools

import jax
import jax.numpy as jnp
from jax import lax
from jax.experimental import pallas as pl
from jax.experimental.pallas import tpu as pltpu
from jax.sharding import PartitionSpec as P

EPS = 1e-06
THETA = 1000000.0
SCALE = 0.0625
NEGATIVE = -1e30
BF16 = jnp.bfloat16
F32 = jnp.float32
MESH = pl.DeviceIdType.MESH
NN = (((1,), (0,)), ((), ()))
NT = (((1,), (1,)), ((), ()))
TN = (((0,), (0,)), ((), ()))


def dot(a, b, dims=NN):
    return lax.dot_general(a, b, dims, preferred_element_type=F32)


def barrier_line(z):
    bar = pltpu.get_barrier_semaphore()

    @pl.when(z > 0)
    def _():
        pl.semaphore_signal(bar, inc=1, device_id={"tp": z - 1}, device_id_type=MESH)

    @pl.when(z < 3)
    def _():
        pl.semaphore_signal(bar, inc=1, device_id={"tp": z + 1}, device_id_type=MESH)

    pl.semaphore_wait(bar, jnp.where((z == 0) | (z == 3), 1, 2))


def sum_kernel(n, tile, x_ref, o_ref, own, got, pair, other, *sems):
    lsem, ssem1, rsem1, ssem2, rsem2, ssem3, rsem3, osem = sems
    z = lax.axis_index("tp")
    hub = (z == 1) | (z == 2)
    leaf = jnp.logical_not(hub)
    other_hub = jnp.where(z == 1, 2, 1)
    my_hub = jnp.where(z == 0, 1, 2)
    my_leaf = jnp.where(z == 1, 0, 3)
    barrier_line(z)

    def rows(t):
        return pl.ds(t * tile, tile)

    def up(t):
        return pltpu.make_async_remote_copy(
            x_ref.at[rows(t)], got.at[rows(t)], ssem1.at[t], rsem1.at[t],
            device_id={"tp": my_hub}, device_id_type=MESH)

    def across(t):
        return pltpu.make_async_remote_copy(
            pair.at[rows(t)], other.at[rows(t)], ssem2.at[t], rsem2.at[t],
            device_id={"tp": other_hub}, device_id_type=MESH)

    def back(t):
        return pltpu.make_async_remote_copy(
            own.at[rows(t)], o_ref.at[rows(t)], ssem3.at[t], rsem3.at[t],
            device_id={"tp": my_leaf}, device_id_type=MESH)

    def load(t):
        return pltpu.make_async_copy(x_ref.at[rows(t)], own.at[rows(t)], lsem.at[t])

    def store(t):
        return pltpu.make_async_copy(own.at[rows(t)], o_ref.at[rows(t)], osem.at[t])

    @pl.when(leaf)
    def _():
        for t in range(n):
            up(t).start()
        for t in range(n):
            back(t).wait_recv()
        for t in range(n):
            up(t).wait_send()

    @pl.when(hub)
    def _():
        for t in range(n):
            load(t).start()

        def finish(t):
            across(t).wait_recv()
            own[rows(t), :] = (pair[rows(t), :].astype(F32) + other[rows(t), :].astype(F32)).astype(BF16)
            back(t).start()
            store(t).start()

        for t in range(n):
            load(t).wait()
            up(t).wait_recv()
            pair[rows(t), :] = (own[rows(t), :].astype(F32) + got[rows(t), :].astype(F32)).astype(BF16)
            across(t).start()
            if t > 0:
                finish(t - 1)
        finish(n - 1)
        for t in range(n):
            across(t).wait_send()
            back(t).wait_send()
            store(t).wait()


def sum_tp(x, ident):
    rows, cols = x.shape
    tile = 128 if rows % 128 == 0 else rows
    n = rows // tile
    dma = pltpu.SemaphoreType.DMA((n,))
    return pl.pallas_call(
        functools.partial(sum_kernel, n, tile),
        out_shape=jax.ShapeDtypeStruct((rows, cols), BF16),
        in_specs=[pl.BlockSpec(memory_space=pl.ANY)],
        out_specs=pl.BlockSpec(memory_space=pl.ANY),
        scratch_shapes=[pltpu.VMEM((rows, cols), BF16)] * 4 + [dma] * 8,
        compiler_params=pltpu.CompilerParams(
            collective_id=ident, has_side_effects=True, vmem_limit_bytes=40 * 2**20),
        name=f"sum_tp_{ident}",
    )(x)


def gather_kernel(n, tile, width, x_ref, o_ref, lsem, *sems):
    su, ru, sd, rd = sems
    z = lax.axis_index("tp")
    barrier_line(z)

    def place(src, t):
        return o_ref.at[pl.ds(t * tile, tile), pl.ds(pl.multiple_of(src * width, width), width)]

    def send(src, t, k, way):
        ss, rs = (su, ru) if way > 0 else (sd, rd)
        here = x_ref.at[pl.ds(t * tile, tile)] if k == 0 else place(src, t)
        return pltpu.make_async_remote_copy(
            here, place(src, t), ss.at[k, t], rs.at[k, t],
            device_id={"tp": z + way}, device_id_type=MESH)

    own = pltpu.make_async_copy(x_ref, o_ref.at[:, pl.ds(pl.multiple_of(z * width, width), width)], lsem)
    own.start()
    for k in range(3):
        for t in range(n):
            for way in (1, -1):
                src = z - way * k
                ok = (z + way >= 0) & (z + way <= 3) & (src >= 0) & (src <= 3)
                if k > 0:
                    came = (src >= 0) & (src <= 3)

                    @pl.when(came)
                    def _():
                        send(src, t, k - 1, way).wait_recv()

                @pl.when(ok)
                def _():
                    send(src, t, k, way).start()
    for way in (1, -1):
        src = z - way * 3
        came = (src >= 0) & (src <= 3)

        @pl.when(came)
        def _():
            for t in range(n):
                send(src, t, 2, way).wait_recv()

    for k in range(3):
        for way in (1, -1):
            src = z - way * k
            ok = (z + way >= 0) & (z + way <= 3) & (src >= 0) & (src <= 3)

            @pl.when(ok)
            def _():
                for t in range(n):
                    send(src, t, k, way).wait_send()
    own.wait()


def gather_tp(x, ident):
    rows, width = x.shape
    tile = 256 if rows % 256 == 0 else rows
    n = rows // tile
    dma = pltpu.SemaphoreType.DMA((3, n))
    return pl.pallas_call(
        functools.partial(gather_kernel, n, tile, width),
        out_shape=jax.ShapeDtypeStruct((rows, 4 * width), x.dtype),
        in_specs=[pl.BlockSpec(memory_space=pl.ANY)],
        out_specs=pl.BlockSpec(memory_space=pl.ANY),
        scratch_shapes=[pltpu.SemaphoreType.DMA] + [dma] * 4,
        compiler_params=pltpu.CompilerParams(collective_id=ident, has_side_effects=True),
        name=f"gather_tp_{ident}",
    )(x)


def block_starts(half, t, blocks, rank):
    if half == 0:
        return t
    return jnp.where(t < blocks, t, t + rank + 1)


def attend_kernel(blocks, q_ref, k_ref, v_ref, qs_ref, ks_ref, o_ref, l_ref):
    rank = lax.axis_index("ctx")
    size = q_ref.shape[2]
    row = lax.broadcasted_iota(jnp.int32, (size, size), 0)
    col = lax.broadcasted_iota(jnp.int32, (size, size), 1)
    for half in range(2):
        q = q_ref[0, half] * jnp.asarray(SCALE, BF16)
        qseg = qs_ref[0, half]

        def part(block):
            start = pl.multiple_of(block * size, size)
            k = k_ref[0, pl.ds(start, size), :]
            v = v_ref[0, pl.ds(start, size), :]
            same = qseg == ks_ref[0, :, pl.ds(start, size)]
            return dot(q, k, NT), v, same

        s, v, same = part(rank + half * blocks)
        order = (col <= row) if half == 0 else (col >= row)
        s = jnp.where((same & order) | (col == row), s, NEGATIVE)
        top = jnp.max(s, axis=1, keepdims=True)
        p = jnp.exp(s - top)
        mass = jnp.sum(p, axis=1, keepdims=True)
        acc = dot(p.astype(BF16), v)

        def step(t, carry):
            top, mass, acc = carry
            s, v, same = part(block_starts(half, t, blocks, rank))
            s = jnp.where(same, s, NEGATIVE)
            new = jnp.maximum(top, jnp.max(s, axis=1, keepdims=True))
            keep = jnp.exp(top - new)
            p = jnp.exp(s - new)
            mass = mass * keep + jnp.sum(p, axis=1, keepdims=True)
            acc = acc * keep + dot(p.astype(BF16), v)
            return new, mass, acc

        count = rank if half == 0 else 2 * blocks - 1 - rank
        top, mass, acc = lax.fori_loop(0, count, step, (top, mass, acc))
        o_ref[0, half] = (acc / mass).astype(BF16)
        l_ref[0, half] = top + jnp.log(mass)


def attend(q, k, v, qseg, kseg):
    groups, _, size, head = q.shape
    length = k.shape[1]
    blocks = length // (2 * size)
    return pl.pallas_call(
        functools.partial(attend_kernel, blocks),
        grid=(groups,),
        out_shape=(
            jax.ShapeDtypeStruct(q.shape, BF16),
            jax.ShapeDtypeStruct((groups, 2, size, 1), F32),
        ),
        in_specs=[
            pl.BlockSpec((1, 2, size, head), lambda g: (g, 0, 0, 0)),
            pl.BlockSpec((1, length, head), lambda g: (g, 0, 0)),
            pl.BlockSpec((1, length, head), lambda g: (g, 0, 0)),
            pl.BlockSpec((1, 2, size, 1), lambda g: (g, 0, 0, 0)),
            pl.BlockSpec((1, 1, length), lambda g: (g, 0, 0)),
        ],
        out_specs=(
            pl.BlockSpec((1, 2, size, head), lambda g: (g, 0, 0, 0)),
            pl.BlockSpec((1, 2, size, 1), lambda g: (g, 0, 0, 0)),
        ),
        compiler_params=pltpu.CompilerParams(vmem_limit_bytes=48 * 2**20),
        name="attend",
    )(q, k, v, qseg, kseg)


def attend_back_kernel(blocks, q_ref, k_ref, v_ref, do_ref, l_ref, d_ref, qs_ref, ks_ref,
                       dq_ref, dkv_ref, dk_acc, dv_acc):
    rank = lax.axis_index("ctx")
    size = q_ref.shape[2]
    head = q_ref.shape[3]
    row = lax.broadcasted_iota(jnp.int32, (size, size), 0)
    col = lax.broadcasted_iota(jnp.int32, (size, size), 1)
    dk_acc[...] = jnp.zeros_like(dk_acc)
    dv_acc[...] = jnp.zeros_like(dv_acc)
    for half in range(2):
        q = q_ref[0, half] * jnp.asarray(SCALE, BF16)
        do = do_ref[0, half]
        qseg = qs_ref[0, half]
        log_mass = l_ref[0, half]
        delta = d_ref[0, half]

        def part(block, own):
            rows = pl.ds(pl.multiple_of(block * size, size), size)
            k = k_ref[0, rows, :]
            v = v_ref[0, rows, :]
            allowed = ks_ref[0, rows, :] == qseg
            if own:
                order = (row <= col) if half == 0 else (row >= col)
                allowed = (allowed & order) | (col == row)
            s = jnp.where(allowed, dot(k, q, NT), NEGATIVE)
            p = jnp.exp(s - log_mass)
            ds = (p * (dot(v, do, NT) - delta)).astype(BF16)
            dv_acc[rows, :] += dot(p.astype(BF16), do)
            dk_acc[rows, :] += dot(ds, q)
            return dot(ds, k, TN)

        def step(t, dq):
            return dq + part(block_starts(half, t, blocks, rank), False)

        dq = part(rank + half * blocks, True)
        count = rank if half == 0 else 2 * blocks - 1 - rank
        dq_ref[0, half] = SCALE * lax.fori_loop(0, count, step, dq)
    dkv_ref[0, :, :head] = dk_acc[...].astype(BF16)
    dkv_ref[0, :, head:] = dv_acc[...].astype(BF16)


def attend_back(q, k, v, do, log_mass, delta, qseg, kseg):
    groups, _, size, head = q.shape
    length = k.shape[1]
    blocks = length // (2 * size)
    halves = pl.BlockSpec((1, 2, size, head), lambda g: (g, 0, 0, 0))
    whole = pl.BlockSpec((1, length, head), lambda g: (g, 0, 0))
    line = pl.BlockSpec((1, 2, 1, size), lambda g: (g, 0, 0, 0))
    return pl.pallas_call(
        functools.partial(attend_back_kernel, blocks),
        grid=(groups,),
        out_shape=(
            jax.ShapeDtypeStruct(q.shape, F32),
            jax.ShapeDtypeStruct((groups, length, 2 * head), BF16),
        ),
        in_specs=[halves, whole, whole, halves, line, line, line,
                  pl.BlockSpec((1, length, 1), lambda g: (g, 0, 0))],
        out_specs=(halves, pl.BlockSpec((1, length, 2 * head), lambda g: (g, 0, 0))),
        scratch_shapes=[pltpu.VMEM((length, head), F32)] * 2,
        compiler_params=pltpu.CompilerParams(vmem_limit_bytes=56 * 2**20),
        name="attend_back",
    )(q, k, v, do, log_mass, delta, qseg, kseg)


def angles(position, half_size, full_size):
    frequency = THETA ** (-2.0 * jnp.arange(half_size, dtype=F32) / full_size)
    turned = position[:, None] * frequency[None, :]
    return (jnp.cos(turned), jnp.sin(turned))


def rotate(tensor, cosine, sine):
    half_size = tensor.shape[-1] // 2
    a = tensor[..., :half_size]
    b = tensor[..., half_size:]
    return jnp.concatenate([a * cosine - b * sine, b * cosine + a * sine], axis=-1)


def norm_parts(values):
    inv = lax.rsqrt(jnp.mean(values * values, axis=-1, keepdims=True) + EPS)
    return (values * inv, inv)


def norm_back(upstream, normalized, inv, gain):
    d_norm = upstream * (1.0 + gain)
    d_values = inv * (d_norm - normalized * jnp.mean(d_norm * normalized, axis=-1, keepdims=True))
    return (d_values, jnp.sum(upstream * normalized, axis=0))


def gelu_tanh(values):
    return jax.nn.gelu(values, approximate=True)


class LineSum:
    def __init__(self, count, chunk, slots, own, near, far, out, sems):
        self.count, self.chunk, self.slots = count, chunk, slots
        self.own, self.near, self.far, self.out = own, near, far, out
        self.sems = sems
        self.z = z = lax.axis_index("tp")
        self.hub = (z == 1) | (z == 2)
        self.leaf = (z == 0) | (z == 3)
        self.other_hub = jnp.where(z == 1, 2, 1)
        self.my_hub = jnp.where(z == 0, 1, 2)
        self.my_leaf = jnp.where(z == 1, 0, 3)

    def slot(self, c):
        return pl.ds(pl.multiple_of(lax.rem(c, self.slots) * self.chunk, self.chunk), self.chunk)

    def rows(self, c):
        return pl.ds(pl.multiple_of(c * self.chunk, self.chunk), self.chunk)

    def inwards(self, c):
        return pltpu.make_async_remote_copy(
            self.own.at[self.slot(c)], self.near.at[self.slot(c)], self.sems[0].at[c], self.sems[1].at[c],
            device_id={"tp": self.my_hub}, device_id_type=MESH)

    def across(self, c):
        return pltpu.make_async_remote_copy(
            self.own.at[self.slot(c)], self.far.at[self.slot(c)], self.sems[2].at[c], self.sems[3].at[c],
            device_id={"tp": self.other_hub}, device_id_type=MESH)

    def outwards(self, c):
        return pltpu.make_async_remote_copy(
            self.far.at[self.slot(c)], self.out.at[self.rows(c)], self.sems[4].at[c], self.sems[5].at[c],
            device_id={"tp": self.my_leaf}, device_id_type=MESH)

    def store(self, c):
        return pltpu.make_async_copy(self.far.at[self.slot(c)], self.out.at[self.rows(c)], self.sems[6].at[c])

    def put(self, c, value):
        ring = self.slots < self.count
        if ring:
            @pl.when(c >= self.slots)
            def _():
                @pl.when(self.leaf)
                def _():
                    self.inwards(c - self.slots).wait_send()

                @pl.when(self.hub)
                def _():
                    self.across(c - self.slots).wait_send()

        self.own[self.slot(c), :] = value

        @pl.when(self.leaf)
        def _():
            if ring:
                @pl.when(c >= self.slots)
                def _():
                    pl.semaphore_wait(self.sems[7], 1)
            self.inwards(c).start()

    def pair(self, c):
        ring = self.slots < self.count

        @pl.when(self.hub)
        def _():
            self.inwards(c).wait_recv()
            at = self.slot(c)
            self.own[at, :] = (self.own[at, :].astype(F32) + self.near[at, :].astype(F32)).astype(BF16)
            if ring:
                @pl.when(c < self.count - self.slots)
                def _():
                    pl.semaphore_signal(self.sems[7], inc=1, device_id={"tp": self.my_leaf}, device_id_type=MESH)

                @pl.when(c >= self.slots)
                def _():
                    pl.semaphore_wait(self.sems[8], 1)
            self.across(c).start()

    def total(self, c):
        @pl.when(self.hub)
        def _():
            self.across(c).wait_recv()
            at = self.slot(c)
            self.far[at, :] = (self.own[at, :].astype(F32) + self.far[at, :].astype(F32)).astype(BF16)
            self.outwards(c).start()
            self.store(c).start()

    def retire(self, c):
        @pl.when(self.hub)
        def _():
            self.outwards(c).wait_send()
            self.store(c).wait()
            if self.slots < self.count:
                @pl.when(c < self.count - self.slots)
                def _():
                    pl.semaphore_signal(self.sems[8], inc=1, device_id={"tp": self.other_hub}, device_id_type=MESH)

    def finish(self):
        first = max(0, self.count - self.slots)

        @pl.when(self.leaf)
        def _():
            for c in range(self.count):
                self.outwards(c).wait_recv()
            for c in range(first, self.count):
                self.inwards(c).wait_send()

        @pl.when(self.hub)
        def _():
            for c in range(first, self.count):
                self.across(c).wait_send()


def line_sum_scratch(count, chunk, slots, cols):
    dma = pltpu.SemaphoreType.DMA((count,))
    regular = pltpu.SemaphoreType.REGULAR
    return [pltpu.VMEM((slots * chunk, cols), BF16)] * 3 + [dma] * 7 + [regular] * 2


def gelu_parts(v):
    c = 0.7978845608028654
    square = v * v
    t = jnp.tanh(v * (c + (c * 0.044715) * square))
    half = 0.5 + 0.5 * t
    value = v * half
    slope = half + (0.5 * v) * (1.0 - t * t) * (c + (3.0 * c * 0.044715) * square)
    return value, slope


def column_parts(cols):
    middle = -(-cols // 256) * 128
    return [(0, middle), (middle, cols)] if middle < cols else [(0, cols)]


def middle_of(x, attn, gain_post_attn):
    hat, inv = norm_parts(attn.astype(F32))
    return x.astype(F32) + hat * (1.0 + gain_post_attn), hat, inv


def ffn_forward_kernel(tiles, tile, chunk, x_ref, h_ref, gain_ref, wo_ref, wg_ref, wu_ref, wd_ref,
                       attn_ref, two_ref, gate_ref, up_ref, out_ref, own, near, far, *sems):
    i = pl.program_id(0)
    per = tile // chunk
    line = LineSum(tiles * per, chunk, tiles * per, own, near, far, out_ref, sems)

    @pl.when(i == 0)
    def _():
        barrier_line(line.z)

    attn = dot(h_ref[...], wo_ref[...], NT).astype(BF16)
    attn_ref[...] = attn
    middle, _, _ = middle_of(x_ref[...], attn, gain_ref[1:2, :])
    hat, _ = norm_parts(middle)
    two = (hat * (1.0 + gain_ref[2:3, :])).astype(BF16)
    two_ref[...] = two
    part = None
    for a, b in column_parts(wg_ref.shape[1]):
        gate = dot(two, wg_ref[:, a:b])
        up = dot(two, wu_ref[:, a:b])
        gate_ref[:, a:b] = gate.astype(BF16)
        up_ref[:, a:b] = up.astype(BF16)
        value, _ = gelu_parts(gate)
        more = dot((value * up).astype(BF16), wd_ref[:, a:b], NT)
        part = more if part is None else part + more
    for j in range(per):
        line.put(i * per + j, part[j * chunk : (j + 1) * chunk].astype(BF16))

    @pl.when(i >= 1)
    def _():
        for j in range(per):
            line.pair((i - 1) * per + j)

    @pl.when(i >= 2)
    def _():
        for j in range(per):
            line.total((i - 2) * per + j)

    @pl.when(i == tiles - 1)
    def _():
        last = tiles * per
        for j in range(per):
            line.pair(last - per + j)
        for c in range(max(0, last - 2 * per), last):
            line.total(c)
        for c in range(last):
            line.retire(c)
        line.finish()


def whole_block(shape):
    return pl.BlockSpec(shape, lambda i: (0,) * len(shape), pipeline_mode=pl.Buffered(1))


def tile_block(tile, cols):
    return pl.BlockSpec((tile, cols), lambda i: (i, 0))


ANY = pl.BlockSpec(memory_space=pl.ANY)


def ffn_forward(x, heads, gains, w_out, w_gate, w_up, w_down_t, ident):
    rows, width = x.shape
    hidden = w_gate.shape[1]
    tile, chunk = 256, 128
    tiles = rows // tile
    count = rows // chunk
    return pl.pallas_call(
        functools.partial(ffn_forward_kernel, tiles, tile, chunk),
        grid=(tiles,),
        out_shape=(
            jax.ShapeDtypeStruct((rows, width), BF16),
            jax.ShapeDtypeStruct((rows, width), BF16),
            jax.ShapeDtypeStruct((rows, hidden), BF16),
            jax.ShapeDtypeStruct((rows, hidden), BF16),
            jax.ShapeDtypeStruct((rows, width), BF16),
        ),
        in_specs=[tile_block(tile, width), tile_block(tile, heads.shape[1])]
        + [whole_block(w.shape) for w in (gains, w_out, w_gate, w_up, w_down_t)],
        out_specs=(tile_block(tile, width), tile_block(tile, width), tile_block(tile, hidden), tile_block(tile, hidden), ANY),
        scratch_shapes=line_sum_scratch(count, chunk, count, width),
        compiler_params=pltpu.CompilerParams(
            collective_id=ident, has_side_effects=True, vmem_limit_bytes=60 * 2**20),
        name="ffn_forward",
    )(x, heads, gains, w_out, w_gate, w_up, w_down_t)


def ffn_backward_kernel(tiles, tile, chunk, slots, x_ref, attn_ref, dy_ref, ffn_ref, two_ref, gate_ref, up_ref,
                        gain_ref, wg_ref, wu_ref, wd_ref,
                        y_ref, dgain_ref, gg_ref, gu_ref, gd_ref, out_ref,
                        acc_g, acc_u, acc_d, keep_g, keep_u, keep_h, stage, stage_sem, own, near, far, *sems):
    i = pl.program_id(0)
    per = tile // chunk
    last = tiles * per
    line = LineSum(last, chunk, slots, own, near, far, out_ref, sems)

    @pl.when(i == 0)
    def _():
        barrier_line(line.z)
        for acc in (acc_g, acc_u, acc_d, dgain_ref):
            acc[...] = jnp.zeros_like(acc)

    middle, _, _ = middle_of(x_ref[...], attn_ref[...], gain_ref[1:2, :])
    hat, inv = norm_parts(ffn_ref[...].astype(F32))
    gain = gain_ref[3:4, :]
    y_ref[...] = (middle + hat * (1.0 + gain)).astype(BF16)
    d_ffn, d_gain = norm_back(dy_ref[...].astype(F32), hat, inv, gain)
    dgain_ref[...] += d_gain[None]
    d_ffn = d_ffn.astype(BF16)
    part = None
    for a, b in column_parts(wg_ref.shape[1]):
        d_hidden = dot(d_ffn, wd_ref[:, a:b])
        up = up_ref[:, a:b].astype(F32)
        value, slope = gelu_parts(gate_ref[:, a:b].astype(F32))
        keep_h[:, a:b] = (value * up).astype(BF16)
        d_gate = (d_hidden * up * slope).astype(BF16)
        d_up = (d_hidden * value).astype(BF16)
        keep_g[:, a:b] = d_gate
        keep_u[:, a:b] = d_up
        more = dot(d_gate, wg_ref[:, a:b], NT) + dot(d_up, wu_ref[:, a:b], NT)
        part = more if part is None else part + more
    for j in range(per):
        line.put(i * per + j, part[j * chunk : (j + 1) * chunk].astype(BF16))

    @pl.when(i >= 1)
    def _():
        for j in range(per):
            line.pair((i - 1) * per + j)

    acc_g[...] += dot(two_ref[...], keep_g[...], TN)
    acc_u[...] += dot(two_ref[...], keep_u[...], TN)
    acc_d[...] += dot(d_ffn, keep_h[...], TN)

    @pl.when(i >= 2)
    def _():
        for j in range(per):
            line.total((i - 2) * per + j)

    @pl.when(i >= 3)
    def _():
        for j in range(per):
            line.retire((i - 3) * per + j)

    @pl.when(i == tiles - 1)
    def _():
        for j in range(per):
            line.pair(last - per + j)
        step = stage.shape[1]
        count = acc_g.shape[0] // step

        def piece(acc, out, k, at):
            @pl.when(k >= 2)
            def _():
                pltpu.make_async_copy(stage.at[at], out.at[pl.ds(0, step)], stage_sem.at[at]).wait()
            rows = pl.ds(pl.multiple_of(k * step, step), step)
            stage[at] = acc[rows, :].astype(BF16)
            pltpu.make_async_copy(stage.at[at], out.at[rows], stage_sem.at[at]).start()

        for acc, out in ((acc_g, gg_ref), (acc_u, gu_ref), (acc_d, gd_ref)):
            def pieces(k, _):
                piece(acc, out, k, lax.rem(k, 2))
                return 0

            lax.fori_loop(0, count, pieces, 0)
            for at in range(2):
                pltpu.make_async_copy(stage.at[at], out.at[pl.ds(0, step)], stage_sem.at[at]).wait()
            if acc is acc_g:
                for c in range(max(0, last - 2 * per), last - per):
                    line.total(c)
            if acc is acc_u:
                for c in range(last - per, last):
                    line.total(c)
        for c in range(max(0, last - 3 * per), last):
            line.retire(c)
        line.finish()


def ffn_backward(x, attn, dy, ffn, two, gate, up, gains, w_gate, w_up, w_down_t, ident):
    rows, width = x.shape
    hidden = w_gate.shape[1]
    tile, chunk = 256, 128
    tiles = rows // tile
    count = rows // chunk
    slots = min(count, 6)
    step = 144
    grad = jax.ShapeDtypeStruct((width, hidden), BF16)
    acc = pltpu.VMEM((width, hidden), F32)
    keep = pltpu.VMEM((tile, hidden), BF16)
    return pl.pallas_call(
        functools.partial(ffn_backward_kernel, tiles, tile, chunk, slots),
        grid=(tiles,),
        out_shape=(
            jax.ShapeDtypeStruct((rows, width), BF16),
            jax.ShapeDtypeStruct((1, width), F32),
            grad, grad, grad,
            jax.ShapeDtypeStruct((rows, width), BF16),
        ),
        in_specs=[tile_block(tile, width)] * 5 + [tile_block(tile, hidden)] * 2
        + [whole_block(w.shape) for w in (gains, w_gate, w_up, w_down_t)],
        out_specs=(tile_block(tile, width), pl.BlockSpec((1, width), lambda i: (0, 0)), ANY, ANY, ANY, ANY),
        scratch_shapes=[acc] * 3 + [keep] * 3
        + [pltpu.VMEM((2, step, hidden), BF16), pltpu.SemaphoreType.DMA((2,))]
        + line_sum_scratch(count, chunk, slots, width),
        compiler_params=pltpu.CompilerParams(
            collective_id=ident, has_side_effects=True, vmem_limit_bytes=63 * 2**20),
        name="ffn_backward",
    )(x, attn, dy, ffn, two, gate, up, gains, w_gate, w_up, w_down_t)


def middle_back_kernel(x_ref, attn_ref, dy_ref, d2_ref, h_ref, gain_ref, wo_ref,
                       dm_ref, dh_ref, delta_ref, dgain_ref, go_ref, acc):
    i = pl.program_id(0)

    @pl.when(i == 0)
    def _():
        acc[...] = jnp.zeros_like(acc)
        dgain_ref[...] = jnp.zeros_like(dgain_ref)

    middle, attn_hat, attn_inv = middle_of(x_ref[...], attn_ref[...], gain_ref[1:2, :])
    hat, inv = norm_parts(middle)
    d_part, d_gain = norm_back(d2_ref[...].astype(F32), hat, inv, gain_ref[2:3, :])
    dgain_ref[1:2, :] += d_gain[None]
    d_middle = dy_ref[...].astype(F32) + d_part
    dm_ref[...] = d_middle
    d_attn, d_gain = norm_back(d_middle, attn_hat, attn_inv, gain_ref[1:2, :])
    dgain_ref[0:1, :] += d_gain[None]
    d_attn = d_attn.astype(BF16)
    d_heads = dot(d_attn, wo_ref[...]).astype(BF16)
    dh_ref[...] = d_heads
    heads = h_ref[...]
    delta_ref[...] = jnp.sum(d_heads.astype(F32) * heads.astype(F32), axis=1, keepdims=True)
    acc[...] += dot(d_attn, heads, TN)

    @pl.when(i == pl.num_programs(0) - 1)
    def _():
        go_ref[...] = acc[...].astype(BF16)


def middle_back(x, attn, dy, d_two, heads, gains, w_out_t):
    rows, width = x.shape
    head = heads.shape[1]
    tile = 256
    return pl.pallas_call(
        middle_back_kernel,
        grid=(rows // tile,),
        out_shape=(
            jax.ShapeDtypeStruct((rows, width), F32),
            jax.ShapeDtypeStruct((rows, head), BF16),
            jax.ShapeDtypeStruct((rows, 1), F32),
            jax.ShapeDtypeStruct((2, width), F32),
            jax.ShapeDtypeStruct((width, head), BF16),
        ),
        in_specs=[tile_block(tile, width)] * 4 + [tile_block(tile, head)] + [whole_block(w.shape) for w in (gains, w_out_t)],
        out_specs=(
            tile_block(tile, width), tile_block(tile, head), tile_block(tile, 1),
            pl.BlockSpec((2, width), lambda i: (0, 0)), pl.BlockSpec((width, head), lambda i: (0, 0)),
        ),
        scratch_shapes=[pltpu.VMEM((width, head), F32)],
        compiler_params=pltpu.CompilerParams(vmem_limit_bytes=48 * 2**20),
        name="middle_back",
    )(x, attn, dy, d_two, heads, gains, w_out_t)


def shards(tokens, segments, cotangent, w_query, w_key, w_value, w_out, w_gate, w_up, w_down,
           g_input, g_post_attn, g_pre_ffn, g_post_ffn, g_query, g_key):
    batches, seq_local, _, size, width = tokens.shape
    head = w_key.shape[1]
    groups = batches * seq_local
    per_group = 2 * size
    rows = groups * per_group
    ctx = lax.axis_size("ctx")
    length = per_group * ctx
    rank = lax.axis_index("ctx")
    shared = ("dp", "ctx")
    own_rows = g_input.shape[0]
    hidden = w_gate.shape[1]

    def column(gain):
        return jnp.pad(gain, (0, own_rows - gain.shape[0]))[:, None]

    gains = jnp.concatenate([column(g) for g in (g_input, g_post_attn, g_pre_ffn, g_post_ffn, g_query, g_key)], axis=1)
    gains = jnp.pad(gains, ((0, 0), (0, 128 - gains.shape[1])))
    first = lax.all_gather(
        jnp.concatenate([w_query, w_key, w_value, gains], axis=1), shared, axis=0, tiled=True)
    key_ids = lax.all_gather(segments, "ctx", axis=3, tiled=True).reshape(groups, length)
    both = lax.all_gather(
        jnp.concatenate([w_query, w_out.T], axis=1), ("dp", "ctx", "tp"), axis=0, tiled=True)
    both = both.reshape(width // own_rows, 4, own_rows, 2 * head)
    both = both.transpose(0, 2, 3, 1).reshape(width, 2, head, 4).transpose(0, 1, 3, 2)
    query_full = both[:, 0].reshape(width, 4 * head)
    out_full = both[:, 1].reshape(width, 4 * head)
    mat_qkv = first[:, : 3 * head]
    gain_cols = first[:, 3 * head :].astype(F32)
    gain_rows = gain_cols[:, :8].T
    gain_input = gain_rows[0]
    short = g_query.shape[0]
    gain_query, gain_key = (
        gain_cols[:, i].reshape(-1, own_rows)[:, :short].reshape(-1) for i in (4, 5))
    tp_rank = lax.axis_index("tp")
    mat_out_t = lax.dynamic_slice_in_dim(out_full, tp_rank * head, head, axis=1)

    offsets = rank * size + jnp.arange(size, dtype=jnp.int32)
    position = jnp.concatenate([offsets, length - 1 - offsets]).astype(F32)
    cosine, sine = angles(position, head // 2, head)
    cosine = jnp.broadcast_to(cosine, (groups, per_group, head // 2)).reshape(rows, head // 2)
    sine = jnp.broadcast_to(sine, (groups, per_group, head // 2)).reshape(rows, head // 2)
    key_ids = jnp.where(key_ids == 0, -1, key_ids)
    own_ids = segments.reshape(groups, 2, size)

    inputs = tokens.reshape(rows, width).astype(F32)

    norm_one, scale_one = norm_parts(inputs)
    hidden_one = (norm_one * (1.0 + gain_input)).astype(BF16)
    raw = dot(hidden_one, mat_qkv)
    q_hat, q_scale = norm_parts(raw[:, :head])
    k_hat, k_scale = norm_parts(raw[:, head : 2 * head])
    queries = rotate(q_hat * (1.0 + gain_query), cosine, sine).astype(BF16)
    keys = rotate(k_hat * (1.0 + gain_key), cosine, sine).astype(BF16)
    values = raw[:, 2 * head :].astype(BF16)
    queries = queries.reshape(groups, 2, size, head)
    key_all = lax.all_gather(keys.reshape(groups, 2, size, head), "ctx", axis=2, tiled=True)
    value_all = lax.all_gather(values.reshape(groups, 2, size, head), "ctx", axis=2, tiled=True)
    key_all = key_all.reshape(groups, length, head)
    value_all = value_all.reshape(groups, length, head)
    stacked = jnp.stack([w_gate, w_up, w_down.T])
    stacked, key_all = lax.optimization_barrier((stacked, key_all))
    ffn = lax.all_gather(stacked, shared, axis=1, tiled=True)
    mat_gate, mat_up, mat_down_t = ffn[0], ffn[1], ffn[2]
    heads, log_mass = attend(queries, key_all, value_all, own_ids[..., None], key_ids[:, None, :])
    heads_own = heads.reshape(rows, head)
    heads_all = gather_tp(heads_own, 0)
    x_rows = tokens.reshape(rows, width)
    dy_rows = cotangent.reshape(rows, width)
    attn, hidden_two, gate, up, ffn_out = ffn_forward(
        x_rows, heads_all, gain_rows, out_full, mat_gate, mat_up, mat_down_t, 1)
    output, d_gain_post_ffn, grad_gate, grad_up, grad_down_t, d_two = ffn_backward(
        x_rows, attn, dy_rows, ffn_out, hidden_two, gate, up, gain_rows, mat_gate, mat_up, mat_down_t, 2)
    grad_ffn = lax.psum_scatter(
        jnp.stack([grad_gate, grad_up, grad_down_t]), shared, scatter_dimension=1, tiled=True).astype(F32)
    d_middle, d_heads, delta, d_gain_mid, grad_out_t = middle_back(
        x_rows, attn, dy_rows, d_two, heads_own, gain_rows, mat_out_t)

    d_query, d_kv = attend_back(
        queries, key_all, value_all, d_heads.reshape(groups, 2, size, head),
        log_mass.reshape(groups, 2, 1, size), delta.reshape(groups, 2, 1, size),
        own_ids[:, :, None, :], key_ids[:, :, None])
    d_kv = lax.psum_scatter(
        d_kv.reshape(groups, 2, length // 2, 2 * head), "ctx", scatter_dimension=2, tiled=True)
    d_kv = sum_tp(d_kv.reshape(rows, 2 * head), 3).astype(F32)
    d_q_rot = rotate(d_query.reshape(rows, head), cosine, -sine)
    d_q_raw, d_gain_query = norm_back(d_q_rot, q_hat, q_scale, gain_query)
    d_q_raw = d_q_raw.astype(BF16)
    d_q_all = gather_tp(d_q_raw, 4)
    d_k_rot = rotate(d_kv[:, :head], cosine, -sine)
    d_k_raw, d_gain_key = norm_back(d_k_rot, k_hat, k_scale, gain_key)
    d_kv_raw = jnp.concatenate([d_k_raw.astype(BF16), d_kv[:, head:].astype(BF16)], axis=1)
    d_one = dot(d_q_all, query_full, NT) + dot(d_kv_raw, mat_qkv[:, head:], NT)
    d_part, d_gain_input = norm_back(d_one, norm_one, scale_one, gain_input)
    d_tokens = d_middle + d_part
    d_gain_query = lax.psum(d_gain_query, "tp")

    def spread(vector):
        return jnp.pad(vector.reshape(-1, short), ((0, 0), (0, own_rows - short))).reshape(-1)

    d_gains = jnp.stack(
        [d_gain_input, d_gain_mid[0], d_gain_mid[1], d_gain_post_ffn[0], spread(d_gain_query), spread(d_gain_key)], axis=1)
    d_gains = jnp.pad(d_gains, ((0, 0), (0, 128 - d_gains.shape[1]))).astype(BF16)
    last = jnp.concatenate(
        [dot(hidden_one, d_q_raw, TN).astype(BF16), dot(hidden_one, d_kv_raw, TN).astype(BF16),
         grad_out_t, d_gains], axis=1)
    last = lax.psum_scatter(last, shared, scatter_dimension=0, tiled=True).astype(F32)
    g = last[:, 4 * head :]
    return (
        output.reshape(tokens.shape),
        d_tokens.reshape(tokens.shape),
        last[:, :head],
        last[:, head : 2 * head],
        last[:, 2 * head : 3 * head],
        last[:, 3 * head : 4 * head].T,
        grad_ffn[0],
        grad_ffn[1],
        grad_ffn[2].T,
        g[:, 0],
        g[:, 1],
        g[:, 2],
        g[:, 3],
        g[:short, 4],
        g[:short, 5],
    )


def solution(mesh):
    shared = ("dp", "ctx")
    rows = P(None, "dp", None, "ctx", None)
    weights = (
        P(shared, "tp"), P(shared, None), P(shared, None), P("tp", shared),
        P(shared, "tp"), P(shared, "tp"), P("tp", shared),
    )
    gains = (P(shared),) * 6
    return jax.shard_map(
        shards,
        mesh=mesh,
        in_specs=(rows, P(None, "dp", None, "ctx"), rows) + weights + gains,
        out_specs=(rows, rows) + weights + gains,
        check_vma=False,
    )
```

```python
import functools

import jax
import jax.numpy as jnp
from jax import lax
from jax.experimental import pallas as pl
from jax.experimental.pallas import tpu as pltpu
from jax.sharding import PartitionSpec as P

EPS = 1e-06
THETA = 1000000.0
SCALE = 0.0625
NEGATIVE = -1e30
BF16 = jnp.bfloat16
F32 = jnp.float32
MESH = pl.DeviceIdType.MESH
NN = (((1,), (0,)), ((), ()))
NT = (((1,), (1,)), ((), ()))
TN = (((0,), (0,)), ((), ()))


def dot(a, b, dims=NN):
    return lax.dot_general(a, b, dims, preferred_element_type=F32)


def barrier_line(z):
    bar = pltpu.get_barrier_semaphore()

    @pl.when(z > 0)
    def _():
        pl.semaphore_signal(bar, inc=1, device_id={"tp": z - 1}, device_id_type=MESH)

    @pl.when(z < 3)
    def _():
        pl.semaphore_signal(bar, inc=1, device_id={"tp": z + 1}, device_id_type=MESH)

    pl.semaphore_wait(bar, jnp.where((z == 0) | (z == 3), 1, 2))


def sum_kernel(n, tile, x_ref, o_ref, own, got, pair, other, *sems):
    lsem, ssem1, rsem1, ssem2, rsem2, ssem3, rsem3, osem = sems
    z = lax.axis_index("tp")
    hub = (z == 1) | (z == 2)
    leaf = jnp.logical_not(hub)
    other_hub = jnp.where(z == 1, 2, 1)
    my_hub = jnp.where(z == 0, 1, 2)
    my_leaf = jnp.where(z == 1, 0, 3)
    barrier_line(z)

    def rows(t):
        return pl.ds(t * tile, tile)

    def up(t):
        return pltpu.make_async_remote_copy(
            x_ref.at[rows(t)], got.at[rows(t)], ssem1.at[t], rsem1.at[t],
            device_id={"tp": my_hub}, device_id_type=MESH)

    def across(t):
        return pltpu.make_async_remote_copy(
            pair.at[rows(t)], other.at[rows(t)], ssem2.at[t], rsem2.at[t],
            device_id={"tp": other_hub}, device_id_type=MESH)

    def back(t):
        return pltpu.make_async_remote_copy(
            own.at[rows(t)], o_ref.at[rows(t)], ssem3.at[t], rsem3.at[t],
            device_id={"tp": my_leaf}, device_id_type=MESH)

    def load(t):
        return pltpu.make_async_copy(x_ref.at[rows(t)], own.at[rows(t)], lsem.at[t])

    def store(t):
        return pltpu.make_async_copy(own.at[rows(t)], o_ref.at[rows(t)], osem.at[t])

    @pl.when(leaf)
    def _():
        for t in range(n):
            up(t).start()
        for t in range(n):
            back(t).wait_recv()
        for t in range(n):
            up(t).wait_send()

    @pl.when(hub)
    def _():
        for t in range(n):
            load(t).start()

        def finish(t):
            across(t).wait_recv()
            own[rows(t), :] = (pair[rows(t), :].astype(F32) + other[rows(t), :].astype(F32)).astype(BF16)
            back(t).start()
            store(t).start()

        for t in range(n):
            load(t).wait()
            up(t).wait_recv()
            pair[rows(t), :] = (own[rows(t), :].astype(F32) + got[rows(t), :].astype(F32)).astype(BF16)
            across(t).start()
            if t > 0:
                finish(t - 1)
        finish(n - 1)
        for t in range(n):
            across(t).wait_send()
            back(t).wait_send()
            store(t).wait()


def sum_tp(x, ident):
    rows, cols = x.shape
    tile = 128 if rows % 128 == 0 else rows
    n = rows // tile
    dma = pltpu.SemaphoreType.DMA((n,))
    return pl.pallas_call(
        functools.partial(sum_kernel, n, tile),
        out_shape=jax.ShapeDtypeStruct((rows, cols), BF16),
        in_specs=[pl.BlockSpec(memory_space=pl.ANY)],
        out_specs=pl.BlockSpec(memory_space=pl.ANY),
        scratch_shapes=[pltpu.VMEM((rows, cols), BF16)] * 4 + [dma] * 8,
        compiler_params=pltpu.CompilerParams(
            collective_id=ident, has_side_effects=True, vmem_limit_bytes=40 * 2**20),
        name=f"sum_tp_{ident}",
    )(x)


def gather_kernel(n, tile, width, x_ref, o_ref, lsem, *sems):
    su, ru, sd, rd = sems
    z = lax.axis_index("tp")
    barrier_line(z)

    def place(src, t):
        return o_ref.at[pl.ds(t * tile, tile), pl.ds(pl.multiple_of(src * width, width), width)]

    def send(src, t, k, way):
        ss, rs = (su, ru) if way > 0 else (sd, rd)
        here = x_ref.at[pl.ds(t * tile, tile)] if k == 0 else place(src, t)
        return pltpu.make_async_remote_copy(
            here, place(src, t), ss.at[k, t], rs.at[k, t],
            device_id={"tp": z + way}, device_id_type=MESH)

    own = pltpu.make_async_copy(x_ref, o_ref.at[:, pl.ds(pl.multiple_of(z * width, width), width)], lsem)
    own.start()
    for k in range(3):
        for t in range(n):
            for way in (1, -1):
                src = z - way * k
                ok = (z + way >= 0) & (z + way <= 3) & (src >= 0) & (src <= 3)
                if k > 0:
                    came = (src >= 0) & (src <= 3)

                    @pl.when(came)
                    def _():
                        send(src, t, k - 1, way).wait_recv()

                @pl.when(ok)
                def _():
                    send(src, t, k, way).start()
    for way in (1, -1):
        src = z - way * 3
        came = (src >= 0) & (src <= 3)

        @pl.when(came)
        def _():
            for t in range(n):
                send(src, t, 2, way).wait_recv()

    for k in range(3):
        for way in (1, -1):
            src = z - way * k
            ok = (z + way >= 0) & (z + way <= 3) & (src >= 0) & (src <= 3)

            @pl.when(ok)
            def _():
                for t in range(n):
                    send(src, t, k, way).wait_send()
    own.wait()


def gather_tp(x, ident):
    rows, width = x.shape
    tile = 256 if rows % 256 == 0 else rows
    n = rows // tile
    dma = pltpu.SemaphoreType.DMA((3, n))
    return pl.pallas_call(
        functools.partial(gather_kernel, n, tile, width),
        out_shape=jax.ShapeDtypeStruct((rows, 4 * width), x.dtype),
        in_specs=[pl.BlockSpec(memory_space=pl.ANY)],
        out_specs=pl.BlockSpec(memory_space=pl.ANY),
        scratch_shapes=[pltpu.SemaphoreType.DMA] + [dma] * 4,
        compiler_params=pltpu.CompilerParams(collective_id=ident, has_side_effects=True),
        name=f"gather_tp_{ident}",
    )(x)


def block_starts(half, t, blocks, rank):
    if half == 0:
        return t
    return jnp.where(t < blocks, t, t + rank + 1)


def attend_kernel(blocks, q_ref, kv_ref, qs_ref, ks_ref, o_ref, l_ref):
    rank = lax.axis_index("ctx")
    size, head = q_ref.shape[2:]
    row = lax.broadcasted_iota(jnp.int32, (size, size), 0)
    col = lax.broadcasted_iota(jnp.int32, (size, size), 1)
    for half in range(2):
        q = q_ref[0, half] * jnp.asarray(SCALE, BF16)
        qseg = qs_ref[0, half]

        def part(block):
            start = pl.multiple_of(block * size, size)
            k = kv_ref[0, pl.ds(start, size), :head]
            v = kv_ref[0, pl.ds(start, size), head:]
            same = qseg == ks_ref[0, :, pl.ds(start, size)]
            return dot(q, k, NT), v, same

        s, v, same = part(rank + half * blocks)
        order = (col <= row) if half == 0 else (col >= row)
        s = jnp.where((same & order) | (col == row), s, NEGATIVE)
        top = jnp.max(s, axis=1, keepdims=True)
        p = jnp.exp(s - top)
        mass = jnp.sum(p, axis=1, keepdims=True)
        acc = dot(p.astype(BF16), v)

        def step(t, carry):
            top, mass, acc = carry
            s, v, same = part(block_starts(half, t, blocks, rank))
            s = jnp.where(same, s, NEGATIVE)
            new = jnp.maximum(top, jnp.max(s, axis=1, keepdims=True))
            keep = jnp.exp(top - new)
            p = jnp.exp(s - new)
            mass = mass * keep + jnp.sum(p, axis=1, keepdims=True)
            acc = acc * keep + dot(p.astype(BF16), v)
            return new, mass, acc

        count = rank if half == 0 else 2 * blocks - 1 - rank
        top, mass, acc = lax.fori_loop(0, count, step, (top, mass, acc))
        o_ref[0, half] = (acc / mass).astype(BF16)
        l_ref[0, half] = top + jnp.log(mass)


def attend(q, kv, qseg, kseg):
    groups, _, size, head = q.shape
    length = kv.shape[1]
    blocks = length // (2 * size)
    return pl.pallas_call(
        functools.partial(attend_kernel, blocks),
        grid=(groups,),
        out_shape=(
            jax.ShapeDtypeStruct(q.shape, BF16),
            jax.ShapeDtypeStruct((groups, 2, size, 1), F32),
        ),
        in_specs=[
            pl.BlockSpec((1, 2, size, head), lambda g: (g, 0, 0, 0)),
            pl.BlockSpec((1, length, 2 * head), lambda g: (g, 0, 0)),
            pl.BlockSpec((1, 2, size, 1), lambda g: (g, 0, 0, 0)),
            pl.BlockSpec((1, 1, length), lambda g: (g, 0, 0)),
        ],
        out_specs=(
            pl.BlockSpec((1, 2, size, head), lambda g: (g, 0, 0, 0)),
            pl.BlockSpec((1, 2, size, 1), lambda g: (g, 0, 0, 0)),
        ),
        compiler_params=pltpu.CompilerParams(vmem_limit_bytes=48 * 2**20),
        name="attend",
    )(q, kv, qseg, kseg)


def attend_back_kernel(blocks, q_ref, kv_ref, do_ref, l_ref, d_ref, qs_ref, ks_ref,
                       dq_ref, dkv_ref, dk_acc, dv_acc):
    rank = lax.axis_index("ctx")
    size = q_ref.shape[2]
    head = q_ref.shape[3]
    row = lax.broadcasted_iota(jnp.int32, (size, size), 0)
    col = lax.broadcasted_iota(jnp.int32, (size, size), 1)
    dk_acc[...] = jnp.zeros_like(dk_acc)
    dv_acc[...] = jnp.zeros_like(dv_acc)
    for half in range(2):
        q = q_ref[0, half] * jnp.asarray(SCALE, BF16)
        do = do_ref[0, half]
        qseg = qs_ref[0, half]
        log_mass = l_ref[0, half]
        delta = d_ref[0, half]

        def part(block, own):
            rows = pl.ds(pl.multiple_of(block * size, size), size)
            k = kv_ref[0, rows, :head]
            v = kv_ref[0, rows, head:]
            allowed = ks_ref[0, rows, :] == qseg
            if own:
                order = (row <= col) if half == 0 else (row >= col)
                allowed = (allowed & order) | (col == row)
            s = jnp.where(allowed, dot(k, q, NT), NEGATIVE)
            p = jnp.exp(s - log_mass)
            ds = (p * (dot(v, do, NT) - delta)).astype(BF16)
            dv_acc[rows, :] += dot(p.astype(BF16), do)
            dk_acc[rows, :] += dot(ds, q)
            return dot(ds, k, TN)

        def step(t, dq):
            return dq + part(block_starts(half, t, blocks, rank), False)

        dq = part(rank + half * blocks, True)
        count = rank if half == 0 else 2 * blocks - 1 - rank
        dq_ref[0, half] = SCALE * lax.fori_loop(0, count, step, dq)
    dkv_ref[0, :, :head] = dk_acc[...].astype(BF16)
    dkv_ref[0, :, head:] = dv_acc[...].astype(BF16)


def attend_back(q, kv, do, log_mass, delta, qseg, kseg):
    groups, _, size, head = q.shape
    length = kv.shape[1]
    blocks = length // (2 * size)
    halves = pl.BlockSpec((1, 2, size, head), lambda g: (g, 0, 0, 0))
    whole = pl.BlockSpec((1, length, 2 * head), lambda g: (g, 0, 0))
    line = pl.BlockSpec((1, 2, 1, size), lambda g: (g, 0, 0, 0))
    return pl.pallas_call(
        functools.partial(attend_back_kernel, blocks),
        grid=(groups,),
        out_shape=(
            jax.ShapeDtypeStruct(q.shape, F32),
            jax.ShapeDtypeStruct((groups, length, 2 * head), BF16),
        ),
        in_specs=[halves, whole, halves, line, line, line,
                  pl.BlockSpec((1, length, 1), lambda g: (g, 0, 0))],
        out_specs=(halves, pl.BlockSpec((1, length, 2 * head), lambda g: (g, 0, 0))),
        scratch_shapes=[pltpu.VMEM((length, head), F32)] * 2,
        compiler_params=pltpu.CompilerParams(vmem_limit_bytes=56 * 2**20),
        name="attend_back",
    )(q, kv, do, log_mass, delta, qseg, kseg)


def angles(position, half_size, full_size):
    frequency = THETA ** (-2.0 * jnp.arange(half_size, dtype=F32) / full_size)
    turned = position[:, None] * frequency[None, :]
    return (jnp.cos(turned), jnp.sin(turned))


def rotate(tensor, cosine, sine):
    half_size = tensor.shape[-1] // 2
    a = tensor[..., :half_size]
    b = tensor[..., half_size:]
    return jnp.concatenate([a * cosine - b * sine, b * cosine + a * sine], axis=-1)


def norm_parts(values):
    inv = lax.rsqrt(jnp.mean(values * values, axis=-1, keepdims=True) + EPS)
    return (values * inv, inv)


def norm_back(upstream, normalized, inv, gain):
    d_norm = upstream * (1.0 + gain)
    d_values = inv * (d_norm - normalized * jnp.mean(d_norm * normalized, axis=-1, keepdims=True))
    return (d_values, jnp.sum(upstream * normalized, axis=0))


def gelu_tanh(values):
    return jax.nn.gelu(values, approximate=True)


class LineSum:
    def __init__(self, count, chunk, slots, own, near, far, out, sems):
        self.count, self.chunk, self.slots = count, chunk, slots
        self.own, self.near, self.far, self.out = own, near, far, out
        self.sems = sems
        self.z = z = lax.axis_index("tp")
        self.hub = (z == 1) | (z == 2)
        self.leaf = (z == 0) | (z == 3)
        self.other_hub = jnp.where(z == 1, 2, 1)
        self.my_hub = jnp.where(z == 0, 1, 2)
        self.my_leaf = jnp.where(z == 1, 0, 3)

    def slot(self, c):
        return pl.ds(pl.multiple_of(lax.rem(c, self.slots) * self.chunk, self.chunk), self.chunk)

    def rows(self, c):
        return pl.ds(pl.multiple_of(c * self.chunk, self.chunk), self.chunk)

    def inwards(self, c):
        return pltpu.make_async_remote_copy(
            self.own.at[self.slot(c)], self.near.at[self.slot(c)], self.sems[0].at[c], self.sems[1].at[c],
            device_id={"tp": self.my_hub}, device_id_type=MESH)

    def across(self, c):
        return pltpu.make_async_remote_copy(
            self.own.at[self.slot(c)], self.far.at[self.slot(c)], self.sems[2].at[c], self.sems[3].at[c],
            device_id={"tp": self.other_hub}, device_id_type=MESH)

    def outwards(self, c):
        return pltpu.make_async_remote_copy(
            self.far.at[self.slot(c)], self.out.at[self.rows(c)], self.sems[4].at[c], self.sems[5].at[c],
            device_id={"tp": self.my_leaf}, device_id_type=MESH)

    def store(self, c):
        return pltpu.make_async_copy(self.far.at[self.slot(c)], self.out.at[self.rows(c)], self.sems[6].at[c])

    def put(self, c, value):
        ring = self.slots < self.count
        if ring:
            @pl.when(c >= self.slots)
            def _():
                @pl.when(self.leaf)
                def _():
                    self.inwards(c - self.slots).wait_send()

                @pl.when(self.hub)
                def _():
                    self.across(c - self.slots).wait_send()

        self.own[self.slot(c), :] = value

        @pl.when(self.leaf)
        def _():
            if ring:
                @pl.when(c >= self.slots)
                def _():
                    pl.semaphore_wait(self.sems[7], 1)
            self.inwards(c).start()

    def pair(self, c):
        ring = self.slots < self.count

        @pl.when(self.hub)
        def _():
            self.inwards(c).wait_recv()
            at = self.slot(c)
            self.own[at, :] = (self.own[at, :].astype(F32) + self.near[at, :].astype(F32)).astype(BF16)
            if ring:
                @pl.when(c < self.count - self.slots)
                def _():
                    pl.semaphore_signal(self.sems[7], inc=1, device_id={"tp": self.my_leaf}, device_id_type=MESH)

                @pl.when(c >= self.slots)
                def _():
                    pl.semaphore_wait(self.sems[8], 1)
            self.across(c).start()

    def total(self, c):
        @pl.when(self.hub)
        def _():
            self.across(c).wait_recv()
            at = self.slot(c)
            self.far[at, :] = (self.own[at, :].astype(F32) + self.far[at, :].astype(F32)).astype(BF16)
            self.outwards(c).start()
            self.store(c).start()

    def retire(self, c):
        @pl.when(self.hub)
        def _():
            self.outwards(c).wait_send()
            self.store(c).wait()
            if self.slots < self.count:
                @pl.when(c < self.count - self.slots)
                def _():
                    pl.semaphore_signal(self.sems[8], inc=1, device_id={"tp": self.other_hub}, device_id_type=MESH)

    def finish(self):
        first = max(0, self.count - self.slots)

        @pl.when(self.leaf)
        def _():
            for c in range(self.count):
                self.outwards(c).wait_recv()
            for c in range(first, self.count):
                self.inwards(c).wait_send()

        @pl.when(self.hub)
        def _():
            for c in range(first, self.count):
                self.across(c).wait_send()


def line_sum_scratch(count, chunk, slots, cols):
    dma = pltpu.SemaphoreType.DMA((count,))
    regular = pltpu.SemaphoreType.REGULAR
    return [pltpu.VMEM((slots * chunk, cols), BF16)] * 3 + [dma] * 7 + [regular] * 2


def gelu_parts(v):
    c = 0.7978845608028654
    square = v * v
    t = jnp.tanh(v * (c + (c * 0.044715) * square))
    half = 0.5 + 0.5 * t
    value = v * half
    slope = half + (0.5 * v) * (1.0 - t * t) * (c + (3.0 * c * 0.044715) * square)
    return value, slope


def column_parts(cols):
    middle = -(-cols // 256) * 128
    return [(0, middle), (middle, cols)] if middle < cols else [(0, cols)]


def middle_of(x, attn, gain_post_attn):
    hat, inv = norm_parts(attn.astype(F32))
    return x.astype(F32) + hat * (1.0 + gain_post_attn), hat, inv


def load_ffn_weights(weights, refs, sem):
    wide = refs[0].shape[1]
    base = weights.shape[1] - 3 * wide
    return [
        pltpu.make_async_copy(weights.at[:, pl.ds(base + j * wide, wide)], ref, sem.at[j])
        for j, ref in enumerate(refs)
    ]


def ffn_forward_kernel(tiles, tile, chunk, hidden, x_ref, h0_ref, h1_ref, gain_ref, w_ref,
                       attn_ref, two_ref, gate_ref, up_ref, out_ref, wo_ref, wg_ref, wu_ref, wd_ref, w_sem, own, near, far, *sems):
    i = pl.program_id(0)
    per = tile // chunk
    line = LineSum(tiles * per, chunk, tiles * per, own, near, far, out_ref, sems)
    head = wo_ref.shape[1] // 4

    @pl.when(i == 0)
    def _():
        copies = load_ffn_weights(w_ref, (wg_ref, wu_ref, wd_ref), w_sem)
        copies += [
            pltpu.make_async_copy(
                w_ref.at[:, pl.ds((2 * j + 1) * head, head)], wo_ref.at[:, pl.ds(j * head, head)], w_sem.at[3 + j])
            for j in range(4)
        ]
        for copy in copies:
            copy.start()
        barrier_line(line.z)
        for copy in copies:
            copy.wait()

    heads = jnp.where(i < tiles // 2, h0_ref[...], h1_ref[...])
    attn = dot(heads, wo_ref[...], NT).astype(BF16)
    attn_ref[...] = attn
    middle, _, _ = middle_of(x_ref[...], attn, gain_ref[1:2, :])
    hat, _ = norm_parts(middle)
    two = (hat * (1.0 + gain_ref[2:3, :])).astype(BF16)
    two_ref[...] = two
    part = None
    for a, b in column_parts(hidden):
        gate = dot(two, wg_ref[:, a:b])
        up = dot(two, wu_ref[:, a:b])
        gate_ref[:, a:b] = gate.astype(BF16)
        up_ref[:, a:b] = up.astype(BF16)
        value, _ = gelu_parts(gate)
        more = dot((value * up).astype(BF16), wd_ref[:, a:b], NT)
        part = more if part is None else part + more
    for j in range(per):
        line.put(i * per + j, part[j * chunk : (j + 1) * chunk].astype(BF16))

    @pl.when(i >= 1)
    def _():
        for j in range(per):
            line.pair((i - 1) * per + j)

    @pl.when(i >= 2)
    def _():
        for j in range(per):
            line.total((i - 2) * per + j)

    @pl.when(i == tiles - 1)
    def _():
        last = tiles * per
        for j in range(per):
            line.pair(last - per + j)
        for c in range(max(0, last - 2 * per), last):
            line.total(c)
        for c in range(last):
            line.retire(c)
        line.finish()


def whole_block(shape):
    return pl.BlockSpec(shape, lambda i: (0,) * len(shape), pipeline_mode=pl.Buffered(1))


def tile_block(tile, cols):
    return pl.BlockSpec((tile, cols), lambda i: (i, 0))


ANY = pl.BlockSpec(memory_space=pl.ANY)


def wide_of(hidden):
    return -(-hidden // 128) * 128


def ffn_forward(x, heads, gains, weights, hidden, ident):
    rows, width = x.shape
    all_heads = heads[0].shape[1]
    tile, chunk = 256, 128
    tiles = rows // tile
    half = tiles // 2
    count = rows // chunk
    wide = wide_of(hidden)
    return pl.pallas_call(
        functools.partial(ffn_forward_kernel, tiles, tile, chunk, hidden),
        grid=(tiles,),
        out_shape=(
            jax.ShapeDtypeStruct((rows, width), BF16),
            jax.ShapeDtypeStruct((rows, width), BF16),
            jax.ShapeDtypeStruct((rows, hidden), BF16),
            jax.ShapeDtypeStruct((rows, hidden), BF16),
            jax.ShapeDtypeStruct((rows, width), BF16),
        ),
        in_specs=[
            tile_block(tile, width),
            pl.BlockSpec((tile, all_heads), lambda i: (jnp.minimum(i, half - 1), 0)),
            pl.BlockSpec((tile, all_heads), lambda i: (jnp.maximum(i - half, 0), 0)),
            whole_block(gains.shape),
            ANY,
        ],
        out_specs=(tile_block(tile, width), tile_block(tile, width), tile_block(tile, hidden), tile_block(tile, hidden), ANY),
        scratch_shapes=[pltpu.VMEM((width, all_heads), BF16)] + [pltpu.VMEM((width, wide), BF16)] * 3
        + [pltpu.SemaphoreType.DMA((7,))]
        + line_sum_scratch(count, chunk, count, width),
        compiler_params=pltpu.CompilerParams(
            collective_id=ident, has_side_effects=True, vmem_limit_bytes=60 * 2**20),
        name="ffn_forward",
    )(x, heads[0], heads[1], gains, weights)


def ffn_backward_kernel(tiles, tile, chunk, slots, hidden, x_ref, attn_ref, dy_ref, ffn_ref, two_ref, gate_ref, up_ref,
                        gain_ref, w_ref,
                        y_ref, dgain_ref, grad_ref, out_ref, wg_ref, wu_ref, wd_ref, w_sem,
                        acc_g, acc_u, acc_d, keep_g, keep_u, keep_h, stage, stage_sem, own, near, far, *sems):
    i = pl.program_id(0)
    per = tile // chunk
    last = tiles * per
    line = LineSum(last, chunk, slots, own, near, far, out_ref, sems)

    @pl.when(i == 0)
    def _():
        copies = load_ffn_weights(w_ref, (wg_ref, wu_ref, wd_ref), w_sem)
        for copy in copies:
            copy.start()
        barrier_line(line.z)
        for acc in (acc_g, acc_u, acc_d, dgain_ref):
            acc[...] = jnp.zeros_like(acc)
        for copy in copies:
            copy.wait()

    middle, _, _ = middle_of(x_ref[...], attn_ref[...], gain_ref[1:2, :])
    hat, inv = norm_parts(ffn_ref[...].astype(F32))
    gain = gain_ref[3:4, :]
    y_ref[...] = (middle + hat * (1.0 + gain)).astype(BF16)
    d_ffn, d_gain = norm_back(dy_ref[...].astype(F32), hat, inv, gain)
    dgain_ref[...] += d_gain[None]
    d_ffn = d_ffn.astype(BF16)
    part = None
    for a, b in column_parts(hidden):
        d_hidden = dot(d_ffn, wd_ref[:, a:b])
        up = up_ref[:, a:b].astype(F32)
        value, slope = gelu_parts(gate_ref[:, a:b].astype(F32))
        keep_h[:, a:b] = (value * up).astype(BF16)
        d_gate = (d_hidden * up * slope).astype(BF16)
        d_up = (d_hidden * value).astype(BF16)
        keep_g[:, a:b] = d_gate
        keep_u[:, a:b] = d_up
        more = dot(d_gate, wg_ref[:, a:b], NT) + dot(d_up, wu_ref[:, a:b], NT)
        part = more if part is None else part + more
    for j in range(per):
        line.put(i * per + j, part[j * chunk : (j + 1) * chunk].astype(BF16))

    @pl.when(i >= 1)
    def _():
        for j in range(per):
            line.pair((i - 1) * per + j)

    acc_g[...] += dot(two_ref[...], keep_g[...], TN)
    acc_u[...] += dot(two_ref[...], keep_u[...], TN)
    acc_d[...] += dot(d_ffn, keep_h[...], TN)

    @pl.when(i >= 2)
    def _():
        for j in range(per):
            line.total((i - 2) * per + j)

    @pl.when(i >= 3)
    def _():
        for j in range(per):
            line.retire((i - 3) * per + j)

    @pl.when(i == tiles - 1)
    def _():
        for j in range(per):
            line.pair(last - per + j)
        step = stage.shape[1]
        count = acc_g.shape[0] // step

        def piece(acc, out, k, at):
            @pl.when(k >= 2)
            def _():
                pltpu.make_async_copy(stage.at[at], out.at[pl.ds(0, step)], stage_sem.at[at]).wait()
            rows = pl.ds(pl.multiple_of(k * step, step), step)
            stage[at] = acc[rows, :].astype(BF16)
            pltpu.make_async_copy(stage.at[at], out.at[rows], stage_sem.at[at]).start()

        for acc, out in ((acc_g, grad_ref.at[0]), (acc_u, grad_ref.at[1]), (acc_d, grad_ref.at[2])):
            def pieces(k, _):
                piece(acc, out, k, lax.rem(k, 2))
                return 0

            lax.fori_loop(0, count, pieces, 0)
            for at in range(2):
                pltpu.make_async_copy(stage.at[at], out.at[pl.ds(0, step)], stage_sem.at[at]).wait()
            if acc is acc_g:
                for c in range(max(0, last - 2 * per), last - per):
                    line.total(c)
            if acc is acc_u:
                for c in range(last - per, last):
                    line.total(c)
        for c in range(max(0, last - 3 * per), last):
            line.retire(c)
        line.finish()


def ffn_backward(x, attn, dy, ffn, two, gate, up, gains, weights, ident):
    rows, width = x.shape
    hidden = gate.shape[1]
    wide = wide_of(hidden)
    tile, chunk = 256, 128
    tiles = rows // tile
    count = rows // chunk
    slots = min(count, 6)
    step = 144
    acc = pltpu.VMEM((width, hidden), F32)
    keep = pltpu.VMEM((tile, hidden), BF16)
    return pl.pallas_call(
        functools.partial(ffn_backward_kernel, tiles, tile, chunk, slots, hidden),
        grid=(tiles,),
        out_shape=(
            jax.ShapeDtypeStruct((rows, width), BF16),
            jax.ShapeDtypeStruct((1, width), F32),
            jax.ShapeDtypeStruct((3, width, hidden), BF16),
            jax.ShapeDtypeStruct((rows, width), BF16),
        ),
        in_specs=[tile_block(tile, width)] * 5 + [tile_block(tile, hidden)] * 2
        + [whole_block(gains.shape), ANY],
        out_specs=(tile_block(tile, width), pl.BlockSpec((1, width), lambda i: (0, 0)), ANY, ANY),
        scratch_shapes=[pltpu.VMEM((width, wide), BF16)] * 3 + [pltpu.SemaphoreType.DMA((3,))] + [acc] * 3 + [keep] * 3
        + [pltpu.VMEM((2, step, hidden), BF16), pltpu.SemaphoreType.DMA((2,))]
        + line_sum_scratch(count, chunk, slots, width),
        compiler_params=pltpu.CompilerParams(
            collective_id=ident, has_side_effects=True, vmem_limit_bytes=63 * 2**20),
        name="ffn_backward",
    )(x, attn, dy, ffn, two, gate, up, gains, weights)


def middle_back_kernel(x_ref, attn_ref, dy_ref, d2_ref, h_ref, gain_ref, w_ref,
                       dm_ref, dh_ref, delta_ref, dgain_ref, go_ref, acc, wo_ref, w_sem):
    i = pl.program_id(0)

    @pl.when(i == 0)
    def _():
        head = wo_ref.shape[1]
        at = pl.multiple_of((2 * lax.axis_index("tp") + 1) * head, head)
        copy = pltpu.make_async_copy(w_ref.at[:, pl.ds(at, head)], wo_ref, w_sem)
        copy.start()
        copy.wait()
        acc[...] = jnp.zeros_like(acc)
        dgain_ref[...] = jnp.zeros_like(dgain_ref)

    middle, attn_hat, attn_inv = middle_of(x_ref[...], attn_ref[...], gain_ref[1:2, :])
    hat, inv = norm_parts(middle)
    d_part, d_gain = norm_back(d2_ref[...].astype(F32), hat, inv, gain_ref[2:3, :])
    dgain_ref[1:2, :] += d_gain[None]
    d_middle = dy_ref[...].astype(F32) + d_part
    dm_ref[...] = d_middle
    d_attn, d_gain = norm_back(d_middle, attn_hat, attn_inv, gain_ref[1:2, :])
    dgain_ref[0:1, :] += d_gain[None]
    d_attn = d_attn.astype(BF16)
    d_heads = dot(d_attn, wo_ref[...]).astype(BF16)
    dh_ref[...] = d_heads
    heads = h_ref[...]
    delta_ref[...] = jnp.sum(d_heads.astype(F32) * heads.astype(F32), axis=1, keepdims=True)
    acc[...] += dot(d_attn, heads, TN)

    @pl.when(i == pl.num_programs(0) - 1)
    def _():
        go_ref[...] = acc[...].astype(BF16)


def middle_back(x, attn, dy, d_two, heads, gains, weights):
    rows, width = x.shape
    head = heads.shape[1]
    tile = 256
    return pl.pallas_call(
        middle_back_kernel,
        grid=(rows // tile,),
        out_shape=(
            jax.ShapeDtypeStruct((rows, width), F32),
            jax.ShapeDtypeStruct((rows, head), BF16),
            jax.ShapeDtypeStruct((rows, 1), F32),
            jax.ShapeDtypeStruct((2, width), F32),
            jax.ShapeDtypeStruct((width, head), BF16),
        ),
        in_specs=[tile_block(tile, width)] * 4 + [tile_block(tile, head)] + [whole_block(gains.shape), ANY],
        out_specs=(
            tile_block(tile, width), tile_block(tile, head), tile_block(tile, 1),
            pl.BlockSpec((2, width), lambda i: (0, 0)), pl.BlockSpec((width, head), lambda i: (0, 0)),
        ),
        scratch_shapes=[pltpu.VMEM((width, head), F32), pltpu.VMEM((width, head), BF16), pltpu.SemaphoreType.DMA],
        compiler_params=pltpu.CompilerParams(vmem_limit_bytes=48 * 2**20),
        name="middle_back",
    )(x, attn, dy, d_two, heads, gains, weights)


def shards(tokens, segments, cotangent, w_query, w_key, w_value, w_out, w_gate, w_up, w_down,
           g_input, g_post_attn, g_pre_ffn, g_post_ffn, g_query, g_key):
    batches, seq_local, _, size, width = tokens.shape
    head = w_key.shape[1]
    groups = batches * seq_local
    per_group = 2 * size
    rows = groups * per_group
    ctx = lax.axis_size("ctx")
    length = per_group * ctx
    rank = lax.axis_index("ctx")
    shared = ("dp", "ctx")
    own_rows = g_input.shape[0]
    hidden = w_gate.shape[1]

    def column(gain):
        return jnp.pad(gain, (0, own_rows - gain.shape[0]))[:, None]

    own_ids = segments.reshape(groups, 2, size)
    id_cols = -(-own_ids.size // own_rows)
    ids = jnp.pad(own_ids.reshape(-1), (0, own_rows * id_cols - own_ids.size)).reshape(own_rows, id_cols)
    extra = jnp.concatenate(
        [column(g) for g in (g_input, g_post_attn, g_pre_ffn, g_post_ffn, g_query, g_key)] + [ids.astype(BF16)], axis=1)
    extra = jnp.pad(extra, ((0, 0), (0, 128 - extra.shape[1])))
    first = lax.all_gather(
        jnp.concatenate([w_query, w_key, w_value, extra], axis=1), shared, axis=0, tiled=True)
    mat_qkv = first[:, : 3 * head]
    side = first[:, 3 * head :]
    gain_cols = side[:, :8].astype(F32)
    gain_rows = gain_cols.T
    gain_input = gain_rows[0]
    short = g_query.shape[0]
    gain_query, gain_key = (
        gain_cols[:, i].reshape(-1, own_rows)[:, :short].reshape(-1) for i in (4, 5))
    ids = side[:, 6 : 6 + id_cols].reshape(-1, ctx, own_rows * id_cols)[:, :, : own_ids.size]
    ids = lax.dynamic_index_in_dim(ids, lax.axis_index("dp"), 0, keepdims=False).astype(jnp.int32)
    key_ids = ids.reshape(ctx, groups, 2, size).transpose(1, 2, 0, 3).reshape(groups, length)
    key_ids = jnp.where(key_ids == 0, -1, key_ids)

    def rows_of_16(w):
        return jnp.pad(w, ((0, -own_rows % 16), (0, 0)))

    wide = wide_of(hidden)
    line = gather_tp(rows_of_16(jnp.concatenate([w_query, w_out.T], axis=1)), 5)[:own_rows]
    second = jnp.concatenate(
        [line] + [jnp.pad(w, ((0, 0), (0, wide - hidden))) for w in (w_gate, w_up, w_down.T)], axis=1)

    offsets = rank * size + jnp.arange(size, dtype=jnp.int32)
    position = jnp.concatenate([offsets, length - 1 - offsets]).astype(F32)
    cosine, sine = angles(position, head // 2, head)
    cosine = jnp.broadcast_to(cosine, (groups, per_group, head // 2)).reshape(rows, head // 2)
    sine = jnp.broadcast_to(sine, (groups, per_group, head // 2)).reshape(rows, head // 2)

    inputs = tokens.reshape(rows, width).astype(F32)

    norm_one, scale_one = norm_parts(inputs)
    hidden_one = (norm_one * (1.0 + gain_input)).astype(BF16)
    raw = dot(hidden_one, mat_qkv)
    q_hat, q_scale = norm_parts(raw[:, :head])
    k_hat, k_scale = norm_parts(raw[:, head : 2 * head])
    queries = rotate(q_hat * (1.0 + gain_query), cosine, sine).astype(BF16)
    keys = rotate(k_hat * (1.0 + gain_key), cosine, sine).astype(BF16)
    values = raw[:, 2 * head :].astype(BF16)
    queries = queries.reshape(groups, 2, size, head)
    pairs = jnp.concatenate([keys, values], axis=1).reshape(batches, seq_local, 2, size, 2 * head)
    kv = [lax.all_gather(pairs[m], "ctx", axis=2, tiled=True).reshape(seq_local, length, 2 * head) for m in range(batches)]
    *kv, second = lax.optimization_barrier((*kv, second))
    weights = lax.all_gather(second, shared, axis=0, tiled=True)
    heads, heads_all, log_mass = [], [], []
    for m in range(batches):
        part = slice(m * seq_local, (m + 1) * seq_local)
        out, log = attend(queries[part], kv[m], own_ids[part, :, :, None], key_ids[part, None, :])
        heads.append(out.reshape(rows // batches, head))
        heads_all.append(gather_tp(heads[m], m * 6))
        log_mass.append(log)
    heads_own = jnp.concatenate(heads)
    log_mass = jnp.concatenate(log_mass)
    x_rows = tokens.reshape(rows, width)
    dy_rows = cotangent.reshape(rows, width)
    attn, hidden_two, gate, up, ffn_out = ffn_forward(x_rows, heads_all, gain_rows, weights, hidden, 1)
    output, d_gain_post_ffn, grad_ffn, d_two = ffn_backward(
        x_rows, attn, dy_rows, ffn_out, hidden_two, gate, up, gain_rows, weights, 2)
    grad_ffn = lax.psum_scatter(grad_ffn, shared, scatter_dimension=1, tiled=True).astype(F32)
    d_middle, d_heads, delta, d_gain_mid, grad_out_t = middle_back(
        x_rows, attn, dy_rows, d_two, heads_own, gain_rows, weights)

    d_query, d_kv = attend_back(
        queries, jnp.concatenate(kv), d_heads.reshape(groups, 2, size, head),
        log_mass.reshape(groups, 2, 1, size), delta.reshape(groups, 2, 1, size),
        own_ids[:, :, None, :], key_ids[:, :, None])
    d_kv = lax.psum_scatter(
        d_kv.reshape(groups, 2, length // 2, 2 * head), "ctx", scatter_dimension=2, tiled=True)
    d_q_rot = rotate(d_query.reshape(rows, head), cosine, -sine)
    d_q_raw, d_gain_query = norm_back(d_q_rot, q_hat, q_scale, gain_query)
    d_q_raw = d_q_raw.astype(BF16)
    d_q_all = gather_tp(d_q_raw, 4)
    d_kv, d_q_all = lax.optimization_barrier((d_kv, d_q_all))
    d_kv = sum_tp(d_kv.reshape(rows, 2 * head), 3).astype(F32)
    d_k_rot = rotate(d_kv[:, :head], cosine, -sine)
    d_k_raw, d_gain_key = norm_back(d_k_rot, k_hat, k_scale, gain_key)
    d_kv_raw = jnp.concatenate([d_k_raw.astype(BF16), d_kv[:, head:].astype(BF16)], axis=1)
    query_full = weights[:, : 8 * head].reshape(width, 4, 2, head)[:, :, 0].reshape(width, 4 * head)
    d_one = dot(d_q_all, query_full, NT) + dot(d_kv_raw, mat_qkv[:, head:], NT)
    d_part, d_gain_input = norm_back(d_one, norm_one, scale_one, gain_input)
    d_tokens = d_middle + d_part
    d_gain_query = lax.psum(d_gain_query, "tp")

    def spread(vector):
        return jnp.pad(vector.reshape(-1, short), ((0, 0), (0, own_rows - short))).reshape(-1)

    d_gains = jnp.stack(
        [d_gain_input, d_gain_mid[0], d_gain_mid[1], d_gain_post_ffn[0], spread(d_gain_query), spread(d_gain_key)], axis=1)
    d_gains = jnp.pad(d_gains, ((0, 0), (0, 128 - d_gains.shape[1]))).astype(BF16)
    last = jnp.concatenate(
        [dot(hidden_one, d_q_raw, TN).astype(BF16), dot(hidden_one, d_kv_raw, TN).astype(BF16),
         grad_out_t, d_gains], axis=1)
    last = lax.psum_scatter(last, shared, scatter_dimension=0, tiled=True).astype(F32)
    g = last[:, 4 * head :]
    return (
        output.reshape(tokens.shape),
        d_tokens.reshape(tokens.shape),
        last[:, :head],
        last[:, head : 2 * head],
        last[:, 2 * head : 3 * head],
        last[:, 3 * head : 4 * head].T,
        grad_ffn[0],
        grad_ffn[1],
        grad_ffn[2].T,
        g[:, 0],
        g[:, 1],
        g[:, 2],
        g[:, 3],
        g[:short, 4],
        g[:short, 5],
    )


def solution(mesh):
    shared = ("dp", "ctx")
    rows = P(None, "dp", None, "ctx", None)
    weights = (
        P(shared, "tp"), P(shared, None), P(shared, None), P("tp", shared),
        P(shared, "tp"), P(shared, "tp"), P("tp", shared),
    )
    gains = (P(shared),) * 6
    return jax.shard_map(
        shards,
        mesh=mesh,
        in_specs=(rows, P(None, "dp", None, "ctx"), rows) + weights + gains,
        out_specs=(rows, rows) + weights + gains,
        check_vma=False,
    )
```

```python
import functools

import jax
import jax.numpy as jnp
from jax import lax
from jax.experimental import pallas as pl
from jax.experimental.pallas import tpu as pltpu
from jax.sharding import PartitionSpec as P

EPS = 1e-06
THETA = 1000000.0
SCALE = 0.0625
NEGATIVE = -1e30
BF16 = jnp.bfloat16
F32 = jnp.float32
MESH = pl.DeviceIdType.MESH
NN = (((1,), (0,)), ((), ()))
NT = (((1,), (1,)), ((), ()))
TN = (((0,), (0,)), ((), ()))


def dot(a, b, dims=NN):
    return lax.dot_general(a, b, dims, preferred_element_type=F32)


def barrier_line(z):
    bar = pltpu.get_barrier_semaphore()

    @pl.when(z > 0)
    def _():
        pl.semaphore_signal(bar, inc=1, device_id={"tp": z - 1}, device_id_type=MESH)

    @pl.when(z < 3)
    def _():
        pl.semaphore_signal(bar, inc=1, device_id={"tp": z + 1}, device_id_type=MESH)

    pl.semaphore_wait(bar, jnp.where((z == 0) | (z == 3), 1, 2))


def gather_kernel(n, tile, width, x_ref, o_ref, lsem, *sems):
    su, ru, sd, rd = sems
    z = lax.axis_index("tp")
    barrier_line(z)

    def place(src, t):
        return o_ref.at[pl.ds(t * tile, tile), pl.ds(pl.multiple_of(src * width, width), width)]

    def send(src, t, k, way):
        ss, rs = (su, ru) if way > 0 else (sd, rd)
        here = x_ref.at[pl.ds(t * tile, tile)] if k == 0 else place(src, t)
        return pltpu.make_async_remote_copy(
            here, place(src, t), ss.at[k, t], rs.at[k, t],
            device_id={"tp": z + way}, device_id_type=MESH)

    own = pltpu.make_async_copy(x_ref, o_ref.at[:, pl.ds(pl.multiple_of(z * width, width), width)], lsem)
    own.start()
    for k in range(3):
        for t in range(n):
            for way in (1, -1):
                src = z - way * k
                ok = (z + way >= 0) & (z + way <= 3) & (src >= 0) & (src <= 3)
                if k > 0:
                    came = (src >= 0) & (src <= 3)

                    @pl.when(came)
                    def _():
                        send(src, t, k - 1, way).wait_recv()

                @pl.when(ok)
                def _():
                    send(src, t, k, way).start()
    for way in (1, -1):
        src = z - way * 3
        came = (src >= 0) & (src <= 3)

        @pl.when(came)
        def _():
            for t in range(n):
                send(src, t, 2, way).wait_recv()

    for k in range(3):
        for way in (1, -1):
            src = z - way * k
            ok = (z + way >= 0) & (z + way <= 3) & (src >= 0) & (src <= 3)

            @pl.when(ok)
            def _():
                for t in range(n):
                    send(src, t, k, way).wait_send()
    own.wait()


def gather_tp(x, ident):
    rows, width = x.shape
    tile = 256 if rows % 256 == 0 else rows
    n = rows // tile
    dma = pltpu.SemaphoreType.DMA((3, n))
    return pl.pallas_call(
        functools.partial(gather_kernel, n, tile, width),
        out_shape=jax.ShapeDtypeStruct((rows, 4 * width), x.dtype),
        in_specs=[pl.BlockSpec(memory_space=pl.ANY)],
        out_specs=pl.BlockSpec(memory_space=pl.ANY),
        scratch_shapes=[pltpu.SemaphoreType.DMA] + [dma] * 4,
        compiler_params=pltpu.CompilerParams(collective_id=ident, has_side_effects=True),
        name=f"gather_tp_{ident}",
    )(x)


def block_starts(half, t, blocks, rank):
    if half == 0:
        return t
    return jnp.where(t < blocks, t, t + rank + 1)


def attend_kernel(blocks, q_ref, kv_ref, qs_ref, ks_ref, o_ref, l_ref):
    rank = lax.axis_index("ctx")
    size, head = q_ref.shape[2:]
    row = lax.broadcasted_iota(jnp.int32, (size, size), 0)
    col = lax.broadcasted_iota(jnp.int32, (size, size), 1)
    for half in range(2):
        q = q_ref[0, half] * jnp.asarray(SCALE, BF16)
        qseg = qs_ref[0, half]

        def part(block):
            start = pl.multiple_of(block * size, size)
            k = kv_ref[0, pl.ds(start, size), :head]
            v = kv_ref[0, pl.ds(start, size), head:]
            same = qseg == ks_ref[0, :, pl.ds(start, size)]
            return dot(q, k, NT), v, same

        s, v, same = part(rank + half * blocks)
        order = (col <= row) if half == 0 else (col >= row)
        s = jnp.where((same & order) | (col == row), s, NEGATIVE)
        top = jnp.max(s, axis=1, keepdims=True)
        p = jnp.exp(s - top)
        mass = jnp.sum(p, axis=1, keepdims=True)
        acc = dot(p.astype(BF16), v)

        def step(t, carry):
            top, mass, acc = carry
            s, v, same = part(block_starts(half, t, blocks, rank))
            s = jnp.where(same, s, NEGATIVE)
            new = jnp.maximum(top, jnp.max(s, axis=1, keepdims=True))
            keep = jnp.exp(top - new)
            p = jnp.exp(s - new)
            mass = mass * keep + jnp.sum(p, axis=1, keepdims=True)
            acc = acc * keep + dot(p.astype(BF16), v)
            return new, mass, acc

        count = rank if half == 0 else 2 * blocks - 1 - rank
        top, mass, acc = lax.fori_loop(0, count, step, (top, mass, acc))
        o_ref[0, half] = (acc / mass).astype(BF16)
        l_ref[0, half] = top + jnp.log(mass)


def attend(q, kv, qseg, kseg):
    groups, _, size, head = q.shape
    length = kv.shape[1]
    blocks = length // (2 * size)
    return pl.pallas_call(
        functools.partial(attend_kernel, blocks),
        grid=(groups,),
        out_shape=(
            jax.ShapeDtypeStruct(q.shape, BF16),
            jax.ShapeDtypeStruct((groups, 2, size, 1), F32),
        ),
        in_specs=[
            pl.BlockSpec((1, 2, size, head), lambda g: (g, 0, 0, 0)),
            pl.BlockSpec((1, length, 2 * head), lambda g: (g, 0, 0)),
            pl.BlockSpec((1, 2, size, 1), lambda g: (g, 0, 0, 0)),
            pl.BlockSpec((1, 1, length), lambda g: (g, 0, 0)),
        ],
        out_specs=(
            pl.BlockSpec((1, 2, size, head), lambda g: (g, 0, 0, 0)),
            pl.BlockSpec((1, 2, size, 1), lambda g: (g, 0, 0, 0)),
        ),
        compiler_params=pltpu.CompilerParams(vmem_limit_bytes=48 * 2**20),
        name="attend",
    )(q, kv, qseg, kseg)


def attend_back_kernel(blocks, q_ref, kv_ref, do_ref, l_ref, d_ref, qs_ref, ks_ref,
                       dq_ref, dkv_ref, dk_acc, dv_acc):
    rank = lax.axis_index("ctx")
    size = q_ref.shape[2]
    head = q_ref.shape[3]
    row = lax.broadcasted_iota(jnp.int32, (size, size), 0)
    col = lax.broadcasted_iota(jnp.int32, (size, size), 1)
    dk_acc[...] = jnp.zeros_like(dk_acc)
    dv_acc[...] = jnp.zeros_like(dv_acc)
    for half in range(2):
        q = q_ref[0, half] * jnp.asarray(SCALE, BF16)
        do = do_ref[0, half]
        qseg = qs_ref[0, half]
        log_mass = l_ref[0, half]
        delta = d_ref[0, half]

        def part(block, own):
            rows = pl.ds(pl.multiple_of(block * size, size), size)
            k = kv_ref[0, rows, :head]
            v = kv_ref[0, rows, head:]
            allowed = ks_ref[0, rows, :] == qseg
            if own:
                order = (row <= col) if half == 0 else (row >= col)
                allowed = (allowed & order) | (col == row)
            s = jnp.where(allowed, dot(k, q, NT), NEGATIVE)
            p = jnp.exp(s - log_mass)
            ds = (p * (dot(v, do, NT) - delta)).astype(BF16)
            dv_acc[rows, :] += dot(p.astype(BF16), do)
            dk_acc[rows, :] += dot(ds, q)
            return dot(ds, k, TN)

        def step(t, dq):
            return dq + part(block_starts(half, t, blocks, rank), False)

        dq = part(rank + half * blocks, True)
        count = rank if half == 0 else 2 * blocks - 1 - rank
        dq_ref[0, half] = SCALE * lax.fori_loop(0, count, step, dq)
    dkv_ref[0, :, :head] = dk_acc[...].astype(BF16)
    dkv_ref[0, :, head:] = dv_acc[...].astype(BF16)


def attend_back(q, kv, do, log_mass, delta, qseg, kseg):
    groups, _, size, head = q.shape
    length = kv.shape[1]
    blocks = length // (2 * size)
    halves = pl.BlockSpec((1, 2, size, head), lambda g: (g, 0, 0, 0))
    whole = pl.BlockSpec((1, length, 2 * head), lambda g: (g, 0, 0))
    line = pl.BlockSpec((1, 2, 1, size), lambda g: (g, 0, 0, 0))
    return pl.pallas_call(
        functools.partial(attend_back_kernel, blocks),
        grid=(groups,),
        out_shape=(
            jax.ShapeDtypeStruct(q.shape, F32),
            jax.ShapeDtypeStruct((groups, length, 2 * head), BF16),
        ),
        in_specs=[halves, whole, halves, line, line, line,
                  pl.BlockSpec((1, length, 1), lambda g: (g, 0, 0))],
        out_specs=(halves, pl.BlockSpec((1, length, 2 * head), lambda g: (g, 0, 0))),
        scratch_shapes=[pltpu.VMEM((length, head), F32)] * 2,
        compiler_params=pltpu.CompilerParams(vmem_limit_bytes=56 * 2**20),
        name="attend_back",
    )(q, kv, do, log_mass, delta, qseg, kseg)


def angles(position, half_size, full_size):
    frequency = THETA ** (-2.0 * jnp.arange(half_size, dtype=F32) / full_size)
    turned = position[:, None] * frequency[None, :]
    return (jnp.cos(turned), jnp.sin(turned))


def rotate(tensor, cosine, sine):
    half_size = tensor.shape[-1] // 2
    a = tensor[..., :half_size]
    b = tensor[..., half_size:]
    return jnp.concatenate([a * cosine - b * sine, b * cosine + a * sine], axis=-1)


def norm_parts(values):
    inv = lax.rsqrt(jnp.mean(values * values, axis=-1, keepdims=True) + EPS)
    return (values * inv, inv)


def norm_back(upstream, normalized, inv, gain):
    d_norm = upstream * (1.0 + gain)
    d_values = inv * (d_norm - normalized * jnp.mean(d_norm * normalized, axis=-1, keepdims=True))
    return (d_values, jnp.sum(upstream * normalized, axis=0))


def gelu_tanh(values):
    return jax.nn.gelu(values, approximate=True)


class LineSum:
    def __init__(self, count, chunk, slots, own, near, far, out, sems):
        self.count, self.chunk, self.slots = count, chunk, slots
        self.own, self.near, self.far, self.out = own, near, far, out
        self.sems = sems
        self.z = z = lax.axis_index("tp")
        self.hub = (z == 1) | (z == 2)
        self.leaf = (z == 0) | (z == 3)
        self.other_hub = jnp.where(z == 1, 2, 1)
        self.my_hub = jnp.where(z == 0, 1, 2)
        self.my_leaf = jnp.where(z == 1, 0, 3)

    def slot(self, c):
        return pl.ds(pl.multiple_of(lax.rem(c, self.slots) * self.chunk, self.chunk), self.chunk)

    def rows(self, c):
        return pl.ds(pl.multiple_of(c * self.chunk, self.chunk), self.chunk)

    def inwards(self, c):
        return pltpu.make_async_remote_copy(
            self.own.at[self.slot(c)], self.near.at[self.slot(c)], self.sems[0].at[c], self.sems[1].at[c],
            device_id={"tp": self.my_hub}, device_id_type=MESH)

    def across(self, c):
        return pltpu.make_async_remote_copy(
            self.own.at[self.slot(c)], self.far.at[self.slot(c)], self.sems[2].at[c], self.sems[3].at[c],
            device_id={"tp": self.other_hub}, device_id_type=MESH)

    def outwards(self, c):
        return pltpu.make_async_remote_copy(
            self.far.at[self.slot(c)], self.out.at[self.rows(c)], self.sems[4].at[c], self.sems[5].at[c],
            device_id={"tp": self.my_leaf}, device_id_type=MESH)

    def store(self, c):
        return pltpu.make_async_copy(self.far.at[self.slot(c)], self.out.at[self.rows(c)], self.sems[6].at[c])

    def put(self, c, value):
        ring = self.slots < self.count
        if ring:
            @pl.when(c >= self.slots)
            def _():
                @pl.when(self.leaf)
                def _():
                    self.inwards(c - self.slots).wait_send()

                @pl.when(self.hub)
                def _():
                    self.across(c - self.slots).wait_send()

        self.own[self.slot(c), :] = value

        @pl.when(self.leaf)
        def _():
            if ring:
                @pl.when(c >= self.slots)
                def _():
                    pl.semaphore_wait(self.sems[7], 1)
            self.inwards(c).start()

    def pair(self, c):
        ring = self.slots < self.count

        @pl.when(self.hub)
        def _():
            self.inwards(c).wait_recv()
            at = self.slot(c)
            self.own[at, :] = (self.own[at, :].astype(F32) + self.near[at, :].astype(F32)).astype(BF16)
            if ring:
                @pl.when(c < self.count - self.slots)
                def _():
                    pl.semaphore_signal(self.sems[7], inc=1, device_id={"tp": self.my_leaf}, device_id_type=MESH)

                @pl.when(c >= self.slots)
                def _():
                    pl.semaphore_wait(self.sems[8], 1)
            self.across(c).start()

    def total(self, c):
        @pl.when(self.hub)
        def _():
            self.across(c).wait_recv()
            at = self.slot(c)
            self.far[at, :] = (self.own[at, :].astype(F32) + self.far[at, :].astype(F32)).astype(BF16)
            self.outwards(c).start()
            self.store(c).start()

    def retire(self, c):
        @pl.when(self.hub)
        def _():
            self.outwards(c).wait_send()
            self.store(c).wait()
            if self.slots < self.count:
                @pl.when(c < self.count - self.slots)
                def _():
                    pl.semaphore_signal(self.sems[8], inc=1, device_id={"tp": self.other_hub}, device_id_type=MESH)

    def finish(self):
        first = max(0, self.count - self.slots)

        @pl.when(self.leaf)
        def _():
            for c in range(self.count):
                self.outwards(c).wait_recv()
            for c in range(first, self.count):
                self.inwards(c).wait_send()

        @pl.when(self.hub)
        def _():
            for c in range(first, self.count):
                self.across(c).wait_send()


def line_sum_scratch(count, chunk, slots, cols):
    dma = pltpu.SemaphoreType.DMA((count,))
    regular = pltpu.SemaphoreType.REGULAR
    return [pltpu.VMEM((slots * chunk, cols), BF16)] * 3 + [dma] * 7 + [regular] * 2


def gelu_parts(v):
    c = 0.7978845608028654
    square = v * v
    t = jnp.tanh(v * (c + (c * 0.044715) * square))
    half = 0.5 + 0.5 * t
    value = v * half
    slope = half + (0.5 * v) * (1.0 - t * t) * (c + (3.0 * c * 0.044715) * square)
    return value, slope


def column_parts(cols):
    middle = -(-cols // 256) * 128
    return [(0, middle), (middle, cols)] if middle < cols else [(0, cols)]


def middle_of(x, attn, gain_post_attn):
    hat, inv = norm_parts(attn.astype(F32))
    return x.astype(F32) + hat * (1.0 + gain_post_attn), hat, inv


def load_ffn_weights(weights, refs, sem):
    wide = refs[0].shape[1]
    base = weights.shape[1] - 3 * wide
    return [
        pltpu.make_async_copy(weights.at[:, pl.ds(base + j * wide, wide)], ref, sem.at[j])
        for j, ref in enumerate(refs)
    ]


def ffn_forward_kernel(tiles, tile, chunk, hidden, x_ref, h0_ref, h1_ref, gain_ref, w_ref,
                       attn_ref, two_ref, gate_ref, up_ref, out_ref, wo_ref, wg_ref, wu_ref, wd_ref, w_sem, own, near, far, *sems):
    i = pl.program_id(0)
    per = tile // chunk
    line = LineSum(tiles * per, chunk, tiles * per, own, near, far, out_ref, sems)
    head = wo_ref.shape[1] // 4

    @pl.when(i == 0)
    def _():
        copies = load_ffn_weights(w_ref, (wg_ref, wu_ref, wd_ref), w_sem)
        copies += [
            pltpu.make_async_copy(
                w_ref.at[:, pl.ds((2 * j + 1) * head, head)], wo_ref.at[:, pl.ds(j * head, head)], w_sem.at[3 + j])
            for j in range(4)
        ]
        for copy in copies:
            copy.start()
        barrier_line(line.z)
        for copy in copies:
            copy.wait()

    heads = jnp.where(i < tiles // 2, h0_ref[...], h1_ref[...])
    attn = dot(heads, wo_ref[...], NT).astype(BF16)
    attn_ref[...] = attn
    middle, _, _ = middle_of(x_ref[...], attn, gain_ref[1:2, :])
    hat, _ = norm_parts(middle)
    two = (hat * (1.0 + gain_ref[2:3, :])).astype(BF16)
    two_ref[...] = two
    part = None
    for a, b in column_parts(hidden):
        gate = dot(two, wg_ref[:, a:b])
        up = dot(two, wu_ref[:, a:b])
        gate_ref[:, a:b] = gate.astype(BF16)
        up_ref[:, a:b] = up.astype(BF16)
        value, _ = gelu_parts(gate)
        more = dot((value * up).astype(BF16), wd_ref[:, a:b], NT)
        part = more if part is None else part + more
    for j in range(per):
        line.put(i * per + j, part[j * chunk : (j + 1) * chunk].astype(BF16))

    @pl.when(i >= 1)
    def _():
        for j in range(per):
            line.pair((i - 1) * per + j)

    @pl.when(i >= 2)
    def _():
        for j in range(per):
            line.total((i - 2) * per + j)

    @pl.when(i == tiles - 1)
    def _():
        last = tiles * per
        for j in range(per):
            line.pair(last - per + j)
        for c in range(max(0, last - 2 * per), last):
            line.total(c)
        for c in range(last):
            line.retire(c)
        line.finish()


def whole_block(shape):
    return pl.BlockSpec(shape, lambda i: (0,) * len(shape), pipeline_mode=pl.Buffered(1))


def tile_block(tile, cols):
    return pl.BlockSpec((tile, cols), lambda i: (i, 0))


ANY = pl.BlockSpec(memory_space=pl.ANY)


def wide_of(hidden):
    return -(-hidden // 128) * 128


def ffn_forward(x, heads, gains, weights, hidden, ident):
    rows, width = x.shape
    all_heads = heads[0].shape[1]
    tile, chunk = 256, 128
    tiles = rows // tile
    half = tiles // 2
    count = rows // chunk
    wide = wide_of(hidden)
    return pl.pallas_call(
        functools.partial(ffn_forward_kernel, tiles, tile, chunk, hidden),
        grid=(tiles,),
        out_shape=(
            jax.ShapeDtypeStruct((rows, width), BF16),
            jax.ShapeDtypeStruct((rows, width), BF16),
            jax.ShapeDtypeStruct((rows, hidden), BF16),
            jax.ShapeDtypeStruct((rows, hidden), BF16),
            jax.ShapeDtypeStruct((rows, width), BF16),
        ),
        in_specs=[
            tile_block(tile, width),
            pl.BlockSpec((tile, all_heads), lambda i: (jnp.minimum(i, half - 1), 0)),
            pl.BlockSpec((tile, all_heads), lambda i: (jnp.maximum(i - half, 0), 0)),
            whole_block(gains.shape),
            ANY,
        ],
        out_specs=(tile_block(tile, width), tile_block(tile, width), tile_block(tile, hidden), tile_block(tile, hidden), ANY),
        scratch_shapes=[pltpu.VMEM((width, all_heads), BF16)] + [pltpu.VMEM((width, wide), BF16)] * 3
        + [pltpu.SemaphoreType.DMA((7,))]
        + line_sum_scratch(count, chunk, count, width),
        compiler_params=pltpu.CompilerParams(
            collective_id=ident, has_side_effects=True, vmem_limit_bytes=60 * 2**20),
        name="ffn_forward",
    )(x, heads[0], heads[1], gains, weights)


def ffn_backward_kernel(tiles, tile, chunk, slots, hidden, x_ref, attn_ref, dy_ref, ffn_ref, two_ref, gate_ref, up_ref,
                        gain_ref, w_ref,
                        y_ref, dgain_ref, grad_ref, out_ref, wg_ref, wu_ref, wd_ref, w_sem,
                        acc_g, acc_u, acc_d, keep_g, keep_u, keep_h, stage, stage_sem, own, near, far, *sems):
    i = pl.program_id(0)
    per = tile // chunk
    last = tiles * per
    line = LineSum(last, chunk, slots, own, near, far, out_ref, sems)

    @pl.when(i == 0)
    def _():
        copies = load_ffn_weights(w_ref, (wg_ref, wu_ref, wd_ref), w_sem)
        for copy in copies:
            copy.start()
        barrier_line(line.z)
        for acc in (acc_g, acc_u, acc_d, dgain_ref):
            acc[...] = jnp.zeros_like(acc)
        for copy in copies:
            copy.wait()

    middle, _, _ = middle_of(x_ref[...], attn_ref[...], gain_ref[1:2, :])
    hat, inv = norm_parts(ffn_ref[...].astype(F32))
    gain = gain_ref[3:4, :]
    y_ref[...] = (middle + hat * (1.0 + gain)).astype(BF16)
    d_ffn, d_gain = norm_back(dy_ref[...].astype(F32), hat, inv, gain)
    dgain_ref[...] += d_gain[None]
    d_ffn = d_ffn.astype(BF16)
    part = None
    for a, b in column_parts(hidden):
        d_hidden = dot(d_ffn, wd_ref[:, a:b])
        up = up_ref[:, a:b].astype(F32)
        value, slope = gelu_parts(gate_ref[:, a:b].astype(F32))
        keep_h[:, a:b] = (value * up).astype(BF16)
        d_gate = (d_hidden * up * slope).astype(BF16)
        d_up = (d_hidden * value).astype(BF16)
        keep_g[:, a:b] = d_gate
        keep_u[:, a:b] = d_up
        more = dot(d_gate, wg_ref[:, a:b], NT) + dot(d_up, wu_ref[:, a:b], NT)
        part = more if part is None else part + more
    for j in range(per):
        line.put(i * per + j, part[j * chunk : (j + 1) * chunk].astype(BF16))

    @pl.when(i >= 1)
    def _():
        for j in range(per):
            line.pair((i - 1) * per + j)

    acc_g[...] += dot(two_ref[...], keep_g[...], TN)
    acc_u[...] += dot(two_ref[...], keep_u[...], TN)
    acc_d[...] += dot(d_ffn, keep_h[...], TN)

    @pl.when(i >= 2)
    def _():
        for j in range(per):
            line.total((i - 2) * per + j)

    @pl.when(i >= 3)
    def _():
        for j in range(per):
            line.retire((i - 3) * per + j)

    @pl.when(i == tiles - 1)
    def _():
        for j in range(per):
            line.pair(last - per + j)
        step = stage.shape[1]
        count = acc_g.shape[0] // step

        def piece(acc, out, k, at):
            @pl.when(k >= 2)
            def _():
                pltpu.make_async_copy(stage.at[at], out.at[pl.ds(0, step)], stage_sem.at[at]).wait()
            rows = pl.ds(pl.multiple_of(k * step, step), step)
            stage[at] = acc[rows, :].astype(BF16)
            pltpu.make_async_copy(stage.at[at], out.at[rows], stage_sem.at[at]).start()

        for acc, out in ((acc_g, grad_ref.at[0]), (acc_u, grad_ref.at[1]), (acc_d, grad_ref.at[2])):
            def pieces(k, _):
                piece(acc, out, k, lax.rem(k, 2))
                return 0

            lax.fori_loop(0, count, pieces, 0)
            for at in range(2):
                pltpu.make_async_copy(stage.at[at], out.at[pl.ds(0, step)], stage_sem.at[at]).wait()
            if acc is acc_g:
                for c in range(max(0, last - 2 * per), last - per):
                    line.total(c)
            if acc is acc_u:
                for c in range(last - per, last):
                    line.total(c)
        for c in range(max(0, last - 3 * per), last):
            line.retire(c)
        line.finish()


def ffn_backward(x, attn, dy, ffn, two, gate, up, gains, weights, ident):
    rows, width = x.shape
    hidden = gate.shape[1]
    wide = wide_of(hidden)
    tile, chunk = 256, 128
    tiles = rows // tile
    count = rows // chunk
    slots = min(count, 6)
    step = 144
    acc = pltpu.VMEM((width, hidden), F32)
    keep = pltpu.VMEM((tile, hidden), BF16)
    return pl.pallas_call(
        functools.partial(ffn_backward_kernel, tiles, tile, chunk, slots, hidden),
        grid=(tiles,),
        out_shape=(
            jax.ShapeDtypeStruct((rows, width), BF16),
            jax.ShapeDtypeStruct((1, width), F32),
            jax.ShapeDtypeStruct((3, width, hidden), BF16),
            jax.ShapeDtypeStruct((rows, width), BF16),
        ),
        in_specs=[tile_block(tile, width)] * 5 + [tile_block(tile, hidden)] * 2
        + [whole_block(gains.shape), ANY],
        out_specs=(tile_block(tile, width), pl.BlockSpec((1, width), lambda i: (0, 0)), ANY, ANY),
        scratch_shapes=[pltpu.VMEM((width, wide), BF16)] * 3 + [pltpu.SemaphoreType.DMA((3,))] + [acc] * 3 + [keep] * 3
        + [pltpu.VMEM((2, step, hidden), BF16), pltpu.SemaphoreType.DMA((2,))]
        + line_sum_scratch(count, chunk, slots, width),
        compiler_params=pltpu.CompilerParams(
            collective_id=ident, has_side_effects=True, vmem_limit_bytes=63 * 2**20),
        name="ffn_backward",
    )(x, attn, dy, ffn, two, gate, up, gains, weights)


def middle_back_kernel(x_ref, attn_ref, dy_ref, d2_ref, h_ref, gain_ref, w_ref,
                       dm_ref, dh_ref, delta_ref, dgain_ref, go_ref, acc, wo_ref, w_sem):
    i = pl.program_id(0)

    @pl.when(i == 0)
    def _():
        head = wo_ref.shape[1]
        at = pl.multiple_of((2 * lax.axis_index("tp") + 1) * head, head)
        copy = pltpu.make_async_copy(w_ref.at[:, pl.ds(at, head)], wo_ref, w_sem)
        copy.start()
        copy.wait()
        acc[...] = jnp.zeros_like(acc)
        dgain_ref[...] = jnp.zeros_like(dgain_ref)

    middle, attn_hat, attn_inv = middle_of(x_ref[...], attn_ref[...], gain_ref[1:2, :])
    hat, inv = norm_parts(middle)
    d_part, d_gain = norm_back(d2_ref[...].astype(F32), hat, inv, gain_ref[2:3, :])
    dgain_ref[1:2, :] += d_gain[None]
    d_middle = dy_ref[...].astype(F32) + d_part
    dm_ref[...] = d_middle
    d_attn, d_gain = norm_back(d_middle, attn_hat, attn_inv, gain_ref[1:2, :])
    dgain_ref[0:1, :] += d_gain[None]
    d_attn = d_attn.astype(BF16)
    d_heads = dot(d_attn, wo_ref[...]).astype(BF16)
    dh_ref[...] = d_heads
    heads = h_ref[...]
    delta_ref[...] = jnp.sum(d_heads.astype(F32) * heads.astype(F32), axis=1, keepdims=True)
    acc[...] += dot(d_attn, heads, TN)

    @pl.when(i == pl.num_programs(0) - 1)
    def _():
        go_ref[...] = acc[...].astype(BF16)


def middle_back(x, attn, dy, d_two, heads, gains, weights):
    rows, width = x.shape
    head = heads.shape[1]
    tile = 256
    return pl.pallas_call(
        middle_back_kernel,
        grid=(rows // tile,),
        out_shape=(
            jax.ShapeDtypeStruct((rows, width), F32),
            jax.ShapeDtypeStruct((rows, head), BF16),
            jax.ShapeDtypeStruct((rows, 1), F32),
            jax.ShapeDtypeStruct((2, width), F32),
            jax.ShapeDtypeStruct((width, head), BF16),
        ),
        in_specs=[tile_block(tile, width)] * 4 + [tile_block(tile, head)] + [whole_block(gains.shape), ANY],
        out_specs=(
            tile_block(tile, width), tile_block(tile, head), tile_block(tile, 1),
            pl.BlockSpec((2, width), lambda i: (0, 0)), pl.BlockSpec((width, head), lambda i: (0, 0)),
        ),
        scratch_shapes=[pltpu.VMEM((width, head), F32), pltpu.VMEM((width, head), BF16), pltpu.SemaphoreType.DMA],
        compiler_params=pltpu.CompilerParams(vmem_limit_bytes=48 * 2**20),
        name="middle_back",
    )(x, attn, dy, d_two, heads, gains, weights)


class ResidentSum(LineSum):
    def outwards(self, c):
        return pltpu.make_async_remote_copy(
            self.out.at[self.rows(c)], self.out.at[self.rows(c)], self.sems[4].at[c], self.sems[5].at[c],
            device_id={"tp": self.my_leaf}, device_id_type=MESH)

    def total(self, c):
        @pl.when(self.hub)
        def _():
            self.across(c).wait_recv()
            at = self.rows(c)
            self.out[at, :] = (self.own[at, :].astype(F32) + self.far[at, :].astype(F32)).astype(BF16)
            self.outwards(c).start()

    def arrived(self, c):
        @pl.when(self.leaf)
        def _():
            self.outwards(c).wait_recv()

    def finish(self):
        @pl.when(self.leaf)
        def _():
            for c in range(self.count):
                self.inwards(c).wait_send()

        @pl.when(self.hub)
        def _():
            for c in range(self.count):
                self.across(c).wait_send()
                self.outwards(c).wait_send()


class LineGather:
    def __init__(self, whole, tile, width, sems):
        self.whole, self.tile, self.width, self.sems = whole, tile, width, sems
        self.z = lax.axis_index("tp")

    def send(self, src, t, hop, way):
        ss, rs = self.sems[:2] if way > 0 else self.sems[2:]
        place = self.whole.at[
            pl.ds(pl.multiple_of(t * self.tile, self.tile), self.tile),
            pl.ds(pl.multiple_of(src * self.width, self.width), self.width)]
        return pltpu.make_async_remote_copy(
            place, place, ss.at[hop, t], rs.at[hop, t],
            device_id={"tp": self.z + way}, device_id_type=MESH)

    def going(self, hop, way):
        src = self.z - way * hop
        return src, (self.z + way >= 0) & (self.z + way <= 3) & (src >= 0) & (src <= 3)

    def coming(self, hop, way):
        src = self.z - way * (hop + 1)
        return src, (src >= 0) & (src <= 3)

    def forward(self, t, hop):
        for way in (1, -1):
            if hop > 0:
                self.wait(t, hop - 1, way)
            src, ok = self.going(hop, way)

            @pl.when(ok)
            def _():
                self.send(src, t, hop, way).start()

    def wait(self, t, hop, way):
        src, ok = self.coming(hop, way)

        @pl.when(ok)
        def _():
            self.send(src, t, hop, way).wait_recv()

    def arrived(self, t):
        for way in (1, -1):
            self.wait(t, 2, way)

    def finish(self, tiles):
        for hop in range(3):
            for way in (1, -1):
                src, ok = self.going(hop, way)

                @pl.when(ok)
                def _():
                    def one(t, _):
                        self.send(src, t, hop, way).wait_send()
                        return 0

                    lax.fori_loop(0, tiles, one, 0)


def query_back_kernel(tiles, tile, dq_ref, hat_ref, inv_ref, cos_ref, sin_ref, x_ref, gain_ref, gq_ref, w_ref,
                      one_ref, grad_ref, dgain_ref, acc, wq_ref, w_sem, whole, *sems):
    i = pl.program_id(0)
    head = hat_ref.shape[1]
    line = LineGather(whole, tile, head, sems)

    @pl.when(i == 0)
    def _():
        copies = [
            pltpu.make_async_copy(w_ref.at[:, pl.ds(2 * j * head, head)], wq_ref.at[:, pl.ds(j * head, head)], w_sem.at[j])
            for j in range(4)
        ]
        for copy in copies:
            copy.start()
        barrier_line(line.z)
        acc[...] = jnp.zeros_like(acc)
        dgain_ref[...] = jnp.zeros_like(dgain_ref)
        for copy in copies:
            copy.wait()

    @pl.when(i < tiles)
    def _():
        d_rot = rotate(dq_ref[...], cos_ref[...], -sin_ref[...])
        d_raw, d_gain = norm_back(d_rot, hat_ref[...], inv_ref[...], gq_ref[...])
        d_raw = d_raw.astype(BF16)
        at = pl.ds(pl.multiple_of(line.z * head, head), head)
        whole[pl.ds(pl.multiple_of(i * tile, tile), tile), at] = d_raw
        line.forward(i, 0)
        dgain_ref[...] += d_gain[None]
        hat, _ = norm_parts(x_ref[...].astype(F32))
        one = (hat * (1.0 + gain_ref[0:1, :])).astype(BF16)
        acc[...] += dot(one, d_raw, TN)

    @pl.when((i >= 1) & (i <= tiles))
    def _():
        line.forward(i - 1, 1)

    @pl.when((i >= 2) & (i <= tiles + 1))
    def _():
        line.forward(i - 2, 2)

    @pl.when(i >= 3)
    def _():
        line.arrived(i - 3)
        one_ref[...] = dot(whole[pl.ds(pl.multiple_of((i - 3) * tile, tile), tile), :], wq_ref[...], NT)

    @pl.when(i == tiles + 2)
    def _():
        grad_ref[...] = acc[...].astype(BF16)
        line.finish(tiles)


def query_back(dq, hat, inv, cosine, sine, x, gains, gain_query, weights, ident):
    rows, width = x.shape
    head = hat.shape[1]
    tile = 256
    tiles = rows // tile
    dma = pltpu.SemaphoreType.DMA((3, tiles))

    def early(cols):
        return pl.BlockSpec((tile, cols), lambda i: (jnp.minimum(i, tiles - 1), 0))

    return pl.pallas_call(
        functools.partial(query_back_kernel, tiles, tile),
        grid=(tiles + 3,),
        out_shape=(
            jax.ShapeDtypeStruct((rows, width), F32),
            jax.ShapeDtypeStruct((width, head), BF16),
            jax.ShapeDtypeStruct((1, head), F32),
        ),
        in_specs=[early(head), early(head), early(1), early(head // 2), early(head // 2), early(width),
                  whole_block(gains.shape), whole_block(gain_query.shape), ANY],
        out_specs=(
            pl.BlockSpec((tile, width), lambda i: (jnp.maximum(i - 3, 0), 0)),
            pl.BlockSpec((width, head), lambda i: (0, 0)),
            pl.BlockSpec((1, head), lambda i: (0, 0)),
        ),
        scratch_shapes=[
            pltpu.VMEM((width, head), F32), pltpu.VMEM((width, 4 * head), BF16), pltpu.SemaphoreType.DMA((4,)),
            pltpu.VMEM((rows, 4 * head), BF16)] + [dma] * 4,
        compiler_params=pltpu.CompilerParams(
            collective_id=ident, has_side_effects=True, vmem_limit_bytes=48 * 2**20),
        name="query_back",
    )(dq, hat, inv, cosine, sine, x, gains, gain_query, weights)


def key_back_kernel(tiles, tile, chunk, own_rows, dkv_ref, hat_ref, inv_ref, cos_ref, sin_ref, x_ref, dm_ref, part_ref,
                    gain_ref, gk_ref, w_ref, dgq_ref, dg_mid_ref, dg_post_ref, grad_q_ref, grad_o_ref,
                    dx_ref, last_ref, acc, acc_in, acc_key, w_kv, w_sem, out, own, near, far, *sems):
    i = pl.program_id(0)
    head = hat_ref.shape[1]
    per = tile // chunk
    count = tiles * per + 1
    line = ResidentSum(count, chunk, count, own, near, far, out, sems)

    @pl.when(i == 0)
    def _():
        copy = pltpu.make_async_copy(w_ref.at[:, pl.ds(head, 2 * head)], w_kv, w_sem)
        copy.start()
        barrier_line(line.z)
        for ref in (acc, acc_in, acc_key):
            ref[...] = jnp.zeros_like(ref)
        copy.wait()
        line.put(count - 1, jnp.broadcast_to(
            jnp.concatenate([dgq_ref[...], dgq_ref[...]], axis=1).astype(BF16), (chunk, 2 * head)))

    @pl.when(i < tiles)
    def _():
        for j in range(per):
            line.put(i * per + j, dkv_ref[j * chunk : (j + 1) * chunk, :])

    @pl.when((i >= 1) & (i <= tiles))
    def _():
        for j in range(per):
            line.pair((i - 1) * per + j)

    @pl.when((i >= 2) & (i <= tiles + 1))
    def _():
        for j in range(per):
            line.total((i - 2) * per + j)

    @pl.when(i == 1)
    def _():
        line.pair(count - 1)

    @pl.when(i == 2)
    def _():
        line.total(count - 1)

    @pl.when(i >= 3)
    def _():
        for j in range(per):
            line.arrived((i - 3) * per + j)
        d_kv = out[pl.ds(pl.multiple_of((i - 3) * tile, tile), tile), :]
        d_rot = rotate(d_kv[:, :head].astype(F32), cos_ref[...], -sin_ref[...])
        d_raw, d_gain = norm_back(d_rot, hat_ref[...], inv_ref[...], gk_ref[...])
        acc_key[...] += d_gain[None]
        d_raw = jnp.concatenate([d_raw.astype(BF16), d_kv[:, head:]], axis=1)
        d_one = part_ref[...] + dot(d_raw, w_kv[...], NT)
        hat, inv = norm_parts(x_ref[...].astype(F32))
        gain = gain_ref[0:1, :]
        d_part, d_gain = norm_back(d_one, hat, inv, gain)
        acc_in[...] += d_gain[None]
        dx_ref[...] = dm_ref[...] + d_part
        acc[...] += dot((hat * (1.0 + gain)).astype(BF16), d_raw, TN)

    @pl.when(i == tiles + 2)
    def _():
        line.arrived(count - 1)
        width = x_ref.shape[1]
        short = head * own_rows // width
        last_ref[:, :head] = grad_q_ref[...]
        last_ref[:, head : 3 * head] = acc[...].astype(BF16)
        last_ref[:, 3 * head : 4 * head] = grad_o_ref[...]
        d_query = out[pl.ds((count - 1) * chunk, 16), :head][0:1].astype(F32)
        pair = jnp.concatenate([d_query, acc_key[...], jnp.zeros((14, head), F32)], axis=0).astype(BF16)
        col = lax.broadcasted_iota(jnp.int32, (head, width), 1)
        row = lax.broadcasted_iota(jnp.int32, (head, width), 0)
        shift = short.bit_length() - 1
        spot = lax.shift_right_logical(row, shift) * own_rows + (row & (short - 1))
        spread = dot(pair, jnp.where(col == spot, 1.0, 0.0).astype(BF16))
        gains = jnp.concatenate(
            [acc_in[...], dg_mid_ref[...], dg_post_ref[...], spread[0:2], jnp.zeros((122, width), F32)], axis=0)
        last_ref[:, 4 * head :] = jnp.transpose(gains).astype(BF16)
        line.finish()


def key_back(d_kv, hat, inv, cosine, sine, x, d_middle, part, gains, gain_key, first, dg_query, dg_mid, dg_post,
             grad_q, grad_o, own_rows, ident):
    rows, width = x.shape
    head = hat.shape[1]
    tile, chunk = 256, 128
    tiles = rows // tile
    count = rows // chunk + 1
    dma = pltpu.SemaphoreType.DMA((count,))

    def late(cols):
        return pl.BlockSpec((tile, cols), lambda i: (jnp.maximum(i - 3, 0), 0))

    comm = pltpu.VMEM((count * chunk, 2 * head), BF16)
    return pl.pallas_call(
        functools.partial(key_back_kernel, tiles, tile, chunk, own_rows),
        grid=(tiles + 3,),
        out_shape=(
            jax.ShapeDtypeStruct((rows, width), F32),
            jax.ShapeDtypeStruct((width, 4 * head + 128), BF16),
        ),
        in_specs=[pl.BlockSpec((tile, 2 * head), lambda i: (jnp.minimum(i, tiles - 1), 0)),
                  late(head), late(1), late(head // 2), late(head // 2), late(width), late(width), late(width),
                  whole_block(gains.shape), whole_block(gain_key.shape), ANY]
        + [whole_block(a.shape) for a in (dg_query, dg_mid, dg_post, grad_q, grad_o)],
        out_specs=(late(width), pl.BlockSpec((width, 4 * head + 128), lambda i: (0, 0))),
        scratch_shapes=[
            pltpu.VMEM((width, 2 * head), F32), pltpu.VMEM((1, width), F32), pltpu.VMEM((1, head), F32),
            pltpu.VMEM((width, 2 * head), BF16), pltpu.SemaphoreType.DMA] + [comm] * 4 + [dma] * 7
        + [pltpu.SemaphoreType.REGULAR] * 2,
        compiler_params=pltpu.CompilerParams(
            collective_id=ident, has_side_effects=True, vmem_limit_bytes=56 * 2**20),
        name="key_back",
    )(d_kv, hat, inv, cosine, sine, x, d_middle, part, gains, gain_key, first, dg_query, dg_mid, dg_post, grad_q, grad_o)


def scatter_kernel(chips, own_rows, x_ref, o_ref, near, pair, far, *sems):
    ss1, rs1, ss2, rs2 = sems
    ctx = lax.axis_size("ctx")
    me = lax.axis_index("dp") * ctx + lax.axis_index("ctx")
    core = lax.rem(me, 2)
    chip = lax.div(me, 2)
    bar = pltpu.get_barrier_semaphore()

    def device(d):
        return {"dp": lax.div(d, ctx), "ctx": lax.rem(d, ctx)}

    partner = device(2 * chip + 1 - core)
    pl.semaphore_signal(bar, inc=1, device_id=partner, device_id_type=MESH)
    for k in range(1, chips):
        other = lax.rem(chip + k, chips)
        pl.semaphore_signal(bar, inc=1, device_id=device(2 * other + core), device_id_type=MESH)
    pl.semaphore_wait(bar, chips)

    def block(d):
        return pl.ds(pl.multiple_of(d * own_rows, 16), own_rows)

    def within(k):
        q = lax.rem(chip + k, chips)
        return pltpu.make_async_remote_copy(
            x_ref.at[block(2 * q + 1 - core)], near.at[k], ss1.at[k], rs1.at[k], device_id=partner, device_id_type=MESH)

    def between(k):
        q = lax.rem(chip + k, chips)
        return pltpu.make_async_remote_copy(
            pair.at[k], far.at[k], ss2.at[k], rs2.at[k], device_id=device(2 * q + core), device_id_type=MESH)

    order = list(range(1, chips)) + [0]
    for k in order:
        within(k).start()
    for k in order:
        within(k).wait_recv()
        q = lax.rem(chip + k, chips)
        both = x_ref[block(2 * q + core), :].astype(F32) + near[k].astype(F32)
        if k > 0:
            pair[k] = both.astype(BF16)
            between(k).start()
        else:
            o_ref[...] = both
    for k in range(1, chips):
        between(k).wait_recv()
        o_ref[...] += far[k].astype(F32)
    for k in range(1, chips):
        between(k).wait_send()
    for k in order:
        within(k).wait_send()


def scatter(x, own_rows, ident):
    n = x.shape[0] // own_rows
    chips = n // 2
    cols = x.shape[1]
    buf = pltpu.VMEM((chips, own_rows, cols), BF16)
    vmem = pl.BlockSpec(memory_space=pltpu.VMEM)
    return pl.pallas_call(
        functools.partial(scatter_kernel, chips, own_rows),
        out_shape=jax.ShapeDtypeStruct((own_rows, cols), F32),
        in_specs=[vmem],
        out_specs=vmem,
        scratch_shapes=[buf] * 3 + [pltpu.SemaphoreType.DMA((chips,))] * 4,
        compiler_params=pltpu.CompilerParams(
            collective_id=ident, has_side_effects=True, vmem_limit_bytes=40 * 2**20),
        name="scatter",
    )(x)


def shards(tokens, segments, cotangent, w_query, w_key, w_value, w_out, w_gate, w_up, w_down,
           g_input, g_post_attn, g_pre_ffn, g_post_ffn, g_query, g_key):
    batches, seq_local, _, size, width = tokens.shape
    head = w_key.shape[1]
    groups = batches * seq_local
    per_group = 2 * size
    rows = groups * per_group
    ctx = lax.axis_size("ctx")
    length = per_group * ctx
    rank = lax.axis_index("ctx")
    shared = ("dp", "ctx")
    own_rows = g_input.shape[0]
    hidden = w_gate.shape[1]

    def column(gain):
        return jnp.pad(gain, (0, own_rows - gain.shape[0]))[:, None]

    own_ids = segments.reshape(groups, 2, size)
    id_cols = -(-own_ids.size // own_rows)
    ids = jnp.pad(own_ids.reshape(-1), (0, own_rows * id_cols - own_ids.size)).reshape(own_rows, id_cols)
    extra = jnp.concatenate(
        [column(g) for g in (g_input, g_post_attn, g_pre_ffn, g_post_ffn, g_query, g_key)] + [ids.astype(BF16)], axis=1)
    extra = jnp.pad(extra, ((0, 0), (0, 128 - extra.shape[1])))
    first = lax.all_gather(
        jnp.concatenate([w_query, w_key, w_value, extra], axis=1), shared, axis=0, tiled=True)
    mat_qkv = first[:, : 3 * head]
    side = first[:, 3 * head :]
    gain_cols = side[:, :8].astype(F32)
    gain_rows = gain_cols.T
    gain_input = gain_rows[0]
    short = g_query.shape[0]
    gain_query, gain_key = (
        gain_cols[:, i].reshape(-1, own_rows)[:, :short].reshape(-1) for i in (4, 5))
    ids = side[:, 6 : 6 + id_cols].reshape(-1, ctx, own_rows * id_cols)[:, :, : own_ids.size]
    ids = lax.dynamic_index_in_dim(ids, lax.axis_index("dp"), 0, keepdims=False).astype(jnp.int32)
    key_ids = ids.reshape(ctx, groups, 2, size).transpose(1, 2, 0, 3).reshape(groups, length)
    key_ids = jnp.where(key_ids == 0, -1, key_ids)

    def rows_of_16(w):
        return jnp.pad(w, ((0, -own_rows % 16), (0, 0)))

    wide = wide_of(hidden)
    line = gather_tp(rows_of_16(jnp.concatenate([w_query, w_out.T], axis=1)), 5)[:own_rows]
    second = jnp.concatenate(
        [line] + [jnp.pad(w, ((0, 0), (0, wide - hidden))) for w in (w_gate, w_up, w_down.T)], axis=1)

    offsets = rank * size + jnp.arange(size, dtype=jnp.int32)
    position = jnp.concatenate([offsets, length - 1 - offsets]).astype(F32)
    cosine, sine = angles(position, head // 2, head)
    cosine = jnp.broadcast_to(cosine, (groups, per_group, head // 2)).reshape(rows, head // 2)
    sine = jnp.broadcast_to(sine, (groups, per_group, head // 2)).reshape(rows, head // 2)

    inputs = tokens.reshape(rows, width).astype(F32)

    norm_one, scale_one = norm_parts(inputs)
    hidden_one = (norm_one * (1.0 + gain_input)).astype(BF16)
    raw = dot(hidden_one, mat_qkv)
    q_hat, q_scale = norm_parts(raw[:, :head])
    k_hat, k_scale = norm_parts(raw[:, head : 2 * head])
    queries = rotate(q_hat * (1.0 + gain_query), cosine, sine).astype(BF16)
    keys = rotate(k_hat * (1.0 + gain_key), cosine, sine).astype(BF16)
    values = raw[:, 2 * head :].astype(BF16)
    queries = queries.reshape(groups, 2, size, head)
    pairs = jnp.concatenate([keys, values], axis=1).reshape(batches, seq_local, 2, size, 2 * head)
    kv = [lax.all_gather(pairs[m], "ctx", axis=2, tiled=True).reshape(seq_local, length, 2 * head) for m in range(batches)]
    kv[-1], second = lax.optimization_barrier((kv[-1], second))
    weights = lax.all_gather(second, shared, axis=0, tiled=True)
    heads, heads_all, log_mass = [], [], []
    for m in range(batches):
        part = slice(m * seq_local, (m + 1) * seq_local)
        out, log = attend(queries[part], kv[m], own_ids[part, :, :, None], key_ids[part, None, :])
        heads.append(out.reshape(rows // batches, head))
        heads_all.append(gather_tp(heads[m], m * 6))
        log_mass.append(log)
    heads_own = jnp.concatenate(heads)
    log_mass = jnp.concatenate(log_mass)
    x_rows = tokens.reshape(rows, width)
    dy_rows = cotangent.reshape(rows, width)
    attn, hidden_two, gate, up, ffn_out = ffn_forward(x_rows, heads_all, gain_rows, weights, hidden, 1)
    output, d_gain_post_ffn, grad_ffn, d_two = ffn_backward(
        x_rows, attn, dy_rows, ffn_out, hidden_two, gate, up, gain_rows, weights, 2)
    grad_ffn = lax.psum_scatter(grad_ffn, shared, scatter_dimension=1, tiled=True).astype(F32)
    d_middle, d_heads, delta, d_gain_mid, grad_out_t = middle_back(
        x_rows, attn, dy_rows, d_two, heads_own, gain_rows, weights)

    d_query, d_kv = attend_back(
        queries, jnp.concatenate(kv), d_heads.reshape(groups, 2, size, head),
        log_mass.reshape(groups, 2, 1, size), delta.reshape(groups, 2, 1, size),
        own_ids[:, :, None, :], key_ids[:, :, None])
    d_kv = lax.psum_scatter(
        d_kv.reshape(groups, 2, length // 2, 2 * head), "ctx", scatter_dimension=2, tiled=True)
    d_one, grad_q, d_gain_query = query_back(
        d_query.reshape(rows, head), q_hat, q_scale, cosine, sine, x_rows, gain_rows, gain_query[None], weights, 4)
    d_kv, d_one = lax.optimization_barrier((d_kv, d_one))
    d_tokens, last = key_back(
        d_kv.reshape(rows, 2 * head), k_hat, k_scale, cosine, sine, x_rows, d_middle, d_one, gain_rows, gain_key[None],
        first, d_gain_query, d_gain_mid, d_gain_post_ffn, grad_q, grad_out_t, own_rows, 3)
    if own_rows % 16 == 0:
        last = scatter(last, own_rows, 7)
    else:
        last = lax.psum_scatter(last, shared, scatter_dimension=0, tiled=True).astype(F32)
    g = last[:, 4 * head :]
    return (
        output.reshape(tokens.shape),
        d_tokens.reshape(tokens.shape),
        last[:, :head],
        last[:, head : 2 * head],
        last[:, 2 * head : 3 * head],
        last[:, 3 * head : 4 * head].T,
        grad_ffn[0],
        grad_ffn[1],
        grad_ffn[2].T,
        g[:, 0],
        g[:, 1],
        g[:, 2],
        g[:, 3],
        g[:short, 4],
        g[:short, 5],
    )


def solution(mesh):
    shared = ("dp", "ctx")
    rows = P(None, "dp", None, "ctx", None)
    weights = (
        P(shared, "tp"), P(shared, None), P(shared, None), P("tp", shared),
        P(shared, "tp"), P(shared, "tp"), P("tp", shared),
    )
    gains = (P(shared),) * 6
    return jax.shard_map(
        shards,
        mesh=mesh,
        in_specs=(rows, P(None, "dp", None, "ctx"), rows) + weights + gains,
        out_specs=(rows, rows) + weights + gains,
        check_vma=False,
    )
```

```python
import functools

import jax
import jax.numpy as jnp
from jax import lax
from jax.experimental import pallas as pl
from jax.experimental.pallas import tpu as pltpu
from jax.sharding import PartitionSpec as P

EPS = 1e-06
THETA = 1000000.0
SCALE = 0.0625
NEGATIVE = -1e30
BF16 = jnp.bfloat16
F32 = jnp.float32
MESH = pl.DeviceIdType.MESH
NN = (((1,), (0,)), ((), ()))
NT = (((1,), (1,)), ((), ()))
TN = (((0,), (0,)), ((), ()))


def dot(a, b, dims=NN):
    return lax.dot_general(a, b, dims, preferred_element_type=F32)


def barrier_line(z):
    bar = pltpu.get_barrier_semaphore()

    @pl.when(z > 0)
    def _():
        pl.semaphore_signal(bar, inc=1, device_id={"tp": z - 1}, device_id_type=MESH)

    @pl.when(z < 3)
    def _():
        pl.semaphore_signal(bar, inc=1, device_id={"tp": z + 1}, device_id_type=MESH)

    pl.semaphore_wait(bar, jnp.where((z == 0) | (z == 3), 1, 2))


def block_starts(half, t, blocks, rank):
    if half == 0:
        return t
    return jnp.where(t < blocks, t, t + rank + 1)


def attend_back_kernel(blocks, q_ref, kv_ref, do_ref, l_ref, d_ref, qs_ref, ks_ref,
                       dq_ref, dkv_ref, dk_acc, dv_acc):
    rank = lax.axis_index("ctx")
    size = q_ref.shape[2]
    head = q_ref.shape[3]
    row = lax.broadcasted_iota(jnp.int32, (size, size), 0)
    col = lax.broadcasted_iota(jnp.int32, (size, size), 1)
    dk_acc[...] = jnp.zeros_like(dk_acc)
    dv_acc[...] = jnp.zeros_like(dv_acc)
    for half in range(2):
        q = q_ref[0, half] * jnp.asarray(SCALE, BF16)
        do = do_ref[0, half]
        qseg = qs_ref[0, half]
        log_mass = l_ref[0, half]
        delta = d_ref[0, half]

        def part(block, own):
            rows = pl.ds(pl.multiple_of(block * size, size), size)
            k = kv_ref[0, rows, :head]
            v = kv_ref[0, rows, head:]
            allowed = ks_ref[0, rows, :] == qseg
            if own:
                order = (row <= col) if half == 0 else (row >= col)
                allowed = (allowed & order) | (col == row)
            s = jnp.where(allowed, dot(k, q, NT), NEGATIVE)
            p = jnp.exp(s - log_mass)
            ds = (p * (dot(v, do, NT) - delta)).astype(BF16)
            dv_acc[rows, :] += dot(p.astype(BF16), do)
            dk_acc[rows, :] += dot(ds, q)
            return dot(ds, k, TN)

        def step(t, dq):
            return dq + part(block_starts(half, t, blocks, rank), False)

        dq = part(rank + half * blocks, True)
        count = rank if half == 0 else 2 * blocks - 1 - rank
        dq_ref[0, half] = SCALE * lax.fori_loop(0, count, step, dq)
    dkv_ref[0, :, :head] = dk_acc[...].astype(BF16)
    dkv_ref[0, :, head:] = dv_acc[...].astype(BF16)


def attend_back(q, kv, do, log_mass, delta, qseg, kseg):
    groups, _, size, head = q.shape
    length = kv.shape[1]
    blocks = length // (2 * size)
    halves = pl.BlockSpec((1, 2, size, head), lambda g: (g, 0, 0, 0))
    whole = pl.BlockSpec((1, length, 2 * head), lambda g: (g, 0, 0))
    line = pl.BlockSpec((1, 2, 1, size), lambda g: (g, 0, 0, 0))
    return pl.pallas_call(
        functools.partial(attend_back_kernel, blocks),
        grid=(groups,),
        out_shape=(
            jax.ShapeDtypeStruct(q.shape, F32),
            jax.ShapeDtypeStruct((groups, length, 2 * head), BF16),
        ),
        in_specs=[halves, whole, halves, line, line, line,
                  pl.BlockSpec((1, length, 1), lambda g: (g, 0, 0))],
        out_specs=(halves, pl.BlockSpec((1, length, 2 * head), lambda g: (g, 0, 0))),
        scratch_shapes=[pltpu.VMEM((length, head), F32)] * 2,
        compiler_params=pltpu.CompilerParams(vmem_limit_bytes=56 * 2**20),
        name="attend_back",
    )(q, kv, do, log_mass, delta, qseg, kseg)


def angles(position, half_size, full_size):
    frequency = THETA ** (-2.0 * jnp.arange(half_size, dtype=F32) / full_size)
    turned = position[:, None] * frequency[None, :]
    return (jnp.cos(turned), jnp.sin(turned))


def rotate(tensor, cosine, sine):
    half_size = tensor.shape[-1] // 2
    a = tensor[..., :half_size]
    b = tensor[..., half_size:]
    return jnp.concatenate([a * cosine - b * sine, b * cosine + a * sine], axis=-1)


def norm_parts(values):
    inv = lax.rsqrt(jnp.mean(values * values, axis=-1, keepdims=True) + EPS)
    return (values * inv, inv)


def norm_back(upstream, normalized, inv, gain):
    d_norm = upstream * (1.0 + gain)
    d_values = inv * (d_norm - normalized * jnp.mean(d_norm * normalized, axis=-1, keepdims=True))
    return (d_values, jnp.sum(upstream * normalized, axis=0))


def gelu_tanh(values):
    return jax.nn.gelu(values, approximate=True)


class LineSum:
    def __init__(self, count, chunk, slots, own, near, far, out, sems):
        self.count, self.chunk, self.slots = count, chunk, slots
        self.own, self.near, self.far, self.out = own, near, far, out
        self.sems = sems
        self.z = z = lax.axis_index("tp")
        self.hub = (z == 1) | (z == 2)
        self.leaf = (z == 0) | (z == 3)
        self.other_hub = jnp.where(z == 1, 2, 1)
        self.my_hub = jnp.where(z == 0, 1, 2)
        self.my_leaf = jnp.where(z == 1, 0, 3)

    def slot(self, c):
        return pl.ds(pl.multiple_of(lax.rem(c, self.slots) * self.chunk, self.chunk), self.chunk)

    def rows(self, c):
        return pl.ds(pl.multiple_of(c * self.chunk, self.chunk), self.chunk)

    def inwards(self, c):
        return pltpu.make_async_remote_copy(
            self.own.at[self.slot(c)], self.near.at[self.slot(c)], self.sems[0].at[c], self.sems[1].at[c],
            device_id={"tp": self.my_hub}, device_id_type=MESH)

    def across(self, c):
        return pltpu.make_async_remote_copy(
            self.own.at[self.slot(c)], self.far.at[self.slot(c)], self.sems[2].at[c], self.sems[3].at[c],
            device_id={"tp": self.other_hub}, device_id_type=MESH)

    def outwards(self, c):
        return pltpu.make_async_remote_copy(
            self.far.at[self.slot(c)], self.out.at[self.rows(c)], self.sems[4].at[c], self.sems[5].at[c],
            device_id={"tp": self.my_leaf}, device_id_type=MESH)

    def store(self, c):
        return pltpu.make_async_copy(self.far.at[self.slot(c)], self.out.at[self.rows(c)], self.sems[6].at[c])

    def put(self, c, value):
        ring = self.slots < self.count
        if ring:
            @pl.when(c >= self.slots)
            def _():
                @pl.when(self.leaf)
                def _():
                    self.inwards(c - self.slots).wait_send()

                @pl.when(self.hub)
                def _():
                    self.across(c - self.slots).wait_send()

        self.own[self.slot(c), :] = value

        @pl.when(self.leaf)
        def _():
            if ring:
                @pl.when(c >= self.slots)
                def _():
                    pl.semaphore_wait(self.sems[7], 1)
            self.inwards(c).start()

    def pair(self, c):
        ring = self.slots < self.count

        @pl.when(self.hub)
        def _():
            self.inwards(c).wait_recv()
            at = self.slot(c)
            self.own[at, :] = (self.own[at, :].astype(F32) + self.near[at, :].astype(F32)).astype(BF16)
            if ring:
                @pl.when(c < self.count - self.slots)
                def _():
                    pl.semaphore_signal(self.sems[7], inc=1, device_id={"tp": self.my_leaf}, device_id_type=MESH)

                @pl.when(c >= self.slots)
                def _():
                    pl.semaphore_wait(self.sems[8], 1)
            self.across(c).start()

    def total(self, c):
        @pl.when(self.hub)
        def _():
            self.across(c).wait_recv()
            at = self.slot(c)
            self.far[at, :] = (self.own[at, :].astype(F32) + self.far[at, :].astype(F32)).astype(BF16)
            self.outwards(c).start()
            self.store(c).start()

    def retire(self, c):
        @pl.when(self.hub)
        def _():
            self.outwards(c).wait_send()
            self.store(c).wait()
            if self.slots < self.count:
                @pl.when(c < self.count - self.slots)
                def _():
                    pl.semaphore_signal(self.sems[8], inc=1, device_id={"tp": self.other_hub}, device_id_type=MESH)

    def finish(self):
        first = max(0, self.count - self.slots)

        @pl.when(self.leaf)
        def _():
            for c in range(self.count):
                self.outwards(c).wait_recv()
            for c in range(first, self.count):
                self.inwards(c).wait_send()

        @pl.when(self.hub)
        def _():
            for c in range(first, self.count):
                self.across(c).wait_send()


def line_sum_scratch(count, chunk, slots, cols):
    dma = pltpu.SemaphoreType.DMA((count,))
    regular = pltpu.SemaphoreType.REGULAR
    return [pltpu.VMEM((slots * chunk, cols), BF16)] * 3 + [dma] * 7 + [regular] * 2


def gelu_parts(v):
    c = 0.7978845608028654
    square = v * v
    t = jnp.tanh(v * (c + (c * 0.044715) * square))
    half = 0.5 + 0.5 * t
    value = v * half
    slope = half + (0.5 * v) * (1.0 - t * t) * (c + (3.0 * c * 0.044715) * square)
    return value, slope


def column_parts(cols):
    middle = -(-cols // 256) * 128
    return [(0, middle), (middle, cols)] if middle < cols else [(0, cols)]


def middle_of(x, attn, gain_post_attn):
    hat, inv = norm_parts(attn.astype(F32))
    return x.astype(F32) + hat * (1.0 + gain_post_attn), hat, inv


def load_ffn_weights(weights, refs, sem):
    wide = refs[0].shape[1]
    base = weights.shape[1] - 3 * wide
    return [
        pltpu.make_async_copy(weights.at[:, pl.ds(base + j * wide, wide)], ref, sem.at[j])
        for j, ref in enumerate(refs)
    ]


def ffn_forward_kernel(tiles, tile, chunk, hidden, x_ref, h_ref, gain_ref, w_ref,
                       attn_ref, two_ref, gate_ref, up_ref, out_ref, wo_ref, wg_ref, wu_ref, wd_ref, w_sem, own, near, far, *sems):
    i = pl.program_id(0)
    per = tile // chunk
    line = LineSum(tiles * per, chunk, tiles * per, own, near, far, out_ref, sems)
    head = wo_ref.shape[1] // 4

    @pl.when(i == 0)
    def _():
        copies = load_ffn_weights(w_ref, (wg_ref, wu_ref, wd_ref), w_sem)
        copies += [
            pltpu.make_async_copy(
                w_ref.at[:, pl.ds((2 * j + 1) * head, head)], wo_ref.at[:, pl.ds(j * head, head)], w_sem.at[3 + j])
            for j in range(4)
        ]
        for copy in copies:
            copy.start()
        barrier_line(line.z)
        for copy in copies:
            copy.wait()

    attn = dot(h_ref[...], wo_ref[...], NT).astype(BF16)
    attn_ref[...] = attn
    middle, _, _ = middle_of(x_ref[...], attn, gain_ref[1:2, :])
    hat, _ = norm_parts(middle)
    two = (hat * (1.0 + gain_ref[2:3, :])).astype(BF16)
    two_ref[...] = two
    part = None
    for a, b in column_parts(hidden):
        gate = dot(two, wg_ref[:, a:b])
        up = dot(two, wu_ref[:, a:b])
        gate_ref[:, a:b] = gate.astype(BF16)
        up_ref[:, a:b] = up.astype(BF16)
        value, _ = gelu_parts(gate)
        more = dot((value * up).astype(BF16), wd_ref[:, a:b], NT)
        part = more if part is None else part + more
    for j in range(per):
        line.put(i * per + j, part[j * chunk : (j + 1) * chunk].astype(BF16))

    @pl.when(i >= 1)
    def _():
        for j in range(per):
            line.pair((i - 1) * per + j)

    @pl.when(i >= 2)
    def _():
        for j in range(per):
            line.total((i - 2) * per + j)

    @pl.when(i == tiles - 1)
    def _():
        last = tiles * per
        for j in range(per):
            line.pair(last - per + j)
        for c in range(max(0, last - 2 * per), last):
            line.total(c)
        for c in range(last):
            line.retire(c)
        line.finish()


def whole_block(shape):
    return pl.BlockSpec(shape, lambda i: (0,) * len(shape), pipeline_mode=pl.Buffered(1))


def tile_block(tile, cols):
    return pl.BlockSpec((tile, cols), lambda i: (i, 0))


ANY = pl.BlockSpec(memory_space=pl.ANY)


def wide_of(hidden):
    return -(-hidden // 128) * 128


def ffn_forward(x, heads, gains, weights, hidden, ident):
    rows, width = x.shape
    all_heads = heads.shape[1]
    tile, chunk = 256, 128
    tiles = rows // tile
    count = rows // chunk
    wide = wide_of(hidden)
    return pl.pallas_call(
        functools.partial(ffn_forward_kernel, tiles, tile, chunk, hidden),
        grid=(tiles,),
        out_shape=(
            jax.ShapeDtypeStruct((rows, width), BF16),
            jax.ShapeDtypeStruct((rows, width), BF16),
            jax.ShapeDtypeStruct((rows, hidden), BF16),
            jax.ShapeDtypeStruct((rows, hidden), BF16),
            jax.ShapeDtypeStruct((rows, width), BF16),
        ),
        in_specs=[
            tile_block(tile, width),
            tile_block(tile, all_heads),
            whole_block(gains.shape),
            ANY,
        ],
        out_specs=(tile_block(tile, width), tile_block(tile, width), tile_block(tile, hidden), tile_block(tile, hidden), ANY),
        scratch_shapes=[pltpu.VMEM((width, all_heads), BF16)] + [pltpu.VMEM((width, wide), BF16)] * 3
        + [pltpu.SemaphoreType.DMA((7,))]
        + line_sum_scratch(count, chunk, count, width),
        compiler_params=pltpu.CompilerParams(
            collective_id=ident, has_side_effects=True, vmem_limit_bytes=60 * 2**20),
        name="ffn_forward",
    )(x, heads, gains, weights)


def ffn_backward_kernel(tiles, tile, chunk, slots, hidden, x_ref, attn_ref, dy_ref, ffn_ref, two_ref, gate_ref, up_ref,
                        gain_ref, w_ref,
                        y_ref, dgain_ref, grad_ref, out_ref, wg_ref, wu_ref, wd_ref, w_sem,
                        acc_g, acc_u, acc_d, keep_g, keep_u, keep_h, stage, stage_sem, own, near, far, *sems):
    i = pl.program_id(0)
    per = tile // chunk
    last = tiles * per
    line = LineSum(last, chunk, slots, own, near, far, out_ref, sems)

    @pl.when(i == 0)
    def _():
        copies = load_ffn_weights(w_ref, (wg_ref, wu_ref, wd_ref), w_sem)
        for copy in copies:
            copy.start()
        barrier_line(line.z)
        for acc in (acc_g, acc_u, acc_d, dgain_ref):
            acc[...] = jnp.zeros_like(acc)
        for copy in copies:
            copy.wait()

    middle, _, _ = middle_of(x_ref[...], attn_ref[...], gain_ref[1:2, :])
    hat, inv = norm_parts(ffn_ref[...].astype(F32))
    gain = gain_ref[3:4, :]
    y_ref[...] = (middle + hat * (1.0 + gain)).astype(BF16)
    d_ffn, d_gain = norm_back(dy_ref[...].astype(F32), hat, inv, gain)
    dgain_ref[...] += d_gain[None]
    d_ffn = d_ffn.astype(BF16)
    part = None
    for a, b in column_parts(hidden):
        d_hidden = dot(d_ffn, wd_ref[:, a:b])
        up = up_ref[:, a:b].astype(F32)
        value, slope = gelu_parts(gate_ref[:, a:b].astype(F32))
        keep_h[:, a:b] = (value * up).astype(BF16)
        d_gate = (d_hidden * up * slope).astype(BF16)
        d_up = (d_hidden * value).astype(BF16)
        keep_g[:, a:b] = d_gate
        keep_u[:, a:b] = d_up
        more = dot(d_gate, wg_ref[:, a:b], NT) + dot(d_up, wu_ref[:, a:b], NT)
        part = more if part is None else part + more
    for j in range(per):
        line.put(i * per + j, part[j * chunk : (j + 1) * chunk].astype(BF16))

    @pl.when(i >= 1)
    def _():
        for j in range(per):
            line.pair((i - 1) * per + j)

    acc_g[...] += dot(two_ref[...], keep_g[...], TN)
    acc_u[...] += dot(two_ref[...], keep_u[...], TN)
    acc_d[...] += dot(d_ffn, keep_h[...], TN)

    @pl.when(i >= 2)
    def _():
        for j in range(per):
            line.total((i - 2) * per + j)

    @pl.when(i >= 3)
    def _():
        for j in range(per):
            line.retire((i - 3) * per + j)

    @pl.when(i == tiles - 1)
    def _():
        for j in range(per):
            line.pair(last - per + j)
        step = stage.shape[1]
        count = acc_g.shape[0] // step

        def piece(acc, out, k, at):
            @pl.when(k >= 2)
            def _():
                pltpu.make_async_copy(stage.at[at], out.at[pl.ds(0, step)], stage_sem.at[at]).wait()
            rows = pl.ds(pl.multiple_of(k * step, step), step)
            stage[at] = acc[rows, :].astype(BF16)
            pltpu.make_async_copy(stage.at[at], out.at[rows], stage_sem.at[at]).start()

        for acc, out in ((acc_g, grad_ref.at[0]), (acc_u, grad_ref.at[1]), (acc_d, grad_ref.at[2])):
            def pieces(k, _):
                piece(acc, out, k, lax.rem(k, 2))
                return 0

            lax.fori_loop(0, count, pieces, 0)
            for at in range(2):
                pltpu.make_async_copy(stage.at[at], out.at[pl.ds(0, step)], stage_sem.at[at]).wait()
            if acc is acc_g:
                for c in range(max(0, last - 2 * per), last - per):
                    line.total(c)
            if acc is acc_u:
                for c in range(last - per, last):
                    line.total(c)
        for c in range(max(0, last - 3 * per), last):
            line.retire(c)
        line.finish()


def ffn_backward(x, attn, dy, ffn, two, gate, up, gains, weights, ident):
    rows, width = x.shape
    hidden = gate.shape[1]
    wide = wide_of(hidden)
    tile, chunk = 256, 128
    tiles = rows // tile
    count = rows // chunk
    slots = min(count, 6)
    step = 144
    acc = pltpu.VMEM((width, hidden), F32)
    keep = pltpu.VMEM((tile, hidden), BF16)
    return pl.pallas_call(
        functools.partial(ffn_backward_kernel, tiles, tile, chunk, slots, hidden),
        grid=(tiles,),
        out_shape=(
            jax.ShapeDtypeStruct((rows, width), BF16),
            jax.ShapeDtypeStruct((1, width), F32),
            jax.ShapeDtypeStruct((3, width, hidden), BF16),
            jax.ShapeDtypeStruct((rows, width), BF16),
        ),
        in_specs=[tile_block(tile, width)] * 5 + [tile_block(tile, hidden)] * 2
        + [whole_block(gains.shape), ANY],
        out_specs=(tile_block(tile, width), pl.BlockSpec((1, width), lambda i: (0, 0)), ANY, ANY),
        scratch_shapes=[pltpu.VMEM((width, wide), BF16)] * 3 + [pltpu.SemaphoreType.DMA((3,))] + [acc] * 3 + [keep] * 3
        + [pltpu.VMEM((2, step, hidden), BF16), pltpu.SemaphoreType.DMA((2,))]
        + line_sum_scratch(count, chunk, slots, width),
        compiler_params=pltpu.CompilerParams(
            collective_id=ident, has_side_effects=True, vmem_limit_bytes=63 * 2**20),
        name="ffn_backward",
    )(x, attn, dy, ffn, two, gate, up, gains, weights)


def middle_back_kernel(x_ref, attn_ref, dy_ref, d2_ref, h_ref, gain_ref, w_ref,
                       dm_ref, dh_ref, delta_ref, dgain_ref, go_ref, acc, wo_ref, w_sem):
    i = pl.program_id(0)

    @pl.when(i == 0)
    def _():
        head = wo_ref.shape[1]
        at = pl.multiple_of((2 * lax.axis_index("tp") + 1) * head, head)
        copy = pltpu.make_async_copy(w_ref.at[:, pl.ds(at, head)], wo_ref, w_sem)
        copy.start()
        copy.wait()
        acc[...] = jnp.zeros_like(acc)
        dgain_ref[...] = jnp.zeros_like(dgain_ref)

    middle, attn_hat, attn_inv = middle_of(x_ref[...], attn_ref[...], gain_ref[1:2, :])
    hat, inv = norm_parts(middle)
    d_part, d_gain = norm_back(d2_ref[...].astype(F32), hat, inv, gain_ref[2:3, :])
    dgain_ref[1:2, :] += d_gain[None]
    d_middle = dy_ref[...].astype(F32) + d_part
    dm_ref[...] = d_middle
    d_attn, d_gain = norm_back(d_middle, attn_hat, attn_inv, gain_ref[1:2, :])
    dgain_ref[0:1, :] += d_gain[None]
    d_attn = d_attn.astype(BF16)
    d_heads = dot(d_attn, wo_ref[...]).astype(BF16)
    dh_ref[...] = d_heads
    heads = h_ref[...]
    delta_ref[...] = jnp.sum(d_heads.astype(F32) * heads.astype(F32), axis=1, keepdims=True)
    acc[...] += dot(d_attn, heads, TN)

    @pl.when(i == pl.num_programs(0) - 1)
    def _():
        go_ref[...] = acc[...].astype(BF16)


def middle_back(x, attn, dy, d_two, heads, gains, weights):
    rows, width = x.shape
    head = heads.shape[1]
    tile = 256
    return pl.pallas_call(
        middle_back_kernel,
        grid=(rows // tile,),
        out_shape=(
            jax.ShapeDtypeStruct((rows, width), F32),
            jax.ShapeDtypeStruct((rows, head), BF16),
            jax.ShapeDtypeStruct((rows, 1), F32),
            jax.ShapeDtypeStruct((2, width), F32),
            jax.ShapeDtypeStruct((width, head), BF16),
        ),
        in_specs=[tile_block(tile, width)] * 4 + [tile_block(tile, head)] + [whole_block(gains.shape), ANY],
        out_specs=(
            tile_block(tile, width), tile_block(tile, head), tile_block(tile, 1),
            pl.BlockSpec((2, width), lambda i: (0, 0)), pl.BlockSpec((width, head), lambda i: (0, 0)),
        ),
        scratch_shapes=[pltpu.VMEM((width, head), F32), pltpu.VMEM((width, head), BF16), pltpu.SemaphoreType.DMA],
        compiler_params=pltpu.CompilerParams(vmem_limit_bytes=48 * 2**20),
        name="middle_back",
    )(x, attn, dy, d_two, heads, gains, weights)


class LineGather:
    def __init__(self, whole, tile, width, sems):
        self.whole, self.tile, self.width, self.sems = whole, tile, width, sems
        self.z = lax.axis_index("tp")

    def send(self, src, t, hop, way):
        ss, rs = self.sems[:2] if way > 0 else self.sems[2:]
        place = self.whole.at[
            pl.ds(pl.multiple_of(t * self.tile, self.tile), self.tile),
            pl.ds(pl.multiple_of(src * self.width, self.width), self.width)]
        return pltpu.make_async_remote_copy(
            place, place, ss.at[hop, t], rs.at[hop, t],
            device_id={"tp": self.z + way}, device_id_type=MESH)

    def going(self, hop, way):
        src = self.z - way * hop
        return src, (self.z + way >= 0) & (self.z + way <= 3) & (src >= 0) & (src <= 3)

    def coming(self, hop, way):
        src = self.z - way * (hop + 1)
        return src, (src >= 0) & (src <= 3)

    def forward(self, t, hop):
        for way in (1, -1):
            if hop > 0:
                self.wait(t, hop - 1, way)
            src, ok = self.going(hop, way)

            @pl.when(ok)
            def _():
                self.send(src, t, hop, way).start()

    def wait(self, t, hop, way):
        src, ok = self.coming(hop, way)

        @pl.when(ok)
        def _():
            self.send(src, t, hop, way).wait_recv()

    def arrived(self, t):
        for way in (1, -1):
            self.wait(t, 2, way)

    def finish(self, tiles):
        for hop in range(3):
            for way in (1, -1):
                src, ok = self.going(hop, way)

                @pl.when(ok)
                def _():
                    def one(t, _):
                        self.send(src, t, hop, way).wait_send()
                        return 0

                    lax.fori_loop(0, tiles, one, 0)


class Shared:
    def __init__(self, over_dp):
        self.ctx = ctx = lax.axis_size("ctx")
        me = lax.axis_index("ctx")
        self.devices = ctx
        if over_dp:
            me = me + lax.axis_index("dp") * ctx
            self.devices = ctx * lax.axis_size("dp")
        self.over_dp = over_dp
        self.me = me
        self.chips = self.devices // 2
        self.core = lax.rem(me, 2)
        self.chip = lax.div(me, 2)

    def ident(self, device):
        if self.over_dp:
            return {"dp": lax.div(device, self.ctx), "ctx": lax.rem(device, self.ctx)}
        return {"ctx": device}

    def other(self, k):
        return 2 * lax.rem(self.chip + k + self.chips, self.chips) + self.core

    def partner(self):
        return self.me + 1 - 2 * self.core

    def greet(self, z):
        bar = pltpu.get_barrier_semaphore()
        for device in [self.partner()] + [self.other(k) for k in range(1, self.chips)]:
            pl.semaphore_signal(bar, inc=1, device_id=self.ident(device), device_id_type=MESH)

        @pl.when(z > 0)
        def _():
            pl.semaphore_signal(bar, inc=1, device_id={"tp": z - 1}, device_id_type=MESH)

        @pl.when(z < 3)
        def _():
            pl.semaphore_signal(bar, inc=1, device_id={"tp": z + 1}, device_id_type=MESH)

        pl.semaphore_wait(bar, self.chips + jnp.where((z == 0) | (z == 3), 1, 2))

    def copy(self, source, target, send, recv, device):
        return pltpu.make_async_remote_copy(
            source, target, send, recv, device_id=self.ident(device), device_id_type=MESH)


def first_gather_kernel(a_ref, b_ref, all_ref, line_ref, lsem, ss1, rs1, ss2, rs2, *sems):
    group = Shared(True)
    line = LineGather(line_ref, b_ref.shape[0], b_ref.shape[1], sems)
    width = b_ref.shape[1]
    own = [
        pltpu.make_async_copy(a_ref, all_ref.at[group.me], lsem.at[0]),
        pltpu.make_async_copy(b_ref, line_ref.at[:, pl.ds(pl.multiple_of(line.z * width, width), width)], lsem.at[1]),
    ]
    for copy in own:
        copy.start()
    group.greet(line.z)

    def direct(k, incoming=False):
        at = all_ref.at[group.other(-k)] if incoming else all_ref.at[group.me]
        return group.copy(a_ref, at, ss1.at[k], rs1.at[k], group.other(k))

    def inner(k, incoming=False):
        at = all_ref.at[group.other(-k)]
        if incoming:
            at = all_ref.at[group.other(-k) + 1 - 2 * group.core]
        return group.copy(a_ref if k == 0 else at, at, ss2.at[k], rs2.at[k], group.partner())

    for k in range(1, group.chips):
        direct(k).start()
    inner(0).start()
    for copy in own:
        copy.wait()
    line.forward(0, 0)
    line.forward(0, 1)
    line.forward(0, 2)
    for k in range(1, group.chips):
        direct(k, True).wait_recv()
        inner(k).start()
    for k in range(group.chips):
        inner(k, True).wait_recv()
    line.arrived(0)
    for k in range(1, group.chips):
        direct(k).wait_send()
    for k in range(group.chips):
        inner(k).wait_send()
    line.finish(1)


def first_gather(a, b, devices, ident):
    dma = pltpu.SemaphoreType.DMA((devices // 2,))
    hop = pltpu.SemaphoreType.DMA((3, 1))
    return pl.pallas_call(
        first_gather_kernel,
        out_shape=(
            jax.ShapeDtypeStruct((devices,) + a.shape, a.dtype),
            jax.ShapeDtypeStruct((b.shape[0], 4 * b.shape[1]), b.dtype),
        ),
        in_specs=[ANY, ANY],
        out_specs=(ANY, ANY),
        scratch_shapes=[pltpu.SemaphoreType.DMA((2,))] + [dma] * 4 + [hop] * 4,
        compiler_params=pltpu.CompilerParams(collective_id=ident, has_side_effects=True),
        name="first_gather",
    )(a, b)


def attention_kernel(groups, size, x_ref, w_ref, gain_ref, gq_ref, gk_ref, cos_ref, sin_ref, qs_ref, ks_ref,
                     q_ref, qhat_ref, qinv_ref, khat_ref, kinv_ref, heads_ref, log_ref, kv_out, all_out,
                     kv, whole, store_kv, store_all, ss1, rs1, ss2, rs2, *sems):
    head = q_ref.shape[1]
    length = kv.shape[1]
    blocks = length // (2 * size)
    group = Shared(False)
    rank = group.me
    line = LineGather(whole, size, head, sems)
    z = line.z
    tile = min(256, size)
    group.greet(z)

    def place(g, half, c):
        return kv.at[g, pl.ds(pl.multiple_of(half * (length // 2) + c * size, size), size)]

    def direct(g, half, k, incoming=False):
        at = place(g, half, group.other(-k) if incoming else rank)
        return group.copy(at, at, ss1.at[g, half, k], rs1.at[g, half, k], group.other(k))

    def inner(g, half, k, incoming=False):
        block = group.other(-k)
        at = place(g, half, block + 1 - 2 * group.core if incoming else block)
        return group.copy(at, at, ss2.at[g, half, k], rs2.at[g, half, k], group.partner())

    def project(g, half, u):
        rows = pl.ds((2 * g + half) * size + u * tile, tile)
        spot = pl.ds(half * size + u * tile, tile)
        cosine, sine = cos_ref[spot, :], sin_ref[spot, :]
        hat, _ = norm_parts(x_ref[rows, :].astype(F32))
        raw = dot((hat * (1.0 + gain_ref[0:1, :])).astype(BF16), w_ref[...])
        hat, inv = norm_parts(raw[:, :head])
        qhat_ref[rows, :] = hat
        qinv_ref[rows, :] = inv
        q_ref[rows, :] = rotate(hat * (1.0 + gq_ref[...]), cosine, sine).astype(BF16)
        hat, inv = norm_parts(raw[:, head : 2 * head])
        khat_ref[rows, :] = hat
        kinv_ref[rows, :] = inv
        at = pl.ds(pl.multiple_of(half * (length // 2) + rank * size + u * tile, tile), tile)
        kv[g, at, :head] = rotate(hat * (1.0 + gk_ref[...]), cosine, sine).astype(BF16)
        kv[g, at, head:] = raw[:, 2 * head :].astype(BF16)

    def attend(g, half):
        row = lax.broadcasted_iota(jnp.int32, (size, size), 0)
        col = lax.broadcasted_iota(jnp.int32, (size, size), 1)
        rows = pl.ds((2 * g + half) * size, size)
        q = q_ref[rows, :] * jnp.asarray(SCALE, BF16)
        qseg = qs_ref[g, half]

        def part(block):
            at = pl.ds(pl.multiple_of(block * size, size), size)
            same = qseg == ks_ref[g, :, at]
            return dot(q, kv[g, at, :head], NT), kv[g, at, head:], same

        s, v, same = part(rank + half * blocks)
        order = (col <= row) if half == 0 else (col >= row)
        s = jnp.where((same & order) | (col == row), s, NEGATIVE)
        top = jnp.max(s, axis=1, keepdims=True)
        p = jnp.exp(s - top)
        mass = jnp.sum(p, axis=1, keepdims=True)
        acc = dot(p.astype(BF16), v)

        def step(t, carry):
            top, mass, acc = carry
            s, v, same = part(block_starts(half, t, blocks, rank))
            s = jnp.where(same, s, NEGATIVE)
            new = jnp.maximum(top, jnp.max(s, axis=1, keepdims=True))
            keep = jnp.exp(top - new)
            p = jnp.exp(s - new)
            mass = mass * keep + jnp.sum(p, axis=1, keepdims=True)
            return new, mass, acc * keep + dot(p.astype(BF16), v)

        count = rank if half == 0 else 2 * blocks - 1 - rank
        top, mass, acc = lax.fori_loop(0, count, step, (top, mass, acc))
        out = (acc / mass).astype(BF16)
        heads_ref[rows, :] = out
        whole[rows, pl.ds(pl.multiple_of(z * head, head), head)] = out
        log_ref[g, half] = top + jnp.log(mass)

    chips = range(1, group.chips)
    for g in range(groups):
        for half in range(2):
            for u in range(size // tile):
                project(g, half, u)
            for k in chips:
                direct(g, half, k).start()
            inner(g, half, 0).start()
    tiles = 2 * groups

    def hops(t):
        for hop in range(3):
            if 0 <= t - hop < tiles:
                line.forward(t - hop, hop)

    def keep(t):
        at = pl.ds(t * size, size)
        return pltpu.make_async_copy(whole.at[at], all_out.at[at], store_all.at[t])

    def save(g):
        return pltpu.make_async_copy(kv.at[g], kv_out.at[g], store_kv.at[g])

    for g in range(groups):
        for half in range(2):
            for k in chips:
                direct(g, half, k, True).wait_recv()
                inner(g, half, k).start()
        for half in range(2):
            for k in range(group.chips):
                inner(g, half, k, True).wait_recv()
        save(g).start()
        for half in range(2):
            attend(g, half)
            hops(2 * g + half)
    for t in range(tiles, tiles + 2):
        hops(t)
    for t in range(tiles):
        line.arrived(t)
        keep(t).start()
    for g in range(groups):
        save(g).wait()
        for half in range(2):
            for k in chips:
                direct(g, half, k).wait_send()
            for k in range(group.chips):
                inner(g, half, k).wait_send()
    line.finish(tiles)
    for t in range(tiles):
        keep(t).wait()


def attention(x, w, gains, gain_query, gain_key, cosine, sine, qseg, kseg, ident):
    rows, width = x.shape
    groups, _, size, _ = qseg.shape
    length = kseg.shape[2]
    head = gain_query.shape[1]
    chips = length // (4 * size)
    tiles = 2 * groups
    vmem = pl.BlockSpec(memory_space=pltpu.VMEM)
    dma = pltpu.SemaphoreType.DMA
    return pl.pallas_call(
        functools.partial(attention_kernel, groups, size),
        out_shape=(
            jax.ShapeDtypeStruct((rows, head), BF16),
            jax.ShapeDtypeStruct((rows, head), F32),
            jax.ShapeDtypeStruct((rows, 1), F32),
            jax.ShapeDtypeStruct((rows, head), F32),
            jax.ShapeDtypeStruct((rows, 1), F32),
            jax.ShapeDtypeStruct((rows, head), BF16),
            jax.ShapeDtypeStruct((groups, 2, size, 1), F32),
            jax.ShapeDtypeStruct((groups, length, 2 * head), BF16),
            jax.ShapeDtypeStruct((rows, 4 * head), BF16),
        ),
        in_specs=[vmem] * 9,
        out_specs=(vmem,) * 7 + (ANY, ANY),
        scratch_shapes=[
            pltpu.VMEM((groups, length, 2 * head), BF16), pltpu.VMEM((rows, 4 * head), BF16),
            dma((groups,)), dma((tiles,))] + [dma((groups, 2, chips))] * 4 + [dma((3, tiles))] * 4,
        compiler_params=pltpu.CompilerParams(
            collective_id=ident, has_side_effects=True, vmem_limit_bytes=60 * 2**20),
        name="attention",
    )(x, w, gains, gain_query, gain_key, cosine, sine, qseg, kseg)


class ResidentSum(LineSum):
    def outwards(self, c):
        return pltpu.make_async_remote_copy(
            self.out.at[self.rows(c)], self.out.at[self.rows(c)], self.sems[4].at[c], self.sems[5].at[c],
            device_id={"tp": self.my_leaf}, device_id_type=MESH)

    def total(self, c):
        @pl.when(self.hub)
        def _():
            self.across(c).wait_recv()
            at = self.rows(c)
            self.out[at, :] = (self.own[at, :].astype(F32) + self.far[at, :].astype(F32)).astype(BF16)
            self.outwards(c).start()

    def arrived(self, c):
        @pl.when(self.leaf)
        def _():
            self.outwards(c).wait_recv()

    def finish(self):
        @pl.when(self.leaf)
        def _():
            for c in range(self.count):
                self.inwards(c).wait_send()

        @pl.when(self.hub)
        def _():
            for c in range(self.count):
                self.across(c).wait_send()
                self.outwards(c).wait_send()


def query_back_kernel(tiles, tile, dq_ref, hat_ref, inv_ref, cos_ref, sin_ref, x_ref, gain_ref, gq_ref, w_ref,
                      one_ref, grad_ref, dgain_ref, acc, wq_ref, w_sem, whole, *sems):
    i = pl.program_id(0)
    head = hat_ref.shape[1]
    line = LineGather(whole, tile, head, sems)

    @pl.when(i == 0)
    def _():
        copies = [
            pltpu.make_async_copy(w_ref.at[:, pl.ds(2 * j * head, head)], wq_ref.at[:, pl.ds(j * head, head)], w_sem.at[j])
            for j in range(4)
        ]
        for copy in copies:
            copy.start()
        barrier_line(line.z)
        acc[...] = jnp.zeros_like(acc)
        dgain_ref[...] = jnp.zeros_like(dgain_ref)
        for copy in copies:
            copy.wait()

    @pl.when(i < tiles)
    def _():
        d_rot = rotate(dq_ref[...], cos_ref[...], -sin_ref[...])
        d_raw, d_gain = norm_back(d_rot, hat_ref[...], inv_ref[...], gq_ref[...])
        d_raw = d_raw.astype(BF16)
        at = pl.ds(pl.multiple_of(line.z * head, head), head)
        whole[pl.ds(pl.multiple_of(i * tile, tile), tile), at] = d_raw
        line.forward(i, 0)
        dgain_ref[...] += d_gain[None]
        hat, _ = norm_parts(x_ref[...].astype(F32))
        one = (hat * (1.0 + gain_ref[0:1, :])).astype(BF16)
        acc[...] += dot(one, d_raw, TN)

    @pl.when((i >= 1) & (i <= tiles))
    def _():
        line.forward(i - 1, 1)

    @pl.when((i >= 2) & (i <= tiles + 1))
    def _():
        line.forward(i - 2, 2)

    @pl.when(i >= 3)
    def _():
        line.arrived(i - 3)
        one_ref[...] = dot(whole[pl.ds(pl.multiple_of((i - 3) * tile, tile), tile), :], wq_ref[...], NT)

    @pl.when(i == tiles + 2)
    def _():
        grad_ref[...] = acc[...].astype(BF16)
        line.finish(tiles)


def query_back(dq, hat, inv, cosine, sine, x, gains, gain_query, weights, ident):
    rows, width = x.shape
    head = hat.shape[1]
    tile = 256
    tiles = rows // tile
    dma = pltpu.SemaphoreType.DMA((3, tiles))

    def early(cols):
        return pl.BlockSpec((tile, cols), lambda i: (jnp.minimum(i, tiles - 1), 0))

    return pl.pallas_call(
        functools.partial(query_back_kernel, tiles, tile),
        grid=(tiles + 3,),
        out_shape=(
            jax.ShapeDtypeStruct((rows, width), F32),
            jax.ShapeDtypeStruct((width, head), BF16),
            jax.ShapeDtypeStruct((1, head), F32),
        ),
        in_specs=[early(head), early(head), early(1), early(head // 2), early(head // 2), early(width),
                  whole_block(gains.shape), whole_block(gain_query.shape), ANY],
        out_specs=(
            pl.BlockSpec((tile, width), lambda i: (jnp.maximum(i - 3, 0), 0)),
            pl.BlockSpec((width, head), lambda i: (0, 0)),
            pl.BlockSpec((1, head), lambda i: (0, 0)),
        ),
        scratch_shapes=[
            pltpu.VMEM((width, head), F32), pltpu.VMEM((width, 4 * head), BF16), pltpu.SemaphoreType.DMA((4,)),
            pltpu.VMEM((rows, 4 * head), BF16)] + [dma] * 4,
        compiler_params=pltpu.CompilerParams(
            collective_id=ident, has_side_effects=True, vmem_limit_bytes=48 * 2**20),
        name="query_back",
    )(dq, hat, inv, cosine, sine, x, gains, gain_query, weights)


def key_back_kernel(tiles, tile, chunk, own_rows, dkv_ref, hat_ref, inv_ref, cos_ref, sin_ref, x_ref, dm_ref, part_ref,
                    gain_ref, gk_ref, w_ref, dgq_ref, dg_mid_ref, dg_post_ref, grad_q_ref, grad_o_ref,
                    dx_ref, last_ref, acc, acc_in, acc_key, w_kv, w_sem, out, own, near, far, *sems):
    i = pl.program_id(0)
    head = hat_ref.shape[1]
    per = tile // chunk
    count = tiles * per + 1
    line = ResidentSum(count, chunk, count, own, near, far, out, sems)

    @pl.when(i == 0)
    def _():
        copy = pltpu.make_async_copy(w_ref.at[:, pl.ds(head, 2 * head)], w_kv, w_sem)
        copy.start()
        barrier_line(line.z)
        for ref in (acc, acc_in, acc_key):
            ref[...] = jnp.zeros_like(ref)
        copy.wait()
        line.put(count - 1, jnp.broadcast_to(
            jnp.concatenate([dgq_ref[...], dgq_ref[...]], axis=1).astype(BF16), (chunk, 2 * head)))

    @pl.when(i < tiles)
    def _():
        for j in range(per):
            line.put(i * per + j, dkv_ref[j * chunk : (j + 1) * chunk, :])

    @pl.when((i >= 1) & (i <= tiles))
    def _():
        for j in range(per):
            line.pair((i - 1) * per + j)

    @pl.when((i >= 2) & (i <= tiles + 1))
    def _():
        for j in range(per):
            line.total((i - 2) * per + j)

    @pl.when(i == 1)
    def _():
        line.pair(count - 1)

    @pl.when(i == 2)
    def _():
        line.total(count - 1)

    @pl.when(i >= 3)
    def _():
        for j in range(per):
            line.arrived((i - 3) * per + j)
        d_kv = out[pl.ds(pl.multiple_of((i - 3) * tile, tile), tile), :]
        d_rot = rotate(d_kv[:, :head].astype(F32), cos_ref[...], -sin_ref[...])
        d_raw, d_gain = norm_back(d_rot, hat_ref[...], inv_ref[...], gk_ref[...])
        acc_key[...] += d_gain[None]
        d_raw = jnp.concatenate([d_raw.astype(BF16), d_kv[:, head:]], axis=1)
        d_one = part_ref[...] + dot(d_raw, w_kv[...], NT)
        hat, inv = norm_parts(x_ref[...].astype(F32))
        gain = gain_ref[0:1, :]
        d_part, d_gain = norm_back(d_one, hat, inv, gain)
        acc_in[...] += d_gain[None]
        dx_ref[...] = dm_ref[...] + d_part
        acc[...] += dot((hat * (1.0 + gain)).astype(BF16), d_raw, TN)

    @pl.when(i == tiles + 2)
    def _():
        line.arrived(count - 1)
        width = x_ref.shape[1]
        short = head * own_rows // width
        last_ref[:, :head] = grad_q_ref[...]
        last_ref[:, head : 3 * head] = acc[...].astype(BF16)
        last_ref[:, 3 * head : 4 * head] = grad_o_ref[...]
        d_query = out[pl.ds((count - 1) * chunk, 16), :head][0:1].astype(F32)
        pair = jnp.concatenate([d_query, acc_key[...], jnp.zeros((14, head), F32)], axis=0).astype(BF16)
        col = lax.broadcasted_iota(jnp.int32, (head, width), 1)
        row = lax.broadcasted_iota(jnp.int32, (head, width), 0)
        shift = short.bit_length() - 1
        spot = lax.shift_right_logical(row, shift) * own_rows + (row & (short - 1))
        spread = dot(pair, jnp.where(col == spot, 1.0, 0.0).astype(BF16))
        gains = jnp.concatenate(
            [acc_in[...], dg_mid_ref[...], dg_post_ref[...], spread[0:2], jnp.zeros((122, width), F32)], axis=0)
        last_ref[:, 4 * head :] = jnp.transpose(gains).astype(BF16)
        line.finish()


def key_back(d_kv, hat, inv, cosine, sine, x, d_middle, part, gains, gain_key, first, dg_query, dg_mid, dg_post,
             grad_q, grad_o, own_rows, ident):
    rows, width = x.shape
    head = hat.shape[1]
    tile, chunk = 256, 128
    tiles = rows // tile
    count = rows // chunk + 1
    dma = pltpu.SemaphoreType.DMA((count,))

    def late(cols):
        return pl.BlockSpec((tile, cols), lambda i: (jnp.maximum(i - 3, 0), 0))

    comm = pltpu.VMEM((count * chunk, 2 * head), BF16)
    return pl.pallas_call(
        functools.partial(key_back_kernel, tiles, tile, chunk, own_rows),
        grid=(tiles + 3,),
        out_shape=(
            jax.ShapeDtypeStruct((rows, width), F32),
            jax.ShapeDtypeStruct((width, 4 * head + 128), BF16),
        ),
        in_specs=[pl.BlockSpec((tile, 2 * head), lambda i: (jnp.minimum(i, tiles - 1), 0)),
                  late(head), late(1), late(head // 2), late(head // 2), late(width), late(width), late(width),
                  whole_block(gains.shape), whole_block(gain_key.shape), ANY]
        + [whole_block(a.shape) for a in (dg_query, dg_mid, dg_post, grad_q, grad_o)],
        out_specs=(late(width), pl.BlockSpec((width, 4 * head + 128), lambda i: (0, 0))),
        scratch_shapes=[
            pltpu.VMEM((width, 2 * head), F32), pltpu.VMEM((1, width), F32), pltpu.VMEM((1, head), F32),
            pltpu.VMEM((width, 2 * head), BF16), pltpu.SemaphoreType.DMA] + [comm] * 4 + [dma] * 7
        + [pltpu.SemaphoreType.REGULAR] * 2,
        compiler_params=pltpu.CompilerParams(
            collective_id=ident, has_side_effects=True, vmem_limit_bytes=56 * 2**20),
        name="key_back",
    )(d_kv, hat, inv, cosine, sine, x, d_middle, part, gains, gain_key, first, dg_query, dg_mid, dg_post, grad_q, grad_o)


def scatter_kernel(chips, own_rows, x_ref, o_ref, near, pair, far, *sems):
    ss1, rs1, ss2, rs2 = sems
    ctx = lax.axis_size("ctx")
    me = lax.axis_index("dp") * ctx + lax.axis_index("ctx")
    core = lax.rem(me, 2)
    chip = lax.div(me, 2)
    bar = pltpu.get_barrier_semaphore()

    def device(d):
        return {"dp": lax.div(d, ctx), "ctx": lax.rem(d, ctx)}

    partner = device(2 * chip + 1 - core)
    pl.semaphore_signal(bar, inc=1, device_id=partner, device_id_type=MESH)
    for k in range(1, chips):
        other = lax.rem(chip + k, chips)
        pl.semaphore_signal(bar, inc=1, device_id=device(2 * other + core), device_id_type=MESH)
    pl.semaphore_wait(bar, chips)

    def block(d):
        return pl.ds(pl.multiple_of(d * own_rows, 16), own_rows)

    def within(k):
        q = lax.rem(chip + k, chips)
        return pltpu.make_async_remote_copy(
            x_ref.at[block(2 * q + 1 - core)], near.at[k], ss1.at[k], rs1.at[k], device_id=partner, device_id_type=MESH)

    def between(k):
        q = lax.rem(chip + k, chips)
        return pltpu.make_async_remote_copy(
            pair.at[k], far.at[k], ss2.at[k], rs2.at[k], device_id=device(2 * q + core), device_id_type=MESH)

    order = list(range(1, chips)) + [0]
    for k in order:
        within(k).start()
    for k in order:
        within(k).wait_recv()
        q = lax.rem(chip + k, chips)
        both = x_ref[block(2 * q + core), :].astype(F32) + near[k].astype(F32)
        if k > 0:
            pair[k] = both.astype(BF16)
            between(k).start()
        else:
            o_ref[...] = both
    for k in range(1, chips):
        between(k).wait_recv()
        o_ref[...] += far[k].astype(F32)
    for k in range(1, chips):
        between(k).wait_send()
    for k in order:
        within(k).wait_send()


def scatter(x, own_rows, ident):
    n = x.shape[0] // own_rows
    chips = n // 2
    cols = x.shape[1]
    buf = pltpu.VMEM((chips, own_rows, cols), BF16)
    vmem = pl.BlockSpec(memory_space=pltpu.VMEM)
    return pl.pallas_call(
        functools.partial(scatter_kernel, chips, own_rows),
        out_shape=jax.ShapeDtypeStruct((own_rows, cols), F32),
        in_specs=[vmem],
        out_specs=vmem,
        scratch_shapes=[buf] * 3 + [pltpu.SemaphoreType.DMA((chips,))] * 4,
        compiler_params=pltpu.CompilerParams(
            collective_id=ident, has_side_effects=True, vmem_limit_bytes=40 * 2**20),
        name="scatter",
    )(x)


def shards(tokens, segments, cotangent, w_query, w_key, w_value, w_out, w_gate, w_up, w_down,
           g_input, g_post_attn, g_pre_ffn, g_post_ffn, g_query, g_key):
    batches, seq_local, _, size, width = tokens.shape
    head = w_key.shape[1]
    groups = batches * seq_local
    per_group = 2 * size
    rows = groups * per_group
    ctx = lax.axis_size("ctx")
    length = per_group * ctx
    rank = lax.axis_index("ctx")
    shared = ("dp", "ctx")
    own_rows = g_input.shape[0]
    hidden = w_gate.shape[1]

    def column(gain):
        return jnp.pad(gain, (0, own_rows - gain.shape[0]))[:, None]

    own_ids = segments.reshape(groups, 2, size)
    id_cols = -(-own_ids.size // own_rows)
    ids = jnp.pad(own_ids.reshape(-1), (0, own_rows * id_cols - own_ids.size)).reshape(own_rows, id_cols)
    extra = jnp.concatenate(
        [column(g) for g in (g_input, g_post_attn, g_pre_ffn, g_post_ffn, g_query, g_key)] + [ids.astype(BF16)], axis=1)
    extra = jnp.pad(extra, ((0, 0), (0, 128 - extra.shape[1])))

    def rows_of_16(w):
        return jnp.pad(w, ((0, -own_rows % 16), (0, 0)))

    first, line = first_gather(
        rows_of_16(jnp.concatenate([w_query, w_key, w_value, extra], axis=1)),
        rows_of_16(jnp.concatenate([w_query, w_out.T], axis=1)), width // own_rows, 5)
    first = first[:, :own_rows].reshape(width, -1)
    line = line[:own_rows]
    mat_qkv = first[:, : 3 * head]
    side = first[:, 3 * head :]
    gain_cols = side[:, :8].astype(F32)
    gain_rows = gain_cols.T
    gain_input = gain_rows[0]
    short = g_query.shape[0]
    gain_query, gain_key = (
        gain_cols[:, i].reshape(-1, own_rows)[:, :short].reshape(-1) for i in (4, 5))
    ids = side[:, 6 : 6 + id_cols].reshape(-1, ctx, own_rows * id_cols)[:, :, : own_ids.size]
    ids = lax.dynamic_index_in_dim(ids, lax.axis_index("dp"), 0, keepdims=False).astype(jnp.int32)
    key_ids = ids.reshape(ctx, groups, 2, size).transpose(1, 2, 0, 3).reshape(groups, length)
    key_ids = jnp.where(key_ids == 0, -1, key_ids)

    wide = wide_of(hidden)
    second = jnp.concatenate(
        [line] + [jnp.pad(w, ((0, 0), (0, wide - hidden))) for w in (w_gate, w_up, w_down.T)], axis=1)
    weights = lax.all_gather(second, shared, axis=0, tiled=True)

    offsets = rank * size + jnp.arange(size, dtype=jnp.int32)
    position = jnp.concatenate([offsets, length - 1 - offsets]).astype(F32)
    cosine, sine = angles(position, head // 2, head)
    turn = (cosine, sine)
    cosine = jnp.broadcast_to(cosine, (groups, per_group, head // 2)).reshape(rows, head // 2)
    sine = jnp.broadcast_to(sine, (groups, per_group, head // 2)).reshape(rows, head // 2)

    x_rows = tokens.reshape(rows, width)
    dy_rows = cotangent.reshape(rows, width)
    queries, q_hat, q_scale, k_hat, k_scale, heads_own, log_mass, kv, heads_all = attention(
        x_rows, mat_qkv, gain_rows, gain_query[None], gain_key[None], *turn, own_ids[..., None], key_ids[:, None, :], 0)

    attn, hidden_two, gate, up, ffn_out = ffn_forward(x_rows, heads_all, gain_rows, weights, hidden, 1)
    output, d_gain_post_ffn, grad_ffn, d_two = ffn_backward(
        x_rows, attn, dy_rows, ffn_out, hidden_two, gate, up, gain_rows, weights, 2)
    grad_ffn = lax.psum_scatter(grad_ffn, shared, scatter_dimension=1, tiled=True).astype(F32)
    d_middle, d_heads, delta, d_gain_mid, grad_out_t = middle_back(
        x_rows, attn, dy_rows, d_two, heads_own, gain_rows, weights)

    d_query, d_kv = attend_back(
        queries.reshape(groups, 2, size, head), kv, d_heads.reshape(groups, 2, size, head),
        log_mass.reshape(groups, 2, 1, size), delta.reshape(groups, 2, 1, size),
        own_ids[:, :, None, :], key_ids[:, :, None])
    d_kv = lax.psum_scatter(
        d_kv.reshape(groups, 2, length // 2, 2 * head), "ctx", scatter_dimension=2, tiled=True)
    d_one, grad_q, d_gain_query = query_back(
        d_query.reshape(rows, head), q_hat, q_scale, cosine, sine, x_rows, gain_rows, gain_query[None], weights, 4)
    d_kv, d_one = lax.optimization_barrier((d_kv, d_one))
    d_tokens, last = key_back(
        d_kv.reshape(rows, 2 * head), k_hat, k_scale, cosine, sine, x_rows, d_middle, d_one, gain_rows, gain_key[None],
        first, d_gain_query, d_gain_mid, d_gain_post_ffn, grad_q, grad_out_t, own_rows, 3)
    if own_rows % 16 == 0:
        last = scatter(last, own_rows, 7)
    else:
        last = lax.psum_scatter(last, shared, scatter_dimension=0, tiled=True).astype(F32)
    g = last[:, 4 * head :]
    return (
        output.reshape(tokens.shape),
        d_tokens.reshape(tokens.shape),
        last[:, :head],
        last[:, head : 2 * head],
        last[:, 2 * head : 3 * head],
        last[:, 3 * head : 4 * head].T,
        grad_ffn[0],
        grad_ffn[1],
        grad_ffn[2].T,
        g[:, 0],
        g[:, 1],
        g[:, 2],
        g[:, 3],
        g[:short, 4],
        g[:short, 5],
    )


def solution(mesh):
    shared = ("dp", "ctx")
    rows = P(None, "dp", None, "ctx", None)
    weights = (
        P(shared, "tp"), P(shared, None), P(shared, None), P("tp", shared),
        P(shared, "tp"), P(shared, "tp"), P("tp", shared),
    )
    gains = (P(shared),) * 6
    return jax.shard_map(
        shards,
        mesh=mesh,
        in_specs=(rows, P(None, "dp", None, "ctx"), rows) + weights + gains,
        out_specs=(rows, rows) + weights + gains,
        check_vma=False,
    )
```

```python
import functools

import jax
import jax.numpy as jnp
from jax import lax
from jax.experimental import pallas as pl
from jax.experimental.pallas import tpu as pltpu
from jax.sharding import PartitionSpec as P

EPS = 1e-06
THETA = 1000000.0
SCALE = 0.0625
NEGATIVE = -1e30
BF16 = jnp.bfloat16
F32 = jnp.float32
MESH = pl.DeviceIdType.MESH
NN = (((1,), (0,)), ((), ()))
NT = (((1,), (1,)), ((), ()))
TN = (((0,), (0,)), ((), ()))


def dot(a, b, dims=NN):
    return lax.dot_general(a, b, dims, preferred_element_type=F32)


def barrier_line(z):
    bar = pltpu.get_barrier_semaphore()

    @pl.when(z > 0)
    def _():
        pl.semaphore_signal(bar, inc=1, device_id={"tp": z - 1}, device_id_type=MESH)

    @pl.when(z < 3)
    def _():
        pl.semaphore_signal(bar, inc=1, device_id={"tp": z + 1}, device_id_type=MESH)

    pl.semaphore_wait(bar, jnp.where((z == 0) | (z == 3), 1, 2))


def block_starts(half, t, blocks, rank):
    if half == 0:
        return t
    return jnp.where(t < blocks, t, t + rank + 1)


def attend_back_kernel(blocks, q_ref, kv_ref, do_ref, l_ref, d_ref, qs_ref, ks_ref,
                       dq_ref, dkv_ref, dk_acc, dv_acc):
    rank = lax.axis_index("ctx")
    size = q_ref.shape[2]
    head = q_ref.shape[3]
    row = lax.broadcasted_iota(jnp.int32, (size, size), 0)
    col = lax.broadcasted_iota(jnp.int32, (size, size), 1)
    dk_acc[...] = jnp.zeros_like(dk_acc)
    dv_acc[...] = jnp.zeros_like(dv_acc)
    for half in range(2):
        q = q_ref[0, half] * jnp.asarray(SCALE, BF16)
        do = do_ref[0, half]
        qseg = qs_ref[0, half]
        log_mass = l_ref[0, half]
        delta = d_ref[0, half]

        def part(block, own):
            rows = pl.ds(pl.multiple_of(block * size, size), size)
            k = kv_ref[0, rows, :head]
            v = kv_ref[0, rows, head:]
            ids = jnp.broadcast_to(ks_ref[0, :, rows], (8, size))
            allowed = jnp.transpose(ids)[:, 0:1] == qseg
            if own:
                order = (row <= col) if half == 0 else (row >= col)
                allowed = (allowed & order) | (col == row)
            s = jnp.where(allowed, dot(k, q, NT), NEGATIVE)
            p = jnp.exp(s - log_mass)
            ds = (p * (dot(v, do, NT) - delta)).astype(BF16)
            dv_acc[rows, :] += dot(p.astype(BF16), do)
            dk_acc[rows, :] += dot(ds, q)
            return dot(ds, k, TN)

        def step(t, dq):
            return dq + part(block_starts(half, t, blocks, rank), False)

        dq = part(rank + half * blocks, True)
        count = rank if half == 0 else 2 * blocks - 1 - rank
        dq_ref[0, half] = SCALE * lax.fori_loop(0, count, step, dq)
    dkv_ref[0, :, :head] = dk_acc[...].astype(BF16)
    dkv_ref[0, :, head:] = dv_acc[...].astype(BF16)


def attend_back(q, kv, do, log_mass, delta, qseg, kseg):
    groups, _, size, head = q.shape
    length = kv.shape[1]
    blocks = length // (2 * size)
    halves = pl.BlockSpec((1, 2, size, head), lambda g: (g, 0, 0, 0))
    whole = pl.BlockSpec((1, length, 2 * head), lambda g: (g, 0, 0))
    line = pl.BlockSpec((1, 2, 1, size), lambda g: (g, 0, 0, 0))
    return pl.pallas_call(
        functools.partial(attend_back_kernel, blocks),
        grid=(groups,),
        out_shape=(
            jax.ShapeDtypeStruct(q.shape, F32),
            jax.ShapeDtypeStruct((groups, length, 2 * head), BF16),
        ),
        in_specs=[halves, whole, halves, line, line, line,
                  pl.BlockSpec((1, 1, length), lambda g: (g, 0, 0))],
        out_specs=(halves, pl.BlockSpec((1, length, 2 * head), lambda g: (g, 0, 0))),
        scratch_shapes=[pltpu.VMEM((length, head), F32)] * 2,
        compiler_params=pltpu.CompilerParams(vmem_limit_bytes=56 * 2**20),
        name="attend_back",
    )(q, kv, do, log_mass, delta, qseg, kseg)


def angles(position, half_size, full_size):
    frequency = THETA ** (-2.0 * jnp.arange(half_size, dtype=F32) / full_size)
    turned = position[:, None] * frequency[None, :]
    return (jnp.cos(turned), jnp.sin(turned))


def rotate(tensor, cosine, sine):
    half_size = tensor.shape[-1] // 2
    a = tensor[..., :half_size]
    b = tensor[..., half_size:]
    return jnp.concatenate([a * cosine - b * sine, b * cosine + a * sine], axis=-1)


def norm_parts(values):
    inv = lax.rsqrt(jnp.mean(values * values, axis=-1, keepdims=True) + EPS)
    return (values * inv, inv)


def norm_back(upstream, normalized, inv, gain):
    d_norm = upstream * (1.0 + gain)
    d_values = inv * (d_norm - normalized * jnp.mean(d_norm * normalized, axis=-1, keepdims=True))
    return (d_values, jnp.sum(upstream * normalized, axis=0))


def gelu_tanh(values):
    return jax.nn.gelu(values, approximate=True)


class LineSum:
    def __init__(self, count, chunk, slots, own, near, far, out, sems):
        self.count, self.chunk, self.slots = count, chunk, slots
        self.own, self.near, self.far, self.out = own, near, far, out
        self.sems = sems
        self.z = z = lax.axis_index("tp")
        self.hub = (z == 1) | (z == 2)
        self.leaf = (z == 0) | (z == 3)
        self.other_hub = jnp.where(z == 1, 2, 1)
        self.my_hub = jnp.where(z == 0, 1, 2)
        self.my_leaf = jnp.where(z == 1, 0, 3)

    def slot(self, c):
        return pl.ds(pl.multiple_of(lax.rem(c, self.slots) * self.chunk, self.chunk), self.chunk)

    def rows(self, c):
        return pl.ds(pl.multiple_of(c * self.chunk, self.chunk), self.chunk)

    def inwards(self, c):
        return pltpu.make_async_remote_copy(
            self.own.at[self.slot(c)], self.near.at[self.slot(c)], self.sems[0].at[c], self.sems[1].at[c],
            device_id={"tp": self.my_hub}, device_id_type=MESH)

    def across(self, c):
        return pltpu.make_async_remote_copy(
            self.own.at[self.slot(c)], self.far.at[self.slot(c)], self.sems[2].at[c], self.sems[3].at[c],
            device_id={"tp": self.other_hub}, device_id_type=MESH)

    def outwards(self, c):
        return pltpu.make_async_remote_copy(
            self.far.at[self.slot(c)], self.out.at[self.rows(c)], self.sems[4].at[c], self.sems[5].at[c],
            device_id={"tp": self.my_leaf}, device_id_type=MESH)

    def store(self, c):
        return pltpu.make_async_copy(self.far.at[self.slot(c)], self.out.at[self.rows(c)], self.sems[6].at[c])

    def put(self, c, value):
        ring = self.slots < self.count
        if ring:
            @pl.when(c >= self.slots)
            def _():
                @pl.when(self.leaf)
                def _():
                    self.inwards(c - self.slots).wait_send()

                @pl.when(self.hub)
                def _():
                    self.across(c - self.slots).wait_send()

        self.own[self.slot(c), :] = value

        @pl.when(self.leaf)
        def _():
            if ring:
                @pl.when(c >= self.slots)
                def _():
                    pl.semaphore_wait(self.sems[7], 1)
            self.inwards(c).start()

    def pair(self, c):
        ring = self.slots < self.count

        @pl.when(self.hub)
        def _():
            self.inwards(c).wait_recv()
            at = self.slot(c)
            self.own[at, :] = (self.own[at, :].astype(F32) + self.near[at, :].astype(F32)).astype(BF16)
            if ring:
                @pl.when(c < self.count - self.slots)
                def _():
                    pl.semaphore_signal(self.sems[7], inc=1, device_id={"tp": self.my_leaf}, device_id_type=MESH)

                @pl.when(c >= self.slots)
                def _():
                    pl.semaphore_wait(self.sems[8], 1)
            self.across(c).start()

    def total(self, c):
        @pl.when(self.hub)
        def _():
            self.across(c).wait_recv()
            at = self.slot(c)
            self.far[at, :] = (self.own[at, :].astype(F32) + self.far[at, :].astype(F32)).astype(BF16)
            self.outwards(c).start()
            self.store(c).start()

    def retire(self, c):
        @pl.when(self.hub)
        def _():
            self.outwards(c).wait_send()
            self.store(c).wait()
            if self.slots < self.count:
                @pl.when(c < self.count - self.slots)
                def _():
                    pl.semaphore_signal(self.sems[8], inc=1, device_id={"tp": self.other_hub}, device_id_type=MESH)

    def finish(self):
        first = max(0, self.count - self.slots)

        @pl.when(self.leaf)
        def _():
            for c in range(self.count):
                self.outwards(c).wait_recv()
            for c in range(first, self.count):
                self.inwards(c).wait_send()

        @pl.when(self.hub)
        def _():
            for c in range(first, self.count):
                self.across(c).wait_send()


def line_sum_scratch(count, chunk, slots, cols):
    dma = pltpu.SemaphoreType.DMA((count,))
    regular = pltpu.SemaphoreType.REGULAR
    return [pltpu.VMEM((slots * chunk, cols), BF16)] * 3 + [dma] * 7 + [regular] * 2


def gelu_parts(v):
    c = 0.7978845608028654
    square = v * v
    t = jnp.tanh(v * (c + (c * 0.044715) * square))
    half = 0.5 + 0.5 * t
    value = v * half
    slope = half + (0.5 * v) * (1.0 - t * t) * (c + (3.0 * c * 0.044715) * square)
    return value, slope


def column_parts(cols):
    middle = -(-cols // 256) * 128
    return [(0, middle), (middle, cols)] if middle < cols else [(0, cols)]


def middle_of(x, attn, gain_post_attn):
    hat, inv = norm_parts(attn.astype(F32))
    return x.astype(F32) + hat * (1.0 + gain_post_attn), hat, inv


def load_ffn_weights(weights, refs, sem):
    wide = refs[0].shape[1]
    base = weights.shape[1] - 3 * wide
    return [
        pltpu.make_async_copy(weights.at[:, pl.ds(base + j * wide, wide)], ref, sem.at[j])
        for j, ref in enumerate(refs)
    ]


def ffn_forward_kernel(tiles, tile, chunk, hidden, x_ref, h_ref, gain_ref, w_ref,
                       attn_ref, two_ref, gate_ref, up_ref, out_ref, wo_ref, wg_ref, wu_ref, wd_ref, w_sem, own, near, far, *sems):
    i = pl.program_id(0)
    per = tile // chunk
    line = LineSum(tiles * per, chunk, tiles * per, own, near, far, out_ref, sems)
    head = wo_ref.shape[1] // 4

    @pl.when(i == 0)
    def _():
        copies = load_ffn_weights(w_ref, (wg_ref, wu_ref, wd_ref), w_sem)
        copies.append(pltpu.make_async_copy(w_ref.at[:, pl.ds(0, 4 * head)], wo_ref, w_sem.at[3]))
        for copy in copies:
            copy.start()
        barrier_line(line.z)
        for copy in copies:
            copy.wait()

    attn = dot(h_ref[...], wo_ref[...], NT).astype(BF16)
    attn_ref[...] = attn
    middle, _, _ = middle_of(x_ref[...], attn, gain_ref[1:2, :])
    hat, _ = norm_parts(middle)
    two = (hat * (1.0 + gain_ref[2:3, :])).astype(BF16)
    two_ref[...] = two
    part = None
    for a, b in column_parts(hidden):
        gate = dot(two, wg_ref[:, a:b])
        up = dot(two, wu_ref[:, a:b])
        gate_ref[:, a:b] = gate.astype(BF16)
        up_ref[:, a:b] = up.astype(BF16)
        value, _ = gelu_parts(gate)
        more = dot((value * up).astype(BF16), wd_ref[:, a:b], NT)
        part = more if part is None else part + more
    for j in range(per):
        line.put(i * per + j, part[j * chunk : (j + 1) * chunk].astype(BF16))

    @pl.when(i >= 1)
    def _():
        for j in range(per):
            line.pair((i - 1) * per + j)

    @pl.when(i >= 2)
    def _():
        for j in range(per):
            line.total((i - 2) * per + j)

    @pl.when(i == tiles - 1)
    def _():
        last = tiles * per
        for j in range(per):
            line.pair(last - per + j)
        for c in range(max(0, last - 2 * per), last):
            line.total(c)
        for c in range(last):
            line.retire(c)
        line.finish()


def whole_block(shape):
    return pl.BlockSpec(shape, lambda i: (0,) * len(shape), pipeline_mode=pl.Buffered(1))


def tile_block(tile, cols):
    return pl.BlockSpec((tile, cols), lambda i: (i, 0))


ANY = pl.BlockSpec(memory_space=pl.ANY)


def wide_of(hidden):
    return -(-hidden // 128) * 128


def ffn_forward(x, heads, gains, weights, hidden, ident):
    rows, width = x.shape
    all_heads = heads.shape[1]
    tile, chunk = 256, 128
    tiles = rows // tile
    count = rows // chunk
    wide = wide_of(hidden)
    return pl.pallas_call(
        functools.partial(ffn_forward_kernel, tiles, tile, chunk, hidden),
        grid=(tiles,),
        out_shape=(
            jax.ShapeDtypeStruct((rows, width), BF16),
            jax.ShapeDtypeStruct((rows, width), BF16),
            jax.ShapeDtypeStruct((rows, hidden), BF16),
            jax.ShapeDtypeStruct((rows, hidden), BF16),
            jax.ShapeDtypeStruct((rows, width), BF16),
        ),
        in_specs=[
            tile_block(tile, width),
            tile_block(tile, all_heads),
            whole_block(gains.shape),
            ANY,
        ],
        out_specs=(tile_block(tile, width), tile_block(tile, width), tile_block(tile, hidden), tile_block(tile, hidden), ANY),
        scratch_shapes=[pltpu.VMEM((width, all_heads), BF16)] + [pltpu.VMEM((width, wide), BF16)] * 3
        + [pltpu.SemaphoreType.DMA((4,))]
        + line_sum_scratch(count, chunk, count, width),
        compiler_params=pltpu.CompilerParams(
            collective_id=ident, has_side_effects=True, vmem_limit_bytes=60 * 2**20),
        name="ffn_forward",
    )(x, heads, gains, weights)


def ffn_backward_kernel(tiles, tile, chunk, slots, hidden, x_ref, attn_ref, dy_ref, ffn_ref, two_ref, gate_ref, up_ref,
                        gain_ref, w_ref,
                        y_ref, dgain_ref, grad_ref, out_ref, wg_ref, wu_ref, wd_ref, w_sem,
                        acc_g, acc_u, acc_d, keep_g, keep_u, keep_h, stage, stage_sem, own, near, far, *sems):
    i = pl.program_id(0)
    per = tile // chunk
    last = tiles * per
    line = LineSum(last, chunk, slots, own, near, far, out_ref, sems)

    @pl.when(i == 0)
    def _():
        copies = load_ffn_weights(w_ref, (wg_ref, wu_ref, wd_ref), w_sem)
        for copy in copies:
            copy.start()
        barrier_line(line.z)
        for acc in (acc_g, acc_u, acc_d, dgain_ref):
            acc[...] = jnp.zeros_like(acc)
        for copy in copies:
            copy.wait()

    middle, _, _ = middle_of(x_ref[...], attn_ref[...], gain_ref[1:2, :])
    hat, inv = norm_parts(ffn_ref[...].astype(F32))
    gain = gain_ref[3:4, :]
    y_ref[...] = (middle + hat * (1.0 + gain)).astype(BF16)
    d_ffn, d_gain = norm_back(dy_ref[...].astype(F32), hat, inv, gain)
    dgain_ref[...] += d_gain[None]
    d_ffn = d_ffn.astype(BF16)
    part = None
    for a, b in column_parts(hidden):
        d_hidden = dot(d_ffn, wd_ref[:, a:b])
        up = up_ref[:, a:b].astype(F32)
        value, slope = gelu_parts(gate_ref[:, a:b].astype(F32))
        keep_h[:, a:b] = (value * up).astype(BF16)
        d_gate = (d_hidden * up * slope).astype(BF16)
        d_up = (d_hidden * value).astype(BF16)
        keep_g[:, a:b] = d_gate
        keep_u[:, a:b] = d_up
        more = dot(d_gate, wg_ref[:, a:b], NT) + dot(d_up, wu_ref[:, a:b], NT)
        part = more if part is None else part + more
    for j in range(per):
        line.put(i * per + j, part[j * chunk : (j + 1) * chunk].astype(BF16))

    @pl.when(i >= 1)
    def _():
        for j in range(per):
            line.pair((i - 1) * per + j)

    acc_g[...] += dot(two_ref[...], keep_g[...], TN)
    acc_u[...] += dot(two_ref[...], keep_u[...], TN)
    acc_d[...] += dot(d_ffn, keep_h[...], TN)

    @pl.when(i >= 2)
    def _():
        for j in range(per):
            line.total((i - 2) * per + j)

    @pl.when(i >= 3)
    def _():
        for j in range(per):
            line.retire((i - 3) * per + j)

    @pl.when(i == tiles - 1)
    def _():
        for j in range(per):
            line.pair(last - per + j)
        step = stage.shape[1]
        count = acc_g.shape[0] // step

        def piece(acc, out, k, at):
            @pl.when(k >= 2)
            def _():
                pltpu.make_async_copy(stage.at[at], out.at[pl.ds(0, step)], stage_sem.at[at]).wait()
            rows = pl.ds(pl.multiple_of(k * step, step), step)
            stage[at] = acc[rows, :].astype(BF16)
            pltpu.make_async_copy(stage.at[at], out.at[rows], stage_sem.at[at]).start()

        for acc, out in ((acc_g, grad_ref.at[0]), (acc_u, grad_ref.at[1]), (acc_d, grad_ref.at[2])):
            def pieces(k, _):
                piece(acc, out, k, lax.rem(k, 2))
                return 0

            lax.fori_loop(0, count, pieces, 0)
            for at in range(2):
                pltpu.make_async_copy(stage.at[at], out.at[pl.ds(0, step)], stage_sem.at[at]).wait()
            if acc is acc_g:
                for c in range(max(0, last - 2 * per), last - per):
                    line.total(c)
            if acc is acc_u:
                for c in range(last - per, last):
                    line.total(c)
        for c in range(max(0, last - 3 * per), last):
            line.retire(c)
        line.finish()


def ffn_backward(x, attn, dy, ffn, two, gate, up, gains, weights, ident):
    rows, width = x.shape
    hidden = gate.shape[1]
    wide = wide_of(hidden)
    tile, chunk = 256, 128
    tiles = rows // tile
    count = rows // chunk
    slots = min(count, 6)
    step = 144
    acc = pltpu.VMEM((width, hidden), F32)
    keep = pltpu.VMEM((tile, hidden), BF16)
    return pl.pallas_call(
        functools.partial(ffn_backward_kernel, tiles, tile, chunk, slots, hidden),
        grid=(tiles,),
        out_shape=(
            jax.ShapeDtypeStruct((rows, width), BF16),
            jax.ShapeDtypeStruct((1, width), F32),
            jax.ShapeDtypeStruct((3, width, hidden), BF16),
            jax.ShapeDtypeStruct((rows, width), BF16),
        ),
        in_specs=[tile_block(tile, width)] * 5 + [tile_block(tile, hidden)] * 2
        + [whole_block(gains.shape), ANY],
        out_specs=(tile_block(tile, width), pl.BlockSpec((1, width), lambda i: (0, 0)), ANY, ANY),
        scratch_shapes=[pltpu.VMEM((width, wide), BF16)] * 3 + [pltpu.SemaphoreType.DMA((3,))] + [acc] * 3 + [keep] * 3
        + [pltpu.VMEM((2, step, hidden), BF16), pltpu.SemaphoreType.DMA((2,))]
        + line_sum_scratch(count, chunk, slots, width),
        compiler_params=pltpu.CompilerParams(
            collective_id=ident, has_side_effects=True, vmem_limit_bytes=63 * 2**20),
        name="ffn_backward",
    )(x, attn, dy, ffn, two, gate, up, gains, weights)


def middle_back_kernel(x_ref, attn_ref, dy_ref, d2_ref, h_ref, gain_ref, w_ref,
                       dm_ref, dh_ref, delta_ref, dgain_ref, go_ref, acc, wo_ref, w_sem):
    i = pl.program_id(0)

    @pl.when(i == 0)
    def _():
        head = wo_ref.shape[1]
        at = pl.multiple_of(lax.axis_index("tp") * head, head)
        copy = pltpu.make_async_copy(w_ref.at[:, pl.ds(at, head)], wo_ref, w_sem)
        copy.start()
        copy.wait()
        acc[...] = jnp.zeros_like(acc)
        dgain_ref[...] = jnp.zeros_like(dgain_ref)

    middle, attn_hat, attn_inv = middle_of(x_ref[...], attn_ref[...], gain_ref[1:2, :])
    hat, inv = norm_parts(middle)
    d_part, d_gain = norm_back(d2_ref[...].astype(F32), hat, inv, gain_ref[2:3, :])
    dgain_ref[1:2, :] += d_gain[None]
    d_middle = dy_ref[...].astype(F32) + d_part
    dm_ref[...] = d_middle
    d_attn, d_gain = norm_back(d_middle, attn_hat, attn_inv, gain_ref[1:2, :])
    dgain_ref[0:1, :] += d_gain[None]
    d_attn = d_attn.astype(BF16)
    d_heads = dot(d_attn, wo_ref[...]).astype(BF16)
    dh_ref[...] = d_heads
    heads = h_ref[...]
    delta_ref[...] = jnp.sum(d_heads.astype(F32) * heads.astype(F32), axis=1, keepdims=True)
    acc[...] += dot(d_attn, heads, TN)

    @pl.when(i == pl.num_programs(0) - 1)
    def _():
        go_ref[...] = acc[...].astype(BF16)


def middle_back(x, attn, dy, d_two, heads, gains, weights):
    rows, width = x.shape
    head = heads.shape[1]
    tile = 256
    return pl.pallas_call(
        middle_back_kernel,
        grid=(rows // tile,),
        out_shape=(
            jax.ShapeDtypeStruct((rows, width), F32),
            jax.ShapeDtypeStruct((rows, head), BF16),
            jax.ShapeDtypeStruct((rows, 1), F32),
            jax.ShapeDtypeStruct((2, width), F32),
            jax.ShapeDtypeStruct((width, head), BF16),
        ),
        in_specs=[tile_block(tile, width)] * 4 + [tile_block(tile, head)] + [whole_block(gains.shape), ANY],
        out_specs=(
            tile_block(tile, width), tile_block(tile, head), tile_block(tile, 1),
            pl.BlockSpec((2, width), lambda i: (0, 0)), pl.BlockSpec((width, head), lambda i: (0, 0)),
        ),
        scratch_shapes=[pltpu.VMEM((width, head), F32), pltpu.VMEM((width, head), BF16), pltpu.SemaphoreType.DMA],
        compiler_params=pltpu.CompilerParams(vmem_limit_bytes=48 * 2**20),
        name="middle_back",
    )(x, attn, dy, d_two, heads, gains, weights)


class LineGather:
    def __init__(self, whole, tile, width, sems):
        self.whole, self.tile, self.width, self.sems = whole, tile, width, sems
        self.z = lax.axis_index("tp")

    def place(self, src, t):
        return self.whole.at[
            pl.ds(pl.multiple_of(t * self.tile, self.tile), self.tile),
            pl.ds(pl.multiple_of(src * self.width, self.width), self.width)]

    def send(self, src, t, hop, way):
        ss, rs = self.sems[:2] if way > 0 else self.sems[2:]
        place = self.place(src, t)
        return pltpu.make_async_remote_copy(
            place, place, ss.at[hop, t], rs.at[hop, t],
            device_id={"tp": self.z + way}, device_id_type=MESH)

    def going(self, hop, way):
        src = self.z - way * hop
        return src, (self.z + way >= 0) & (self.z + way <= 3) & (src >= 0) & (src <= 3)

    def coming(self, hop, way):
        src = self.z - way * (hop + 1)
        return src, (src >= 0) & (src <= 3)

    def forward(self, t, hop):
        for way in (1, -1):
            if hop > 0:
                self.wait(t, hop - 1, way)
            src, ok = self.going(hop, way)

            @pl.when(ok)
            def _():
                self.send(src, t, hop, way).start()

    def wait(self, t, hop, way):
        src, ok = self.coming(hop, way)

        @pl.when(ok)
        def _():
            self.send(src, t, hop, way).wait_recv()

    def arrived(self, t):
        for way in (1, -1):
            self.wait(t, 2, way)

    def finish(self, tiles):
        for hop in range(3):
            for way in (1, -1):
                src, ok = self.going(hop, way)

                @pl.when(ok)
                def _():
                    def one(t, _):
                        self.send(src, t, hop, way).wait_send()
                        return 0

                    lax.fori_loop(0, tiles, one, 0)


class KeyGather(LineGather):
    def __init__(self, block, chips, sems):
        self.block, self.chips, self.sems = block, chips, sems
        self.z = lax.axis_index("tp")

    def tile_of(self, g, half, k):
        return (2 * g + half) * (self.chips - 1) + k - 1

    def place(self, src, t):
        pair, k = divmod(t, self.chips - 1)
        return self.quarter(pair // 2, pair % 2, k + 1, src)

    def quarter(self, g, half, k, src, own=False):
        ref, start, size = self.block(g, half, k, own)
        rows = size // 4
        return ref.at[pl.ds(pl.multiple_of(start + src * rows, rows), rows)]

    def finish(self, tiles):
        for hop in range(3):
            for way in (1, -1):
                src, ok = self.going(hop, way)

                @pl.when(ok)
                def _():
                    for t in range(tiles):
                        self.send(src, t, hop, way).wait_send()


class Shared:
    def __init__(self, over_dp):
        self.ctx = ctx = lax.axis_size("ctx")
        me = lax.axis_index("ctx")
        self.devices = ctx
        if over_dp:
            me = me + lax.axis_index("dp") * ctx
            self.devices = ctx * lax.axis_size("dp")
        self.over_dp = over_dp
        self.me = me
        self.chips = self.devices // 2
        self.core = lax.rem(me, 2)
        self.chip = lax.div(me, 2)

    def ident(self, device):
        if self.over_dp:
            return {"dp": lax.div(device, self.ctx), "ctx": lax.rem(device, self.ctx)}
        return {"ctx": device}

    def other(self, k):
        return 2 * lax.rem(self.chip + k + self.chips, self.chips) + self.core

    def partner(self):
        return self.me + 1 - 2 * self.core

    def greet(self, z):
        bar = pltpu.get_barrier_semaphore()
        for device in [self.partner()] + [self.other(k) for k in range(1, self.chips)]:
            pl.semaphore_signal(bar, inc=1, device_id=self.ident(device), device_id_type=MESH)

        @pl.when(z > 0)
        def _():
            pl.semaphore_signal(bar, inc=1, device_id={"tp": z - 1}, device_id_type=MESH)

        @pl.when(z < 3)
        def _():
            pl.semaphore_signal(bar, inc=1, device_id={"tp": z + 1}, device_id_type=MESH)

        pl.semaphore_wait(bar, self.chips + jnp.where((z == 0) | (z == 3), 1, 2))

    def copy(self, source, target, send, recv, device):
        return pltpu.make_async_remote_copy(
            source, target, send, recv, device_id=self.ident(device), device_id_type=MESH)


def first_gather_kernel(a_ref, b_ref, i_ref, all_ref, line_ref, ids_ref, lsem, ss1, rs1, ss2, rs2, si1, ri1, si2, ri2, *sems):
    group = Shared(True)
    line = LineGather(line_ref, b_ref.shape[0], b_ref.shape[1], sems)
    width = b_ref.shape[1]
    own = [
        pltpu.make_async_copy(b_ref, line_ref.at[:, pl.ds(pl.multiple_of(line.z * width, width), width)], lsem.at[0]),
        pltpu.make_async_copy(a_ref, all_ref.at[group.me], lsem.at[1]),
        pltpu.make_async_copy(i_ref, ids_ref.at[group.me], lsem.at[2]),
    ]
    for copy in own:
        copy.start()
    group.greet(line.z)
    arrays = ((a_ref, all_ref, ss1, rs1, ss2, rs2), (i_ref, ids_ref, si1, ri1, si2, ri2))

    def direct(n, k, incoming=False):
        ref, whole, ss, rs = arrays[n][:4]
        at = whole.at[group.other(-k)] if incoming else whole.at[group.me]
        return group.copy(ref, at, ss.at[k], rs.at[k], group.other(k))

    def inner(n, k, incoming=False):
        ref, whole, _, _, ss, rs = arrays[n]
        at = whole.at[group.other(-k)]
        if incoming:
            at = whole.at[group.other(-k) + 1 - 2 * group.core]
        return group.copy(ref if k == 0 else at, at, ss.at[k], rs.at[k], group.partner())

    both = range(2)
    for k in range(1, group.chips):
        for n in both:
            direct(n, k).start()
    own[0].wait()
    line.forward(0, 0)
    for n in both:
        inner(n, 0).start()
    for k in range(1, group.chips):
        if k < 3:
            line.forward(0, k)
        for n in both:
            direct(n, k, True).wait_recv()
            inner(n, k).start()
    for hop in range(min(3, group.chips), 3):
        line.forward(0, hop)
    for k in range(group.chips):
        for n in both:
            inner(n, k, True).wait_recv()
    line.arrived(0)
    for copy in own[1:]:
        copy.wait()
    for n in both:
        for k in range(1, group.chips):
            direct(n, k).wait_send()
        for k in range(group.chips):
            inner(n, k).wait_send()
    line.finish(1)


def first_gather(a, b, ids, devices, ident):
    dma = pltpu.SemaphoreType.DMA((devices // 2,))
    hop = pltpu.SemaphoreType.DMA((3, 1))
    return pl.pallas_call(
        first_gather_kernel,
        out_shape=(
            jax.ShapeDtypeStruct((devices,) + a.shape, a.dtype),
            jax.ShapeDtypeStruct((b.shape[0], 4 * b.shape[1]), b.dtype),
            jax.ShapeDtypeStruct((devices,) + ids.shape, ids.dtype),
        ),
        in_specs=[ANY] * 3,
        out_specs=(ANY,) * 3,
        scratch_shapes=[pltpu.SemaphoreType.DMA((3,))] + [dma] * 8 + [hop] * 4,
        compiler_params=pltpu.CompilerParams(collective_id=ident, has_side_effects=True),
        name="first_gather",
    )(a, b, ids)


def attention_kernel(groups, size, x_ref, w_ref, gain_ref, gq_ref, gk_ref, cos_ref, sin_ref, qs_ref, ks_ref,
                     q_ref, qhat_ref, qinv_ref, khat_ref, kinv_ref, heads_ref, log_ref, kv_out, all_out,
                     kv, whole, store_kv, store_all, ss1, rs1, ss2, rs2, *sems):
    head = q_ref.shape[1]
    length = kv.shape[1]
    id_rows = size // 128
    blocks = length // (2 * size)
    group = Shared(False)
    rank = group.me
    line = LineGather(whole, size, head, sems[:4])
    z = line.z
    tile = min(256, size)
    group.greet(z)

    def block(g, half, k, own):
        c = rank if own else group.other(-k)
        return kv.at[g], half * (length // 2) + c * size, size

    keys = KeyGather(block, group.chips, sems[4:])

    def place(g, half, c):
        return kv.at[g, pl.ds(pl.multiple_of(half * (length // 2) + c * size, size), size)]

    def direct(g, half, k, incoming=False):
        at = keys.quarter(g, half, k, z, own=not incoming)
        return group.copy(at, at, ss1.at[g, half, k], rs1.at[g, half, k], group.other(k))

    def inner(g, half, k, incoming=False):
        block = group.other(-k)
        at = place(g, half, block + 1 - 2 * group.core if incoming else block)
        return group.copy(at, at, ss2.at[g, half, k], rs2.at[g, half, k], group.partner())

    def project(g, half, u):
        rows = pl.ds((2 * g + half) * size + u * tile, tile)
        spot = pl.ds(half * size + u * tile, tile)
        cosine, sine = cos_ref[spot, :], sin_ref[spot, :]
        hat, _ = norm_parts(x_ref[rows, :].astype(F32))
        raw = dot((hat * (1.0 + gain_ref[0:1, :])).astype(BF16), w_ref[...])
        hat, inv = norm_parts(raw[:, :head])
        qhat_ref[rows, :] = hat
        qinv_ref[rows, :] = inv
        q_ref[rows, :] = rotate(hat * (1.0 + gq_ref[...]), cosine, sine).astype(BF16)
        hat, inv = norm_parts(raw[:, head : 2 * head])
        khat_ref[rows, :] = hat
        kinv_ref[rows, :] = inv
        at = pl.ds(pl.multiple_of(half * (length // 2) + rank * size + u * tile, tile), tile)
        kv[g, at, :head] = rotate(hat * (1.0 + gk_ref[...]), cosine, sine).astype(BF16)
        kv[g, at, head:] = raw[:, 2 * head :].astype(BF16)

    def attend(g, half):
        row = lax.broadcasted_iota(jnp.int32, (size, size), 0)
        col = lax.broadcasted_iota(jnp.int32, (size, size), 1)
        rows = pl.ds((2 * g + half) * size, size)
        q = q_ref[rows, :] * jnp.asarray(SCALE, BF16)
        qseg = qs_ref[g, half]

        def part(block):
            at = pl.ds(pl.multiple_of(block * size, size), size)
            device = lax.axis_index("dp") * lax.axis_size("ctx") + lax.rem(block, blocks)
            ids = ks_ref[device, pl.ds((2 * g + lax.div(block, blocks)) * id_rows, id_rows), :]
            ids = jnp.concatenate([ids[j : j + 1] for j in range(id_rows)], axis=1)
            same = qseg == jnp.where(ids == 0, -1, ids)
            return dot(q, kv[g, at, :head], NT), kv[g, at, head:], same

        s, v, same = part(rank + half * blocks)
        order = (col <= row) if half == 0 else (col >= row)
        s = jnp.where((same & order) | (col == row), s, NEGATIVE)
        top = jnp.max(s, axis=1, keepdims=True)
        p = jnp.exp(s - top)
        mass = jnp.sum(p, axis=1, keepdims=True)
        acc = dot(p.astype(BF16), v)

        def step(t, carry):
            top, mass, acc = carry
            s, v, same = part(block_starts(half, t, blocks, rank))
            s = jnp.where(same, s, NEGATIVE)
            new = jnp.maximum(top, jnp.max(s, axis=1, keepdims=True))
            keep = jnp.exp(top - new)
            p = jnp.exp(s - new)
            mass = mass * keep + jnp.sum(p, axis=1, keepdims=True)
            return new, mass, acc * keep + dot(p.astype(BF16), v)

        count = rank if half == 0 else 2 * blocks - 1 - rank
        top, mass, acc = lax.fori_loop(0, count, step, (top, mass, acc))
        out = (acc / mass).astype(BF16)
        heads_ref[rows, :] = out
        whole[rows, pl.ds(pl.multiple_of(z * head, head), head)] = out
        log_ref[g, half] = top + jnp.log(mass)

    chips = range(1, group.chips)
    tiles = 2 * groups

    def exchange(t):
        for stage in (4, 3, 2, 1):
            if not 0 <= t - stage < tiles:
                continue
            g, half = divmod(t - stage, 2)
            for k in chips:
                spot = keys.tile_of(g, half, k)
                if stage == 1:
                    direct(g, half, k, True).wait_recv()
                if stage <= 3:
                    keys.forward(spot, stage - 1)
                else:
                    keys.arrived(spot)
                    inner(g, half, k).start()

    def hops(t):
        for hop in range(3):
            if 0 <= t - hop < tiles:
                line.forward(t - hop, hop)

    def keep(t):
        at = pl.ds(t * size, size)
        return pltpu.make_async_copy(whole.at[at], all_out.at[at], store_all.at[t])

    def save(g):
        return pltpu.make_async_copy(kv.at[g], kv_out.at[g], store_kv.at[g])

    for t in range(tiles):
        g, half = divmod(t, 2)
        for u in range(size // tile):
            project(g, half, u)
        for k in chips:
            direct(g, half, k).start()
        inner(g, half, 0).start()
        exchange(t)
    at_step = tiles
    for g in range(groups):
        while at_step < min(2 * g + 6, tiles + 4):
            exchange(at_step)
            at_step += 1
        for half in range(2):
            for k in range(group.chips):
                inner(g, half, k, True).wait_recv()
        save(g).start()
        for half in range(2):
            attend(g, half)
            if at_step < tiles + 4:
                exchange(at_step)
                at_step += 1
            hops(2 * g + half)
    for t in range(tiles, tiles + 2):
        hops(t)
    for t in range(tiles):
        line.arrived(t)
        keep(t).start()
    for g in range(groups):
        save(g).wait()
        for half in range(2):
            for k in chips:
                direct(g, half, k).wait_send()
            for k in range(group.chips):
                inner(g, half, k).wait_send()
    line.finish(tiles)
    keys.finish(tiles * (group.chips - 1))
    for t in range(tiles):
        keep(t).wait()


def attention(x, w, gains, gain_query, gain_key, cosine, sine, qseg, ids, length, ident):
    rows, width = x.shape
    groups, _, size, _ = qseg.shape
    head = gain_query.shape[1]
    chips = length // (4 * size)
    tiles = 2 * groups
    vmem = pl.BlockSpec(memory_space=pltpu.VMEM)
    dma = pltpu.SemaphoreType.DMA
    return pl.pallas_call(
        functools.partial(attention_kernel, groups, size),
        out_shape=(
            jax.ShapeDtypeStruct((rows, head), BF16),
            jax.ShapeDtypeStruct((rows, head), F32),
            jax.ShapeDtypeStruct((rows, 1), F32),
            jax.ShapeDtypeStruct((rows, head), F32),
            jax.ShapeDtypeStruct((rows, 1), F32),
            jax.ShapeDtypeStruct((rows, head), BF16),
            jax.ShapeDtypeStruct((groups, 2, size, 1), F32),
            jax.ShapeDtypeStruct((groups, length, 2 * head), BF16),
            jax.ShapeDtypeStruct((rows, 4 * head), BF16),
        ),
        in_specs=[vmem] * 9,
        out_specs=(vmem,) * 7 + (ANY, ANY),
        scratch_shapes=[
            pltpu.VMEM((groups, length, 2 * head), BF16), pltpu.VMEM((rows, 4 * head), BF16),
            dma((groups,)), dma((tiles,))] + [dma((groups, 2, chips))] * 4 + [dma((3, tiles))] * 4
        + [dma((3, tiles * (chips - 1)))] * 4,
        compiler_params=pltpu.CompilerParams(
            collective_id=ident, has_side_effects=True, vmem_limit_bytes=60 * 2**20),
        name="attention",
    )(x, w, gains, gain_query, gain_key, cosine, sine, qseg, ids)


class ResidentSum(LineSum):
    def outwards(self, c):
        return pltpu.make_async_remote_copy(
            self.out.at[self.rows(c)], self.out.at[self.rows(c)], self.sems[4].at[c], self.sems[5].at[c],
            device_id={"tp": self.my_leaf}, device_id_type=MESH)

    def total(self, c):
        @pl.when(self.hub)
        def _():
            self.across(c).wait_recv()
            at = self.rows(c)
            self.out[at, :] = (self.own[at, :].astype(F32) + self.far[at, :].astype(F32)).astype(BF16)
            self.outwards(c).start()

    def arrived(self, c):
        @pl.when(self.leaf)
        def _():
            self.outwards(c).wait_recv()

    def finish(self):
        @pl.when(self.leaf)
        def _():
            for c in range(self.count):
                self.inwards(c).wait_send()

        @pl.when(self.hub)
        def _():
            for c in range(self.count):
                self.across(c).wait_send()
                self.outwards(c).wait_send()


def query_back_kernel(tiles, tile, dq_ref, hat_ref, inv_ref, cos_ref, sin_ref, x_ref, gain_ref, gq_ref, wq_ref,
                      one_ref, grad_ref, dgain_ref, acc, whole, *sems):
    i = pl.program_id(0)
    head = hat_ref.shape[1]
    line = LineGather(whole, tile, head, sems)

    @pl.when(i == 0)
    def _():
        barrier_line(line.z)
        acc[...] = jnp.zeros_like(acc)
        dgain_ref[...] = jnp.zeros_like(dgain_ref)

    @pl.when(i < tiles)
    def _():
        d_rot = rotate(dq_ref[...], cos_ref[...], -sin_ref[...])
        d_raw, d_gain = norm_back(d_rot, hat_ref[...], inv_ref[...], gq_ref[...])
        d_raw = d_raw.astype(BF16)
        at = pl.ds(pl.multiple_of(line.z * head, head), head)
        whole[pl.ds(pl.multiple_of(i * tile, tile), tile), at] = d_raw
        line.forward(i, 0)
        dgain_ref[...] += d_gain[None]
        hat, _ = norm_parts(x_ref[...].astype(F32))
        one = (hat * (1.0 + gain_ref[0:1, :])).astype(BF16)
        acc[...] += dot(one, d_raw, TN)

    @pl.when((i >= 1) & (i <= tiles))
    def _():
        line.forward(i - 1, 1)

    @pl.when((i >= 2) & (i <= tiles + 1))
    def _():
        line.forward(i - 2, 2)

    @pl.when(i >= 3)
    def _():
        line.arrived(i - 3)
        one_ref[...] = dot(whole[pl.ds(pl.multiple_of((i - 3) * tile, tile), tile), :], wq_ref[...], NT)

    @pl.when(i == tiles + 2)
    def _():
        grad_ref[...] = acc[...].astype(BF16)
        line.finish(tiles)


def query_back(dq, hat, inv, cosine, sine, x, gains, gain_query, weights, ident):
    rows, width = x.shape
    head = hat.shape[1]
    tile = 256
    tiles = rows // tile
    dma = pltpu.SemaphoreType.DMA((3, tiles))

    def early(cols):
        return pl.BlockSpec((tile, cols), lambda i: (jnp.minimum(i, tiles - 1), 0))

    return pl.pallas_call(
        functools.partial(query_back_kernel, tiles, tile),
        grid=(tiles + 3,),
        out_shape=(
            jax.ShapeDtypeStruct((rows, width), F32),
            jax.ShapeDtypeStruct((width, head), BF16),
            jax.ShapeDtypeStruct((1, head), F32),
        ),
        in_specs=[early(head), early(head), early(1), early(head // 2), early(head // 2), early(width),
                  whole_block(gains.shape), whole_block(gain_query.shape), whole_block(weights.shape)],
        out_specs=(
            pl.BlockSpec((tile, width), lambda i: (jnp.maximum(i - 3, 0), 0)),
            pl.BlockSpec((width, head), lambda i: (0, 0)),
            pl.BlockSpec((1, head), lambda i: (0, 0)),
        ),
        scratch_shapes=[
            pltpu.VMEM((width, head), F32), pltpu.VMEM((rows, 4 * head), BF16)] + [dma] * 4,
        compiler_params=pltpu.CompilerParams(
            collective_id=ident, has_side_effects=True, vmem_limit_bytes=48 * 2**20),
        name="query_back",
    )(dq, hat, inv, cosine, sine, x, gains, gain_query, weights)


def key_back_kernel(tiles, tile, chunk, own_rows, dkv_ref, hat_ref, inv_ref, cos_ref, sin_ref, x_ref, dm_ref, part_ref,
                    gain_ref, gk_ref, w_ref, dgq_ref, dg_mid_ref, dg_post_ref, grad_q_ref, grad_o_ref,
                    dx_ref, last_ref, acc, acc_in, acc_key, w_kv, w_sem, out, own, near, far, *sems):
    i = pl.program_id(0)
    head = hat_ref.shape[1]
    per = tile // chunk
    count = tiles * per + 1
    line = ResidentSum(count, chunk, count, own, near, far, out, sems)

    @pl.when(i == 0)
    def _():
        copy = pltpu.make_async_copy(w_ref.at[:, pl.ds(head, 2 * head)], w_kv, w_sem)
        copy.start()
        barrier_line(line.z)
        for ref in (acc, acc_in, acc_key):
            ref[...] = jnp.zeros_like(ref)
        copy.wait()
        line.put(count - 1, jnp.broadcast_to(
            jnp.concatenate([dgq_ref[...], dgq_ref[...]], axis=1).astype(BF16), (chunk, 2 * head)))

    @pl.when(i < tiles)
    def _():
        for j in range(per):
            line.put(i * per + j, dkv_ref[j * chunk : (j + 1) * chunk, :])

    @pl.when((i >= 1) & (i <= tiles))
    def _():
        for j in range(per):
            line.pair((i - 1) * per + j)

    @pl.when((i >= 2) & (i <= tiles + 1))
    def _():
        for j in range(per):
            line.total((i - 2) * per + j)

    @pl.when(i == 1)
    def _():
        line.pair(count - 1)

    @pl.when(i == 2)
    def _():
        line.total(count - 1)

    @pl.when(i >= 3)
    def _():
        for j in range(per):
            line.arrived((i - 3) * per + j)
        d_kv = out[pl.ds(pl.multiple_of((i - 3) * tile, tile), tile), :]
        d_rot = rotate(d_kv[:, :head].astype(F32), cos_ref[...], -sin_ref[...])
        d_raw, d_gain = norm_back(d_rot, hat_ref[...], inv_ref[...], gk_ref[...])
        acc_key[...] += d_gain[None]
        d_raw = jnp.concatenate([d_raw.astype(BF16), d_kv[:, head:]], axis=1)
        d_one = part_ref[...] + dot(d_raw, w_kv[...], NT)
        hat, inv = norm_parts(x_ref[...].astype(F32))
        gain = gain_ref[0:1, :]
        d_part, d_gain = norm_back(d_one, hat, inv, gain)
        acc_in[...] += d_gain[None]
        dx_ref[...] = dm_ref[...] + d_part
        acc[...] += dot((hat * (1.0 + gain)).astype(BF16), d_raw, TN)

    @pl.when(i == tiles + 2)
    def _():
        line.arrived(count - 1)
        width = x_ref.shape[1]
        short = head * own_rows // width
        last_ref[:, :head] = grad_q_ref[...]
        last_ref[:, head : 3 * head] = acc[...].astype(BF16)
        last_ref[:, 3 * head : 4 * head] = grad_o_ref[...]
        d_query = out[pl.ds((count - 1) * chunk, 16), :head][0:1].astype(F32)
        pair = jnp.concatenate([d_query, acc_key[...], jnp.zeros((14, head), F32)], axis=0).astype(BF16)
        col = lax.broadcasted_iota(jnp.int32, (head, width), 1)
        row = lax.broadcasted_iota(jnp.int32, (head, width), 0)
        shift = short.bit_length() - 1
        spot = lax.shift_right_logical(row, shift) * own_rows + (row & (short - 1))
        spread = dot(pair, jnp.where(col == spot, 1.0, 0.0).astype(BF16))
        gains = jnp.concatenate(
            [acc_in[...], dg_mid_ref[...], dg_post_ref[...], spread[0:2], jnp.zeros((122, width), F32)], axis=0)
        last_ref[:, 4 * head :] = jnp.transpose(gains).astype(BF16)
        line.finish()


def key_back(d_kv, hat, inv, cosine, sine, x, d_middle, part, gains, gain_key, first, dg_query, dg_mid, dg_post,
             grad_q, grad_o, own_rows, ident):
    rows, width = x.shape
    head = hat.shape[1]
    tile, chunk = 256, 128
    tiles = rows // tile
    count = rows // chunk + 1
    dma = pltpu.SemaphoreType.DMA((count,))

    def late(cols):
        return pl.BlockSpec((tile, cols), lambda i: (jnp.maximum(i - 3, 0), 0))

    comm = pltpu.VMEM((count * chunk, 2 * head), BF16)
    return pl.pallas_call(
        functools.partial(key_back_kernel, tiles, tile, chunk, own_rows),
        grid=(tiles + 3,),
        out_shape=(
            jax.ShapeDtypeStruct((rows, width), F32),
            jax.ShapeDtypeStruct((width, 4 * head + 128), BF16),
        ),
        in_specs=[pl.BlockSpec((tile, 2 * head), lambda i: (jnp.minimum(i, tiles - 1), 0)),
                  late(head), late(1), late(head // 2), late(head // 2), late(width), late(width), late(width),
                  whole_block(gains.shape), whole_block(gain_key.shape), ANY]
        + [whole_block(a.shape) for a in (dg_query, dg_mid, dg_post, grad_q, grad_o)],
        out_specs=(late(width), pl.BlockSpec((width, 4 * head + 128), lambda i: (0, 0))),
        scratch_shapes=[
            pltpu.VMEM((width, 2 * head), F32), pltpu.VMEM((1, width), F32), pltpu.VMEM((1, head), F32),
            pltpu.VMEM((width, 2 * head), BF16), pltpu.SemaphoreType.DMA] + [comm] * 4 + [dma] * 7
        + [pltpu.SemaphoreType.REGULAR] * 2,
        compiler_params=pltpu.CompilerParams(
            collective_id=ident, has_side_effects=True, vmem_limit_bytes=56 * 2**20),
        name="key_back",
    )(d_kv, hat, inv, cosine, sine, x, d_middle, part, gains, gain_key, first, dg_query, dg_mid, dg_post, grad_q, grad_o)


def scatter_kernel(chips, own_rows, x_ref, o_ref, near, pair, far, *sems):
    ss1, rs1, ss2, rs2 = sems
    ctx = lax.axis_size("ctx")
    me = lax.axis_index("dp") * ctx + lax.axis_index("ctx")
    core = lax.rem(me, 2)
    chip = lax.div(me, 2)
    bar = pltpu.get_barrier_semaphore()

    def device(d):
        return {"dp": lax.div(d, ctx), "ctx": lax.rem(d, ctx)}

    partner = device(2 * chip + 1 - core)
    pl.semaphore_signal(bar, inc=1, device_id=partner, device_id_type=MESH)
    for k in range(1, chips):
        other = lax.rem(chip + k, chips)
        pl.semaphore_signal(bar, inc=1, device_id=device(2 * other + core), device_id_type=MESH)
    pl.semaphore_wait(bar, chips)

    def block(d):
        return pl.ds(pl.multiple_of(d * own_rows, 16), own_rows)

    def within(k):
        q = lax.rem(chip + k, chips)
        return pltpu.make_async_remote_copy(
            x_ref.at[block(2 * q + 1 - core)], near.at[k], ss1.at[k], rs1.at[k], device_id=partner, device_id_type=MESH)

    def between(k):
        q = lax.rem(chip + k, chips)
        return pltpu.make_async_remote_copy(
            pair.at[k], far.at[k], ss2.at[k], rs2.at[k], device_id=device(2 * q + core), device_id_type=MESH)

    order = list(range(1, chips)) + [0]
    for k in order:
        within(k).start()
    for k in order:
        within(k).wait_recv()
        q = lax.rem(chip + k, chips)
        both = x_ref[block(2 * q + core), :].astype(F32) + near[k].astype(F32)
        if k > 0:
            pair[k] = both.astype(BF16)
            between(k).start()
        else:
            o_ref[...] = both
    for k in range(1, chips):
        between(k).wait_recv()
        o_ref[...] += far[k].astype(F32)
    for k in range(1, chips):
        between(k).wait_send()
    for k in order:
        within(k).wait_send()


def scatter(x, own_rows, ident):
    n = x.shape[0] // own_rows
    chips = n // 2
    cols = x.shape[1]
    buf = pltpu.VMEM((chips, own_rows, cols), BF16)
    vmem = pl.BlockSpec(memory_space=pltpu.VMEM)
    return pl.pallas_call(
        functools.partial(scatter_kernel, chips, own_rows),
        out_shape=jax.ShapeDtypeStruct((own_rows, cols), F32),
        in_specs=[vmem],
        out_specs=vmem,
        scratch_shapes=[buf] * 3 + [pltpu.SemaphoreType.DMA((chips,))] * 4,
        compiler_params=pltpu.CompilerParams(
            collective_id=ident, has_side_effects=True, vmem_limit_bytes=40 * 2**20),
        name="scatter",
    )(x)


def shards(tokens, segments, cotangent, w_query, w_key, w_value, w_out, w_gate, w_up, w_down,
           g_input, g_post_attn, g_pre_ffn, g_post_ffn, g_query, g_key):
    batches, seq_local, _, size, width = tokens.shape
    head = w_key.shape[1]
    groups = batches * seq_local
    per_group = 2 * size
    rows = groups * per_group
    ctx = lax.axis_size("ctx")
    length = per_group * ctx
    rank = lax.axis_index("ctx")
    shared = ("dp", "ctx")
    own_rows = g_input.shape[0]
    hidden = w_gate.shape[1]

    def column(gain):
        return jnp.pad(gain, (0, own_rows - gain.shape[0]))[:, None]

    own_ids = segments.reshape(groups, 2, size)
    id_rows = own_ids.size // 128
    ids = jnp.pad(own_ids.reshape(id_rows, 128), ((0, -id_rows % 16), (0, 0)))
    extra = jnp.concatenate(
        [column(g) for g in (g_input, g_post_attn, g_pre_ffn, g_post_ffn, g_query, g_key)], axis=1)
    extra = jnp.pad(extra, ((0, 0), (0, 128 - extra.shape[1])))

    def rows_of_16(w):
        return jnp.pad(w, ((0, -own_rows % 16), (0, 0)))

    first, line, ids = first_gather(
        rows_of_16(jnp.concatenate([w_query, w_key, w_value, extra], axis=1)),
        rows_of_16(jnp.concatenate([w_query, w_out.T], axis=1)), ids, width // own_rows, 5)
    first = first[:, :own_rows].reshape(width, -1)
    line = line[:own_rows].reshape(own_rows, 4, 2, head).transpose(2, 0, 1, 3).reshape(2, own_rows, 4 * head)
    mat_qkv = first[:, : 3 * head]
    side = first[:, 3 * head :]
    gain_cols = side[:, :8].astype(F32)
    gain_rows = gain_cols.T
    gain_input = gain_rows[0]
    short = g_query.shape[0]
    gain_query, gain_key = (
        gain_cols[:, i].reshape(-1, own_rows)[:, :short].reshape(-1) for i in (4, 5))
    key_ids = lax.dynamic_index_in_dim(ids.reshape((-1, ctx) + ids.shape[1:]), lax.axis_index("dp"), 0, keepdims=False)
    key_ids = key_ids[:, :id_rows].reshape(ctx, groups, 2, size).transpose(1, 2, 0, 3).reshape(groups, length)
    key_ids = jnp.where(key_ids == 0, -1, key_ids)

    wide = wide_of(hidden)
    second = jnp.concatenate(
        [line[1]] + [jnp.pad(w, ((0, 0), (0, wide - hidden))) for w in (w_gate, w_up, w_down.T)], axis=1)
    weights = lax.all_gather(second, shared, axis=0, tiled=True)

    offsets = rank * size + jnp.arange(size, dtype=jnp.int32)
    position = jnp.concatenate([offsets, length - 1 - offsets]).astype(F32)
    cosine, sine = angles(position, head // 2, head)
    turn = (cosine, sine)
    cosine = jnp.broadcast_to(cosine, (groups, per_group, head // 2)).reshape(rows, head // 2)
    sine = jnp.broadcast_to(sine, (groups, per_group, head // 2)).reshape(rows, head // 2)

    x_rows = tokens.reshape(rows, width)
    dy_rows = cotangent.reshape(rows, width)
    queries, q_hat, q_scale, k_hat, k_scale, heads_own, log_mass, kv, heads_all = attention(
        x_rows, mat_qkv, gain_rows, gain_query[None], gain_key[None], *turn, own_ids[..., None], ids, length, 0)

    line, heads_all = lax.optimization_barrier((line[0], heads_all))
    query_full = lax.all_gather(line, shared, axis=0, tiled=True)
    attn, hidden_two, gate, up, ffn_out = ffn_forward(x_rows, heads_all, gain_rows, weights, hidden, 1)
    output, d_gain_post_ffn, grad_ffn, d_two = ffn_backward(
        x_rows, attn, dy_rows, ffn_out, hidden_two, gate, up, gain_rows, weights, 2)
    grad_ffn = lax.psum_scatter(grad_ffn, shared, scatter_dimension=1, tiled=True).astype(F32)
    d_middle, d_heads, delta, d_gain_mid, grad_out_t = middle_back(
        x_rows, attn, dy_rows, d_two, heads_own, gain_rows, weights)

    d_query, d_kv = attend_back(
        queries.reshape(groups, 2, size, head), kv, d_heads.reshape(groups, 2, size, head),
        log_mass.reshape(groups, 2, 1, size), delta.reshape(groups, 2, 1, size),
        own_ids[:, :, None, :], key_ids[:, None, :])
    d_kv = lax.psum_scatter(
        d_kv.reshape(groups, 2, length // 2, 2 * head), "ctx", scatter_dimension=2, tiled=True)
    d_one, grad_q, d_gain_query = query_back(
        d_query.reshape(rows, head), q_hat, q_scale, cosine, sine, x_rows, gain_rows, gain_query[None], query_full, 4)
    d_kv, d_one = lax.optimization_barrier((d_kv, d_one))
    d_tokens, last = key_back(
        d_kv.reshape(rows, 2 * head), k_hat, k_scale, cosine, sine, x_rows, d_middle, d_one, gain_rows, gain_key[None],
        first, d_gain_query, d_gain_mid, d_gain_post_ffn, grad_q, grad_out_t, own_rows, 3)
    if own_rows % 16 == 0:
        last = scatter(last, own_rows, 7)
    else:
        last = lax.psum_scatter(last, shared, scatter_dimension=0, tiled=True).astype(F32)
    g = last[:, 4 * head :]
    return (
        output.reshape(tokens.shape),
        d_tokens.reshape(tokens.shape),
        last[:, :head],
        last[:, head : 2 * head],
        last[:, 2 * head : 3 * head],
        last[:, 3 * head : 4 * head].T,
        grad_ffn[0],
        grad_ffn[1],
        grad_ffn[2].T,
        g[:, 0],
        g[:, 1],
        g[:, 2],
        g[:, 3],
        g[:short, 4],
        g[:short, 5],
    )


def solution(mesh):
    shared = ("dp", "ctx")
    rows = P(None, "dp", None, "ctx", None)
    weights = (
        P(shared, "tp"), P(shared, None), P(shared, None), P("tp", shared),
        P(shared, "tp"), P(shared, "tp"), P("tp", shared),
    )
    gains = (P(shared),) * 6
    return jax.shard_map(
        shards,
        mesh=mesh,
        in_specs=(rows, P(None, "dp", None, "ctx"), rows) + weights + gains,
        out_specs=(rows, rows) + weights + gains,
        check_vma=False,
    )
```

```python
import functools

import jax
import jax.numpy as jnp
from jax import lax
from jax.experimental import pallas as pl
from jax.experimental.pallas import tpu as pltpu
from jax.sharding import PartitionSpec as P

EPS = 1e-06
THETA = 1000000.0
SCALE = 0.0625
NEGATIVE = -1e30
BF16 = jnp.bfloat16
F32 = jnp.float32
MESH = pl.DeviceIdType.MESH
NN = (((1,), (0,)), ((), ()))
NT = (((1,), (1,)), ((), ()))
TN = (((0,), (0,)), ((), ()))


def dot(a, b, dims=NN):
    return lax.dot_general(a, b, dims, preferred_element_type=F32)


def barrier_line(z):
    bar = pltpu.get_barrier_semaphore()

    @pl.when(z > 0)
    def _():
        pl.semaphore_signal(bar, inc=1, device_id={"tp": z - 1}, device_id_type=MESH)

    @pl.when(z < 3)
    def _():
        pl.semaphore_signal(bar, inc=1, device_id={"tp": z + 1}, device_id_type=MESH)

    pl.semaphore_wait(bar, jnp.where((z == 0) | (z == 3), 1, 2))


def block_starts(half, t, blocks, rank):
    if half == 0:
        return t
    return jnp.where(t < blocks, t, t + rank + 1)


def angles(position, half_size, full_size):
    frequency = THETA ** (-2.0 * jnp.arange(half_size, dtype=F32) / full_size)
    turned = position[:, None] * frequency[None, :]
    return (jnp.cos(turned), jnp.sin(turned))


def rotate(tensor, cosine, sine):
    half_size = tensor.shape[-1] // 2
    a = tensor[..., :half_size]
    b = tensor[..., half_size:]
    return jnp.concatenate([a * cosine - b * sine, b * cosine + a * sine], axis=-1)


def norm_parts(values):
    inv = lax.rsqrt(jnp.mean(values * values, axis=-1, keepdims=True) + EPS)
    return (values * inv, inv)


def norm_back(upstream, normalized, inv, gain):
    d_norm = upstream * (1.0 + gain)
    d_values = inv * (d_norm - normalized * jnp.mean(d_norm * normalized, axis=-1, keepdims=True))
    return (d_values, jnp.sum(upstream * normalized, axis=0))


def gelu_tanh(values):
    return jax.nn.gelu(values, approximate=True)


class LineSum:
    def __init__(self, count, chunk, slots, own, near, far, out, sems):
        self.count, self.chunk, self.slots = count, chunk, slots
        self.own, self.near, self.far, self.out = own, near, far, out
        self.sems = sems
        self.z = z = lax.axis_index("tp")
        self.hub = (z == 1) | (z == 2)
        self.leaf = (z == 0) | (z == 3)
        self.other_hub = jnp.where(z == 1, 2, 1)
        self.my_hub = jnp.where(z == 0, 1, 2)
        self.my_leaf = jnp.where(z == 1, 0, 3)

    def slot(self, c):
        return pl.ds(pl.multiple_of(lax.rem(c, self.slots) * self.chunk, self.chunk), self.chunk)

    def rows(self, c):
        return pl.ds(pl.multiple_of(c * self.chunk, self.chunk), self.chunk)

    def inwards(self, c):
        return pltpu.make_async_remote_copy(
            self.own.at[self.slot(c)], self.near.at[self.slot(c)], self.sems[0].at[c], self.sems[1].at[c],
            device_id={"tp": self.my_hub}, device_id_type=MESH)

    def across(self, c):
        return pltpu.make_async_remote_copy(
            self.own.at[self.slot(c)], self.far.at[self.slot(c)], self.sems[2].at[c], self.sems[3].at[c],
            device_id={"tp": self.other_hub}, device_id_type=MESH)

    def outwards(self, c):
        return pltpu.make_async_remote_copy(
            self.far.at[self.slot(c)], self.out.at[self.rows(c)], self.sems[4].at[c], self.sems[5].at[c],
            device_id={"tp": self.my_leaf}, device_id_type=MESH)

    def store(self, c):
        return pltpu.make_async_copy(self.far.at[self.slot(c)], self.out.at[self.rows(c)], self.sems[6].at[c])

    def put(self, c, value):
        ring = self.slots < self.count
        if ring:
            @pl.when(c >= self.slots)
            def _():
                @pl.when(self.leaf)
                def _():
                    self.inwards(c - self.slots).wait_send()

                @pl.when(self.hub)
                def _():
                    self.across(c - self.slots).wait_send()

        self.own[self.slot(c), :] = value

        @pl.when(self.leaf)
        def _():
            if ring:
                @pl.when(c >= self.slots)
                def _():
                    pl.semaphore_wait(self.sems[7], 1)
            self.inwards(c).start()

    def pair(self, c):
        ring = self.slots < self.count

        @pl.when(self.hub)
        def _():
            self.inwards(c).wait_recv()
            at = self.slot(c)
            self.own[at, :] = (self.own[at, :].astype(F32) + self.near[at, :].astype(F32)).astype(BF16)
            if ring:
                @pl.when(c < self.count - self.slots)
                def _():
                    pl.semaphore_signal(self.sems[7], inc=1, device_id={"tp": self.my_leaf}, device_id_type=MESH)

                @pl.when(c >= self.slots)
                def _():
                    pl.semaphore_wait(self.sems[8], 1)
            self.across(c).start()

    def total(self, c):
        @pl.when(self.hub)
        def _():
            self.across(c).wait_recv()
            at = self.slot(c)
            self.far[at, :] = (self.own[at, :].astype(F32) + self.far[at, :].astype(F32)).astype(BF16)
            self.outwards(c).start()
            self.store(c).start()

    def retire(self, c):
        @pl.when(self.hub)
        def _():
            self.outwards(c).wait_send()
            self.store(c).wait()
            if self.slots < self.count:
                @pl.when(c < self.count - self.slots)
                def _():
                    pl.semaphore_signal(self.sems[8], inc=1, device_id={"tp": self.other_hub}, device_id_type=MESH)

    def finish(self):
        first = max(0, self.count - self.slots)

        @pl.when(self.leaf)
        def _():
            for c in range(self.count):
                self.outwards(c).wait_recv()
            for c in range(first, self.count):
                self.inwards(c).wait_send()

        @pl.when(self.hub)
        def _():
            for c in range(first, self.count):
                self.across(c).wait_send()


def line_sum_scratch(count, chunk, slots, cols):
    dma = pltpu.SemaphoreType.DMA((count,))
    regular = pltpu.SemaphoreType.REGULAR
    return [pltpu.VMEM((slots * chunk, cols), BF16)] * 3 + [dma] * 7 + [regular] * 2


def gelu_parts(v):
    c = 0.7978845608028654
    square = v * v
    t = jnp.tanh(v * (c + (c * 0.044715) * square))
    half = 0.5 + 0.5 * t
    value = v * half
    slope = half + (0.5 * v) * (1.0 - t * t) * (c + (3.0 * c * 0.044715) * square)
    return value, slope


def column_parts(cols):
    middle = -(-cols // 256) * 128
    return [(0, middle), (middle, cols)] if middle < cols else [(0, cols)]


def middle_of(x, attn, gain_post_attn):
    hat, inv = norm_parts(attn.astype(F32))
    return x.astype(F32) + hat * (1.0 + gain_post_attn), hat, inv


def load_ffn_weights(weights, refs, sem):
    wide = refs[0].shape[1]
    base = weights.shape[1] - 3 * wide
    return [
        pltpu.make_async_copy(weights.at[:, pl.ds(base + j * wide, wide)], ref, sem.at[j])
        for j, ref in enumerate(refs)
    ]


def ffn_forward_kernel(tiles, tile, chunk, hidden, x_ref, h_ref, gain_ref, w_ref,
                       attn_ref, two_ref, gate_ref, up_ref, out_ref, wo_ref, wg_ref, wu_ref, wd_ref, w_sem, own, near, far, *sems):
    i = pl.program_id(0)
    per = tile // chunk
    line = LineSum(tiles * per, chunk, tiles * per, own, near, far, out_ref, sems)
    head = wo_ref.shape[1] // 4

    @pl.when(i == 0)
    def _():
        copies = load_ffn_weights(w_ref, (wg_ref, wu_ref, wd_ref), w_sem)
        copies.append(pltpu.make_async_copy(w_ref.at[:, pl.ds(0, 4 * head)], wo_ref, w_sem.at[3]))
        for copy in copies:
            copy.start()
        barrier_line(line.z)
        for copy in copies:
            copy.wait()

    attn = dot(h_ref[...], wo_ref[...], NT).astype(BF16)
    attn_ref[...] = attn
    middle, _, _ = middle_of(x_ref[...], attn, gain_ref[1:2, :])
    hat, _ = norm_parts(middle)
    two = (hat * (1.0 + gain_ref[2:3, :])).astype(BF16)
    two_ref[...] = two
    part = None
    for a, b in column_parts(hidden):
        gate = dot(two, wg_ref[:, a:b])
        up = dot(two, wu_ref[:, a:b])
        gate_ref[:, a:b] = gate.astype(BF16)
        up_ref[:, a:b] = up.astype(BF16)
        value, _ = gelu_parts(gate)
        more = dot((value * up).astype(BF16), wd_ref[:, a:b], NT)
        part = more if part is None else part + more
    for j in range(per):
        line.put(i * per + j, part[j * chunk : (j + 1) * chunk].astype(BF16))

    @pl.when(i >= 1)
    def _():
        for j in range(per):
            line.pair((i - 1) * per + j)

    @pl.when(i >= 2)
    def _():
        for j in range(per):
            line.total((i - 2) * per + j)

    @pl.when(i == tiles - 1)
    def _():
        last = tiles * per
        for j in range(per):
            line.pair(last - per + j)
        for c in range(max(0, last - 2 * per), last):
            line.total(c)
        for c in range(last):
            line.retire(c)
        line.finish()


def whole_block(shape):
    return pl.BlockSpec(shape, lambda i: (0,) * len(shape), pipeline_mode=pl.Buffered(1))


def tile_block(tile, cols):
    return pl.BlockSpec((tile, cols), lambda i: (i, 0))


ANY = pl.BlockSpec(memory_space=pl.ANY)


def wide_of(hidden):
    return -(-hidden // 128) * 128


def ffn_forward(x, heads, gains, weights, hidden, ident):
    rows, width = x.shape
    all_heads = heads.shape[1]
    tile, chunk = 256, 128
    tiles = rows // tile
    count = rows // chunk
    wide = wide_of(hidden)
    return pl.pallas_call(
        functools.partial(ffn_forward_kernel, tiles, tile, chunk, hidden),
        grid=(tiles,),
        out_shape=(
            jax.ShapeDtypeStruct((rows, width), BF16),
            jax.ShapeDtypeStruct((rows, width), BF16),
            jax.ShapeDtypeStruct((rows, hidden), BF16),
            jax.ShapeDtypeStruct((rows, hidden), BF16),
            jax.ShapeDtypeStruct((rows, width), BF16),
        ),
        in_specs=[
            tile_block(tile, width),
            tile_block(tile, all_heads),
            whole_block(gains.shape),
            ANY,
        ],
        out_specs=(tile_block(tile, width), tile_block(tile, width), tile_block(tile, hidden), tile_block(tile, hidden), ANY),
        scratch_shapes=[pltpu.VMEM((width, all_heads), BF16)] + [pltpu.VMEM((width, wide), BF16)] * 3
        + [pltpu.SemaphoreType.DMA((4,))]
        + line_sum_scratch(count, chunk, count, width),
        compiler_params=pltpu.CompilerParams(
            collective_id=ident, has_side_effects=True, vmem_limit_bytes=60 * 2**20),
        name="ffn_forward",
    )(x, heads, gains, weights)


def ffn_backward_kernel(tiles, tile, chunk, slots, hidden, x_ref, attn_ref, dy_ref, ffn_ref, two_ref, gate_ref, up_ref,
                        gain_ref, w_ref,
                        y_ref, dgain_ref, grad_ref, out_ref, wg_ref, wu_ref, wd_ref, w_sem,
                        acc_g, acc_u, acc_d, keep_g, keep_u, keep_h, stage, stage_sem, own, near, far, *sems):
    i = pl.program_id(0)
    per = tile // chunk
    last = tiles * per
    line = LineSum(last, chunk, slots, own, near, far, out_ref, sems)

    @pl.when(i == 0)
    def _():
        copies = load_ffn_weights(w_ref, (wg_ref, wu_ref, wd_ref), w_sem)
        for copy in copies:
            copy.start()
        barrier_line(line.z)
        for acc in (acc_g, acc_u, acc_d, dgain_ref):
            acc[...] = jnp.zeros_like(acc)
        for copy in copies:
            copy.wait()

    middle, _, _ = middle_of(x_ref[...], attn_ref[...], gain_ref[1:2, :])
    hat, inv = norm_parts(ffn_ref[...].astype(F32))
    gain = gain_ref[3:4, :]
    y_ref[...] = (middle + hat * (1.0 + gain)).astype(BF16)
    d_ffn, d_gain = norm_back(dy_ref[...].astype(F32), hat, inv, gain)
    dgain_ref[...] += d_gain[None]
    d_ffn = d_ffn.astype(BF16)
    part = None
    for a, b in column_parts(hidden):
        d_hidden = dot(d_ffn, wd_ref[:, a:b])
        up = up_ref[:, a:b].astype(F32)
        value, slope = gelu_parts(gate_ref[:, a:b].astype(F32))
        keep_h[:, a:b] = (value * up).astype(BF16)
        d_gate = (d_hidden * up * slope).astype(BF16)
        d_up = (d_hidden * value).astype(BF16)
        keep_g[:, a:b] = d_gate
        keep_u[:, a:b] = d_up
        more = dot(d_gate, wg_ref[:, a:b], NT) + dot(d_up, wu_ref[:, a:b], NT)
        part = more if part is None else part + more
    for j in range(per):
        line.put(i * per + j, part[j * chunk : (j + 1) * chunk].astype(BF16))

    @pl.when(i >= 1)
    def _():
        for j in range(per):
            line.pair((i - 1) * per + j)

    acc_g[...] += dot(two_ref[...], keep_g[...], TN)
    acc_u[...] += dot(two_ref[...], keep_u[...], TN)
    acc_d[...] += dot(d_ffn, keep_h[...], TN)

    @pl.when(i >= 2)
    def _():
        for j in range(per):
            line.total((i - 2) * per + j)

    @pl.when(i >= 3)
    def _():
        for j in range(per):
            line.retire((i - 3) * per + j)

    @pl.when(i == tiles - 1)
    def _():
        for j in range(per):
            line.pair(last - per + j)
        step = stage.shape[1]
        count = acc_g.shape[0] // step

        def piece(acc, out, k, at):
            @pl.when(k >= 2)
            def _():
                pltpu.make_async_copy(stage.at[at], out.at[pl.ds(0, step)], stage_sem.at[at]).wait()
            rows = pl.ds(pl.multiple_of(k * step, step), step)
            stage[at] = acc[rows, :].astype(BF16)
            pltpu.make_async_copy(stage.at[at], out.at[rows], stage_sem.at[at]).start()

        for acc, out in ((acc_g, grad_ref.at[0]), (acc_u, grad_ref.at[1]), (acc_d, grad_ref.at[2])):
            def pieces(k, _):
                piece(acc, out, k, lax.rem(k, 2))
                return 0

            lax.fori_loop(0, count, pieces, 0)
            for at in range(2):
                pltpu.make_async_copy(stage.at[at], out.at[pl.ds(0, step)], stage_sem.at[at]).wait()
            if acc is acc_g:
                for c in range(max(0, last - 2 * per), last - per):
                    line.total(c)
            if acc is acc_u:
                for c in range(last - per, last):
                    line.total(c)
        for c in range(max(0, last - 3 * per), last):
            line.retire(c)
        line.finish()


def ffn_backward(x, attn, dy, ffn, two, gate, up, gains, weights, ident):
    rows, width = x.shape
    hidden = gate.shape[1]
    wide = wide_of(hidden)
    tile, chunk = 256, 128
    tiles = rows // tile
    count = rows // chunk
    slots = min(count, 6)
    step = 144
    acc = pltpu.VMEM((width, hidden), F32)
    keep = pltpu.VMEM((tile, hidden), BF16)
    return pl.pallas_call(
        functools.partial(ffn_backward_kernel, tiles, tile, chunk, slots, hidden),
        grid=(tiles,),
        out_shape=(
            jax.ShapeDtypeStruct((rows, width), BF16),
            jax.ShapeDtypeStruct((1, width), F32),
            jax.ShapeDtypeStruct((3, width, hidden), BF16),
            jax.ShapeDtypeStruct((rows, width), BF16),
        ),
        in_specs=[tile_block(tile, width)] * 5 + [tile_block(tile, hidden)] * 2
        + [whole_block(gains.shape), ANY],
        out_specs=(tile_block(tile, width), pl.BlockSpec((1, width), lambda i: (0, 0)), ANY, ANY),
        scratch_shapes=[pltpu.VMEM((width, wide), BF16)] * 3 + [pltpu.SemaphoreType.DMA((3,))] + [acc] * 3 + [keep] * 3
        + [pltpu.VMEM((2, step, hidden), BF16), pltpu.SemaphoreType.DMA((2,))]
        + line_sum_scratch(count, chunk, slots, width),
        compiler_params=pltpu.CompilerParams(
            collective_id=ident, has_side_effects=True, vmem_limit_bytes=63 * 2**20),
        name="ffn_backward",
    )(x, attn, dy, ffn, two, gate, up, gains, weights)


def middle_back_kernel(x_ref, attn_ref, dy_ref, d2_ref, h_ref, gain_ref, w_ref,
                       dm_ref, dh_ref, delta_ref, dgain_ref, go_ref, acc, wo_ref, w_sem):
    i = pl.program_id(0)

    @pl.when(i == 0)
    def _():
        head = wo_ref.shape[1]
        at = pl.multiple_of(lax.axis_index("tp") * head, head)
        copy = pltpu.make_async_copy(w_ref.at[:, pl.ds(at, head)], wo_ref, w_sem)
        copy.start()
        copy.wait()
        acc[...] = jnp.zeros_like(acc)
        dgain_ref[...] = jnp.zeros_like(dgain_ref)

    middle, attn_hat, attn_inv = middle_of(x_ref[...], attn_ref[...], gain_ref[1:2, :])
    hat, inv = norm_parts(middle)
    d_part, d_gain = norm_back(d2_ref[...].astype(F32), hat, inv, gain_ref[2:3, :])
    dgain_ref[1:2, :] += d_gain[None]
    d_middle = dy_ref[...].astype(F32) + d_part
    dm_ref[...] = d_middle
    d_attn, d_gain = norm_back(d_middle, attn_hat, attn_inv, gain_ref[1:2, :])
    dgain_ref[0:1, :] += d_gain[None]
    d_attn = d_attn.astype(BF16)
    d_heads = dot(d_attn, wo_ref[...]).astype(BF16)
    dh_ref[...] = d_heads
    heads = h_ref[...]
    delta_ref[...] = jnp.sum(d_heads.astype(F32) * heads.astype(F32), axis=1, keepdims=True)
    acc[...] += dot(d_attn, heads, TN)

    @pl.when(i == pl.num_programs(0) - 1)
    def _():
        go_ref[...] = acc[...].astype(BF16)


def middle_back(x, attn, dy, d_two, heads, gains, weights):
    rows, width = x.shape
    head = heads.shape[1]
    tile = 256
    return pl.pallas_call(
        middle_back_kernel,
        grid=(rows // tile,),
        out_shape=(
            jax.ShapeDtypeStruct((rows, width), F32),
            jax.ShapeDtypeStruct((rows, head), BF16),
            jax.ShapeDtypeStruct((rows, 1), F32),
            jax.ShapeDtypeStruct((2, width), F32),
            jax.ShapeDtypeStruct((width, head), BF16),
        ),
        in_specs=[tile_block(tile, width)] * 4 + [tile_block(tile, head)] + [whole_block(gains.shape), ANY],
        out_specs=(
            tile_block(tile, width), tile_block(tile, head), tile_block(tile, 1),
            pl.BlockSpec((2, width), lambda i: (0, 0)), pl.BlockSpec((width, head), lambda i: (0, 0)),
        ),
        scratch_shapes=[pltpu.VMEM((width, head), F32), pltpu.VMEM((width, head), BF16), pltpu.SemaphoreType.DMA],
        compiler_params=pltpu.CompilerParams(vmem_limit_bytes=48 * 2**20),
        name="middle_back",
    )(x, attn, dy, d_two, heads, gains, weights)


class LineGather:
    def __init__(self, whole, tile, width, sems):
        self.whole, self.tile, self.width, self.sems = whole, tile, width, sems
        self.z = lax.axis_index("tp")

    def place(self, src, t):
        return self.whole.at[
            pl.ds(pl.multiple_of(t * self.tile, self.tile), self.tile),
            pl.ds(pl.multiple_of(src * self.width, self.width), self.width)]

    def send(self, src, t, hop, way):
        ss, rs = self.sems[:2] if way > 0 else self.sems[2:]
        place = self.place(src, t)
        return pltpu.make_async_remote_copy(
            place, place, ss.at[hop, t], rs.at[hop, t],
            device_id={"tp": self.z + way}, device_id_type=MESH)

    def going(self, hop, way):
        src = self.z - way * hop
        return src, (self.z + way >= 0) & (self.z + way <= 3) & (src >= 0) & (src <= 3)

    def coming(self, hop, way):
        src = self.z - way * (hop + 1)
        return src, (src >= 0) & (src <= 3)

    def forward(self, t, hop):
        for way in (1, -1):
            if hop > 0:
                self.wait(t, hop - 1, way)
            src, ok = self.going(hop, way)

            @pl.when(ok)
            def _():
                self.send(src, t, hop, way).start()

    def wait(self, t, hop, way):
        src, ok = self.coming(hop, way)

        @pl.when(ok)
        def _():
            self.send(src, t, hop, way).wait_recv()

    def arrived(self, t):
        for way in (1, -1):
            self.wait(t, 2, way)

    def finish(self, tiles):
        for hop in range(3):
            for way in (1, -1):
                src, ok = self.going(hop, way)

                @pl.when(ok)
                def _():
                    def one(t, _):
                        self.send(src, t, hop, way).wait_send()
                        return 0

                    lax.fori_loop(0, tiles, one, 0)


class KeyGather(LineGather):
    def __init__(self, block, chips, sems):
        self.block, self.chips, self.sems = block, chips, sems
        self.z = lax.axis_index("tp")

    def tile_of(self, g, half, k):
        return (2 * g + half) * (self.chips - 1) + k - 1

    def place(self, src, t):
        pair, k = divmod(t, self.chips - 1)
        return self.quarter(pair // 2, pair % 2, k + 1, src)

    def quarter(self, g, half, k, src, own=False):
        ref, start, size = self.block(g, half, k, own)
        rows = size // 4
        return ref.at[pl.ds(pl.multiple_of(start + src * rows, rows), rows)]

    def finish(self, tiles):
        for hop in range(3):
            for way in (1, -1):
                src, ok = self.going(hop, way)

                @pl.when(ok)
                def _():
                    for t in range(tiles):
                        self.send(src, t, hop, way).wait_send()


class Shared:
    def __init__(self, over_dp):
        self.ctx = ctx = lax.axis_size("ctx")
        me = lax.axis_index("ctx")
        self.devices = ctx
        if over_dp:
            me = me + lax.axis_index("dp") * ctx
            self.devices = ctx * lax.axis_size("dp")
        self.over_dp = over_dp
        self.me = me
        self.chips = self.devices // 2
        self.core = lax.rem(me, 2)
        self.chip = lax.div(me, 2)

    def ident(self, device):
        if self.over_dp:
            return {"dp": lax.div(device, self.ctx), "ctx": lax.rem(device, self.ctx)}
        return {"ctx": device}

    def other(self, k):
        return 2 * lax.rem(self.chip + k + self.chips, self.chips) + self.core

    def partner(self):
        return self.me + 1 - 2 * self.core

    def greet(self, z):
        bar = pltpu.get_barrier_semaphore()
        for device in [self.partner()] + [self.other(k) for k in range(1, self.chips)]:
            pl.semaphore_signal(bar, inc=1, device_id=self.ident(device), device_id_type=MESH)

        @pl.when(z > 0)
        def _():
            pl.semaphore_signal(bar, inc=1, device_id={"tp": z - 1}, device_id_type=MESH)

        @pl.when(z < 3)
        def _():
            pl.semaphore_signal(bar, inc=1, device_id={"tp": z + 1}, device_id_type=MESH)

        pl.semaphore_wait(bar, self.chips + jnp.where((z == 0) | (z == 3), 1, 2))

    def copy(self, source, target, send, recv, device):
        return pltpu.make_async_remote_copy(
            source, target, send, recv, device_id=self.ident(device), device_id_type=MESH)


def first_gather_kernel(a_ref, b_ref, i_ref, all_ref, line_ref, ids_ref, lsem, ss1, rs1, ss2, rs2, si1, ri1, si2, ri2, *sems):
    group = Shared(True)
    line = LineGather(line_ref, b_ref.shape[0], b_ref.shape[1], sems)
    width = b_ref.shape[1]
    own = [
        pltpu.make_async_copy(b_ref, line_ref.at[:, pl.ds(pl.multiple_of(line.z * width, width), width)], lsem.at[0]),
        pltpu.make_async_copy(a_ref, all_ref.at[group.me], lsem.at[1]),
        pltpu.make_async_copy(i_ref, ids_ref.at[group.me], lsem.at[2]),
    ]
    for copy in own:
        copy.start()
    group.greet(line.z)
    arrays = ((a_ref, all_ref, ss1, rs1, ss2, rs2), (i_ref, ids_ref, si1, ri1, si2, ri2))

    def direct(n, k, incoming=False):
        ref, whole, ss, rs = arrays[n][:4]
        at = whole.at[group.other(-k)] if incoming else whole.at[group.me]
        return group.copy(ref, at, ss.at[k], rs.at[k], group.other(k))

    def inner(n, k, incoming=False):
        ref, whole, _, _, ss, rs = arrays[n]
        at = whole.at[group.other(-k)]
        if incoming:
            at = whole.at[group.other(-k) + 1 - 2 * group.core]
        return group.copy(ref if k == 0 else at, at, ss.at[k], rs.at[k], group.partner())

    both = range(2)
    for k in range(1, group.chips):
        for n in both:
            direct(n, k).start()
    own[0].wait()
    line.forward(0, 0)
    for n in both:
        inner(n, 0).start()
    for k in range(1, group.chips):
        if k < 3:
            line.forward(0, k)
        for n in both:
            direct(n, k, True).wait_recv()
            inner(n, k).start()
    for hop in range(min(3, group.chips), 3):
        line.forward(0, hop)
    for k in range(group.chips):
        for n in both:
            inner(n, k, True).wait_recv()
    line.arrived(0)
    for copy in own[1:]:
        copy.wait()
    for n in both:
        for k in range(1, group.chips):
            direct(n, k).wait_send()
        for k in range(group.chips):
            inner(n, k).wait_send()
    line.finish(1)


def first_gather(a, b, ids, devices, ident):
    dma = pltpu.SemaphoreType.DMA((devices // 2,))
    hop = pltpu.SemaphoreType.DMA((3, 1))
    return pl.pallas_call(
        first_gather_kernel,
        out_shape=(
            jax.ShapeDtypeStruct((devices,) + a.shape, a.dtype),
            jax.ShapeDtypeStruct((b.shape[0], 4 * b.shape[1]), b.dtype),
            jax.ShapeDtypeStruct((devices,) + ids.shape, ids.dtype),
        ),
        in_specs=[ANY] * 3,
        out_specs=(ANY,) * 3,
        scratch_shapes=[pltpu.SemaphoreType.DMA((3,))] + [dma] * 8 + [hop] * 4,
        compiler_params=pltpu.CompilerParams(collective_id=ident, has_side_effects=True),
        name="first_gather",
    )(a, b, ids)


def attention_kernel(groups, size, x_ref, w_ref, gain_ref, gq_ref, gk_ref, cos_ref, sin_ref, qs_ref, ks_ref,
                     q_ref, qhat_ref, qinv_ref, khat_ref, kinv_ref, heads_ref, log_ref, kv_out, all_out,
                     kv, whole, store_kv, store_all, ss1, rs1, ss2, rs2, *sems):
    head = q_ref.shape[1]
    length = kv.shape[1]
    id_rows = size // 128
    blocks = length // (2 * size)
    group = Shared(False)
    rank = group.me
    line = LineGather(whole, size, head, sems[:4])
    z = line.z
    tile = min(256, size)
    group.greet(z)

    def block(g, half, k, own):
        c = rank if own else group.other(-k)
        return kv.at[g], half * (length // 2) + c * size, size

    keys = KeyGather(block, group.chips, sems[4:])

    def place(g, half, c):
        return kv.at[g, pl.ds(pl.multiple_of(half * (length // 2) + c * size, size), size)]

    def direct(g, half, k, incoming=False):
        at = keys.quarter(g, half, k, z, own=not incoming)
        return group.copy(at, at, ss1.at[g, half, k], rs1.at[g, half, k], group.other(k))

    def inner(g, half, k, incoming=False):
        block = group.other(-k)
        at = place(g, half, block + 1 - 2 * group.core if incoming else block)
        return group.copy(at, at, ss2.at[g, half, k], rs2.at[g, half, k], group.partner())

    def project(g, half, u):
        rows = pl.ds((2 * g + half) * size + u * tile, tile)
        spot = pl.ds(half * size + u * tile, tile)
        cosine, sine = cos_ref[spot, :], sin_ref[spot, :]
        hat, _ = norm_parts(x_ref[rows, :].astype(F32))
        raw = dot((hat * (1.0 + gain_ref[0:1, :])).astype(BF16), w_ref[:, : 3 * head])
        hat, inv = norm_parts(raw[:, :head])
        qhat_ref[rows, :] = hat
        qinv_ref[rows, :] = inv
        q_ref[rows, :] = rotate(hat * (1.0 + gq_ref[...]), cosine, sine).astype(BF16)
        hat, inv = norm_parts(raw[:, head : 2 * head])
        khat_ref[rows, :] = hat
        kinv_ref[rows, :] = inv
        at = pl.ds(pl.multiple_of(half * (length // 2) + rank * size + u * tile, tile), tile)
        kv[g, at, :head] = rotate(hat * (1.0 + gk_ref[...]), cosine, sine).astype(BF16)
        kv[g, at, head:] = raw[:, 2 * head :].astype(BF16)

    def attend(g, half):
        row = lax.broadcasted_iota(jnp.int32, (size, size), 0)
        col = lax.broadcasted_iota(jnp.int32, (size, size), 1)
        rows = pl.ds((2 * g + half) * size, size)
        q = q_ref[rows, :] * jnp.asarray(SCALE, BF16)
        qseg = qs_ref[g, half]

        def part(block):
            at = pl.ds(pl.multiple_of(block * size, size), size)
            device = lax.axis_index("dp") * lax.axis_size("ctx") + lax.rem(block, blocks)
            ids = ks_ref[device, pl.ds((2 * g + lax.div(block, blocks)) * id_rows, id_rows), :]
            ids = jnp.concatenate([ids[j : j + 1] for j in range(id_rows)], axis=1)
            same = qseg == jnp.where(ids == 0, -1, ids)
            return dot(q, kv[g, at, :head], NT), kv[g, at, head:], same

        s, v, same = part(rank + half * blocks)
        order = (col <= row) if half == 0 else (col >= row)
        s = jnp.where((same & order) | (col == row), s, NEGATIVE)
        top = jnp.max(s, axis=1, keepdims=True)
        p = jnp.exp(s - top)
        mass = jnp.sum(p, axis=1, keepdims=True)
        acc = dot(p.astype(BF16), v)

        def step(t, carry):
            top, mass, acc = carry
            s, v, same = part(block_starts(half, t, blocks, rank))
            s = jnp.where(same, s, NEGATIVE)
            new = jnp.maximum(top, jnp.max(s, axis=1, keepdims=True))
            keep = jnp.exp(top - new)
            p = jnp.exp(s - new)
            mass = mass * keep + jnp.sum(p, axis=1, keepdims=True)
            return new, mass, acc * keep + dot(p.astype(BF16), v)

        count = rank if half == 0 else 2 * blocks - 1 - rank
        top, mass, acc = lax.fori_loop(0, count, step, (top, mass, acc))
        out = (acc / mass).astype(BF16)
        heads_ref[rows, :] = out
        whole[rows, pl.ds(pl.multiple_of(z * head, head), head)] = out
        log_ref[g, half] = top + jnp.log(mass)

    chips = range(1, group.chips)
    tiles = 2 * groups

    def exchange(t):
        for stage in (4, 3, 2, 1):
            if not 0 <= t - stage < tiles:
                continue
            g, half = divmod(t - stage, 2)
            for k in chips:
                spot = keys.tile_of(g, half, k)
                if stage == 1:
                    direct(g, half, k, True).wait_recv()
                if stage <= 3:
                    keys.forward(spot, stage - 1)
                else:
                    keys.arrived(spot)
                    inner(g, half, k).start()

    def hops(t):
        for hop in range(3):
            if 0 <= t - hop < tiles:
                line.forward(t - hop, hop)

    def keep(t):
        at = pl.ds(t * size, size)
        return pltpu.make_async_copy(whole.at[at], all_out.at[at], store_all.at[t])

    def save(g):
        return pltpu.make_async_copy(kv.at[g], kv_out.at[g], store_kv.at[g])

    for t in range(tiles):
        g, half = divmod(t, 2)
        for u in range(size // tile):
            project(g, half, u)
        for k in chips:
            direct(g, half, k).start()
        inner(g, half, 0).start()
        exchange(t)
    at_step = tiles
    for g in range(groups):
        while at_step < min(2 * g + 6, tiles + 4):
            exchange(at_step)
            at_step += 1
        for half in range(2):
            for k in range(group.chips):
                inner(g, half, k, True).wait_recv()
        save(g).start()
        for half in range(2):
            attend(g, half)
            if at_step < tiles + 4:
                exchange(at_step)
                at_step += 1
            hops(2 * g + half)
    for t in range(tiles, tiles + 2):
        hops(t)
    for t in range(tiles):
        line.arrived(t)
        keep(t).start()
    for g in range(groups):
        save(g).wait()
        for half in range(2):
            for k in chips:
                direct(g, half, k).wait_send()
            for k in range(group.chips):
                inner(g, half, k).wait_send()
    line.finish(tiles)
    keys.finish(tiles * (group.chips - 1))
    for t in range(tiles):
        keep(t).wait()


def attention(x, w, gains, gain_query, gain_key, cosine, sine, qseg, ids, length, ident):
    rows, width = x.shape
    groups, _, size, _ = qseg.shape
    head = gain_query.shape[1]
    chips = length // (4 * size)
    tiles = 2 * groups
    vmem = pl.BlockSpec(memory_space=pltpu.VMEM)
    dma = pltpu.SemaphoreType.DMA
    return pl.pallas_call(
        functools.partial(attention_kernel, groups, size),
        out_shape=(
            jax.ShapeDtypeStruct((rows, head), BF16),
            jax.ShapeDtypeStruct((rows, head), F32),
            jax.ShapeDtypeStruct((rows, 1), F32),
            jax.ShapeDtypeStruct((rows, head), F32),
            jax.ShapeDtypeStruct((rows, 1), F32),
            jax.ShapeDtypeStruct((rows, head), BF16),
            jax.ShapeDtypeStruct((groups, 2, size, 1), F32),
            jax.ShapeDtypeStruct((groups, length, 2 * head), BF16),
            jax.ShapeDtypeStruct((rows, 4 * head), BF16),
        ),
        in_specs=[vmem] * 9,
        out_specs=(vmem,) * 7 + (ANY, ANY),
        scratch_shapes=[
            pltpu.VMEM((groups, length, 2 * head), BF16), pltpu.VMEM((rows, 4 * head), BF16),
            dma((groups,)), dma((tiles,))] + [dma((groups, 2, chips))] * 4 + [dma((3, tiles))] * 4
        + [dma((3, tiles * (chips - 1)))] * 4,
        compiler_params=pltpu.CompilerParams(
            collective_id=ident, has_side_effects=True, vmem_limit_bytes=60 * 2**20),
        name="attention",
    )(x, w, gains, gain_query, gain_key, cosine, sine, qseg, ids)


class ResidentSum(LineSum):
    def outwards(self, c):
        return pltpu.make_async_remote_copy(
            self.out.at[self.rows(c)], self.out.at[self.rows(c)], self.sems[4].at[c], self.sems[5].at[c],
            device_id={"tp": self.my_leaf}, device_id_type=MESH)

    def total(self, c):
        @pl.when(self.hub)
        def _():
            self.across(c).wait_recv()
            at = self.rows(c)
            self.out[at, :] = (self.own[at, :].astype(F32) + self.far[at, :].astype(F32)).astype(BF16)
            self.outwards(c).start()

    def arrived(self, c):
        @pl.when(self.leaf)
        def _():
            self.outwards(c).wait_recv()

    def finish(self):
        @pl.when(self.leaf)
        def _():
            for c in range(self.count):
                self.inwards(c).wait_send()

        @pl.when(self.hub)
        def _():
            for c in range(self.count):
                self.across(c).wait_send()
                self.outwards(c).wait_send()


def turned(column, size):
    return jnp.transpose(jnp.broadcast_to(column, (size, 128)))[0:1, :]


def attention_back_kernel(groups, size, q_ref, do_ref, log_ref, delta_ref, qs_ref, ids_ref, hat_ref, inv_ref, cos_ref, sin_ref,
                          x_ref, gain_ref, gq_ref, go_ref, kv_hbm, all_out, dkv_ref, dgain_ref, grad_ref,
                          kv, dk, dv, part, near, pair, far, whole, acc, load, store, ss1, rs1, ss2, rs2, *sems):
    head = q_ref.shape[1]
    length = kv.shape[1]
    blocks = length // (2 * size)
    id_rows = size // 128
    tiles = 2 * groups
    group = Shared(False)
    rank, core = group.me, group.core
    line = LineGather(whole, size, head, sems)
    z = line.z
    others = range(1, group.chips)
    order = list(others) + [0]

    def fetch(g):
        return pltpu.make_async_copy(kv_hbm.at[g], kv.at[g], load.at[g])

    for g in range(groups):
        fetch(g).start()
    group.greet(z)
    acc[...] = jnp.zeros_like(acc)
    dgain_ref[...] = jnp.zeros_like(dgain_ref)

    def rows_of(half, device):
        return pl.ds(pl.multiple_of(half * (length // 2) + device * size, size), size)

    def within(g, half, k):
        to = group.other(k) + 1 - 2 * core
        return group.copy(
            part.at[g, rows_of(half, to)], near.at[g, half, k], ss1.at[g, half, k], rs1.at[g, half, k], group.partner())

    def between(g, half, k):
        return group.copy(
            pair.at[g, half, k - 1], far.at[g, half, k - 1], ss2.at[g, half, k], rs2.at[g, half, k], group.other(k))

    def both_cores(g):
        for half in range(2):
            for k in order:
                within(g, half, k).wait_recv()
                total = part[g, rows_of(half, group.other(k)), :].astype(F32) + near[g, half, k].astype(F32)
                if k > 0:
                    pair[g, half, k - 1] = total.astype(BF16)
                    between(g, half, k).start()
                else:
                    dkv_ref[pl.ds((2 * g + half) * size, size), :] = total.astype(BF16)

    def all_chips(g):
        for half in range(2):
            at = pl.ds((2 * g + half) * size, size)
            total = dkv_ref[at, :].astype(F32)
            for k in others:
                between(g, half, k).wait_recv()
                total = total + far[g, half, k - 1].astype(F32)
            dkv_ref[at, :] = total.astype(BF16)

    def hops(t):
        for hop in range(3):
            if 0 <= t - hop < tiles:
                line.forward(t - hop, hop)

    def attend(g, half):
        row = lax.broadcasted_iota(jnp.int32, (size, size), 0)
        col = lax.broadcasted_iota(jnp.int32, (size, size), 1)
        own = pl.ds((2 * g + half) * size, size)
        q = q_ref[own, :] * jnp.asarray(SCALE, BF16)
        do = do_ref[own, :]
        qseg = qs_ref[g, half]
        log_mass = turned(log_ref[g, half], size)
        delta = turned(delta_ref[own, :], size)

        def step_of(block, mine):
            at = pl.ds(pl.multiple_of(block * size, size), size)
            k = kv[g, at, :head]
            v = kv[g, at, head:]
            device = lax.axis_index("dp") * lax.axis_size("ctx") + lax.rem(block, blocks)
            ids = ids_ref[device, pl.ds((2 * g + lax.div(block, blocks)) * id_rows, id_rows), :]
            ids = jnp.concatenate([ids[j : j + 1] for j in range(id_rows)], axis=1)
            ids = jnp.transpose(jnp.broadcast_to(jnp.where(ids == 0, -1, ids), (8, size)))[:, 0:1]
            allowed = ids == qseg
            if mine:
                ahead = (row <= col) if half == 0 else (row >= col)
                allowed = (allowed & ahead) | (col == row)
            s = jnp.where(allowed, dot(k, q, NT), NEGATIVE)
            p = jnp.exp(s - log_mass)
            ds = (p * (dot(v, do, NT) - delta)).astype(BF16)
            dv[at, :] += dot(p.astype(BF16), do)
            dk[at, :] += dot(ds, q)
            return dot(ds, k, TN)

        def step(t, dq):
            return dq + step_of(block_starts(half, t, blocks, rank), False)

        dq = step_of(rank + half * blocks, True)
        count = rank if half == 0 else 2 * blocks - 1 - rank
        dq = SCALE * lax.fori_loop(0, count, step, dq)
        spot = pl.ds(half * size, size)
        d_rot = rotate(dq, cos_ref[spot, :], -sin_ref[spot, :])
        d_raw, d_gain = norm_back(d_rot, hat_ref[own, :], inv_ref[own, :], gq_ref[...])
        dgain_ref[...] += d_gain[None]
        whole[own, pl.ds(pl.multiple_of(z * head, head), head)] = d_raw.astype(BF16)

    def weight_gradient(t):
        own = pl.ds(t * size, size)
        hat, _ = norm_parts(x_ref[own, :].astype(F32))
        one = (hat * (1.0 + gain_ref[0:1, :])).astype(BF16)
        acc[...] += dot(one, whole[own, pl.ds(pl.multiple_of(z * head, head), head)], TN)

    def keep(t):
        at = pl.ds(t * size, size)
        return pltpu.make_async_copy(whole.at[at], all_out.at[at], store.at[t])

    for g in range(groups):
        fetch(g).wait()
        dk[...] = jnp.zeros_like(dk)
        dv[...] = jnp.zeros_like(dv)
        for half in range(2):
            attend(g, half)
            hops(2 * g + half)
            if half == 0 and g > 0:
                both_cores(g - 1)
        part[g, :, :head] = dk[...].astype(BF16)
        part[g, :, head:] = dv[...].astype(BF16)
        for half in range(2):
            for k in order:
                within(g, half, k).start()
        for half in range(2):
            weight_gradient(2 * g + half)
        if g > 0:
            all_chips(g - 1)
    hops(tiles)
    both_cores(groups - 1)
    hops(tiles + 1)
    grad_ref[:, :head] = acc[...].astype(BF16)
    grad_ref[:, head:] = go_ref[...]
    for t in range(tiles):
        line.arrived(t)
        keep(t).start()
    all_chips(groups - 1)
    for g in range(groups):
        for half in range(2):
            for k in others:
                between(g, half, k).wait_send()
            for k in order:
                within(g, half, k).wait_send()
    line.finish(tiles)
    for t in range(tiles):
        keep(t).wait()


def attention_back(q, d_heads, log_mass, delta, qseg, ids, hat, inv, cosine, sine, x, gains, gain_query, grad_o, kv, ident):
    rows, head = q.shape
    width = x.shape[1]
    groups, length, _ = kv.shape
    size = rows // (2 * groups)
    chips = length // (4 * size)
    tiles = 2 * groups
    vmem = pl.BlockSpec(memory_space=pltpu.VMEM)
    dma = pltpu.SemaphoreType.DMA
    return pl.pallas_call(
        functools.partial(attention_back_kernel, groups, size),
        out_shape=(
            jax.ShapeDtypeStruct((rows, 4 * head), BF16),
            jax.ShapeDtypeStruct((rows, 2 * head), BF16),
            jax.ShapeDtypeStruct((1, head), F32),
            jax.ShapeDtypeStruct((width, 2 * head), BF16),
        ),
        in_specs=[vmem] * 14 + [ANY],
        out_specs=(ANY, vmem, vmem, vmem),
        scratch_shapes=[
            pltpu.VMEM((groups, length, 2 * head), BF16),
            pltpu.VMEM((length, head), F32), pltpu.VMEM((length, head), F32),
            pltpu.VMEM((groups, length, 2 * head), BF16),
            pltpu.VMEM((groups, 2, chips, size, 2 * head), BF16),
            pltpu.VMEM((groups, 2, chips - 1, size, 2 * head), BF16),
            pltpu.VMEM((groups, 2, chips - 1, size, 2 * head), BF16),
            pltpu.VMEM((rows, 4 * head), BF16),
            pltpu.VMEM((width, head), F32),
            dma((groups,)), dma((tiles,))] + [dma((groups, 2, chips))] * 4 + [dma((3, tiles))] * 4,
        compiler_params=pltpu.CompilerParams(
            collective_id=ident, has_side_effects=True, vmem_limit_bytes=63 * 2**20),
        name="attention_back",
    )(q, d_heads, log_mass, delta, qseg, ids, hat, inv, cosine, sine, x, gains, gain_query, grad_o, kv)


def key_back_kernel(tiles, tile, chunk, own_rows, dkv_ref, hat_ref, inv_ref, cos_ref, sin_ref, x_ref, dm_ref, dq_ref,
                    gain_ref, gk_ref, w_ref, wq_ref, dgq_ref, dg_mid_ref, dg_post_ref, rs_ref,
                    dx_ref, last_ref, gate_ref, up_ref, down_ref, acc, acc_in, acc_key, w_kv, w_sem, out, own, near, far, *sems):
    i = pl.program_id(0)
    head = hat_ref.shape[1]
    per = tile // chunk
    count = tiles * per + 1
    line = ResidentSum(count, chunk, count, own, near, far, out, sems)

    @pl.when(i == 0)
    def _():
        copy = pltpu.make_async_copy(w_ref.at[:, pl.ds(head, 2 * head)], w_kv, w_sem)
        copy.start()
        barrier_line(line.z)
        for ref in (acc, acc_in, acc_key):
            ref[...] = jnp.zeros_like(ref)
        copy.wait()
        line.put(count - 1, jnp.broadcast_to(
            jnp.concatenate([dgq_ref[...], dgq_ref[...]], axis=1).astype(BF16), (chunk, 2 * head)))

    @pl.when(i < tiles)
    def _():
        for j in range(per):
            line.put(i * per + j, dkv_ref[j * chunk : (j + 1) * chunk, :])

    @pl.when((i >= 1) & (i <= tiles))
    def _():
        for j in range(per):
            line.pair((i - 1) * per + j)

    @pl.when((i >= 2) & (i <= tiles + 1))
    def _():
        for j in range(per):
            line.total((i - 2) * per + j)

    @pl.when(i == 0)
    def _():
        gate_ref[...] = rs_ref[0].astype(F32)
        up_ref[...] = rs_ref[1].astype(F32)
        row = lax.broadcasted_iota(jnp.int32, (own_rows, own_rows), 0)
        col = lax.broadcasted_iota(jnp.int32, (own_rows, own_rows), 1)
        down_ref[...] = dot(rs_ref[2], jnp.where(row == col, 1.0, 0.0).astype(BF16), TN)

    @pl.when(i == 1)
    def _():
        line.pair(count - 1)

    @pl.when(i == 2)
    def _():
        line.total(count - 1)

    @pl.when(i >= 3)
    def _():
        for j in range(per):
            line.arrived((i - 3) * per + j)
        d_kv = out[pl.ds(pl.multiple_of((i - 3) * tile, tile), tile), :]
        d_rot = rotate(d_kv[:, :head].astype(F32), cos_ref[...], -sin_ref[...])
        d_raw, d_gain = norm_back(d_rot, hat_ref[...], inv_ref[...], gk_ref[...])
        acc_key[...] += d_gain[None]
        d_raw = jnp.concatenate([d_raw.astype(BF16), d_kv[:, head:]], axis=1)
        d_one = dot(dq_ref[...], wq_ref[...], NT) + dot(d_raw, w_kv[...], NT)
        hat, inv = norm_parts(x_ref[...].astype(F32))
        gain = gain_ref[0:1, :]
        d_part, d_gain = norm_back(d_one, hat, inv, gain)
        acc_in[...] += d_gain[None]
        dx_ref[...] = dm_ref[...] + d_part
        acc[...] += dot((hat * (1.0 + gain)).astype(BF16), d_raw, TN)

    @pl.when(i == tiles + 2)
    def _():
        line.arrived(count - 1)
        width = x_ref.shape[1]
        short = head * own_rows // width
        last_ref[:, : 2 * head] = acc[...].astype(BF16)
        d_query = out[pl.ds((count - 1) * chunk, 16), :head][0:1].astype(F32)
        pair = jnp.concatenate([d_query, acc_key[...], jnp.zeros((14, head), F32)], axis=0).astype(BF16)
        col = lax.broadcasted_iota(jnp.int32, (head, width), 1)
        row = lax.broadcasted_iota(jnp.int32, (head, width), 0)
        shift = short.bit_length() - 1
        spot = lax.shift_right_logical(row, shift) * own_rows + (row & (short - 1))
        spread = dot(pair, jnp.where(col == spot, 1.0, 0.0).astype(BF16))
        gains = jnp.concatenate(
            [acc_in[...], dg_mid_ref[...], dg_post_ref[...], spread[0:2], jnp.zeros((122, width), F32)], axis=0)
        last_ref[:, 2 * head :] = jnp.transpose(gains).astype(BF16)
        line.finish()


def key_back(d_kv, hat, inv, cosine, sine, x, d_middle, d_query, gains, gain_key, first, w_query, dg_query, dg_mid, dg_post,
             ffn_grads, own_rows, ident):
    rows, width = x.shape
    head = hat.shape[1]
    tile, chunk = 256, 128
    tiles = rows // tile
    count = rows // chunk + 1
    dma = pltpu.SemaphoreType.DMA((count,))

    def late(cols):
        return pl.BlockSpec((tile, cols), lambda i: (jnp.maximum(i - 3, 0), 0))

    def fixed(shape):
        return pl.BlockSpec(shape, lambda i: (0, 0))

    turns = cosine.shape[0] // tile
    turn = pl.BlockSpec((tile, head // 2), lambda i: (lax.rem(jnp.maximum(i - 3, 0), turns), 0))
    comm = pltpu.VMEM((count * chunk, 2 * head), BF16)
    return pl.pallas_call(
        functools.partial(key_back_kernel, tiles, tile, chunk, own_rows),
        grid=(tiles + 3,),
        out_shape=(
            jax.ShapeDtypeStruct((rows, width), F32),
            jax.ShapeDtypeStruct((width, 2 * head + 128), BF16),
            jax.ShapeDtypeStruct(ffn_grads.shape[1:], F32),
            jax.ShapeDtypeStruct(ffn_grads.shape[1:], F32),
            jax.ShapeDtypeStruct(ffn_grads.shape[:0:-1], F32),
        ),
        in_specs=[pl.BlockSpec((tile, 2 * head), lambda i: (jnp.minimum(i, tiles - 1), 0)),
                  late(head), late(1), turn, turn, late(width), late(width), late(4 * head),
                  whole_block(gains.shape), whole_block(gain_key.shape), ANY]
        + [whole_block(a.shape) for a in (w_query, dg_query, dg_mid, dg_post, ffn_grads)],
        out_specs=(late(width), fixed((width, 2 * head + 128)), fixed(ffn_grads.shape[1:]), fixed(ffn_grads.shape[1:]),
                   fixed(ffn_grads.shape[:0:-1])),
        scratch_shapes=[
            pltpu.VMEM((width, 2 * head), F32), pltpu.VMEM((1, width), F32), pltpu.VMEM((1, head), F32),
            pltpu.VMEM((width, 2 * head), BF16), pltpu.SemaphoreType.DMA] + [comm] * 4 + [dma] * 7
        + [pltpu.SemaphoreType.REGULAR] * 2,
        compiler_params=pltpu.CompilerParams(
            collective_id=ident, has_side_effects=True, vmem_limit_bytes=56 * 2**20),
        name="key_back",
    )(d_kv, hat, inv, cosine, sine, x, d_middle, d_query, gains, gain_key, first, w_query, dg_query, dg_mid, dg_post, ffn_grads)


def scatter_kernel(chips, own_rows, x_ref, o_ref, near, pair, far, *sems):
    ss1, rs1, ss2, rs2 = sems
    ctx = lax.axis_size("ctx")
    me = lax.axis_index("dp") * ctx + lax.axis_index("ctx")
    core = lax.rem(me, 2)
    chip = lax.div(me, 2)
    bar = pltpu.get_barrier_semaphore()

    def device(d):
        return {"dp": lax.div(d, ctx), "ctx": lax.rem(d, ctx)}

    partner = device(2 * chip + 1 - core)
    pl.semaphore_signal(bar, inc=1, device_id=partner, device_id_type=MESH)
    for k in range(1, chips):
        other = lax.rem(chip + k, chips)
        pl.semaphore_signal(bar, inc=1, device_id=device(2 * other + core), device_id_type=MESH)
    pl.semaphore_wait(bar, chips)

    def block(d):
        return pl.ds(pl.multiple_of(d * own_rows, 16), own_rows)

    def within(k):
        q = lax.rem(chip + k, chips)
        return pltpu.make_async_remote_copy(
            x_ref.at[block(2 * q + 1 - core)], near.at[k], ss1.at[k], rs1.at[k], device_id=partner, device_id_type=MESH)

    def between(k):
        q = lax.rem(chip + k, chips)
        return pltpu.make_async_remote_copy(
            pair.at[k], far.at[k], ss2.at[k], rs2.at[k], device_id=device(2 * q + core), device_id_type=MESH)

    order = list(range(1, chips)) + [0]
    for k in order:
        within(k).start()
    for k in order:
        within(k).wait_recv()
        q = lax.rem(chip + k, chips)
        both = x_ref[block(2 * q + core), :].astype(F32) + near[k].astype(F32)
        if k > 0:
            pair[k] = both.astype(BF16)
            between(k).start()
        else:
            o_ref[...] = both
    for k in range(1, chips):
        between(k).wait_recv()
        o_ref[...] += far[k].astype(F32)
    for k in range(1, chips):
        between(k).wait_send()
    for k in order:
        within(k).wait_send()


def scatter(x, own_rows, ident):
    n = x.shape[0] // own_rows
    chips = n // 2
    cols = x.shape[1]
    buf = pltpu.VMEM((chips, own_rows, cols), BF16)
    vmem = pl.BlockSpec(memory_space=pltpu.VMEM)
    return pl.pallas_call(
        functools.partial(scatter_kernel, chips, own_rows),
        out_shape=jax.ShapeDtypeStruct((own_rows, cols), F32),
        in_specs=[vmem],
        out_specs=vmem,
        scratch_shapes=[buf] * 3 + [pltpu.SemaphoreType.DMA((chips,))] * 4,
        compiler_params=pltpu.CompilerParams(
            collective_id=ident, has_side_effects=True, vmem_limit_bytes=40 * 2**20),
        name="scatter",
    )(x)


def shards(tokens, segments, cotangent, w_query, w_key, w_value, w_out, w_gate, w_up, w_down,
           g_input, g_post_attn, g_pre_ffn, g_post_ffn, g_query, g_key):
    batches, seq_local, _, size, width = tokens.shape
    head = w_key.shape[1]
    groups = batches * seq_local
    per_group = 2 * size
    rows = groups * per_group
    ctx = lax.axis_size("ctx")
    length = per_group * ctx
    rank = lax.axis_index("ctx")
    shared = ("dp", "ctx")
    own_rows = g_input.shape[0]
    hidden = w_gate.shape[1]

    def column(gain):
        return jnp.pad(gain, (0, own_rows - gain.shape[0]))[:, None]

    own_ids = segments.reshape(groups, 2, size)
    id_rows = own_ids.size // 128
    ids = jnp.pad(own_ids.reshape(id_rows, 128), ((0, -id_rows % 16), (0, 0)))
    extra = jnp.concatenate(
        [column(g) for g in (g_input, g_post_attn, g_pre_ffn, g_post_ffn, g_query, g_key)], axis=1)
    extra = jnp.pad(extra, ((0, 0), (0, 128 - extra.shape[1])))

    def rows_of_16(w):
        return jnp.pad(w, ((0, -own_rows % 16), (0, 0)))

    first, line, ids = first_gather(
        rows_of_16(jnp.concatenate([w_query, w_key, w_value, extra], axis=1)),
        rows_of_16(jnp.concatenate([w_query, w_out.T], axis=1)), ids, width // own_rows, 5)
    first = first[:, :own_rows].reshape(width, -1)
    line = line[:own_rows].reshape(own_rows, 4, 2, head).transpose(2, 0, 1, 3).reshape(2, own_rows, 4 * head)
    side = first[:, 3 * head :]
    gain_cols = side[:, :8].astype(F32)
    gain_rows = gain_cols.T
    gain_input = gain_rows[0]
    short = g_query.shape[0]
    gain_query, gain_key = (
        gain_cols[:, i].reshape(-1, own_rows)[:, :short].reshape(-1) for i in (4, 5))

    wide = wide_of(hidden)
    second = jnp.concatenate(
        [line[1]] + [jnp.pad(w, ((0, 0), (0, wide - hidden))) for w in (w_gate, w_up, w_down.T)], axis=1)
    weights = lax.all_gather(second, shared, axis=0, tiled=True)

    offsets = rank * size + jnp.arange(size, dtype=jnp.int32)
    position = jnp.concatenate([offsets, length - 1 - offsets]).astype(F32)
    cosine, sine = angles(position, head // 2, head)

    x_rows = tokens.reshape(rows, width)
    dy_rows = cotangent.reshape(rows, width)
    queries, q_hat, q_scale, k_hat, k_scale, heads_own, log_mass, kv, heads_all = attention(
        x_rows, first, gain_rows, gain_query[None], gain_key[None], cosine, sine, own_ids[..., None], ids, length, 0)

    line, heads_all = lax.optimization_barrier((line[0], heads_all))
    query_full = lax.all_gather(line, shared, axis=0, tiled=True)
    attn, hidden_two, gate, up, ffn_out = ffn_forward(x_rows, heads_all, gain_rows, weights, hidden, 1)
    output, d_gain_post_ffn, grad_ffn, d_two = ffn_backward(
        x_rows, attn, dy_rows, ffn_out, hidden_two, gate, up, gain_rows, weights, 2)
    grad_ffn = lax.psum_scatter(grad_ffn, shared, scatter_dimension=1, tiled=True)
    d_middle, d_heads, delta, d_gain_mid, grad_out_t = middle_back(
        x_rows, attn, dy_rows, d_two, heads_own, gain_rows, weights)

    d_q_all, d_kv, d_gain_query, grad_qo = attention_back(
        queries, d_heads, log_mass, delta, own_ids[:, :, None, :], ids, q_hat, q_scale, cosine, sine, x_rows, gain_rows,
        gain_query[None], grad_out_t, kv, 4)
    grad_qo = lax.psum_scatter(grad_qo, shared, scatter_dimension=0, tiled=True).astype(F32)
    d_tokens, last, grad_gate, grad_up, grad_down = key_back(
        d_kv, k_hat, k_scale, cosine, sine, x_rows, d_middle, d_q_all, gain_rows, gain_key[None],
        first, query_full, d_gain_query, d_gain_mid, d_gain_post_ffn, grad_ffn, own_rows, 3)
    if own_rows % 16 == 0:
        last = scatter(last, own_rows, 7)
    else:
        last = lax.psum_scatter(last, shared, scatter_dimension=0, tiled=True).astype(F32)
    g = last[:, 2 * head :]
    return (
        output.reshape(tokens.shape),
        d_tokens.reshape(tokens.shape),
        grad_qo[:, :head],
        last[:, :head],
        last[:, head : 2 * head],
        grad_qo[:, head:].T,
        grad_gate,
        grad_up,
        grad_down,
        g[:, 0],
        g[:, 1],
        g[:, 2],
        g[:, 3],
        g[:short, 4],
        g[:short, 5],
    )


def solution(mesh):
    shared = ("dp", "ctx")
    rows = P(None, "dp", None, "ctx", None)
    weights = (
        P(shared, "tp"), P(shared, None), P(shared, None), P("tp", shared),
        P(shared, "tp"), P(shared, "tp"), P("tp", shared),
    )
    gains = (P(shared),) * 6
    return jax.shard_map(
        shards,
        mesh=mesh,
        in_specs=(rows, P(None, "dp", None, "ctx"), rows) + weights + gains,
        out_specs=(rows, rows) + weights + gains,
        check_vma=False,
    )
```

```python
import functools

import jax
import jax.numpy as jnp
from jax import lax
from jax.experimental import pallas as pl
from jax.experimental.pallas import tpu as pltpu
from jax.sharding import PartitionSpec as P

EPS = 1e-06
THETA = 1000000.0
SCALE = 0.0625
NEGATIVE = -1e30
BF16 = jnp.bfloat16
F32 = jnp.float32
MESH = pl.DeviceIdType.MESH
NN = (((1,), (0,)), ((), ()))
NT = (((1,), (1,)), ((), ()))
TN = (((0,), (0,)), ((), ()))


def dot(a, b, dims=NN):
    return lax.dot_general(a, b, dims, preferred_element_type=F32)


def cost(us):
    return pl.CostEstimate(flops=int(us * 1.1e9), bytes_accessed=0, transcendentals=0)


def barrier_line(z):
    bar = pltpu.get_barrier_semaphore()

    @pl.when(z > 0)
    def _():
        pl.semaphore_signal(bar, inc=1, device_id={"tp": z - 1}, device_id_type=MESH)

    @pl.when(z < 3)
    def _():
        pl.semaphore_signal(bar, inc=1, device_id={"tp": z + 1}, device_id_type=MESH)

    pl.semaphore_wait(bar, jnp.where((z == 0) | (z == 3), 1, 2))


def block_starts(half, t, blocks, rank):
    if half == 0:
        return t
    return jnp.where(t < blocks, t, t + rank + 1)


def angles(position, half_size, full_size):
    frequency = THETA ** (-2.0 * jnp.arange(half_size, dtype=F32) / full_size)
    turned = position[:, None] * frequency[None, :]
    return (jnp.cos(turned), jnp.sin(turned))


def rotate(tensor, cosine, sine):
    half_size = tensor.shape[-1] // 2
    a = tensor[..., :half_size]
    b = tensor[..., half_size:]
    return jnp.concatenate([a * cosine - b * sine, b * cosine + a * sine], axis=-1)


def norm_parts(values):
    inv = lax.rsqrt(jnp.mean(values * values, axis=-1, keepdims=True) + EPS)
    return (values * inv, inv)


def norm_back(upstream, normalized, inv, gain):
    d_norm = upstream * (1.0 + gain)
    d_values = inv * (d_norm - normalized * jnp.mean(d_norm * normalized, axis=-1, keepdims=True))
    return (d_values, jnp.sum(upstream * normalized, axis=0))


def gelu_tanh(values):
    return jax.nn.gelu(values, approximate=True)


class LineSum:
    def __init__(self, count, chunk, slots, own, near, far, out, sems):
        self.count, self.chunk, self.slots = count, chunk, slots
        self.own, self.near, self.far, self.out = own, near, far, out
        self.sems = sems
        self.z = z = lax.axis_index("tp")
        self.hub = (z == 1) | (z == 2)
        self.leaf = (z == 0) | (z == 3)
        self.other_hub = jnp.where(z == 1, 2, 1)
        self.my_hub = jnp.where(z == 0, 1, 2)
        self.my_leaf = jnp.where(z == 1, 0, 3)

    def slot(self, c):
        return pl.ds(pl.multiple_of(lax.rem(c, self.slots) * self.chunk, self.chunk), self.chunk)

    def rows(self, c):
        return pl.ds(pl.multiple_of(c * self.chunk, self.chunk), self.chunk)

    def inwards(self, c):
        return pltpu.make_async_remote_copy(
            self.own.at[self.slot(c)], self.near.at[self.slot(c)], self.sems[0].at[c], self.sems[1].at[c],
            device_id={"tp": self.my_hub}, device_id_type=MESH)

    def across(self, c):
        return pltpu.make_async_remote_copy(
            self.own.at[self.slot(c)], self.far.at[self.slot(c)], self.sems[2].at[c], self.sems[3].at[c],
            device_id={"tp": self.other_hub}, device_id_type=MESH)

    def outwards(self, c):
        return pltpu.make_async_remote_copy(
            self.far.at[self.slot(c)], self.out.at[self.rows(c)], self.sems[4].at[c], self.sems[5].at[c],
            device_id={"tp": self.my_leaf}, device_id_type=MESH)

    def store(self, c):
        return pltpu.make_async_copy(self.far.at[self.slot(c)], self.out.at[self.rows(c)], self.sems[6].at[c])

    def put(self, c, value):
        ring = self.slots < self.count
        if ring:
            @pl.when(c >= self.slots)
            def _():
                @pl.when(self.leaf)
                def _():
                    self.inwards(c - self.slots).wait_send()

                @pl.when(self.hub)
                def _():
                    self.across(c - self.slots).wait_send()

        self.own[self.slot(c), :] = value

        @pl.when(self.leaf)
        def _():
            if ring:
                @pl.when(c >= self.slots)
                def _():
                    pl.semaphore_wait(self.sems[7], 1)
            self.inwards(c).start()

    def pair(self, c):
        ring = self.slots < self.count

        @pl.when(self.hub)
        def _():
            self.inwards(c).wait_recv()
            at = self.slot(c)
            self.own[at, :] = (self.own[at, :].astype(F32) + self.near[at, :].astype(F32)).astype(BF16)
            if ring:
                @pl.when(c < self.count - self.slots)
                def _():
                    pl.semaphore_signal(self.sems[7], inc=1, device_id={"tp": self.my_leaf}, device_id_type=MESH)

                @pl.when(c >= self.slots)
                def _():
                    pl.semaphore_wait(self.sems[8], 1)
            self.across(c).start()

    def total(self, c):
        @pl.when(self.hub)
        def _():
            self.across(c).wait_recv()
            at = self.slot(c)
            self.far[at, :] = (self.own[at, :].astype(F32) + self.far[at, :].astype(F32)).astype(BF16)
            self.outwards(c).start()
            self.store(c).start()

    def retire(self, c):
        @pl.when(self.hub)
        def _():
            self.outwards(c).wait_send()
            self.store(c).wait()
            if self.slots < self.count:
                @pl.when(c < self.count - self.slots)
                def _():
                    pl.semaphore_signal(self.sems[8], inc=1, device_id={"tp": self.other_hub}, device_id_type=MESH)

    def finish(self):
        first = max(0, self.count - self.slots)

        @pl.when(self.leaf)
        def _():
            for c in range(self.count):
                self.outwards(c).wait_recv()
            for c in range(first, self.count):
                self.inwards(c).wait_send()

        @pl.when(self.hub)
        def _():
            for c in range(first, self.count):
                self.across(c).wait_send()


def line_sum_scratch(count, chunk, slots, cols):
    dma = pltpu.SemaphoreType.DMA((count,))
    regular = pltpu.SemaphoreType.REGULAR
    return [pltpu.VMEM((slots * chunk, cols), BF16)] * 3 + [dma] * 7 + [regular] * 2


def gelu_parts(v):
    c = 0.7978845608028654
    square = v * v
    t = jnp.tanh(v * (c + (c * 0.044715) * square))
    half = 0.5 + 0.5 * t
    value = v * half
    slope = half + (0.5 * v) * (1.0 - t * t) * (c + (3.0 * c * 0.044715) * square)
    return value, slope


def column_parts(cols):
    middle = -(-cols // 256) * 128
    return [(0, middle), (middle, cols)] if middle < cols else [(0, cols)]


def middle_of(x, attn, gain_post_attn):
    hat, inv = norm_parts(attn.astype(F32))
    return x.astype(F32) + hat * (1.0 + gain_post_attn), hat, inv


def load_ffn_weights(weights, refs, sem):
    wide = refs[0].shape[1]
    base = weights.shape[1] - 3 * wide
    return [
        pltpu.make_async_copy(weights.at[:, pl.ds(base + j * wide, wide)], ref, sem.at[j])
        for j, ref in enumerate(refs)
    ]


def ffn_forward_kernel(tiles, tile, chunk, hidden, x_ref, h_ref, gain_ref, w_ref,
                       attn_ref, two_ref, gate_ref, up_ref, out_ref, wo_ref, wg_ref, wu_ref, wd_ref, w_sem, own, near, far, *sems):
    i = pl.program_id(0)
    per = tile // chunk
    line = LineSum(tiles * per, chunk, tiles * per, own, near, far, out_ref, sems)
    head = wo_ref.shape[1] // 4

    @pl.when(i == 0)
    def _():
        copies = load_ffn_weights(w_ref, (wg_ref, wu_ref, wd_ref), w_sem)
        copies.append(pltpu.make_async_copy(w_ref.at[:, pl.ds(0, 4 * head)], wo_ref, w_sem.at[3]))
        for copy in copies:
            copy.start()
        barrier_line(line.z)
        for copy in copies:
            copy.wait()

    attn = dot(h_ref[...], wo_ref[...], NT).astype(BF16)
    attn_ref[...] = attn
    middle, _, _ = middle_of(x_ref[...], attn, gain_ref[1:2, :])
    hat, _ = norm_parts(middle)
    two = (hat * (1.0 + gain_ref[2:3, :])).astype(BF16)
    two_ref[...] = two
    part = None
    for a, b in column_parts(hidden):
        gate = dot(two, wg_ref[:, a:b])
        up = dot(two, wu_ref[:, a:b])
        gate_ref[:, a:b] = gate.astype(BF16)
        up_ref[:, a:b] = up.astype(BF16)
        value, _ = gelu_parts(gate)
        more = dot((value * up).astype(BF16), wd_ref[:, a:b], NT)
        part = more if part is None else part + more
    for j in range(per):
        line.put(i * per + j, part[j * chunk : (j + 1) * chunk].astype(BF16))

    @pl.when(i >= 1)
    def _():
        for j in range(per):
            line.pair((i - 1) * per + j)

    @pl.when(i >= 2)
    def _():
        for j in range(per):
            line.total((i - 2) * per + j)

    @pl.when(i == tiles - 1)
    def _():
        last = tiles * per
        for j in range(per):
            line.pair(last - per + j)
        for c in range(max(0, last - 2 * per), last):
            line.total(c)
        for c in range(last):
            line.retire(c)
        line.finish()


def whole_block(shape):
    return pl.BlockSpec(shape, lambda i: (0,) * len(shape), pipeline_mode=pl.Buffered(1))


def tile_block(tile, cols):
    return pl.BlockSpec((tile, cols), lambda i: (i, 0))


ANY = pl.BlockSpec(memory_space=pl.ANY)


def wide_of(hidden):
    return -(-hidden // 128) * 128


def ffn_forward(x, heads, gains, weights, hidden, ident):
    rows, width = x.shape
    all_heads = heads.shape[1]
    tile, chunk = 256, 128
    tiles = rows // tile
    count = rows // chunk
    wide = wide_of(hidden)
    return pl.pallas_call(
        functools.partial(ffn_forward_kernel, tiles, tile, chunk, hidden),
        grid=(tiles,),
        out_shape=(
            jax.ShapeDtypeStruct((rows, width), BF16),
            jax.ShapeDtypeStruct((rows, width), BF16),
            jax.ShapeDtypeStruct((rows, hidden), BF16),
            jax.ShapeDtypeStruct((rows, hidden), BF16),
            jax.ShapeDtypeStruct((rows, width), BF16),
        ),
        in_specs=[
            tile_block(tile, width),
            tile_block(tile, all_heads),
            whole_block(gains.shape),
            ANY,
        ],
        out_specs=(tile_block(tile, width), tile_block(tile, width), tile_block(tile, hidden), tile_block(tile, hidden), ANY),
        scratch_shapes=[pltpu.VMEM((width, all_heads), BF16)] + [pltpu.VMEM((width, wide), BF16)] * 3
        + [pltpu.SemaphoreType.DMA((4,))]
        + line_sum_scratch(count, chunk, count, width),
        compiler_params=pltpu.CompilerParams(
            collective_id=ident, has_side_effects=True, vmem_limit_bytes=60 * 2**20),
        cost_estimate=cost(140),
        name="ffn_forward",
    )(x, heads, gains, weights)


def ffn_backward_kernel(tiles, tile, chunk, slots, hidden, x_ref, attn_ref, dy_ref, ffn_ref, two_ref, gate_ref, up_ref,
                        gain_ref, w_ref,
                        y_ref, dgain_ref, grad_ref, out_ref, wg_ref, wu_ref, wd_ref, w_sem,
                        acc_g, acc_u, acc_d, keep_g, keep_u, keep_h, stage, stage_sem, own, near, far, *sems):
    i = pl.program_id(0)
    per = tile // chunk
    last = tiles * per
    line = LineSum(last, chunk, slots, own, near, far, out_ref, sems)

    @pl.when(i == 0)
    def _():
        copies = load_ffn_weights(w_ref, (wg_ref, wu_ref, wd_ref), w_sem)
        for copy in copies:
            copy.start()
        barrier_line(line.z)
        for acc in (acc_g, acc_u, acc_d, dgain_ref):
            acc[...] = jnp.zeros_like(acc)
        for copy in copies:
            copy.wait()

    middle, _, _ = middle_of(x_ref[...], attn_ref[...], gain_ref[1:2, :])
    hat, inv = norm_parts(ffn_ref[...].astype(F32))
    gain = gain_ref[3:4, :]
    y_ref[...] = (middle + hat * (1.0 + gain)).astype(BF16)
    d_ffn, d_gain = norm_back(dy_ref[...].astype(F32), hat, inv, gain)
    dgain_ref[...] += d_gain[None]
    d_ffn = d_ffn.astype(BF16)
    part = None
    for a, b in column_parts(hidden):
        d_hidden = dot(d_ffn, wd_ref[:, a:b])
        up = up_ref[:, a:b].astype(F32)
        value, slope = gelu_parts(gate_ref[:, a:b].astype(F32))
        keep_h[:, a:b] = (value * up).astype(BF16)
        d_gate = (d_hidden * up * slope).astype(BF16)
        d_up = (d_hidden * value).astype(BF16)
        keep_g[:, a:b] = d_gate
        keep_u[:, a:b] = d_up
        more = dot(d_gate, wg_ref[:, a:b], NT) + dot(d_up, wu_ref[:, a:b], NT)
        part = more if part is None else part + more
    for j in range(per):
        line.put(i * per + j, part[j * chunk : (j + 1) * chunk].astype(BF16))

    @pl.when(i >= 1)
    def _():
        for j in range(per):
            line.pair((i - 1) * per + j)

    acc_g[...] += dot(two_ref[...], keep_g[...], TN)
    acc_u[...] += dot(two_ref[...], keep_u[...], TN)
    acc_d[...] += dot(d_ffn, keep_h[...], TN)

    @pl.when(i >= 2)
    def _():
        for j in range(per):
            line.total((i - 2) * per + j)

    @pl.when(i >= 3)
    def _():
        for j in range(per):
            line.retire((i - 3) * per + j)

    @pl.when(i == tiles - 1)
    def _():
        for j in range(per):
            line.pair(last - per + j)
        step = stage.shape[1]
        count = acc_g.shape[0] // step

        def piece(acc, out, k, at):
            @pl.when(k >= 2)
            def _():
                pltpu.make_async_copy(stage.at[at], out.at[pl.ds(0, step)], stage_sem.at[at]).wait()
            rows = pl.ds(pl.multiple_of(k * step, step), step)
            stage[at] = acc[rows, :].astype(BF16)
            pltpu.make_async_copy(stage.at[at], out.at[rows], stage_sem.at[at]).start()

        for acc, out in ((acc_g, grad_ref.at[0]), (acc_u, grad_ref.at[1]), (acc_d, grad_ref.at[2])):
            def pieces(k, _):
                piece(acc, out, k, lax.rem(k, 2))
                return 0

            lax.fori_loop(0, count, pieces, 0)
            for at in range(2):
                pltpu.make_async_copy(stage.at[at], out.at[pl.ds(0, step)], stage_sem.at[at]).wait()
            if acc is acc_g:
                for c in range(max(0, last - 2 * per), last - per):
                    line.total(c)
            if acc is acc_u:
                for c in range(last - per, last):
                    line.total(c)
        for c in range(max(0, last - 3 * per), last):
            line.retire(c)
        line.finish()


def ffn_backward(x, attn, dy, ffn, two, gate, up, gains, weights, ident):
    rows, width = x.shape
    hidden = gate.shape[1]
    wide = wide_of(hidden)
    tile, chunk = 256, 128
    tiles = rows // tile
    count = rows // chunk
    slots = min(count, 6)
    step = 144
    acc = pltpu.VMEM((width, hidden), F32)
    keep = pltpu.VMEM((tile, hidden), BF16)
    return pl.pallas_call(
        functools.partial(ffn_backward_kernel, tiles, tile, chunk, slots, hidden),
        grid=(tiles,),
        out_shape=(
            jax.ShapeDtypeStruct((rows, width), BF16),
            jax.ShapeDtypeStruct((1, width), F32),
            jax.ShapeDtypeStruct((3, width, hidden), BF16),
            jax.ShapeDtypeStruct((rows, width), BF16),
        ),
        in_specs=[tile_block(tile, width)] * 5 + [tile_block(tile, hidden)] * 2
        + [whole_block(gains.shape), ANY],
        out_specs=(tile_block(tile, width), pl.BlockSpec((1, width), lambda i: (0, 0)), ANY, ANY),
        scratch_shapes=[pltpu.VMEM((width, wide), BF16)] * 3 + [pltpu.SemaphoreType.DMA((3,))] + [acc] * 3 + [keep] * 3
        + [pltpu.VMEM((2, step, hidden), BF16), pltpu.SemaphoreType.DMA((2,))]
        + line_sum_scratch(count, chunk, slots, width),
        compiler_params=pltpu.CompilerParams(
            collective_id=ident, has_side_effects=True, vmem_limit_bytes=63 * 2**20),
        cost_estimate=cost(145),
        name="ffn_backward",
    )(x, attn, dy, ffn, two, gate, up, gains, weights)


def middle_back_kernel(x_ref, attn_ref, dy_ref, d2_ref, h_ref, gain_ref, w_ref,
                       dm_ref, dh_ref, delta_ref, dgain_ref, go_ref, acc, wo_ref, w_sem):
    i = pl.program_id(0)

    @pl.when(i == 0)
    def _():
        head = wo_ref.shape[1]
        at = pl.multiple_of(lax.axis_index("tp") * head, head)
        copy = pltpu.make_async_copy(w_ref.at[:, pl.ds(at, head)], wo_ref, w_sem)
        copy.start()
        copy.wait()
        acc[...] = jnp.zeros_like(acc)
        dgain_ref[...] = jnp.zeros_like(dgain_ref)

    middle, attn_hat, attn_inv = middle_of(x_ref[...], attn_ref[...], gain_ref[1:2, :])
    hat, inv = norm_parts(middle)
    d_part, d_gain = norm_back(d2_ref[...].astype(F32), hat, inv, gain_ref[2:3, :])
    dgain_ref[1:2, :] += d_gain[None]
    d_middle = dy_ref[...].astype(F32) + d_part
    dm_ref[...] = d_middle
    d_attn, d_gain = norm_back(d_middle, attn_hat, attn_inv, gain_ref[1:2, :])
    dgain_ref[0:1, :] += d_gain[None]
    d_attn = d_attn.astype(BF16)
    d_heads = dot(d_attn, wo_ref[...]).astype(BF16)
    dh_ref[...] = d_heads
    heads = h_ref[...]
    delta_ref[...] = jnp.sum(d_heads.astype(F32) * heads.astype(F32), axis=1, keepdims=True)
    acc[...] += dot(d_attn, heads, TN)

    @pl.when(i == pl.num_programs(0) - 1)
    def _():
        go_ref[...] = acc[...].astype(BF16)


def middle_back(x, attn, dy, d_two, heads, gains, weights):
    rows, width = x.shape
    head = heads.shape[1]
    tile = 256
    return pl.pallas_call(
        middle_back_kernel,
        grid=(rows // tile,),
        out_shape=(
            jax.ShapeDtypeStruct((rows, width), F32),
            jax.ShapeDtypeStruct((rows, head), BF16),
            jax.ShapeDtypeStruct((rows, 1), F32),
            jax.ShapeDtypeStruct((2, width), F32),
            jax.ShapeDtypeStruct((width, head), BF16),
        ),
        in_specs=[tile_block(tile, width)] * 4 + [tile_block(tile, head)] + [whole_block(gains.shape), ANY],
        out_specs=(
            tile_block(tile, width), tile_block(tile, head), tile_block(tile, 1),
            pl.BlockSpec((2, width), lambda i: (0, 0)), pl.BlockSpec((width, head), lambda i: (0, 0)),
        ),
        scratch_shapes=[pltpu.VMEM((width, head), F32), pltpu.VMEM((width, head), BF16), pltpu.SemaphoreType.DMA],
        compiler_params=pltpu.CompilerParams(vmem_limit_bytes=48 * 2**20),
        cost_estimate=cost(19),
        name="middle_back",
    )(x, attn, dy, d_two, heads, gains, weights)


class LineGather:
    def __init__(self, whole, tile, width, sems):
        self.whole, self.tile, self.width, self.sems = whole, tile, width, sems
        self.z = lax.axis_index("tp")

    def place(self, src, t):
        return self.whole.at[
            pl.ds(pl.multiple_of(t * self.tile, self.tile), self.tile),
            pl.ds(pl.multiple_of(src * self.width, self.width), self.width)]

    def send(self, src, t, hop, way):
        ss, rs = self.sems[:2] if way > 0 else self.sems[2:]
        place = self.place(src, t)
        return pltpu.make_async_remote_copy(
            place, place, ss.at[hop, t], rs.at[hop, t],
            device_id={"tp": self.z + way}, device_id_type=MESH)

    def going(self, hop, way):
        src = self.z - way * hop
        return src, (self.z + way >= 0) & (self.z + way <= 3) & (src >= 0) & (src <= 3)

    def coming(self, hop, way):
        src = self.z - way * (hop + 1)
        return src, (src >= 0) & (src <= 3)

    def forward(self, t, hop):
        for way in (1, -1):
            if hop > 0:
                self.wait(t, hop - 1, way)
            src, ok = self.going(hop, way)

            @pl.when(ok)
            def _():
                self.send(src, t, hop, way).start()

    def wait(self, t, hop, way):
        src, ok = self.coming(hop, way)

        @pl.when(ok)
        def _():
            self.send(src, t, hop, way).wait_recv()

    def arrived(self, t):
        for way in (1, -1):
            self.wait(t, 2, way)

    def finish(self, tiles):
        for hop in range(3):
            for way in (1, -1):
                src, ok = self.going(hop, way)

                @pl.when(ok)
                def _():
                    def one(t, _):
                        self.send(src, t, hop, way).wait_send()
                        return 0

                    lax.fori_loop(0, tiles, one, 0)


class KeyGather(LineGather):
    def __init__(self, block, chips, sems):
        self.block, self.chips, self.sems = block, chips, sems
        self.z = lax.axis_index("tp")

    def tile_of(self, g, half, k):
        return (2 * g + half) * (self.chips - 1) + k - 1

    def place(self, src, t):
        pair, k = divmod(t, self.chips - 1)
        return self.quarter(pair // 2, pair % 2, k + 1, src)

    def quarter(self, g, half, k, src, own=False):
        ref, start, size = self.block(g, half, k, own)
        rows = size // 4
        return ref.at[pl.ds(pl.multiple_of(start + src * rows, rows), rows)]

    def finish(self, tiles):
        for hop in range(3):
            for way in (1, -1):
                src, ok = self.going(hop, way)

                @pl.when(ok)
                def _():
                    for t in range(tiles):
                        self.send(src, t, hop, way).wait_send()


class Shared:
    def __init__(self, over_dp):
        self.ctx = ctx = lax.axis_size("ctx")
        me = lax.axis_index("ctx")
        self.devices = ctx
        if over_dp:
            me = me + lax.axis_index("dp") * ctx
            self.devices = ctx * lax.axis_size("dp")
        self.over_dp = over_dp
        self.me = me
        self.chips = self.devices // 2
        self.core = lax.rem(me, 2)
        self.chip = lax.div(me, 2)

    def ident(self, device):
        if self.over_dp:
            return {"dp": lax.div(device, self.ctx), "ctx": lax.rem(device, self.ctx)}
        return {"ctx": device}

    def other(self, k):
        return 2 * lax.rem(self.chip + k + self.chips, self.chips) + self.core

    def partner(self):
        return self.me + 1 - 2 * self.core

    def greet(self, z):
        bar = pltpu.get_barrier_semaphore()
        for device in [self.partner()] + [self.other(k) for k in range(1, self.chips)]:
            pl.semaphore_signal(bar, inc=1, device_id=self.ident(device), device_id_type=MESH)

        @pl.when(z > 0)
        def _():
            pl.semaphore_signal(bar, inc=1, device_id={"tp": z - 1}, device_id_type=MESH)

        @pl.when(z < 3)
        def _():
            pl.semaphore_signal(bar, inc=1, device_id={"tp": z + 1}, device_id_type=MESH)

        pl.semaphore_wait(bar, self.chips + jnp.where((z == 0) | (z == 3), 1, 2))

    def copy(self, source, target, send, recv, device):
        return pltpu.make_async_remote_copy(
            source, target, send, recv, device_id=self.ident(device), device_id_type=MESH)


def first_gather_kernel(a_ref, b_ref, i_ref, all_ref, line_ref, ids_ref, lsem, ss1, rs1, ss2, rs2, si1, ri1, si2, ri2, *sems):
    group = Shared(True)
    line = LineGather(line_ref, b_ref.shape[0], b_ref.shape[1], sems)
    width = b_ref.shape[1]
    own = [
        pltpu.make_async_copy(b_ref, line_ref.at[:, pl.ds(pl.multiple_of(line.z * width, width), width)], lsem.at[0]),
        pltpu.make_async_copy(a_ref, all_ref.at[group.me], lsem.at[1]),
        pltpu.make_async_copy(i_ref, ids_ref.at[group.me], lsem.at[2]),
    ]
    for copy in own:
        copy.start()
    group.greet(line.z)
    arrays = ((a_ref, all_ref, ss1, rs1, ss2, rs2), (i_ref, ids_ref, si1, ri1, si2, ri2))

    def direct(n, k, incoming=False):
        ref, whole, ss, rs = arrays[n][:4]
        at = whole.at[group.other(-k)] if incoming else whole.at[group.me]
        return group.copy(ref, at, ss.at[k], rs.at[k], group.other(k))

    def inner(n, k, incoming=False):
        ref, whole, _, _, ss, rs = arrays[n]
        at = whole.at[group.other(-k)]
        if incoming:
            at = whole.at[group.other(-k) + 1 - 2 * group.core]
        return group.copy(ref if k == 0 else at, at, ss.at[k], rs.at[k], group.partner())

    both = range(2)
    for k in range(1, group.chips):
        for n in both:
            direct(n, k).start()
    own[0].wait()
    line.forward(0, 0)
    for n in both:
        inner(n, 0).start()
    for k in range(1, group.chips):
        if k < 3:
            line.forward(0, k)
        for n in both:
            direct(n, k, True).wait_recv()
            inner(n, k).start()
    for hop in range(min(3, group.chips), 3):
        line.forward(0, hop)
    for k in range(group.chips):
        for n in both:
            inner(n, k, True).wait_recv()
    line.arrived(0)
    for copy in own[1:]:
        copy.wait()
    for n in both:
        for k in range(1, group.chips):
            direct(n, k).wait_send()
        for k in range(group.chips):
            inner(n, k).wait_send()
    line.finish(1)


def first_gather(a, b, ids, devices, ident):
    dma = pltpu.SemaphoreType.DMA((devices // 2,))
    hop = pltpu.SemaphoreType.DMA((3, 1))
    return pl.pallas_call(
        first_gather_kernel,
        out_shape=(
            jax.ShapeDtypeStruct((devices,) + a.shape, a.dtype),
            jax.ShapeDtypeStruct((b.shape[0], 4 * b.shape[1]), b.dtype),
            jax.ShapeDtypeStruct((devices,) + ids.shape, ids.dtype),
        ),
        in_specs=[ANY] * 3,
        out_specs=(ANY,) * 3,
        scratch_shapes=[pltpu.SemaphoreType.DMA((3,))] + [dma] * 8 + [hop] * 4,
        compiler_params=pltpu.CompilerParams(collective_id=ident, has_side_effects=True),
        cost_estimate=cost(20),
        name="first_gather",
    )(a, b, ids)


def attention_kernel(groups, size, x_ref, w_ref, gain_ref, gq_ref, gk_ref, cos_ref, sin_ref, qs_ref, ks_ref,
                     q_ref, qhat_ref, qinv_ref, khat_ref, kinv_ref, heads_ref, log_ref, kv_out, all_out,
                     kv, whole, store_kv, store_all, ss1, rs1, ss2, rs2, *sems):
    head = q_ref.shape[1]
    length = kv.shape[1]
    id_rows = size // 128
    blocks = length // (2 * size)
    group = Shared(False)
    rank = group.me
    line = LineGather(whole, size, head, sems[:4])
    z = line.z
    tile = min(256, size)
    group.greet(z)

    def block(g, half, k, own):
        c = rank if own else group.other(-k)
        return kv.at[g], half * (length // 2) + c * size, size

    keys = KeyGather(block, group.chips, sems[4:])

    def place(g, half, c):
        return kv.at[g, pl.ds(pl.multiple_of(half * (length // 2) + c * size, size), size)]

    def direct(g, half, k, incoming=False):
        at = keys.quarter(g, half, k, z, own=not incoming)
        return group.copy(at, at, ss1.at[g, half, k], rs1.at[g, half, k], group.other(k))

    def inner(g, half, k, incoming=False):
        block = group.other(-k)
        at = place(g, half, block + 1 - 2 * group.core if incoming else block)
        return group.copy(at, at, ss2.at[g, half, k], rs2.at[g, half, k], group.partner())

    def project(g, half, u):
        rows = pl.ds((2 * g + half) * size + u * tile, tile)
        spot = pl.ds(half * size + u * tile, tile)
        cosine, sine = cos_ref[spot, :], sin_ref[spot, :]
        hat, _ = norm_parts(x_ref[rows, :].astype(F32))
        raw = dot((hat * (1.0 + gain_ref[0:1, :])).astype(BF16), w_ref[:, : 3 * head])
        hat, inv = norm_parts(raw[:, :head])
        qhat_ref[rows, :] = hat
        qinv_ref[rows, :] = inv
        q_ref[rows, :] = rotate(hat * (1.0 + gq_ref[...]), cosine, sine).astype(BF16)
        hat, inv = norm_parts(raw[:, head : 2 * head])
        khat_ref[rows, :] = hat
        kinv_ref[rows, :] = inv
        at = pl.ds(pl.multiple_of(half * (length // 2) + rank * size + u * tile, tile), tile)
        kv[g, at, :head] = rotate(hat * (1.0 + gk_ref[...]), cosine, sine).astype(BF16)
        kv[g, at, head:] = raw[:, 2 * head :].astype(BF16)

    def attend(g, half):
        row = lax.broadcasted_iota(jnp.int32, (size, size), 0)
        col = lax.broadcasted_iota(jnp.int32, (size, size), 1)
        rows = pl.ds((2 * g + half) * size, size)
        q = q_ref[rows, :] * jnp.asarray(SCALE, BF16)
        qseg = qs_ref[g, half]

        def part(block):
            at = pl.ds(pl.multiple_of(block * size, size), size)
            device = lax.axis_index("dp") * lax.axis_size("ctx") + lax.rem(block, blocks)
            ids = ks_ref[device, pl.ds((2 * g + lax.div(block, blocks)) * id_rows, id_rows), :]
            ids = jnp.concatenate([ids[j : j + 1] for j in range(id_rows)], axis=1)
            same = qseg == jnp.where(ids == 0, -1, ids)
            return dot(q, kv[g, at, :head], NT), kv[g, at, head:], same

        s, v, same = part(rank + half * blocks)
        order = (col <= row) if half == 0 else (col >= row)
        s = jnp.where((same & order) | (col == row), s, NEGATIVE)
        top = jnp.max(s, axis=1, keepdims=True)
        p = jnp.exp(s - top)
        mass = jnp.sum(p, axis=1, keepdims=True)
        acc = dot(p.astype(BF16), v)

        def step(t, carry):
            top, mass, acc = carry
            s, v, same = part(block_starts(half, t, blocks, rank))
            s = jnp.where(same, s, NEGATIVE)
            new = jnp.maximum(top, jnp.max(s, axis=1, keepdims=True))
            keep = jnp.exp(top - new)
            p = jnp.exp(s - new)
            mass = mass * keep + jnp.sum(p, axis=1, keepdims=True)
            return new, mass, acc * keep + dot(p.astype(BF16), v)

        count = rank if half == 0 else 2 * blocks - 1 - rank
        top, mass, acc = lax.fori_loop(0, count, step, (top, mass, acc))
        out = (acc / mass).astype(BF16)
        heads_ref[rows, :] = out
        whole[rows, pl.ds(pl.multiple_of(z * head, head), head)] = out
        log_ref[g, half] = top + jnp.log(mass)

    chips = range(1, group.chips)
    tiles = 2 * groups

    def exchange(t):
        for stage in (4, 3, 2, 1):
            if not 0 <= t - stage < tiles:
                continue
            g, half = divmod(t - stage, 2)
            for k in chips:
                spot = keys.tile_of(g, half, k)
                if stage == 1:
                    direct(g, half, k, True).wait_recv()
                if stage <= 3:
                    keys.forward(spot, stage - 1)
                else:
                    keys.arrived(spot)
                    inner(g, half, k).start()

    def hops(t):
        for hop in range(3):
            if 0 <= t - hop < tiles:
                line.forward(t - hop, hop)

    def keep(t):
        at = pl.ds(t * size, size)
        return pltpu.make_async_copy(whole.at[at], all_out.at[at], store_all.at[t])

    def save(g):
        return pltpu.make_async_copy(kv.at[g], kv_out.at[g], store_kv.at[g])

    for t in range(tiles):
        g, half = divmod(t, 2)
        for u in range(size // tile):
            project(g, half, u)
        for k in chips:
            direct(g, half, k).start()
        inner(g, half, 0).start()
        exchange(t)
    at_step = tiles
    for g in range(groups):
        while at_step < min(2 * g + 6, tiles + 4):
            exchange(at_step)
            at_step += 1
        for half in range(2):
            for k in range(group.chips):
                inner(g, half, k, True).wait_recv()
        save(g).start()
        for half in range(2):
            attend(g, half)
            if at_step < tiles + 4:
                exchange(at_step)
                at_step += 1
            hops(2 * g + half)
    for t in range(tiles, tiles + 2):
        hops(t)
    for t in range(tiles):
        line.arrived(t)
        keep(t).start()
    for g in range(groups):
        save(g).wait()
        for half in range(2):
            for k in chips:
                direct(g, half, k).wait_send()
            for k in range(group.chips):
                inner(g, half, k).wait_send()
    line.finish(tiles)
    keys.finish(tiles * (group.chips - 1))
    for t in range(tiles):
        keep(t).wait()


def attention(x, w, gains, gain_query, gain_key, cosine, sine, qseg, ids, length, ident):
    rows, width = x.shape
    groups, _, size, _ = qseg.shape
    head = gain_query.shape[1]
    chips = length // (4 * size)
    tiles = 2 * groups
    vmem = pl.BlockSpec(memory_space=pltpu.VMEM)
    dma = pltpu.SemaphoreType.DMA
    return pl.pallas_call(
        functools.partial(attention_kernel, groups, size),
        out_shape=(
            jax.ShapeDtypeStruct((rows, head), BF16),
            jax.ShapeDtypeStruct((rows, head), F32),
            jax.ShapeDtypeStruct((rows, 1), F32),
            jax.ShapeDtypeStruct((rows, head), F32),
            jax.ShapeDtypeStruct((rows, 1), F32),
            jax.ShapeDtypeStruct((rows, head), BF16),
            jax.ShapeDtypeStruct((groups, 2, size, 1), F32),
            jax.ShapeDtypeStruct((groups, length, 2 * head), BF16),
            jax.ShapeDtypeStruct((rows, 4 * head), BF16),
        ),
        in_specs=[vmem] * 9,
        out_specs=(vmem,) * 7 + (ANY, ANY),
        scratch_shapes=[
            pltpu.VMEM((groups, length, 2 * head), BF16), pltpu.VMEM((rows, 4 * head), BF16),
            dma((groups,)), dma((tiles,))] + [dma((groups, 2, chips))] * 4 + [dma((3, tiles))] * 4
        + [dma((3, tiles * (chips - 1)))] * 4,
        compiler_params=pltpu.CompilerParams(
            collective_id=ident, has_side_effects=True, vmem_limit_bytes=60 * 2**20),
        cost_estimate=cost(110),
        name="attention",
    )(x, w, gains, gain_query, gain_key, cosine, sine, qseg, ids)


class ResidentSum(LineSum):
    def outwards(self, c):
        return pltpu.make_async_remote_copy(
            self.out.at[self.rows(c)], self.out.at[self.rows(c)], self.sems[4].at[c], self.sems[5].at[c],
            device_id={"tp": self.my_leaf}, device_id_type=MESH)

    def total(self, c):
        @pl.when(self.hub)
        def _():
            self.across(c).wait_recv()
            at = self.rows(c)
            self.out[at, :] = (self.own[at, :].astype(F32) + self.far[at, :].astype(F32)).astype(BF16)
            self.outwards(c).start()

    def arrived(self, c):
        @pl.when(self.leaf)
        def _():
            self.outwards(c).wait_recv()

    def finish(self):
        @pl.when(self.leaf)
        def _():
            for c in range(self.count):
                self.inwards(c).wait_send()

        @pl.when(self.hub)
        def _():
            for c in range(self.count):
                self.across(c).wait_send()
                self.outwards(c).wait_send()


def turned(column, size):
    return jnp.transpose(jnp.broadcast_to(column, (size, 128)))[0:1, :]


def attention_back_kernel(groups, size, q_ref, do_ref, log_ref, delta_ref, qs_ref, ids_ref, hat_ref, inv_ref, cos_ref, sin_ref,
                          x_ref, gain_ref, gq_ref, go_ref, kv_hbm, all_out, dkv_ref, dgain_ref, grad_ref,
                          kv, dk, dv, part, near, pair, far, whole, acc, load, store, ss1, rs1, ss2, rs2, *sems):
    head = q_ref.shape[1]
    length = kv.shape[1]
    blocks = length // (2 * size)
    id_rows = size // 128
    tiles = 2 * groups
    group = Shared(False)
    rank, core = group.me, group.core
    line = LineGather(whole, size, head, sems)
    z = line.z
    others = range(1, group.chips)
    order = list(others) + [0]

    def fetch(g):
        return pltpu.make_async_copy(kv_hbm.at[g], kv.at[g], load.at[g])

    for g in range(groups):
        fetch(g).start()
    group.greet(z)
    acc[...] = jnp.zeros_like(acc)
    dgain_ref[...] = jnp.zeros_like(dgain_ref)

    def rows_of(half, device):
        return pl.ds(pl.multiple_of(half * (length // 2) + device * size, size), size)

    def within(g, half, k):
        to = group.other(k) + 1 - 2 * core
        return group.copy(
            part.at[g, rows_of(half, to)], near.at[g, half, k], ss1.at[g, half, k], rs1.at[g, half, k], group.partner())

    def between(g, half, k):
        return group.copy(
            pair.at[g, half, k - 1], far.at[g, half, k - 1], ss2.at[g, half, k], rs2.at[g, half, k], group.other(k))

    def both_cores(g):
        for half in range(2):
            for k in order:
                within(g, half, k).wait_recv()
                total = part[g, rows_of(half, group.other(k)), :].astype(F32) + near[g, half, k].astype(F32)
                if k > 0:
                    pair[g, half, k - 1] = total.astype(BF16)
                    between(g, half, k).start()
                else:
                    dkv_ref[pl.ds((2 * g + half) * size, size), :] = total.astype(BF16)

    def all_chips(g):
        for half in range(2):
            at = pl.ds((2 * g + half) * size, size)
            total = dkv_ref[at, :].astype(F32)
            for k in others:
                between(g, half, k).wait_recv()
                total = total + far[g, half, k - 1].astype(F32)
            dkv_ref[at, :] = total.astype(BF16)

    def hops(t):
        for hop in range(3):
            if 0 <= t - hop < tiles:
                line.forward(t - hop, hop)

    def attend(g, half):
        row = lax.broadcasted_iota(jnp.int32, (size, size), 0)
        col = lax.broadcasted_iota(jnp.int32, (size, size), 1)
        own = pl.ds((2 * g + half) * size, size)
        q = q_ref[own, :] * jnp.asarray(SCALE, BF16)
        do = do_ref[own, :]
        qseg = qs_ref[g, half]
        log_mass = turned(log_ref[g, half], size)
        delta = turned(delta_ref[own, :], size)

        def step_of(block, mine):
            at = pl.ds(pl.multiple_of(block * size, size), size)
            k = kv[g, at, :head]
            v = kv[g, at, head:]
            device = lax.axis_index("dp") * lax.axis_size("ctx") + lax.rem(block, blocks)
            ids = ids_ref[device, pl.ds((2 * g + lax.div(block, blocks)) * id_rows, id_rows), :]
            ids = jnp.concatenate([ids[j : j + 1] for j in range(id_rows)], axis=1)
            ids = jnp.transpose(jnp.broadcast_to(jnp.where(ids == 0, -1, ids), (8, size)))[:, 0:1]
            allowed = ids == qseg
            if mine:
                ahead = (row <= col) if half == 0 else (row >= col)
                allowed = (allowed & ahead) | (col == row)
            s = jnp.where(allowed, dot(k, q, NT), NEGATIVE)
            p = jnp.exp(s - log_mass)
            ds = (p * (dot(v, do, NT) - delta)).astype(BF16)
            dv[at, :] += dot(p.astype(BF16), do)
            dk[at, :] += dot(ds, q)
            return dot(ds, k, TN)

        def step(t, dq):
            return dq + step_of(block_starts(half, t, blocks, rank), False)

        dq = step_of(rank + half * blocks, True)
        count = rank if half == 0 else 2 * blocks - 1 - rank
        dq = SCALE * lax.fori_loop(0, count, step, dq)
        spot = pl.ds(half * size, size)
        d_rot = rotate(dq, cos_ref[spot, :], -sin_ref[spot, :])
        d_raw, d_gain = norm_back(d_rot, hat_ref[own, :], inv_ref[own, :], gq_ref[...])
        dgain_ref[...] += d_gain[None]
        whole[own, pl.ds(pl.multiple_of(z * head, head), head)] = d_raw.astype(BF16)

    def weight_gradient(t):
        own = pl.ds(t * size, size)
        hat, _ = norm_parts(x_ref[own, :].astype(F32))
        one = (hat * (1.0 + gain_ref[0:1, :])).astype(BF16)
        acc[...] += dot(one, whole[own, pl.ds(pl.multiple_of(z * head, head), head)], TN)

    def keep(t):
        at = pl.ds(t * size, size)
        return pltpu.make_async_copy(whole.at[at], all_out.at[at], store.at[t])

    for g in range(groups):
        fetch(g).wait()
        dk[...] = jnp.zeros_like(dk)
        dv[...] = jnp.zeros_like(dv)
        for half in range(2):
            attend(g, half)
            hops(2 * g + half)
            if half == 0 and g > 0:
                both_cores(g - 1)
        part[g, :, :head] = dk[...].astype(BF16)
        part[g, :, head:] = dv[...].astype(BF16)
        for half in range(2):
            for k in order:
                within(g, half, k).start()
        for half in range(2):
            weight_gradient(2 * g + half)
        if g > 0:
            all_chips(g - 1)
    hops(tiles)
    both_cores(groups - 1)
    hops(tiles + 1)
    grad_ref[:, :head] = acc[...].astype(BF16)
    grad_ref[:, head:] = go_ref[...]
    for t in range(tiles):
        line.arrived(t)
        keep(t).start()
    all_chips(groups - 1)
    for g in range(groups):
        for half in range(2):
            for k in others:
                between(g, half, k).wait_send()
            for k in order:
                within(g, half, k).wait_send()
    line.finish(tiles)
    for t in range(tiles):
        keep(t).wait()


def attention_back(q, d_heads, log_mass, delta, qseg, ids, hat, inv, cosine, sine, x, gains, gain_query, grad_o, kv, ident):
    rows, head = q.shape
    width = x.shape[1]
    groups, length, _ = kv.shape
    size = rows // (2 * groups)
    chips = length // (4 * size)
    tiles = 2 * groups
    vmem = pl.BlockSpec(memory_space=pltpu.VMEM)
    dma = pltpu.SemaphoreType.DMA
    return pl.pallas_call(
        functools.partial(attention_back_kernel, groups, size),
        out_shape=(
            jax.ShapeDtypeStruct((rows, 4 * head), BF16),
            jax.ShapeDtypeStruct((rows, 2 * head), BF16),
            jax.ShapeDtypeStruct((1, head), F32),
            jax.ShapeDtypeStruct((width, 2 * head), BF16),
        ),
        in_specs=[vmem] * 14 + [ANY],
        out_specs=(ANY, vmem, vmem, vmem),
        scratch_shapes=[
            pltpu.VMEM((groups, length, 2 * head), BF16),
            pltpu.VMEM((length, head), F32), pltpu.VMEM((length, head), F32),
            pltpu.VMEM((groups, length, 2 * head), BF16),
            pltpu.VMEM((groups, 2, chips, size, 2 * head), BF16),
            pltpu.VMEM((groups, 2, chips - 1, size, 2 * head), BF16),
            pltpu.VMEM((groups, 2, chips - 1, size, 2 * head), BF16),
            pltpu.VMEM((rows, 4 * head), BF16),
            pltpu.VMEM((width, head), F32),
            dma((groups,)), dma((tiles,))] + [dma((groups, 2, chips))] * 4 + [dma((3, tiles))] * 4,
        compiler_params=pltpu.CompilerParams(
            collective_id=ident, has_side_effects=True, vmem_limit_bytes=63 * 2**20),
        cost_estimate=cost(80),
        name="attention_back",
    )(q, d_heads, log_mass, delta, qseg, ids, hat, inv, cosine, sine, x, gains, gain_query, grad_o, kv)


class RowScatter:
    def __init__(self, group, own_rows, source, near, pair, far, sems):
        self.group, self.own_rows, self.source = group, own_rows, source
        self.near, self.pair, self.far, self.sems = near, pair, far, sems
        self.others = list(range(1, group.chips))
        self.order = self.others + [0]

    def block(self, device):
        return pl.ds(pl.multiple_of(device * self.own_rows, 16), self.own_rows)

    def within(self, k):
        g = self.group
        return g.copy(self.source.at[self.block(g.other(k) + 1 - 2 * g.core)], self.near.at[k],
                      self.sems[0].at[k], self.sems[1].at[k], g.partner())

    def between(self, k):
        g = self.group
        return g.copy(self.pair.at[k], self.far.at[k], self.sems[2].at[k], self.sems[3].at[k], g.other(k))

    def send(self):
        for k in self.order:
            self.within(k).start()

    def middle(self, out):
        for k in self.order:
            self.within(k).wait_recv()
            both = self.source[self.block(self.group.other(k)), :].astype(F32) + self.near[k].astype(F32)
            if k > 0:
                self.pair[k] = both.astype(BF16)
                self.between(k).start()
            else:
                out[...] = both

    def final(self, out):
        for k in self.others:
            self.between(k).wait_recv()
            out[...] += self.far[k].astype(F32)
        for k in self.others:
            self.between(k).wait_send()
        for k in self.order:
            self.within(k).wait_send()


def row_scatter_scratch(chips, own_rows, cols):
    return [pltpu.VMEM((chips, own_rows, cols), BF16)] * 3 + [pltpu.SemaphoreType.DMA((chips,))] * 4


def key_back_kernel(tiles, tile, chunk, own_rows, scattered, dkv_ref, hat_ref, inv_ref, cos_ref, sin_ref, x_ref, dm_ref, dq_ref,
                    gain_ref, gk_ref, w_ref, wq_ref, dgq_ref, dg_mid_ref, dg_post_ref, rs_ref, qo_ref,
                    dx_ref, last_out, qo_out, gate_ref, up_ref, down_ref, acc, acc_in, acc_key, w_kv, w_sem, last_ref,
                    out, own, near, far, *sems):
    i = pl.program_id(0)
    head = hat_ref.shape[1]
    per = tile // chunk
    count = tiles * per + 1
    line = ResidentSum(count, chunk, count, own, near, far, out, sems[:9])
    group = Shared(True)
    if scattered:
        early = RowScatter(group, own_rows, qo_ref, *sems[9:12], sems[12:16])
        late = RowScatter(group, own_rows, last_ref, *sems[16:19], sems[19:23])

    @pl.when(i == 0)
    def _():
        copy = pltpu.make_async_copy(w_ref.at[:, pl.ds(head, 2 * head)], w_kv, w_sem)
        copy.start()
        if scattered:
            group.greet(line.z)
            early.send()
        else:
            barrier_line(line.z)
            qo_out[...] = qo_ref[...]
        for ref in (acc, acc_in, acc_key):
            ref[...] = jnp.zeros_like(ref)
        copy.wait()
        line.put(count - 1, jnp.broadcast_to(
            jnp.concatenate([dgq_ref[...], dgq_ref[...]], axis=1).astype(BF16), (chunk, 2 * head)))

    @pl.when(i < tiles)
    def _():
        for j in range(per):
            line.put(i * per + j, dkv_ref[j * chunk : (j + 1) * chunk, :])

    @pl.when((i >= 1) & (i <= tiles))
    def _():
        for j in range(per):
            line.pair((i - 1) * per + j)

    @pl.when((i >= 2) & (i <= tiles + 1))
    def _():
        for j in range(per):
            line.total((i - 2) * per + j)

    @pl.when(i == 0)
    def _():
        gate_ref[...] = rs_ref[0].astype(F32)
        up_ref[...] = rs_ref[1].astype(F32)
        row = lax.broadcasted_iota(jnp.int32, (own_rows, own_rows), 0)
        col = lax.broadcasted_iota(jnp.int32, (own_rows, own_rows), 1)
        down_ref[...] = dot(rs_ref[2], jnp.where(row == col, 1.0, 0.0).astype(BF16), TN)

    @pl.when(i == 1)
    def _():
        line.pair(count - 1)

    @pl.when(i == 2)
    def _():
        line.total(count - 1)
        if scattered:
            early.middle(qo_out)

    if scattered:
        @pl.when(i == tiles)
        def _():
            early.final(qo_out)

    @pl.when(i >= 3)
    def _():
        for j in range(per):
            line.arrived((i - 3) * per + j)
        d_kv = out[pl.ds(pl.multiple_of((i - 3) * tile, tile), tile), :]
        d_rot = rotate(d_kv[:, :head].astype(F32), cos_ref[...], -sin_ref[...])
        d_raw, d_gain = norm_back(d_rot, hat_ref[...], inv_ref[...], gk_ref[...])
        acc_key[...] += d_gain[None]
        d_raw = jnp.concatenate([d_raw.astype(BF16), d_kv[:, head:]], axis=1)
        d_one = dot(dq_ref[...], wq_ref[...], NT) + dot(d_raw, w_kv[...], NT)
        hat, inv = norm_parts(x_ref[...].astype(F32))
        gain = gain_ref[0:1, :]
        d_part, d_gain = norm_back(d_one, hat, inv, gain)
        acc_in[...] += d_gain[None]
        dx_ref[...] = dm_ref[...] + d_part
        acc[...] += dot((hat * (1.0 + gain)).astype(BF16), d_raw, TN)

    @pl.when(i == tiles + 2)
    def _():
        line.arrived(count - 1)
        width = x_ref.shape[1]
        short = head * own_rows // width
        last_ref[:, : 2 * head] = acc[...].astype(BF16)
        d_query = out[pl.ds((count - 1) * chunk, 16), :head][0:1].astype(F32)
        pair = jnp.concatenate([d_query, acc_key[...], jnp.zeros((14, head), F32)], axis=0).astype(BF16)
        col = lax.broadcasted_iota(jnp.int32, (head, width), 1)
        row = lax.broadcasted_iota(jnp.int32, (head, width), 0)
        shift = short.bit_length() - 1
        spot = lax.shift_right_logical(row, shift) * own_rows + (row & (short - 1))
        spread = dot(pair, jnp.where(col == spot, 1.0, 0.0).astype(BF16))
        gains = jnp.concatenate(
            [acc_in[...], dg_mid_ref[...], dg_post_ref[...], spread[0:2], jnp.zeros((122, width), F32)], axis=0)
        last_ref[:, 2 * head :] = jnp.transpose(gains).astype(BF16)
        if scattered:
            late.send()
            line.finish()
            late.middle(last_out)
            late.final(last_out)
        else:
            last_out[...] = last_ref[...]
            line.finish()


def key_back(d_kv, hat, inv, cosine, sine, x, d_middle, d_query, gains, gain_key, first, w_query, dg_query, dg_mid, dg_post,
             ffn_grads, grad_qo, own_rows, ident):
    rows, width = x.shape
    head = hat.shape[1]
    tile, chunk = 256, 128
    tiles = rows // tile
    count = rows // chunk + 1
    dma = pltpu.SemaphoreType.DMA((count,))

    def late(cols):
        return pl.BlockSpec((tile, cols), lambda i: (jnp.maximum(i - 3, 0), 0))

    def fixed(shape):
        return pl.BlockSpec(shape, lambda i: (0, 0))

    turns = cosine.shape[0] // tile
    turn = pl.BlockSpec((tile, head // 2), lambda i: (lax.rem(jnp.maximum(i - 3, 0), turns), 0))
    comm = pltpu.VMEM((count * chunk, 2 * head), BF16)
    scattered = own_rows % 16 == 0
    chips = width // (2 * own_rows)
    last = (width, 2 * head + 128)
    more = []
    if scattered:
        last_out, qo_out, kind = (own_rows, last[1]), (own_rows, 2 * head), F32
        for cols in (2 * head, last[1]):
            more += row_scatter_scratch(chips, own_rows, cols)
    else:
        last_out, qo_out, kind = last, grad_qo.shape, BF16
    return pl.pallas_call(
        functools.partial(key_back_kernel, tiles, tile, chunk, own_rows, scattered),
        grid=(tiles + 3,),
        out_shape=(
            jax.ShapeDtypeStruct((rows, width), F32),
            jax.ShapeDtypeStruct(last_out, kind),
            jax.ShapeDtypeStruct(qo_out, kind),
            jax.ShapeDtypeStruct(ffn_grads.shape[1:], F32),
            jax.ShapeDtypeStruct(ffn_grads.shape[1:], F32),
            jax.ShapeDtypeStruct(ffn_grads.shape[:0:-1], F32),
        ),
        in_specs=[pl.BlockSpec((tile, 2 * head), lambda i: (jnp.minimum(i, tiles - 1), 0)),
                  late(head), late(1), turn, turn, late(width), late(width), late(4 * head),
                  whole_block(gains.shape), whole_block(gain_key.shape), ANY]
        + [whole_block(a.shape) for a in (w_query, dg_query, dg_mid, dg_post, ffn_grads, grad_qo)],
        out_specs=(late(width), fixed(last_out), fixed(qo_out), fixed(ffn_grads.shape[1:]), fixed(ffn_grads.shape[1:]),
                   fixed(ffn_grads.shape[:0:-1])),
        scratch_shapes=[
            pltpu.VMEM((width, 2 * head), F32), pltpu.VMEM((1, width), F32), pltpu.VMEM((1, head), F32),
            pltpu.VMEM((width, 2 * head), BF16), pltpu.SemaphoreType.DMA, pltpu.VMEM(last, BF16)] + [comm] * 4 + [dma] * 7
        + [pltpu.SemaphoreType.REGULAR] * 2 + more,
        compiler_params=pltpu.CompilerParams(
            collective_id=ident, has_side_effects=True, vmem_limit_bytes=56 * 2**20),
        cost_estimate=cost(75),
        name="key_back",
    )(d_kv, hat, inv, cosine, sine, x, d_middle, d_query, gains, gain_key, first, w_query, dg_query, dg_mid, dg_post, ffn_grads, grad_qo)


def shards(tokens, segments, cotangent, w_query, w_key, w_value, w_out, w_gate, w_up, w_down,
           g_input, g_post_attn, g_pre_ffn, g_post_ffn, g_query, g_key):
    batches, seq_local, _, size, width = tokens.shape
    head = w_key.shape[1]
    groups = batches * seq_local
    per_group = 2 * size
    rows = groups * per_group
    ctx = lax.axis_size("ctx")
    length = per_group * ctx
    rank = lax.axis_index("ctx")
    shared = ("dp", "ctx")
    own_rows = g_input.shape[0]
    hidden = w_gate.shape[1]

    def column(gain):
        return jnp.pad(gain, (0, own_rows - gain.shape[0]))[:, None]

    own_ids = segments.reshape(groups, 2, size)
    id_rows = own_ids.size // 128
    ids = jnp.pad(own_ids.reshape(id_rows, 128), ((0, -id_rows % 16), (0, 0)))
    extra = jnp.concatenate(
        [column(g) for g in (g_input, g_post_attn, g_pre_ffn, g_post_ffn, g_query, g_key)], axis=1)
    extra = jnp.pad(extra, ((0, 0), (0, 128 - extra.shape[1])))

    def rows_of_16(w):
        return jnp.pad(w, ((0, -own_rows % 16), (0, 0)))

    first, line, ids = first_gather(
        rows_of_16(jnp.concatenate([w_query, w_key, w_value, extra], axis=1)),
        rows_of_16(jnp.concatenate([w_query, w_out.T], axis=1)), ids, width // own_rows, 5)
    first = first[:, :own_rows].reshape(width, -1)
    line = line[:own_rows].reshape(own_rows, 4, 2, head).transpose(2, 0, 1, 3).reshape(2, own_rows, 4 * head)
    side = first[:, 3 * head :]
    gain_cols = side[:, :8].astype(F32)
    gain_rows = gain_cols.T
    gain_input = gain_rows[0]
    short = g_query.shape[0]
    gain_query, gain_key = (
        gain_cols[:, i].reshape(-1, own_rows)[:, :short].reshape(-1) for i in (4, 5))

    wide = wide_of(hidden)
    second = jnp.concatenate(
        [line[1]] + [jnp.pad(w, ((0, 0), (0, wide - hidden))) for w in (w_gate, w_up, w_down.T)], axis=1)
    weights = lax.all_gather(second, shared, axis=0, tiled=True)

    offsets = rank * size + jnp.arange(size, dtype=jnp.int32)
    position = jnp.concatenate([offsets, length - 1 - offsets]).astype(F32)
    cosine, sine = angles(position, head // 2, head)

    x_rows = tokens.reshape(rows, width)
    dy_rows = cotangent.reshape(rows, width)
    queries, q_hat, q_scale, k_hat, k_scale, heads_own, log_mass, kv, heads_all = attention(
        x_rows, first, gain_rows, gain_query[None], gain_key[None], cosine, sine, own_ids[..., None], ids, length, 0)

    line, heads_all = lax.optimization_barrier((line[0], heads_all))
    query_full = lax.all_gather(line, shared, axis=0, tiled=True)
    attn, hidden_two, gate, up, ffn_out = ffn_forward(x_rows, heads_all, gain_rows, weights, hidden, 1)
    ffn_out, query_full = lax.optimization_barrier((ffn_out, query_full))
    output, d_gain_post_ffn, grad_ffn, d_two = ffn_backward(
        x_rows, attn, dy_rows, ffn_out, hidden_two, gate, up, gain_rows, weights, 2)
    grad_ffn = lax.psum_scatter(grad_ffn, shared, scatter_dimension=1, tiled=True)
    d_middle, d_heads, delta, d_gain_mid, grad_out_t = middle_back(
        x_rows, attn, dy_rows, d_two, heads_own, gain_rows, weights)

    d_q_all, d_kv, d_gain_query, grad_qo = attention_back(
        queries, d_heads, log_mass, delta, own_ids[:, :, None, :], ids, q_hat, q_scale, cosine, sine, x_rows, gain_rows,
        gain_query[None], grad_out_t, kv, 4)
    d_tokens, last, grad_qo, grad_gate, grad_up, grad_down = key_back(
        d_kv, k_hat, k_scale, cosine, sine, x_rows, d_middle, d_q_all, gain_rows, gain_key[None],
        first, query_full, d_gain_query, d_gain_mid, d_gain_post_ffn, grad_ffn, grad_qo, own_rows, 3)
    if own_rows % 16:
        last = lax.psum_scatter(last, shared, scatter_dimension=0, tiled=True).astype(F32)
        grad_qo = lax.psum_scatter(grad_qo, shared, scatter_dimension=0, tiled=True).astype(F32)
    g = last[:, 2 * head :]
    return (
        output.reshape(tokens.shape),
        d_tokens.reshape(tokens.shape),
        grad_qo[:, :head],
        last[:, :head],
        last[:, head : 2 * head],
        grad_qo[:, head:].T,
        grad_gate,
        grad_up,
        grad_down,
        g[:, 0],
        g[:, 1],
        g[:, 2],
        g[:, 3],
        g[:short, 4],
        g[:short, 5],
    )


def solution(mesh):
    shared = ("dp", "ctx")
    rows = P(None, "dp", None, "ctx", None)
    weights = (
        P(shared, "tp"), P(shared, None), P(shared, None), P("tp", shared),
        P(shared, "tp"), P(shared, "tp"), P("tp", shared),
    )
    gains = (P(shared),) * 6
    return jax.shard_map(
        shards,
        mesh=mesh,
        in_specs=(rows, P(None, "dp", None, "ctx"), rows) + weights + gains,
        out_specs=(rows, rows) + weights + gains,
        check_vma=False,
    )
```

```python
import functools

import jax
import jax.numpy as jnp
from jax import lax
from jax.experimental import pallas as pl
from jax.experimental.pallas import tpu as pltpu
from jax.sharding import PartitionSpec as P

EPS = 1e-06
THETA = 1000000.0
SCALE = 0.0625
NEGATIVE = -1e30
BF16 = jnp.bfloat16
F32 = jnp.float32
MESH = pl.DeviceIdType.MESH
NN = (((1,), (0,)), ((), ()))
NT = (((1,), (1,)), ((), ()))
TN = (((0,), (0,)), ((), ()))


def dot(a, b, dims=NN):
    return lax.dot_general(a, b, dims, preferred_element_type=F32)


def cost(us):
    return pl.CostEstimate(flops=int(us * 1.1e9), bytes_accessed=0, transcendentals=0)


def barrier_line(z):
    bar = pltpu.get_barrier_semaphore()

    @pl.when(z > 0)
    def _():
        pl.semaphore_signal(bar, inc=1, device_id={"tp": z - 1}, device_id_type=MESH)

    @pl.when(z < 3)
    def _():
        pl.semaphore_signal(bar, inc=1, device_id={"tp": z + 1}, device_id_type=MESH)

    pl.semaphore_wait(bar, jnp.where((z == 0) | (z == 3), 1, 2))


def block_starts(half, t, blocks, rank):
    if half == 0:
        return t
    return jnp.where(t < blocks, t, t + rank + 1)


def angles(position, half_size, full_size):
    frequency = THETA ** (-2.0 * jnp.arange(half_size, dtype=F32) / full_size)
    turned = position[:, None] * frequency[None, :]
    return (jnp.cos(turned), jnp.sin(turned))


def rotate(tensor, cosine, sine):
    half_size = tensor.shape[-1] // 2
    a = tensor[..., :half_size]
    b = tensor[..., half_size:]
    return jnp.concatenate([a * cosine - b * sine, b * cosine + a * sine], axis=-1)


def norm_parts(values):
    inv = lax.rsqrt(jnp.mean(values * values, axis=-1, keepdims=True) + EPS)
    return (values * inv, inv)


def norm_back(upstream, normalized, inv, gain):
    d_norm = upstream * (1.0 + gain)
    d_values = inv * (d_norm - normalized * jnp.mean(d_norm * normalized, axis=-1, keepdims=True))
    return (d_values, jnp.sum(upstream * normalized, axis=0))


def gelu_tanh(values):
    return jax.nn.gelu(values, approximate=True)


class LineSum:
    def __init__(self, count, chunk, slots, own, near, far, out, sems):
        self.count, self.chunk, self.slots = count, chunk, slots
        self.own, self.near, self.far, self.out = own, near, far, out
        self.sems = sems
        self.z = z = lax.axis_index("tp")
        self.hub = (z == 1) | (z == 2)
        self.leaf = (z == 0) | (z == 3)
        self.other_hub = jnp.where(z == 1, 2, 1)
        self.my_hub = jnp.where(z == 0, 1, 2)
        self.my_leaf = jnp.where(z == 1, 0, 3)

    def slot(self, c):
        return pl.ds(pl.multiple_of(lax.rem(c, self.slots) * self.chunk, self.chunk), self.chunk)

    def rows(self, c):
        return pl.ds(pl.multiple_of(c * self.chunk, self.chunk), self.chunk)

    def inwards(self, c):
        return pltpu.make_async_remote_copy(
            self.own.at[self.slot(c)], self.near.at[self.slot(c)], self.sems[0].at[c], self.sems[1].at[c],
            device_id={"tp": self.my_hub}, device_id_type=MESH)

    def across(self, c):
        return pltpu.make_async_remote_copy(
            self.own.at[self.slot(c)], self.far.at[self.slot(c)], self.sems[2].at[c], self.sems[3].at[c],
            device_id={"tp": self.other_hub}, device_id_type=MESH)

    def outwards(self, c):
        return pltpu.make_async_remote_copy(
            self.far.at[self.slot(c)], self.out.at[self.rows(c)], self.sems[4].at[c], self.sems[5].at[c],
            device_id={"tp": self.my_leaf}, device_id_type=MESH)

    def store(self, c):
        return pltpu.make_async_copy(self.far.at[self.slot(c)], self.out.at[self.rows(c)], self.sems[6].at[c])

    def put(self, c, value):
        ring = self.slots < self.count
        if ring:
            @pl.when(c >= self.slots)
            def _():
                @pl.when(self.leaf)
                def _():
                    self.inwards(c - self.slots).wait_send()

                @pl.when(self.hub)
                def _():
                    self.across(c - self.slots).wait_send()

        self.own[self.slot(c), :] = value

        @pl.when(self.leaf)
        def _():
            if ring:
                @pl.when(c >= self.slots)
                def _():
                    pl.semaphore_wait(self.sems[7], 1)
            self.inwards(c).start()

    def pair(self, c):
        ring = self.slots < self.count

        @pl.when(self.hub)
        def _():
            self.inwards(c).wait_recv()
            at = self.slot(c)
            self.own[at, :] = (self.own[at, :].astype(F32) + self.near[at, :].astype(F32)).astype(BF16)
            if ring:
                @pl.when(c < self.count - self.slots)
                def _():
                    pl.semaphore_signal(self.sems[7], inc=1, device_id={"tp": self.my_leaf}, device_id_type=MESH)

                @pl.when(c >= self.slots)
                def _():
                    pl.semaphore_wait(self.sems[8], 1)
            self.across(c).start()

    def total(self, c):
        @pl.when(self.hub)
        def _():
            self.across(c).wait_recv()
            at = self.slot(c)
            self.far[at, :] = (self.own[at, :].astype(F32) + self.far[at, :].astype(F32)).astype(BF16)
            self.outwards(c).start()
            self.store(c).start()

    def retire(self, c):
        @pl.when(self.hub)
        def _():
            self.outwards(c).wait_send()
            self.store(c).wait()
            if self.slots < self.count:
                @pl.when(c < self.count - self.slots)
                def _():
                    pl.semaphore_signal(self.sems[8], inc=1, device_id={"tp": self.other_hub}, device_id_type=MESH)

    def finish(self):
        first = max(0, self.count - self.slots)

        @pl.when(self.leaf)
        def _():
            for c in range(self.count):
                self.outwards(c).wait_recv()
            for c in range(first, self.count):
                self.inwards(c).wait_send()

        @pl.when(self.hub)
        def _():
            for c in range(first, self.count):
                self.across(c).wait_send()


def line_sum_scratch(count, chunk, slots, cols):
    dma = pltpu.SemaphoreType.DMA((count,))
    regular = pltpu.SemaphoreType.REGULAR
    return [pltpu.VMEM((slots * chunk, cols), BF16)] * 3 + [dma] * 7 + [regular] * 2


def gelu_parts(v):
    c = 0.7978845608028654
    square = v * v
    t = jnp.tanh(v * (c + (c * 0.044715) * square))
    half = 0.5 + 0.5 * t
    value = v * half
    slope = half + (0.5 * v) * (1.0 - t * t) * (c + (3.0 * c * 0.044715) * square)
    return value, slope


def column_parts(cols):
    middle = -(-cols // 256) * 128
    return [(0, middle), (middle, cols)] if middle < cols else [(0, cols)]


def middle_of(x, attn, gain_post_attn):
    hat, inv = norm_parts(attn.astype(F32))
    return x.astype(F32) + hat * (1.0 + gain_post_attn), hat, inv


def load_ffn_weights(weights, refs, sem):
    wide = refs[0].shape[1]
    base = weights.shape[1] - 3 * wide
    return [
        pltpu.make_async_copy(weights.at[:, pl.ds(base + j * wide, wide)], ref, sem.at[j])
        for j, ref in enumerate(refs)
    ]


def ffn_forward_kernel(tiles, tile, chunk, hidden, x_ref, h_ref, gain_ref, w_ref,
                       attn_ref, two_ref, gate_ref, up_ref, out_ref, wo_ref, wg_ref, wu_ref, wd_ref, w_sem, own, near, far, *sems):
    i = pl.program_id(0)
    per = tile // chunk
    line = LineSum(tiles * per, chunk, tiles * per, own, near, far, out_ref, sems)
    head = wo_ref.shape[1] // 4

    @pl.when(i == 0)
    def _():
        copies = load_ffn_weights(w_ref, (wg_ref, wu_ref, wd_ref), w_sem)
        copies.append(pltpu.make_async_copy(w_ref.at[:, pl.ds(0, 4 * head)], wo_ref, w_sem.at[3]))
        for copy in copies:
            copy.start()
        barrier_line(line.z)
        for copy in copies:
            copy.wait()

    attn = dot(h_ref[...], wo_ref[...], NT).astype(BF16)
    attn_ref[...] = attn
    middle, _, _ = middle_of(x_ref[...], attn, gain_ref[1:2, :])
    hat, _ = norm_parts(middle)
    two = (hat * (1.0 + gain_ref[2:3, :])).astype(BF16)
    two_ref[...] = two
    part = None
    for a, b in column_parts(hidden):
        gate = dot(two, wg_ref[:, a:b])
        up = dot(two, wu_ref[:, a:b])
        gate_ref[:, a:b] = gate.astype(BF16)
        up_ref[:, a:b] = up.astype(BF16)
        value, _ = gelu_parts(gate)
        more = dot((value * up).astype(BF16), wd_ref[:, a:b], NT)
        part = more if part is None else part + more
    for j in range(per):
        line.put(i * per + j, part[j * chunk : (j + 1) * chunk].astype(BF16))

    @pl.when(i >= 1)
    def _():
        for j in range(per):
            line.pair((i - 1) * per + j)

    @pl.when(i >= 2)
    def _():
        for j in range(per):
            line.total((i - 2) * per + j)

    @pl.when(i == tiles - 1)
    def _():
        last = tiles * per
        for j in range(per):
            line.pair(last - per + j)
        for c in range(max(0, last - 2 * per), last):
            line.total(c)
        for c in range(last):
            line.retire(c)
        line.finish()


def whole_block(shape):
    return pl.BlockSpec(shape, lambda i: (0,) * len(shape), pipeline_mode=pl.Buffered(1))


def tile_block(tile, cols):
    return pl.BlockSpec((tile, cols), lambda i: (i, 0))


ANY = pl.BlockSpec(memory_space=pl.ANY)


def wide_of(hidden):
    return -(-hidden // 128) * 128


def ffn_forward(x, heads, gains, weights, hidden, ident):
    rows, width = x.shape
    all_heads = heads.shape[1]
    tile, chunk = 128, 128
    tiles = rows // tile
    count = rows // chunk
    wide = wide_of(hidden)
    return pl.pallas_call(
        functools.partial(ffn_forward_kernel, tiles, tile, chunk, hidden),
        grid=(tiles,),
        out_shape=(
            jax.ShapeDtypeStruct((rows, width), BF16),
            jax.ShapeDtypeStruct((rows, width), BF16),
            jax.ShapeDtypeStruct((rows, hidden), BF16),
            jax.ShapeDtypeStruct((rows, hidden), BF16),
            jax.ShapeDtypeStruct((rows, width), BF16),
        ),
        in_specs=[
            tile_block(tile, width),
            tile_block(tile, all_heads),
            whole_block(gains.shape),
            ANY,
        ],
        out_specs=(tile_block(tile, width), tile_block(tile, width), tile_block(tile, hidden), tile_block(tile, hidden), ANY),
        scratch_shapes=[pltpu.VMEM((width, all_heads), BF16)] + [pltpu.VMEM((width, wide), BF16)] * 3
        + [pltpu.SemaphoreType.DMA((4,))]
        + line_sum_scratch(count, chunk, count, width),
        compiler_params=pltpu.CompilerParams(
            collective_id=ident, has_side_effects=True, vmem_limit_bytes=60 * 2**20),
        cost_estimate=cost(140),
        name="ffn_forward",
    )(x, heads, gains, weights)


def ffn_backward_kernel(tiles, tile, chunk, slots, hidden, dy_ref, ffn_ref, two_ref, gate_ref, up_ref,
                        gain_ref, w_ref,
                        dgain_ref, grad_ref, out_ref, wg_ref, wu_ref, wd_ref, w_sem,
                        acc_g, acc_u, acc_d, keep_g, keep_u, keep_h, stage, stage_sem, own, near, far, *sems):
    i = pl.program_id(0)
    per = tile // chunk
    last = tiles * per
    line = LineSum(last, chunk, slots, own, near, far, out_ref, sems)

    @pl.when(i == 0)
    def _():
        copies = load_ffn_weights(w_ref, (wg_ref, wu_ref, wd_ref), w_sem)
        for copy in copies:
            copy.start()
        barrier_line(line.z)
        for acc in (acc_g, acc_u, acc_d, dgain_ref):
            acc[...] = jnp.zeros_like(acc)
        for copy in copies:
            copy.wait()

    hat, inv = norm_parts(ffn_ref[...].astype(F32))
    gain = gain_ref[3:4, :]
    d_ffn, d_gain = norm_back(dy_ref[...].astype(F32), hat, inv, gain)
    dgain_ref[...] += d_gain[None]
    d_ffn = d_ffn.astype(BF16)
    part = None
    for a, b in column_parts(hidden):
        d_hidden = dot(d_ffn, wd_ref[:, a:b])
        up = up_ref[:, a:b].astype(F32)
        value, slope = gelu_parts(gate_ref[:, a:b].astype(F32))
        keep_h[:, a:b] = (value * up).astype(BF16)
        d_gate = (d_hidden * up * slope).astype(BF16)
        d_up = (d_hidden * value).astype(BF16)
        keep_g[:, a:b] = d_gate
        keep_u[:, a:b] = d_up
        more = dot(d_gate, wg_ref[:, a:b], NT) + dot(d_up, wu_ref[:, a:b], NT)
        part = more if part is None else part + more
    for j in range(per):
        line.put(i * per + j, part[j * chunk : (j + 1) * chunk].astype(BF16))

    @pl.when(i >= 1)
    def _():
        for j in range(per):
            line.pair((i - 1) * per + j)

    acc_g[...] += dot(two_ref[...], keep_g[...], TN)
    acc_u[...] += dot(two_ref[...], keep_u[...], TN)
    acc_d[...] += dot(d_ffn, keep_h[...], TN)

    @pl.when(i >= 2)
    def _():
        for j in range(per):
            line.total((i - 2) * per + j)

    @pl.when(i >= 3)
    def _():
        for j in range(per):
            line.retire((i - 3) * per + j)

    @pl.when(i == tiles - 1)
    def _():
        for j in range(per):
            line.pair(last - per + j)
        step = stage.shape[1]
        count = acc_g.shape[0] // step

        def piece(acc, out, k, at):
            @pl.when(k >= 2)
            def _():
                pltpu.make_async_copy(stage.at[at], out.at[pl.ds(0, step)], stage_sem.at[at]).wait()
            rows = pl.ds(pl.multiple_of(k * step, step), step)
            stage[at] = acc[rows, :].astype(BF16)
            pltpu.make_async_copy(stage.at[at], out.at[rows], stage_sem.at[at]).start()

        for acc, out in ((acc_g, grad_ref.at[0]), (acc_u, grad_ref.at[1]), (acc_d, grad_ref.at[2])):
            def pieces(k, _):
                piece(acc, out, k, lax.rem(k, 2))
                return 0

            lax.fori_loop(0, count, pieces, 0)
            for at in range(2):
                pltpu.make_async_copy(stage.at[at], out.at[pl.ds(0, step)], stage_sem.at[at]).wait()
            if acc is acc_g:
                for c in range(max(0, last - 2 * per), last - per):
                    line.total(c)
            if acc is acc_u:
                for c in range(last - per, last):
                    line.total(c)
        for c in range(max(0, last - 3 * per), last):
            line.retire(c)
        line.finish()


def ffn_backward(dy, ffn, two, gate, up, gains, weights, ident):
    rows, width = dy.shape
    hidden = gate.shape[1]
    wide = wide_of(hidden)
    tile, chunk = 256, 128
    tiles = rows // tile
    count = rows // chunk
    slots = min(count, 6)
    step = 144
    acc = pltpu.VMEM((width, hidden), F32)
    keep = pltpu.VMEM((tile, hidden), BF16)
    return pl.pallas_call(
        functools.partial(ffn_backward_kernel, tiles, tile, chunk, slots, hidden),
        grid=(tiles,),
        out_shape=(
            jax.ShapeDtypeStruct((1, width), F32),
            jax.ShapeDtypeStruct((3, width, hidden), BF16),
            jax.ShapeDtypeStruct((rows, width), BF16),
        ),
        in_specs=[tile_block(tile, width)] * 3 + [tile_block(tile, hidden)] * 2
        + [whole_block(gains.shape), ANY],
        out_specs=(pl.BlockSpec((1, width), lambda i: (0, 0)), ANY, ANY),
        scratch_shapes=[pltpu.VMEM((width, wide), BF16)] * 3 + [pltpu.SemaphoreType.DMA((3,))] + [acc] * 3 + [keep] * 3
        + [pltpu.VMEM((2, step, hidden), BF16), pltpu.SemaphoreType.DMA((2,))]
        + line_sum_scratch(count, chunk, slots, width),
        compiler_params=pltpu.CompilerParams(
            collective_id=ident, has_side_effects=True, vmem_limit_bytes=63 * 2**20),
        cost_estimate=cost(145),
        name="ffn_backward",
    )(dy, ffn, two, gate, up, gains, weights)


def middle_back_kernel(x_ref, attn_ref, dy_ref, d2_ref, ffn_ref, h_ref, gain_ref, w_ref,
                       y_ref, dm_ref, dh_ref, delta_ref, dgain_ref, go_ref, acc, wo_ref, w_sem):
    i = pl.program_id(0)

    @pl.when(i == 0)
    def _():
        head = wo_ref.shape[1]
        at = pl.multiple_of(lax.axis_index("tp") * head, head)
        copy = pltpu.make_async_copy(w_ref.at[:, pl.ds(at, head)], wo_ref, w_sem)
        copy.start()
        copy.wait()
        acc[...] = jnp.zeros_like(acc)
        dgain_ref[...] = jnp.zeros_like(dgain_ref)

    middle, attn_hat, attn_inv = middle_of(x_ref[...], attn_ref[...], gain_ref[1:2, :])
    hat, _ = norm_parts(ffn_ref[...].astype(F32))
    y_ref[...] = (middle + hat * (1.0 + gain_ref[3:4, :])).astype(BF16)
    hat, inv = norm_parts(middle)
    d_part, d_gain = norm_back(d2_ref[...].astype(F32), hat, inv, gain_ref[2:3, :])
    dgain_ref[1:2, :] += d_gain[None]
    d_middle = dy_ref[...].astype(F32) + d_part
    dm_ref[...] = d_middle
    d_attn, d_gain = norm_back(d_middle, attn_hat, attn_inv, gain_ref[1:2, :])
    dgain_ref[0:1, :] += d_gain[None]
    d_attn = d_attn.astype(BF16)
    d_heads = dot(d_attn, wo_ref[...]).astype(BF16)
    dh_ref[...] = d_heads
    heads = h_ref[...]
    delta_ref[...] = jnp.sum(d_heads.astype(F32) * heads.astype(F32), axis=1, keepdims=True)
    acc[...] += dot(d_attn, heads, TN)

    @pl.when(i == pl.num_programs(0) - 1)
    def _():
        go_ref[...] = acc[...].astype(BF16)


def middle_back(x, attn, dy, d_two, ffn, heads, gains, weights):
    rows, width = x.shape
    head = heads.shape[1]
    tile = 256
    return pl.pallas_call(
        middle_back_kernel,
        grid=(rows // tile,),
        out_shape=(
            jax.ShapeDtypeStruct((rows, width), BF16),
            jax.ShapeDtypeStruct((rows, width), F32),
            jax.ShapeDtypeStruct((rows, head), BF16),
            jax.ShapeDtypeStruct((rows, 1), F32),
            jax.ShapeDtypeStruct((2, width), F32),
            jax.ShapeDtypeStruct((width, head), BF16),
        ),
        in_specs=[tile_block(tile, width)] * 5 + [tile_block(tile, head)] + [whole_block(gains.shape), ANY],
        out_specs=(
            tile_block(tile, width), tile_block(tile, width), tile_block(tile, head), tile_block(tile, 1),
            pl.BlockSpec((2, width), lambda i: (0, 0)), pl.BlockSpec((width, head), lambda i: (0, 0)),
        ),
        scratch_shapes=[pltpu.VMEM((width, head), F32), pltpu.VMEM((width, head), BF16), pltpu.SemaphoreType.DMA],
        compiler_params=pltpu.CompilerParams(vmem_limit_bytes=48 * 2**20),
        cost_estimate=cost(19),
        name="middle_back",
    )(x, attn, dy, d_two, ffn, heads, gains, weights)


class LineGather:
    def __init__(self, whole, tile, width, sems):
        self.whole, self.tile, self.width, self.sems = whole, tile, width, sems
        self.z = lax.axis_index("tp")

    def place(self, src, t):
        return self.whole.at[
            pl.ds(pl.multiple_of(t * self.tile, self.tile), self.tile),
            pl.ds(pl.multiple_of(src * self.width, self.width), self.width)]

    def send(self, src, t, hop, way):
        ss, rs = self.sems[:2] if way > 0 else self.sems[2:]
        place = self.place(src, t)
        return pltpu.make_async_remote_copy(
            place, place, ss.at[hop, t], rs.at[hop, t],
            device_id={"tp": self.z + way}, device_id_type=MESH)

    def going(self, hop, way):
        src = self.z - way * hop
        return src, (self.z + way >= 0) & (self.z + way <= 3) & (src >= 0) & (src <= 3)

    def coming(self, hop, way):
        src = self.z - way * (hop + 1)
        return src, (src >= 0) & (src <= 3)

    def forward(self, t, hop):
        for way in (1, -1):
            if hop > 0:
                self.wait(t, hop - 1, way)
            src, ok = self.going(hop, way)

            @pl.when(ok)
            def _():
                self.send(src, t, hop, way).start()

    def wait(self, t, hop, way):
        src, ok = self.coming(hop, way)

        @pl.when(ok)
        def _():
            self.send(src, t, hop, way).wait_recv()

    def arrived(self, t):
        for way in (1, -1):
            self.wait(t, 2, way)

    def finish(self, tiles):
        for hop in range(3):
            for way in (1, -1):
                src, ok = self.going(hop, way)

                @pl.when(ok)
                def _():
                    def one(t, _):
                        self.send(src, t, hop, way).wait_send()
                        return 0

                    lax.fori_loop(0, tiles, one, 0)


class KeyGather(LineGather):
    def __init__(self, block, chips, sems):
        self.block, self.chips, self.sems = block, chips, sems
        self.z = lax.axis_index("tp")

    def tile_of(self, g, half, k):
        return (2 * g + half) * (self.chips - 1) + k - 1

    def place(self, src, t):
        pair, k = divmod(t, self.chips - 1)
        return self.quarter(pair // 2, pair % 2, k + 1, src)

    def quarter(self, g, half, k, src, own=False):
        ref, start, size = self.block(g, half, k, own)
        rows = size // 4
        return ref.at[pl.ds(pl.multiple_of(start + src * rows, rows), rows)]

    def finish(self, tiles):
        for hop in range(3):
            for way in (1, -1):
                src, ok = self.going(hop, way)

                @pl.when(ok)
                def _():
                    for t in range(tiles):
                        self.send(src, t, hop, way).wait_send()


class Shared:
    def __init__(self, over_dp):
        self.ctx = ctx = lax.axis_size("ctx")
        me = lax.axis_index("ctx")
        self.devices = ctx
        if over_dp:
            me = me + lax.axis_index("dp") * ctx
            self.devices = ctx * lax.axis_size("dp")
        self.over_dp = over_dp
        self.me = me
        self.chips = self.devices // 2
        self.core = lax.rem(me, 2)
        self.chip = lax.div(me, 2)

    def ident(self, device):
        if self.over_dp:
            return {"dp": lax.div(device, self.ctx), "ctx": lax.rem(device, self.ctx)}
        return {"ctx": device}

    def other(self, k):
        return 2 * lax.rem(self.chip + k + self.chips, self.chips) + self.core

    def partner(self):
        return self.me + 1 - 2 * self.core

    def greet(self, z):
        bar = pltpu.get_barrier_semaphore()
        for device in [self.partner()] + [self.other(k) for k in range(1, self.chips)]:
            pl.semaphore_signal(bar, inc=1, device_id=self.ident(device), device_id_type=MESH)

        @pl.when(z > 0)
        def _():
            pl.semaphore_signal(bar, inc=1, device_id={"tp": z - 1}, device_id_type=MESH)

        @pl.when(z < 3)
        def _():
            pl.semaphore_signal(bar, inc=1, device_id={"tp": z + 1}, device_id_type=MESH)

        pl.semaphore_wait(bar, self.chips + jnp.where((z == 0) | (z == 3), 1, 2))

    def copy(self, source, target, send, recv, device):
        return pltpu.make_async_remote_copy(
            source, target, send, recv, device_id=self.ident(device), device_id_type=MESH)


def first_gather_kernel(a_ref, b_ref, c_ref, i_ref, all_ref, line_ref, more_ref, ids_ref, lsem, ss1, rs1, ss2, rs2, si1, ri1, si2, ri2, *sems):
    group = Shared(True)
    line = LineGather(line_ref, b_ref.shape[0], b_ref.shape[1], sems[:4])
    more = LineGather(more_ref, c_ref.shape[0], c_ref.shape[1], sems[4:])
    width = b_ref.shape[1]
    own = [
        pltpu.make_async_copy(b_ref, line_ref.at[:, pl.ds(pl.multiple_of(line.z * width, width), width)], lsem.at[0]),
        pltpu.make_async_copy(c_ref, more_ref.at[:, pl.ds(pl.multiple_of(line.z * width, width), width)], lsem.at[3]),
        pltpu.make_async_copy(a_ref, all_ref.at[group.me], lsem.at[1]),
        pltpu.make_async_copy(i_ref, ids_ref.at[group.me], lsem.at[2]),
    ]
    for copy in own:
        copy.start()
    group.greet(line.z)
    arrays = ((a_ref, all_ref, ss1, rs1, ss2, rs2), (i_ref, ids_ref, si1, ri1, si2, ri2))

    def direct(n, k, incoming=False):
        ref, whole, ss, rs = arrays[n][:4]
        at = whole.at[group.other(-k)] if incoming else whole.at[group.me]
        return group.copy(ref, at, ss.at[k], rs.at[k], group.other(k))

    def inner(n, k, incoming=False):
        ref, whole, _, _, ss, rs = arrays[n]
        at = whole.at[group.other(-k)]
        if incoming:
            at = whole.at[group.other(-k) + 1 - 2 * group.core]
        return group.copy(ref if k == 0 else at, at, ss.at[k], rs.at[k], group.partner())

    both = range(2)
    for k in range(1, group.chips):
        for n in both:
            direct(n, k).start()
    for n in both:
        inner(n, 0).start()
    own[0].wait()
    line.forward(0, 0)
    own[1].wait()
    more.forward(0, 0)
    for k in range(1, group.chips):
        if k < 3:
            line.forward(0, k)
            more.forward(0, k)
        for n in both:
            direct(n, k, True).wait_recv()
            inner(n, k).start()
    for hop in range(min(3, group.chips), 3):
        line.forward(0, hop)
        more.forward(0, hop)
    for k in range(group.chips):
        for n in both:
            inner(n, k, True).wait_recv()
    line.arrived(0)
    more.arrived(0)
    for copy in own[2:]:
        copy.wait()
    for n in both:
        for k in range(1, group.chips):
            direct(n, k).wait_send()
        for k in range(group.chips):
            inner(n, k).wait_send()
    line.finish(1)
    more.finish(1)


def first_gather(a, b, c, ids, devices, ident):
    dma = pltpu.SemaphoreType.DMA((devices // 2,))
    hop = pltpu.SemaphoreType.DMA((3, 1))
    return pl.pallas_call(
        first_gather_kernel,
        out_shape=(
            jax.ShapeDtypeStruct((devices,) + a.shape, a.dtype),
            jax.ShapeDtypeStruct((b.shape[0], 4 * b.shape[1]), b.dtype),
            jax.ShapeDtypeStruct((c.shape[0], 4 * c.shape[1]), c.dtype),
            jax.ShapeDtypeStruct((devices,) + ids.shape, ids.dtype),
        ),
        in_specs=[ANY] * 4,
        out_specs=(ANY,) * 4,
        scratch_shapes=[pltpu.SemaphoreType.DMA((4,))] + [dma] * 8 + [hop] * 8,
        compiler_params=pltpu.CompilerParams(collective_id=ident, has_side_effects=True),
        cost_estimate=cost(20),
        name="first_gather",
    )(a, b, c, ids)


def attention_kernel(groups, size, x_ref, w_ref, gain_ref, gq_ref, gk_ref, cos_ref, sin_ref, qs_ref, ks_ref,
                     q_ref, qhat_ref, qinv_ref, khat_ref, kinv_ref, heads_ref, log_ref, kv_out, all_out,
                     kv, whole, store_kv, store_all, ss1, rs1, ss2, rs2, *sems):
    head = q_ref.shape[1]
    length = kv.shape[1]
    id_rows = size // 128
    blocks = length // (2 * size)
    group = Shared(False)
    rank = group.me
    line = LineGather(whole, size, head, sems[:4])
    z = line.z
    tile = min(256, size)
    group.greet(z)

    def block(g, half, k, own):
        c = rank if own else group.other(-k)
        return kv.at[g], half * (length // 2) + c * size, size

    keys = KeyGather(block, group.chips, sems[4:])

    def place(g, half, c):
        return kv.at[g, pl.ds(pl.multiple_of(half * (length // 2) + c * size, size), size)]

    def direct(g, half, k, incoming=False):
        at = keys.quarter(g, half, k, z, own=not incoming)
        return group.copy(at, at, ss1.at[g, half, k], rs1.at[g, half, k], group.other(k))

    def inner(g, half, k, incoming=False):
        block = group.other(-k)
        at = place(g, half, block + 1 - 2 * group.core if incoming else block)
        return group.copy(at, at, ss2.at[g, half, k], rs2.at[g, half, k], group.partner())

    def project(g, half, u):
        rows = pl.ds((2 * g + half) * size + u * tile, tile)
        spot = pl.ds(half * size + u * tile, tile)
        cosine, sine = cos_ref[spot, :], sin_ref[spot, :]
        hat, _ = norm_parts(x_ref[rows, :].astype(F32))
        raw = dot((hat * (1.0 + gain_ref[0:1, :])).astype(BF16), w_ref[:, : 3 * head])
        hat, inv = norm_parts(raw[:, :head])
        qhat_ref[rows, :] = hat
        qinv_ref[rows, :] = inv
        q_ref[rows, :] = rotate(hat * (1.0 + gq_ref[...]), cosine, sine).astype(BF16)
        hat, inv = norm_parts(raw[:, head : 2 * head])
        khat_ref[rows, :] = hat
        kinv_ref[rows, :] = inv
        at = pl.ds(pl.multiple_of(half * (length // 2) + rank * size + u * tile, tile), tile)
        kv[g, at, :head] = rotate(hat * (1.0 + gk_ref[...]), cosine, sine).astype(BF16)
        kv[g, at, head:] = raw[:, 2 * head :].astype(BF16)

    def attend(g, half):
        row = lax.broadcasted_iota(jnp.int32, (size, size), 0)
        col = lax.broadcasted_iota(jnp.int32, (size, size), 1)
        rows = pl.ds((2 * g + half) * size, size)
        q = q_ref[rows, :] * jnp.asarray(SCALE, BF16)
        qseg = qs_ref[g, half]

        def part(block):
            at = pl.ds(pl.multiple_of(block * size, size), size)
            device = lax.axis_index("dp") * lax.axis_size("ctx") + lax.rem(block, blocks)
            ids = ks_ref[device, pl.ds((2 * g + lax.div(block, blocks)) * id_rows, id_rows), :]
            ids = jnp.concatenate([ids[j : j + 1] for j in range(id_rows)], axis=1)
            same = qseg == jnp.where(ids == 0, -1, ids)
            return dot(q, kv[g, at, :head], NT), kv[g, at, head:], same

        s, v, same = part(rank + half * blocks)
        order = (col <= row) if half == 0 else (col >= row)
        s = jnp.where((same & order) | (col == row), s, NEGATIVE)
        top = jnp.max(s, axis=1, keepdims=True)
        p = jnp.exp(s - top)
        mass = jnp.sum(p, axis=1, keepdims=True)
        acc = dot(p.astype(BF16), v)

        def step(t, carry):
            top, mass, acc = carry
            s, v, same = part(block_starts(half, t, blocks, rank))
            s = jnp.where(same, s, NEGATIVE)
            new = jnp.maximum(top, jnp.max(s, axis=1, keepdims=True))
            keep = jnp.exp(top - new)
            p = jnp.exp(s - new)
            mass = mass * keep + jnp.sum(p, axis=1, keepdims=True)
            return new, mass, acc * keep + dot(p.astype(BF16), v)

        count = rank if half == 0 else 2 * blocks - 1 - rank
        top, mass, acc = lax.fori_loop(0, count, step, (top, mass, acc))
        out = (acc / mass).astype(BF16)
        heads_ref[rows, :] = out
        whole[rows, pl.ds(pl.multiple_of(z * head, head), head)] = out
        log_ref[g, half] = top + jnp.log(mass)

    chips = range(1, group.chips)
    tiles = 2 * groups

    def exchange(t):
        for stage in (4, 3, 2, 1):
            if not 0 <= t - stage < tiles:
                continue
            g, half = divmod(t - stage, 2)
            for k in chips:
                spot = keys.tile_of(g, half, k)
                if stage == 1:
                    direct(g, half, k, True).wait_recv()
                if stage <= 3:
                    keys.forward(spot, stage - 1)
                else:
                    keys.arrived(spot)
                    inner(g, half, k).start()

    def hops(t):
        for hop in range(3):
            if 0 <= t - hop < tiles:
                line.forward(t - hop, hop)

    def keep(t):
        at = pl.ds(t * size, size)
        return pltpu.make_async_copy(whole.at[at], all_out.at[at], store_all.at[t])

    def save(g):
        return pltpu.make_async_copy(kv.at[g], kv_out.at[g], store_kv.at[g])

    for t in range(tiles):
        g, half = divmod(t, 2)
        for u in range(size // tile):
            project(g, half, u)
        for k in chips:
            direct(g, half, k).start()
        inner(g, half, 0).start()
        exchange(t)
    at_step = tiles
    for g in range(groups):
        while at_step < min(2 * g + 6, tiles + 4):
            exchange(at_step)
            at_step += 1
        for half in range(2):
            for k in range(group.chips):
                inner(g, half, k, True).wait_recv()
        save(g).start()
        for half in range(2):
            attend(g, half)
            if at_step < tiles + 4:
                exchange(at_step)
                at_step += 1
            hops(2 * g + half)
    for t in range(tiles, tiles + 2):
        hops(t)
    for t in range(tiles):
        line.arrived(t)
        keep(t).start()
    for g in range(groups):
        save(g).wait()
        for half in range(2):
            for k in chips:
                direct(g, half, k).wait_send()
            for k in range(group.chips):
                inner(g, half, k).wait_send()
    line.finish(tiles)
    keys.finish(tiles * (group.chips - 1))
    for t in range(tiles):
        keep(t).wait()


def attention(x, w, gains, gain_query, gain_key, cosine, sine, qseg, ids, length, ident):
    rows, width = x.shape
    groups, _, size, _ = qseg.shape
    head = gain_query.shape[1]
    chips = length // (4 * size)
    tiles = 2 * groups
    vmem = pl.BlockSpec(memory_space=pltpu.VMEM)
    dma = pltpu.SemaphoreType.DMA
    return pl.pallas_call(
        functools.partial(attention_kernel, groups, size),
        out_shape=(
            jax.ShapeDtypeStruct((rows, head), BF16),
            jax.ShapeDtypeStruct((rows, head), F32),
            jax.ShapeDtypeStruct((rows, 1), F32),
            jax.ShapeDtypeStruct((rows, head), F32),
            jax.ShapeDtypeStruct((rows, 1), F32),
            jax.ShapeDtypeStruct((rows, head), BF16),
            jax.ShapeDtypeStruct((groups, 2, size, 1), F32),
            jax.ShapeDtypeStruct((groups, length, 2 * head), BF16),
            jax.ShapeDtypeStruct((rows, 4 * head), BF16),
        ),
        in_specs=[vmem] * 9,
        out_specs=(vmem,) * 7 + (ANY, ANY),
        scratch_shapes=[
            pltpu.VMEM((groups, length, 2 * head), BF16), pltpu.VMEM((rows, 4 * head), BF16),
            dma((groups,)), dma((tiles,))] + [dma((groups, 2, chips))] * 4 + [dma((3, tiles))] * 4
        + [dma((3, tiles * (chips - 1)))] * 4,
        compiler_params=pltpu.CompilerParams(
            collective_id=ident, has_side_effects=True, vmem_limit_bytes=60 * 2**20),
        cost_estimate=cost(110),
        name="attention",
    )(x, w, gains, gain_query, gain_key, cosine, sine, qseg, ids)


class ResidentSum(LineSum):
    def outwards(self, c):
        return pltpu.make_async_remote_copy(
            self.out.at[self.rows(c)], self.out.at[self.rows(c)], self.sems[4].at[c], self.sems[5].at[c],
            device_id={"tp": self.my_leaf}, device_id_type=MESH)

    def total(self, c):
        @pl.when(self.hub)
        def _():
            self.across(c).wait_recv()
            at = self.rows(c)
            self.out[at, :] = (self.own[at, :].astype(F32) + self.far[at, :].astype(F32)).astype(BF16)
            self.outwards(c).start()

    def arrived(self, c):
        @pl.when(self.leaf)
        def _():
            self.outwards(c).wait_recv()

    def finish(self):
        @pl.when(self.leaf)
        def _():
            for c in range(self.count):
                self.inwards(c).wait_send()

        @pl.when(self.hub)
        def _():
            for c in range(self.count):
                self.across(c).wait_send()
                self.outwards(c).wait_send()


def turned(column, size):
    return jnp.transpose(jnp.broadcast_to(column, (size, 128)))[0:1, :]


def attention_back_kernel(groups, size, q_ref, do_ref, log_ref, delta_ref, qs_ref, ids_ref, hat_ref, inv_ref, cos_ref, sin_ref,
                          x_ref, gain_ref, gq_ref, go_ref, kv_hbm, all_out, dkv_ref, dgain_ref, grad_ref,
                          kv, dk, dv, part, near, pair, far, whole, acc, load, store, ss1, rs1, ss2, rs2, *sems):
    head = q_ref.shape[1]
    length = kv.shape[1]
    blocks = length // (2 * size)
    id_rows = size // 128
    tiles = 2 * groups
    group = Shared(False)
    rank, core = group.me, group.core
    line = LineGather(whole, size, head, sems)
    z = line.z
    others = range(1, group.chips)
    order = list(others) + [0]

    def fetch(g):
        return pltpu.make_async_copy(kv_hbm.at[g], kv.at[g], load.at[g])

    for g in range(groups):
        fetch(g).start()
    group.greet(z)
    acc[...] = jnp.zeros_like(acc)
    dgain_ref[...] = jnp.zeros_like(dgain_ref)

    def rows_of(half, device):
        return pl.ds(pl.multiple_of(half * (length // 2) + device * size, size), size)

    def within(g, half, k):
        to = group.other(k) + 1 - 2 * core
        return group.copy(
            part.at[g, rows_of(half, to)], near.at[g, half, k], ss1.at[g, half, k], rs1.at[g, half, k], group.partner())

    def between(g, half, k):
        return group.copy(
            pair.at[g, half, k - 1], far.at[g, half, k - 1], ss2.at[g, half, k], rs2.at[g, half, k], group.other(k))

    def both_cores(g):
        for half in range(2):
            for k in order:
                within(g, half, k).wait_recv()
                total = part[g, rows_of(half, group.other(k)), :].astype(F32) + near[g, half, k].astype(F32)
                if k > 0:
                    pair[g, half, k - 1] = total.astype(BF16)
                    between(g, half, k).start()
                else:
                    dkv_ref[pl.ds((2 * g + half) * size, size), :] = total.astype(BF16)

    def all_chips(g):
        for half in range(2):
            at = pl.ds((2 * g + half) * size, size)
            total = dkv_ref[at, :].astype(F32)
            for k in others:
                between(g, half, k).wait_recv()
                total = total + far[g, half, k - 1].astype(F32)
            dkv_ref[at, :] = total.astype(BF16)

    def hops(t):
        for hop in range(3):
            if 0 <= t - hop < tiles:
                line.forward(t - hop, hop)

    def attend(g, half):
        row = lax.broadcasted_iota(jnp.int32, (size, size), 0)
        col = lax.broadcasted_iota(jnp.int32, (size, size), 1)
        own = pl.ds((2 * g + half) * size, size)
        q = q_ref[own, :] * jnp.asarray(SCALE, BF16)
        do = do_ref[own, :]
        qseg = qs_ref[g, half]
        log_mass = turned(log_ref[g, half], size)
        delta = turned(delta_ref[own, :], size)

        def step_of(block, mine):
            at = pl.ds(pl.multiple_of(block * size, size), size)
            k = kv[g, at, :head]
            v = kv[g, at, head:]
            device = lax.axis_index("dp") * lax.axis_size("ctx") + lax.rem(block, blocks)
            ids = ids_ref[device, pl.ds((2 * g + lax.div(block, blocks)) * id_rows, id_rows), :]
            ids = jnp.concatenate([ids[j : j + 1] for j in range(id_rows)], axis=1)
            ids = jnp.transpose(jnp.broadcast_to(jnp.where(ids == 0, -1, ids), (8, size)))[:, 0:1]
            allowed = ids == qseg
            if mine:
                ahead = (row <= col) if half == 0 else (row >= col)
                allowed = (allowed & ahead) | (col == row)
            s = jnp.where(allowed, dot(k, q, NT), NEGATIVE)
            p = jnp.exp(s - log_mass)
            ds = (p * (dot(v, do, NT) - delta)).astype(BF16)
            dv[at, :] += dot(p.astype(BF16), do)
            dk[at, :] += dot(ds, q)
            return dot(ds, k, TN)

        def step(t, dq):
            return dq + step_of(block_starts(half, t, blocks, rank), False)

        dq = step_of(rank + half * blocks, True)
        count = rank if half == 0 else 2 * blocks - 1 - rank
        dq = SCALE * lax.fori_loop(0, count, step, dq)
        spot = pl.ds(half * size, size)
        d_rot = rotate(dq, cos_ref[spot, :], -sin_ref[spot, :])
        d_raw, d_gain = norm_back(d_rot, hat_ref[own, :], inv_ref[own, :], gq_ref[...])
        dgain_ref[...] += d_gain[None]
        whole[own, pl.ds(pl.multiple_of(z * head, head), head)] = d_raw.astype(BF16)

    def weight_gradient(t):
        own = pl.ds(t * size, size)
        hat, _ = norm_parts(x_ref[own, :].astype(F32))
        one = (hat * (1.0 + gain_ref[0:1, :])).astype(BF16)
        acc[...] += dot(one, whole[own, pl.ds(pl.multiple_of(z * head, head), head)], TN)

    def keep(t):
        at = pl.ds(t * size, size)
        return pltpu.make_async_copy(whole.at[at], all_out.at[at], store.at[t])

    for g in range(groups):
        fetch(g).wait()
        dk[...] = jnp.zeros_like(dk)
        dv[...] = jnp.zeros_like(dv)
        for half in range(2):
            attend(g, half)
            hops(2 * g + half)
            if half == 0 and g > 0:
                both_cores(g - 1)
        part[g, :, :head] = dk[...].astype(BF16)
        part[g, :, head:] = dv[...].astype(BF16)
        for half in range(2):
            for k in order:
                within(g, half, k).start()
        for half in range(2):
            weight_gradient(2 * g + half)
        if g > 0:
            all_chips(g - 1)
    hops(tiles)
    both_cores(groups - 1)
    hops(tiles + 1)
    grad_ref[:, :head] = acc[...].astype(BF16)
    grad_ref[:, head:] = go_ref[...]
    for t in range(tiles):
        line.arrived(t)
        keep(t).start()
    all_chips(groups - 1)
    for g in range(groups):
        for half in range(2):
            for k in others:
                between(g, half, k).wait_send()
            for k in order:
                within(g, half, k).wait_send()
    line.finish(tiles)
    for t in range(tiles):
        keep(t).wait()


def attention_back(q, d_heads, log_mass, delta, qseg, ids, hat, inv, cosine, sine, x, gains, gain_query, grad_o, kv, ident):
    rows, head = q.shape
    width = x.shape[1]
    groups, length, _ = kv.shape
    size = rows // (2 * groups)
    chips = length // (4 * size)
    tiles = 2 * groups
    vmem = pl.BlockSpec(memory_space=pltpu.VMEM)
    dma = pltpu.SemaphoreType.DMA
    return pl.pallas_call(
        functools.partial(attention_back_kernel, groups, size),
        out_shape=(
            jax.ShapeDtypeStruct((rows, 4 * head), BF16),
            jax.ShapeDtypeStruct((rows, 2 * head), BF16),
            jax.ShapeDtypeStruct((1, head), F32),
            jax.ShapeDtypeStruct((width, 2 * head), BF16),
        ),
        in_specs=[vmem] * 14 + [ANY],
        out_specs=(ANY, vmem, vmem, vmem),
        scratch_shapes=[
            pltpu.VMEM((groups, length, 2 * head), BF16),
            pltpu.VMEM((length, head), F32), pltpu.VMEM((length, head), F32),
            pltpu.VMEM((groups, length, 2 * head), BF16),
            pltpu.VMEM((groups, 2, chips, size, 2 * head), BF16),
            pltpu.VMEM((groups, 2, chips - 1, size, 2 * head), BF16),
            pltpu.VMEM((groups, 2, chips - 1, size, 2 * head), BF16),
            pltpu.VMEM((rows, 4 * head), BF16),
            pltpu.VMEM((width, head), F32),
            dma((groups,)), dma((tiles,))] + [dma((groups, 2, chips))] * 4 + [dma((3, tiles))] * 4,
        compiler_params=pltpu.CompilerParams(
            collective_id=ident, has_side_effects=True, vmem_limit_bytes=63 * 2**20),
        cost_estimate=cost(80),
        name="attention_back",
    )(q, d_heads, log_mass, delta, qseg, ids, hat, inv, cosine, sine, x, gains, gain_query, grad_o, kv)


class RowScatter:
    def __init__(self, group, own_rows, source, near, pair, far, sems):
        self.group, self.own_rows, self.source = group, own_rows, source
        self.near, self.pair, self.far, self.sems = near, pair, far, sems
        self.others = list(range(1, group.chips))
        self.order = self.others + [0]

    def block(self, device):
        return pl.ds(pl.multiple_of(device * self.own_rows, 16), self.own_rows)

    def within(self, k):
        g = self.group
        return g.copy(self.source.at[self.block(g.other(k) + 1 - 2 * g.core)], self.near.at[k],
                      self.sems[0].at[k], self.sems[1].at[k], g.partner())

    def between(self, k):
        g = self.group
        return g.copy(self.pair.at[k], self.far.at[k], self.sems[2].at[k], self.sems[3].at[k], g.other(k))

    def send(self):
        for k in self.order:
            self.within(k).start()

    def middle(self, out):
        for k in self.order:
            self.within(k).wait_recv()
            both = self.source[self.block(self.group.other(k)), :].astype(F32) + self.near[k].astype(F32)
            if k > 0:
                self.pair[k] = both.astype(BF16)
                self.between(k).start()
            else:
                out[...] = both

    def final(self, out):
        for k in self.others:
            self.between(k).wait_recv()
            out[...] += self.far[k].astype(F32)
        for k in self.others:
            self.between(k).wait_send()
        for k in self.order:
            self.within(k).wait_send()


def row_scatter_scratch(chips, own_rows, cols):
    return [pltpu.VMEM((chips, own_rows, cols), BF16)] * 3 + [pltpu.SemaphoreType.DMA((chips,))] * 4


def key_back_kernel(tiles, tile, chunk, own_rows, scattered, dkv_ref, hat_ref, inv_ref, cos_ref, sin_ref, x_ref, dm_ref, dq_ref,
                    gain_ref, gk_ref, w_ref, wq_ref, dgq_ref, dg_mid_ref, dg_post_ref, qo_ref,
                    dx_ref, last_out, qo_out, acc, acc_in, acc_key, w_kv, w_sem, last_ref, part,
                    out, own, near, far, *sems):
    i = pl.program_id(0)
    head = hat_ref.shape[1]
    per = tile // chunk
    count = tiles * per + 1
    line = ResidentSum(count, chunk, count, own, near, far, out, sems[:9])
    group = Shared(True)
    if scattered:
        early = RowScatter(group, own_rows, qo_ref, *sems[9:12], sems[12:16])
        late = RowScatter(group, own_rows, last_ref, *sems[16:19], sems[19:23])

    @pl.when(i == 0)
    def _():
        copy = pltpu.make_async_copy(w_ref.at[:, pl.ds(head, 2 * head)], w_kv, w_sem)
        copy.start()
        if scattered:
            group.greet(line.z)
            early.send()
        else:
            barrier_line(line.z)
            qo_out[...] = qo_ref[...]
        for ref in (acc, acc_in, acc_key):
            ref[...] = jnp.zeros_like(ref)
        copy.wait()
        line.put(count - 1, jnp.broadcast_to(
            jnp.concatenate([dgq_ref[...], dgq_ref[...]], axis=1).astype(BF16), (chunk, 2 * head)))

    @pl.when(i < tiles)
    def _():
        for j in range(per):
            line.put(i * per + j, dkv_ref[j * chunk : (j + 1) * chunk, :])
        part[pl.ds(pl.multiple_of(i * tile, tile), tile), :] = dot(dq_ref[...], wq_ref[...], NT)

    @pl.when((i >= 1) & (i <= tiles))
    def _():
        for j in range(per):
            line.pair((i - 1) * per + j)

    @pl.when((i >= 2) & (i <= tiles + 1))
    def _():
        for j in range(per):
            line.total((i - 2) * per + j)

    @pl.when(i == 1)
    def _():
        line.pair(count - 1)

    @pl.when(i == 2)
    def _():
        line.total(count - 1)
        if scattered:
            early.middle(qo_out)

    if scattered:
        @pl.when(i == tiles)
        def _():
            early.final(qo_out)

    @pl.when(i >= 3)
    def _():
        for j in range(per):
            line.arrived((i - 3) * per + j)
        d_kv = out[pl.ds(pl.multiple_of((i - 3) * tile, tile), tile), :]
        d_rot = rotate(d_kv[:, :head].astype(F32), cos_ref[...], -sin_ref[...])
        d_raw, d_gain = norm_back(d_rot, hat_ref[...], inv_ref[...], gk_ref[...])
        acc_key[...] += d_gain[None]
        d_raw = jnp.concatenate([d_raw.astype(BF16), d_kv[:, head:]], axis=1)
        d_one = part[pl.ds(pl.multiple_of((i - 3) * tile, tile), tile), :] + dot(d_raw, w_kv[...], NT)
        hat, inv = norm_parts(x_ref[...].astype(F32))
        gain = gain_ref[0:1, :]
        d_part, d_gain = norm_back(d_one, hat, inv, gain)
        acc_in[...] += d_gain[None]
        dx_ref[...] = dm_ref[...] + d_part
        acc[...] += dot((hat * (1.0 + gain)).astype(BF16), d_raw, TN)

    @pl.when(i == tiles + 2)
    def _():
        line.arrived(count - 1)
        width = x_ref.shape[1]
        short = head * own_rows // width
        last_ref[:, : 2 * head] = acc[...].astype(BF16)
        d_query = out[pl.ds((count - 1) * chunk, 16), :head][0:1].astype(F32)
        pair = jnp.concatenate([d_query, acc_key[...], jnp.zeros((14, head), F32)], axis=0).astype(BF16)
        col = lax.broadcasted_iota(jnp.int32, (head, width), 1)
        row = lax.broadcasted_iota(jnp.int32, (head, width), 0)
        shift = short.bit_length() - 1
        spot = lax.shift_right_logical(row, shift) * own_rows + (row & (short - 1))
        spread = dot(pair, jnp.where(col == spot, 1.0, 0.0).astype(BF16))
        gains = jnp.concatenate(
            [acc_in[...], dg_mid_ref[...], dg_post_ref[...], spread[0:2], jnp.zeros((122, width), F32)], axis=0)
        last_ref[:, 2 * head :] = jnp.transpose(gains).astype(BF16)
        if scattered:
            late.send()
            line.finish()
            late.middle(last_out)
            late.final(last_out)
        else:
            last_out[...] = last_ref[...]
            line.finish()


def key_back(d_kv, hat, inv, cosine, sine, x, d_middle, d_query, gains, gain_key, first, w_query, dg_query, dg_mid, dg_post,
             grad_qo, own_rows, ident):
    rows, width = x.shape
    head = hat.shape[1]
    tile, chunk = 256, 128
    tiles = rows // tile
    count = rows // chunk + 1
    dma = pltpu.SemaphoreType.DMA((count,))

    def late(cols):
        return pl.BlockSpec((tile, cols), lambda i: (jnp.maximum(i - 3, 0), 0))

    def fixed(shape):
        return pl.BlockSpec(shape, lambda i: (0, 0))

    turns = cosine.shape[0] // tile
    turn = pl.BlockSpec((tile, head // 2), lambda i: (lax.rem(jnp.maximum(i - 3, 0), turns), 0))
    comm = pltpu.VMEM((count * chunk, 2 * head), BF16)
    scattered = own_rows % 16 == 0
    chips = width // (2 * own_rows)
    last = (width, 2 * head + 128)
    more = []
    if scattered:
        last_out, qo_out, kind = (own_rows, last[1]), (own_rows, 2 * head), F32
        for cols in (2 * head, last[1]):
            more += row_scatter_scratch(chips, own_rows, cols)
    else:
        last_out, qo_out, kind = last, grad_qo.shape, BF16
    return pl.pallas_call(
        functools.partial(key_back_kernel, tiles, tile, chunk, own_rows, scattered),
        grid=(tiles + 3,),
        out_shape=(
            jax.ShapeDtypeStruct((rows, width), F32),
            jax.ShapeDtypeStruct(last_out, kind),
            jax.ShapeDtypeStruct(qo_out, kind),
        ),
        in_specs=[pl.BlockSpec((tile, 2 * head), lambda i: (jnp.minimum(i, tiles - 1), 0)),
                  late(head), late(1), turn, turn, late(width), late(width),
                  pl.BlockSpec((tile, 4 * head), lambda i: (jnp.minimum(i, tiles - 1), 0)),
                  whole_block(gains.shape), whole_block(gain_key.shape), ANY]
        + [whole_block(a.shape) for a in (w_query, dg_query, dg_mid, dg_post, grad_qo)],
        out_specs=(late(width), fixed(last_out), fixed(qo_out)),
        scratch_shapes=[
            pltpu.VMEM((width, 2 * head), F32), pltpu.VMEM((1, width), F32), pltpu.VMEM((1, head), F32),
            pltpu.VMEM((width, 2 * head), BF16), pltpu.SemaphoreType.DMA, pltpu.VMEM(last, BF16),
            pltpu.VMEM((rows, width), F32)] + [comm] * 4 + [dma] * 7
        + [pltpu.SemaphoreType.REGULAR] * 2 + more,
        compiler_params=pltpu.CompilerParams(
            collective_id=ident, has_side_effects=True, vmem_limit_bytes=56 * 2**20),
        cost_estimate=cost(75),
        name="key_back",
    )(d_kv, hat, inv, cosine, sine, x, d_middle, d_query, gains, gain_key, first, w_query, dg_query, dg_mid, dg_post, grad_qo)


def shards(tokens, segments, cotangent, w_query, w_key, w_value, w_out, w_gate, w_up, w_down,
           g_input, g_post_attn, g_pre_ffn, g_post_ffn, g_query, g_key):
    batches, seq_local, _, size, width = tokens.shape
    head = w_key.shape[1]
    groups = batches * seq_local
    per_group = 2 * size
    rows = groups * per_group
    ctx = lax.axis_size("ctx")
    length = per_group * ctx
    rank = lax.axis_index("ctx")
    shared = ("dp", "ctx")
    own_rows = g_input.shape[0]
    hidden = w_gate.shape[1]

    def column(gain):
        return jnp.pad(gain, (0, own_rows - gain.shape[0]))[:, None]

    own_ids = segments.reshape(groups, 2, size)
    id_rows = own_ids.size // 128
    ids = jnp.pad(own_ids.reshape(id_rows, 128), ((0, -id_rows % 16), (0, 0)))
    extra = jnp.concatenate(
        [column(g) for g in (g_input, g_post_attn, g_pre_ffn, g_post_ffn, g_query, g_key)], axis=1)
    extra = jnp.pad(extra, ((0, 0), (0, 128 - extra.shape[1])))

    def rows_of_16(w):
        return jnp.pad(w, ((0, -own_rows % 16), (0, 0)))

    first, line_query, line_out, ids = first_gather(
        rows_of_16(jnp.concatenate([w_query, w_key, w_value, extra], axis=1)),
        rows_of_16(w_query), rows_of_16(w_out.T), ids, width // own_rows, 5)
    first = first[:, :own_rows].reshape(width, -1)
    side = first[:, 3 * head :]
    gain_cols = side[:, :8].astype(F32)
    gain_rows = gain_cols.T
    gain_input = gain_rows[0]
    short = g_query.shape[0]
    gain_query, gain_key = (
        gain_cols[:, i].reshape(-1, own_rows)[:, :short].reshape(-1) for i in (4, 5))

    wide = wide_of(hidden)
    second = jnp.concatenate(
        [line_out[:own_rows]] + [jnp.pad(w, ((0, 0), (0, wide - hidden))) for w in (w_gate, w_up, w_down.T)], axis=1)
    weights = lax.all_gather(second, shared, axis=0, tiled=True)

    offsets = rank * size + jnp.arange(size, dtype=jnp.int32)
    position = jnp.concatenate([offsets, length - 1 - offsets]).astype(F32)
    cosine, sine = angles(position, head // 2, head)

    x_rows = tokens.reshape(rows, width)
    dy_rows = cotangent.reshape(rows, width)
    queries, q_hat, q_scale, k_hat, k_scale, heads_own, log_mass, kv, heads_all = attention(
        x_rows, first, gain_rows, gain_query[None], gain_key[None], cosine, sine, own_ids[..., None], ids, length, 0)

    line_query, heads_all = lax.optimization_barrier((line_query[:own_rows], heads_all))
    query_full = lax.all_gather(line_query, shared, axis=0, tiled=True)
    attn, hidden_two, gate, up, ffn_out = ffn_forward(x_rows, heads_all, gain_rows, weights, hidden, 1)
    ffn_out, query_full = lax.optimization_barrier((ffn_out, query_full))
    d_gain_post_ffn, grad_ffn, d_two = ffn_backward(
        dy_rows, ffn_out, hidden_two, gate, up, gain_rows, weights, 2)
    grad_ffn = lax.psum_scatter(grad_ffn, shared, scatter_dimension=1, tiled=True)
    output, d_middle, d_heads, delta, d_gain_mid, grad_out_t = middle_back(
        x_rows, attn, dy_rows, d_two, ffn_out, heads_own, gain_rows, weights)

    d_q_all, d_kv, d_gain_query, grad_qo = attention_back(
        queries, d_heads, log_mass, delta, own_ids[:, :, None, :], ids, q_hat, q_scale, cosine, sine, x_rows, gain_rows,
        gain_query[None], grad_out_t, kv, 4)
    d_tokens, last, grad_qo = key_back(
        d_kv, k_hat, k_scale, cosine, sine, x_rows, d_middle, d_q_all, gain_rows, gain_key[None],
        first, query_full, d_gain_query, d_gain_mid, d_gain_post_ffn, grad_qo, own_rows, 3)
    grad_ffn = grad_ffn.astype(F32)
    if own_rows % 16:
        last = lax.psum_scatter(last, shared, scatter_dimension=0, tiled=True).astype(F32)
        grad_qo = lax.psum_scatter(grad_qo, shared, scatter_dimension=0, tiled=True).astype(F32)
    g = last[:, 2 * head :]
    return (
        output.reshape(tokens.shape),
        d_tokens.reshape(tokens.shape),
        grad_qo[:, :head],
        last[:, :head],
        last[:, head : 2 * head],
        grad_qo[:, head:].T,
        grad_ffn[0],
        grad_ffn[1],
        grad_ffn[2].T,
        g[:, 0],
        g[:, 1],
        g[:, 2],
        g[:, 3],
        g[:short, 4],
        g[:short, 5],
    )


def solution(mesh):
    shared = ("dp", "ctx")
    rows = P(None, "dp", None, "ctx", None)
    weights = (
        P(shared, "tp"), P(shared, None), P(shared, None), P("tp", shared),
        P(shared, "tp"), P(shared, "tp"), P("tp", shared),
    )
    gains = (P(shared),) * 6
    return jax.shard_map(
        shards,
        mesh=mesh,
        in_specs=(rows, P(None, "dp", None, "ctx"), rows) + weights + gains,
        out_specs=(rows, rows) + weights + gains,
        check_vma=False,
    )
```

```python
import functools

import jax
import jax.numpy as jnp
from jax import lax
from jax.experimental import pallas as pl
from jax.experimental.pallas import tpu as pltpu
from jax.sharding import PartitionSpec as P

EPS = 1e-06
THETA = 1000000.0
SCALE = 0.0625
NEGATIVE = -1e30
BF16 = jnp.bfloat16
F32 = jnp.float32
MESH = pl.DeviceIdType.MESH
NN = (((1,), (0,)), ((), ()))
NT = (((1,), (1,)), ((), ()))
TN = (((0,), (0,)), ((), ()))


def dot(a, b, dims=NN):
    return lax.dot_general(a, b, dims, preferred_element_type=F32)


def cost(us):
    return pl.CostEstimate(flops=int(us * 1.1e9), bytes_accessed=0, transcendentals=0)


def barrier_line(z):
    bar = pltpu.get_barrier_semaphore()

    @pl.when(z > 0)
    def _():
        pl.semaphore_signal(bar, inc=1, device_id={"tp": z - 1}, device_id_type=MESH)

    @pl.when(z < 3)
    def _():
        pl.semaphore_signal(bar, inc=1, device_id={"tp": z + 1}, device_id_type=MESH)

    pl.semaphore_wait(bar, jnp.where((z == 0) | (z == 3), 1, 2))


def block_starts(half, t, blocks, rank):
    if half == 0:
        return t
    return jnp.where(t < blocks, t, t + rank + 1)


def angles(position, half_size, full_size):
    frequency = THETA ** (-2.0 * jnp.arange(half_size, dtype=F32) / full_size)
    turned = position[:, None] * frequency[None, :]
    return (jnp.cos(turned), jnp.sin(turned))


def rotate(tensor, cosine, sine):
    half_size = tensor.shape[-1] // 2
    a = tensor[..., :half_size]
    b = tensor[..., half_size:]
    return jnp.concatenate([a * cosine - b * sine, b * cosine + a * sine], axis=-1)


def norm_parts(values):
    inv = lax.rsqrt(jnp.mean(values * values, axis=-1, keepdims=True) + EPS)
    return (values * inv, inv)


def norm_back(upstream, normalized, inv, gain):
    d_norm = upstream * (1.0 + gain)
    d_values = inv * (d_norm - normalized * jnp.mean(d_norm * normalized, axis=-1, keepdims=True))
    return (d_values, jnp.sum(upstream * normalized, axis=0))


def gelu_tanh(values):
    return jax.nn.gelu(values, approximate=True)


class LineSum:
    def __init__(self, count, chunk, slots, own, near, far, out, sems):
        self.count, self.chunk, self.slots = count, chunk, slots
        self.own, self.near, self.far, self.out = own, near, far, out
        self.sems = sems
        self.z = z = lax.axis_index("tp")
        self.hub = (z == 1) | (z == 2)
        self.leaf = (z == 0) | (z == 3)
        self.other_hub = jnp.where(z == 1, 2, 1)
        self.my_hub = jnp.where(z == 0, 1, 2)
        self.my_leaf = jnp.where(z == 1, 0, 3)

    def slot(self, c):
        return pl.ds(pl.multiple_of(lax.rem(c, self.slots) * self.chunk, self.chunk), self.chunk)

    def rows(self, c):
        return pl.ds(pl.multiple_of(c * self.chunk, self.chunk), self.chunk)

    def inwards(self, c):
        return pltpu.make_async_remote_copy(
            self.own.at[self.slot(c)], self.near.at[self.slot(c)], self.sems[0].at[c], self.sems[1].at[c],
            device_id={"tp": self.my_hub}, device_id_type=MESH)

    def across(self, c):
        return pltpu.make_async_remote_copy(
            self.own.at[self.slot(c)], self.far.at[self.slot(c)], self.sems[2].at[c], self.sems[3].at[c],
            device_id={"tp": self.other_hub}, device_id_type=MESH)

    def outwards(self, c):
        return pltpu.make_async_remote_copy(
            self.far.at[self.slot(c)], self.out.at[self.rows(c)], self.sems[4].at[c], self.sems[5].at[c],
            device_id={"tp": self.my_leaf}, device_id_type=MESH)

    def store(self, c):
        return pltpu.make_async_copy(self.far.at[self.slot(c)], self.out.at[self.rows(c)], self.sems[6].at[c])

    def put(self, c, value):
        ring = self.slots < self.count
        if ring:
            @pl.when(c >= self.slots)
            def _():
                @pl.when(self.leaf)
                def _():
                    self.inwards(c - self.slots).wait_send()

                @pl.when(self.hub)
                def _():
                    self.across(c - self.slots).wait_send()

        self.own[self.slot(c), :] = value

        @pl.when(self.leaf)
        def _():
            if ring:
                @pl.when(c >= self.slots)
                def _():
                    pl.semaphore_wait(self.sems[7], 1)
            self.inwards(c).start()

    def pair(self, c):
        ring = self.slots < self.count

        @pl.when(self.hub)
        def _():
            self.inwards(c).wait_recv()
            at = self.slot(c)
            self.own[at, :] = (self.own[at, :].astype(F32) + self.near[at, :].astype(F32)).astype(BF16)
            if ring:
                @pl.when(c < self.count - self.slots)
                def _():
                    pl.semaphore_signal(self.sems[7], inc=1, device_id={"tp": self.my_leaf}, device_id_type=MESH)

                @pl.when(c >= self.slots)
                def _():
                    pl.semaphore_wait(self.sems[8], 1)
            self.across(c).start()

    def total(self, c):
        @pl.when(self.hub)
        def _():
            self.across(c).wait_recv()
            at = self.slot(c)
            self.far[at, :] = (self.own[at, :].astype(F32) + self.far[at, :].astype(F32)).astype(BF16)
            self.outwards(c).start()
            self.store(c).start()

    def retire(self, c):
        @pl.when(self.hub)
        def _():
            self.outwards(c).wait_send()
            self.store(c).wait()
            if self.slots < self.count:
                @pl.when(c < self.count - self.slots)
                def _():
                    pl.semaphore_signal(self.sems[8], inc=1, device_id={"tp": self.other_hub}, device_id_type=MESH)

    def finish(self):
        first = max(0, self.count - self.slots)

        @pl.when(self.leaf)
        def _():
            for c in range(self.count):
                self.outwards(c).wait_recv()
            for c in range(first, self.count):
                self.inwards(c).wait_send()

        @pl.when(self.hub)
        def _():
            for c in range(first, self.count):
                self.across(c).wait_send()


def line_sum_scratch(count, chunk, slots, cols):
    dma = pltpu.SemaphoreType.DMA((count,))
    regular = pltpu.SemaphoreType.REGULAR
    return [pltpu.VMEM((slots * chunk, cols), BF16)] * 3 + [dma] * 7 + [regular] * 2


def gelu_parts(v):
    c = 0.7978845608028654
    square = v * v
    t = jnp.tanh(v * (c + (c * 0.044715) * square))
    half = 0.5 + 0.5 * t
    value = v * half
    slope = half + (0.5 * v) * (1.0 - t * t) * (c + (3.0 * c * 0.044715) * square)
    return value, slope


def column_parts(cols):
    middle = -(-cols // 256) * 128
    return [(0, middle), (middle, cols)] if middle < cols else [(0, cols)]


def middle_of(x, attn, gain_post_attn):
    hat, inv = norm_parts(attn.astype(F32))
    return x.astype(F32) + hat * (1.0 + gain_post_attn), hat, inv


def load_ffn_weights(weights, refs, sem):
    wide = refs[0].shape[1]
    base = weights.shape[1] - 3 * wide
    return [
        pltpu.make_async_copy(weights.at[:, pl.ds(base + j * wide, wide)], ref, sem.at[j])
        for j, ref in enumerate(refs)
    ]


def ffn_forward_kernel(tiles, tile, chunk, hidden, x_ref, h_ref, gain_ref, w_ref,
                       attn_ref, two_ref, gate_ref, up_ref, out_ref, wo_ref, wg_ref, wu_ref, wd_ref, w_sem, own, near, far, *sems):
    i = pl.program_id(0)
    per = tile // chunk
    line = LineSum(tiles * per, chunk, tiles * per, own, near, far, out_ref, sems)
    head = wo_ref.shape[1] // 4

    @pl.when(i == 0)
    def _():
        copies = load_ffn_weights(w_ref, (wg_ref, wu_ref, wd_ref), w_sem)
        copies.append(pltpu.make_async_copy(w_ref.at[:, pl.ds(0, 4 * head)], wo_ref, w_sem.at[3]))
        for copy in copies:
            copy.start()
        barrier_line(line.z)
        for copy in copies:
            copy.wait()

    attn = dot(h_ref[...], wo_ref[...], NT).astype(BF16)
    attn_ref[...] = attn
    middle, _, _ = middle_of(x_ref[...], attn, gain_ref[1:2, :])
    hat, _ = norm_parts(middle)
    two = (hat * (1.0 + gain_ref[2:3, :])).astype(BF16)
    two_ref[...] = two
    part = None
    for a, b in column_parts(hidden):
        gate = dot(two, wg_ref[:, a:b])
        up = dot(two, wu_ref[:, a:b])
        gate_ref[:, a:b] = gate.astype(BF16)
        up_ref[:, a:b] = up.astype(BF16)
        value, _ = gelu_parts(gate)
        more = dot((value * up).astype(BF16), wd_ref[:, a:b], NT)
        part = more if part is None else part + more
    for j in range(per):
        line.put(i * per + j, part[j * chunk : (j + 1) * chunk].astype(BF16))

    @pl.when(i >= 1)
    def _():
        for j in range(per):
            line.pair((i - 1) * per + j)

    @pl.when(i >= 2)
    def _():
        for j in range(per):
            line.total((i - 2) * per + j)

    @pl.when(i == tiles - 1)
    def _():
        last = tiles * per
        for j in range(per):
            line.pair(last - per + j)
        for c in range(max(0, last - 2 * per), last):
            line.total(c)
        for c in range(last):
            line.retire(c)
        line.finish()


def whole_block(shape):
    return pl.BlockSpec(shape, lambda i: (0,) * len(shape), pipeline_mode=pl.Buffered(1))


def tile_block(tile, cols):
    return pl.BlockSpec((tile, cols), lambda i: (i, 0))


ANY = pl.BlockSpec(memory_space=pl.ANY)


def wide_of(hidden):
    return -(-hidden // 128) * 128


def ffn_forward(x, heads, gains, weights, hidden, ident):
    rows, width = x.shape
    all_heads = heads.shape[1]
    tile, chunk = 128, 128
    tiles = rows // tile
    count = rows // chunk
    wide = wide_of(hidden)
    return pl.pallas_call(
        functools.partial(ffn_forward_kernel, tiles, tile, chunk, hidden),
        grid=(tiles,),
        out_shape=(
            jax.ShapeDtypeStruct((rows, width), BF16),
            jax.ShapeDtypeStruct((rows, width), BF16),
            jax.ShapeDtypeStruct((rows, hidden), BF16),
            jax.ShapeDtypeStruct((rows, hidden), BF16),
            jax.ShapeDtypeStruct((rows, width), BF16),
        ),
        in_specs=[
            tile_block(tile, width),
            tile_block(tile, all_heads),
            whole_block(gains.shape),
            ANY,
        ],
        out_specs=(tile_block(tile, width), tile_block(tile, width), tile_block(tile, hidden), tile_block(tile, hidden), ANY),
        scratch_shapes=[pltpu.VMEM((width, all_heads), BF16)] + [pltpu.VMEM((width, wide), BF16)] * 3
        + [pltpu.SemaphoreType.DMA((4,))]
        + line_sum_scratch(count, chunk, count, width),
        compiler_params=pltpu.CompilerParams(
            collective_id=ident, has_side_effects=True, vmem_limit_bytes=60 * 2**20),
        cost_estimate=cost(140),
        name="ffn_forward",
    )(x, heads, gains, weights)


def ffn_backward_kernel(tiles, tile, chunk, slots, hidden, dy_ref, ffn_ref, two_ref, gate_ref, up_ref,
                        gain_ref, w_ref,
                        dgain_ref, grad_ref, out_ref, wg_ref, wu_ref, wd_ref, w_sem,
                        acc_g, acc_u, acc_d, keep_g, keep_u, keep_h, stage, stage_sem, own, near, far, *sems):
    i = pl.program_id(0)
    per = tile // chunk
    last = tiles * per
    line = LineSum(last, chunk, slots, own, near, far, out_ref, sems)

    @pl.when(i == 0)
    def _():
        copies = load_ffn_weights(w_ref, (wg_ref, wu_ref, wd_ref), w_sem)
        for copy in copies:
            copy.start()
        barrier_line(line.z)
        for acc in (acc_g, acc_u, acc_d, dgain_ref):
            acc[...] = jnp.zeros_like(acc)
        for copy in copies:
            copy.wait()

    hat, inv = norm_parts(ffn_ref[...].astype(F32))
    gain = gain_ref[3:4, :]
    d_ffn, d_gain = norm_back(dy_ref[...].astype(F32), hat, inv, gain)
    dgain_ref[...] += d_gain[None]
    d_ffn = d_ffn.astype(BF16)
    part = None
    for a, b in column_parts(hidden):
        d_hidden = dot(d_ffn, wd_ref[:, a:b])
        up = up_ref[:, a:b].astype(F32)
        value, slope = gelu_parts(gate_ref[:, a:b].astype(F32))
        keep_h[:, a:b] = (value * up).astype(BF16)
        d_gate = (d_hidden * up * slope).astype(BF16)
        d_up = (d_hidden * value).astype(BF16)
        keep_g[:, a:b] = d_gate
        keep_u[:, a:b] = d_up
        more = dot(d_gate, wg_ref[:, a:b], NT) + dot(d_up, wu_ref[:, a:b], NT)
        part = more if part is None else part + more
    for j in range(per):
        line.put(i * per + j, part[j * chunk : (j + 1) * chunk].astype(BF16))

    @pl.when(i >= 1)
    def _():
        for j in range(per):
            line.pair((i - 1) * per + j)

    acc_g[...] += dot(two_ref[...], keep_g[...], TN)
    acc_u[...] += dot(two_ref[...], keep_u[...], TN)
    acc_d[...] += dot(d_ffn, keep_h[...], TN)

    @pl.when(i >= 2)
    def _():
        for j in range(per):
            line.total((i - 2) * per + j)

    @pl.when(i >= 3)
    def _():
        for j in range(per):
            line.retire((i - 3) * per + j)

    @pl.when(i == tiles - 1)
    def _():
        for j in range(per):
            line.pair(last - per + j)
        step = stage.shape[1]
        count = acc_g.shape[0] // step

        def piece(acc, out, k, at):
            @pl.when(k >= 2)
            def _():
                pltpu.make_async_copy(stage.at[at], out.at[pl.ds(0, step)], stage_sem.at[at]).wait()
            rows = pl.ds(pl.multiple_of(k * step, step), step)
            stage[at] = acc[rows, :].astype(BF16)
            pltpu.make_async_copy(stage.at[at], out.at[rows], stage_sem.at[at]).start()

        for acc, out in ((acc_g, grad_ref.at[0]), (acc_u, grad_ref.at[1]), (acc_d, grad_ref.at[2])):
            def pieces(k, _):
                piece(acc, out, k, lax.rem(k, 2))
                return 0

            lax.fori_loop(0, count, pieces, 0)
            for at in range(2):
                pltpu.make_async_copy(stage.at[at], out.at[pl.ds(0, step)], stage_sem.at[at]).wait()
            if acc is acc_g:
                for c in range(max(0, last - 2 * per), last - per):
                    line.total(c)
            if acc is acc_u:
                for c in range(last - per, last):
                    line.total(c)
        for c in range(max(0, last - 3 * per), last):
            line.retire(c)
        line.finish()


def ffn_backward(dy, ffn, two, gate, up, gains, weights, ident):
    rows, width = dy.shape
    hidden = gate.shape[1]
    wide = wide_of(hidden)
    tile, chunk = 256, 128
    tiles = rows // tile
    count = rows // chunk
    slots = min(count, 6)
    step = 144
    acc = pltpu.VMEM((width, hidden), F32)
    keep = pltpu.VMEM((tile, hidden), BF16)
    return pl.pallas_call(
        functools.partial(ffn_backward_kernel, tiles, tile, chunk, slots, hidden),
        grid=(tiles,),
        out_shape=(
            jax.ShapeDtypeStruct((1, width), F32),
            jax.ShapeDtypeStruct((3, width, hidden), BF16),
            jax.ShapeDtypeStruct((rows, width), BF16),
        ),
        in_specs=[tile_block(tile, width)] * 3 + [tile_block(tile, hidden)] * 2
        + [whole_block(gains.shape), ANY],
        out_specs=(pl.BlockSpec((1, width), lambda i: (0, 0)), ANY, ANY),
        scratch_shapes=[pltpu.VMEM((width, wide), BF16)] * 3 + [pltpu.SemaphoreType.DMA((3,))] + [acc] * 3 + [keep] * 3
        + [pltpu.VMEM((2, step, hidden), BF16), pltpu.SemaphoreType.DMA((2,))]
        + line_sum_scratch(count, chunk, slots, width),
        compiler_params=pltpu.CompilerParams(
            collective_id=ident, has_side_effects=True, vmem_limit_bytes=63 * 2**20),
        cost_estimate=cost(145),
        name="ffn_backward",
    )(dy, ffn, two, gate, up, gains, weights)


def middle_back_kernel(x_ref, attn_ref, dy_ref, d2_ref, ffn_ref, h_ref, gain_ref, w_ref,
                       y_ref, dm_ref, dh_ref, delta_ref, dgain_ref, go_ref, acc, wo_ref, w_sem):
    i = pl.program_id(0)

    @pl.when(i == 0)
    def _():
        head = wo_ref.shape[1]
        at = pl.multiple_of(lax.axis_index("tp") * head, head)
        copy = pltpu.make_async_copy(w_ref.at[:, pl.ds(at, head)], wo_ref, w_sem)
        copy.start()
        copy.wait()
        acc[...] = jnp.zeros_like(acc)
        dgain_ref[...] = jnp.zeros_like(dgain_ref)

    middle, attn_hat, attn_inv = middle_of(x_ref[...], attn_ref[...], gain_ref[1:2, :])
    hat, _ = norm_parts(ffn_ref[...].astype(F32))
    y_ref[...] = (middle + hat * (1.0 + gain_ref[3:4, :])).astype(BF16)
    hat, inv = norm_parts(middle)
    d_part, d_gain = norm_back(d2_ref[...].astype(F32), hat, inv, gain_ref[2:3, :])
    dgain_ref[1:2, :] += d_gain[None]
    d_middle = dy_ref[...].astype(F32) + d_part
    dm_ref[...] = d_middle
    d_attn, d_gain = norm_back(d_middle, attn_hat, attn_inv, gain_ref[1:2, :])
    dgain_ref[0:1, :] += d_gain[None]
    d_attn = d_attn.astype(BF16)
    d_heads = dot(d_attn, wo_ref[...]).astype(BF16)
    dh_ref[...] = d_heads
    heads = h_ref[...]
    delta_ref[...] = jnp.sum(d_heads.astype(F32) * heads.astype(F32), axis=1, keepdims=True)
    acc[...] += dot(d_attn, heads, TN)

    @pl.when(i == pl.num_programs(0) - 1)
    def _():
        go_ref[...] = acc[...].astype(BF16)


def middle_back(x, attn, dy, d_two, ffn, heads, gains, weights):
    rows, width = x.shape
    head = heads.shape[1]
    tile = 256
    return pl.pallas_call(
        middle_back_kernel,
        grid=(rows // tile,),
        out_shape=(
            jax.ShapeDtypeStruct((rows, width), BF16),
            jax.ShapeDtypeStruct((rows, width), F32),
            jax.ShapeDtypeStruct((rows, head), BF16),
            jax.ShapeDtypeStruct((rows, 1), F32),
            jax.ShapeDtypeStruct((2, width), F32),
            jax.ShapeDtypeStruct((width, head), BF16),
        ),
        in_specs=[tile_block(tile, width)] * 5 + [tile_block(tile, head)] + [whole_block(gains.shape), ANY],
        out_specs=(
            tile_block(tile, width), tile_block(tile, width), tile_block(tile, head), tile_block(tile, 1),
            pl.BlockSpec((2, width), lambda i: (0, 0)), pl.BlockSpec((width, head), lambda i: (0, 0)),
        ),
        scratch_shapes=[pltpu.VMEM((width, head), F32), pltpu.VMEM((width, head), BF16), pltpu.SemaphoreType.DMA],
        compiler_params=pltpu.CompilerParams(vmem_limit_bytes=48 * 2**20),
        cost_estimate=cost(19),
        name="middle_back",
    )(x, attn, dy, d_two, ffn, heads, gains, weights)


class LineGather:
    def __init__(self, whole, tile, width, sems):
        self.whole, self.tile, self.width, self.sems = whole, tile, width, sems
        self.z = lax.axis_index("tp")

    def place(self, src, t):
        return self.whole.at[
            pl.ds(pl.multiple_of(t * self.tile, self.tile), self.tile),
            pl.ds(pl.multiple_of(src * self.width, self.width), self.width)]

    def send(self, src, t, hop, way):
        ss, rs = self.sems[:2] if way > 0 else self.sems[2:]
        place = self.place(src, t)
        return pltpu.make_async_remote_copy(
            place, place, ss.at[hop, t], rs.at[hop, t],
            device_id={"tp": self.z + way}, device_id_type=MESH)

    def going(self, hop, way):
        src = self.z - way * hop
        return src, (self.z + way >= 0) & (self.z + way <= 3) & (src >= 0) & (src <= 3)

    def coming(self, hop, way):
        src = self.z - way * (hop + 1)
        return src, (src >= 0) & (src <= 3)

    def forward(self, t, hop):
        for way in (1, -1):
            if hop > 0:
                self.wait(t, hop - 1, way)
            src, ok = self.going(hop, way)

            @pl.when(ok)
            def _():
                self.send(src, t, hop, way).start()

    def wait(self, t, hop, way):
        src, ok = self.coming(hop, way)

        @pl.when(ok)
        def _():
            self.send(src, t, hop, way).wait_recv()

    def arrived(self, t):
        for way in (1, -1):
            self.wait(t, 2, way)

    def finish(self, tiles):
        for hop in range(3):
            for way in (1, -1):
                src, ok = self.going(hop, way)

                @pl.when(ok)
                def _():
                    def one(t, _):
                        self.send(src, t, hop, way).wait_send()
                        return 0

                    lax.fori_loop(0, tiles, one, 0)


class KeyGather(LineGather):
    def __init__(self, block, chips, sems):
        self.block, self.chips, self.sems = block, chips, sems
        self.z = lax.axis_index("tp")

    def tile_of(self, g, half, k):
        return (2 * g + half) * (self.chips - 1) + k - 1

    def place(self, src, t):
        pair, k = divmod(t, self.chips - 1)
        return self.quarter(pair // 2, pair % 2, k + 1, src)

    def quarter(self, g, half, k, src, own=False):
        ref, start, size = self.block(g, half, k, own)
        rows = size // 4
        return ref.at[pl.ds(pl.multiple_of(start + src * rows, rows), rows)]

    def finish(self, tiles):
        for hop in range(3):
            for way in (1, -1):
                src, ok = self.going(hop, way)

                @pl.when(ok)
                def _():
                    for t in range(tiles):
                        self.send(src, t, hop, way).wait_send()


class Shared:
    def __init__(self, over_dp):
        self.ctx = ctx = lax.axis_size("ctx")
        me = lax.axis_index("ctx")
        self.devices = ctx
        if over_dp:
            me = me + lax.axis_index("dp") * ctx
            self.devices = ctx * lax.axis_size("dp")
        self.over_dp = over_dp
        self.me = me
        self.chips = self.devices // 2
        self.core = lax.rem(me, 2)
        self.chip = lax.div(me, 2)

    def ident(self, device):
        if self.over_dp:
            return {"dp": lax.div(device, self.ctx), "ctx": lax.rem(device, self.ctx)}
        return {"ctx": device}

    def other(self, k):
        return 2 * lax.rem(self.chip + k + self.chips, self.chips) + self.core

    def partner(self):
        return self.me + 1 - 2 * self.core

    def greet(self, z):
        bar = pltpu.get_barrier_semaphore()
        for device in [self.partner()] + [self.other(k) for k in range(1, self.chips)]:
            pl.semaphore_signal(bar, inc=1, device_id=self.ident(device), device_id_type=MESH)

        @pl.when(z > 0)
        def _():
            pl.semaphore_signal(bar, inc=1, device_id={"tp": z - 1}, device_id_type=MESH)

        @pl.when(z < 3)
        def _():
            pl.semaphore_signal(bar, inc=1, device_id={"tp": z + 1}, device_id_type=MESH)

        pl.semaphore_wait(bar, self.chips + jnp.where((z == 0) | (z == 3), 1, 2))

    def copy(self, source, target, send, recv, device):
        return pltpu.make_async_remote_copy(
            source, target, send, recv, device_id=self.ident(device), device_id_type=MESH)


def first_gather_kernel(a_ref, b_ref, c_ref, i_ref, all_ref, line_ref, more_ref, ids_ref, lsem, ss1, rs1, ss2, rs2, si1, ri1, si2, ri2, *sems):
    group = Shared(True)
    line = LineGather(line_ref, b_ref.shape[0], b_ref.shape[1], sems[:4])
    more = LineGather(more_ref, c_ref.shape[0], c_ref.shape[1], sems[4:])
    width = b_ref.shape[1]
    own = [
        pltpu.make_async_copy(b_ref, line_ref.at[:, pl.ds(pl.multiple_of(line.z * width, width), width)], lsem.at[0]),
        pltpu.make_async_copy(c_ref, more_ref.at[:, pl.ds(pl.multiple_of(line.z * width, width), width)], lsem.at[3]),
        pltpu.make_async_copy(a_ref, all_ref.at[group.me], lsem.at[1]),
        pltpu.make_async_copy(i_ref, ids_ref.at[group.me], lsem.at[2]),
    ]
    for copy in own:
        copy.start()
    group.greet(line.z)
    arrays = ((a_ref, all_ref, ss1, rs1, ss2, rs2), (i_ref, ids_ref, si1, ri1, si2, ri2))

    def direct(n, k, incoming=False):
        ref, whole, ss, rs = arrays[n][:4]
        at = whole.at[group.other(-k)] if incoming else whole.at[group.me]
        return group.copy(ref, at, ss.at[k], rs.at[k], group.other(k))

    def inner(n, k, incoming=False):
        ref, whole, _, _, ss, rs = arrays[n]
        at = whole.at[group.other(-k)]
        if incoming:
            at = whole.at[group.other(-k) + 1 - 2 * group.core]
        return group.copy(ref if k == 0 else at, at, ss.at[k], rs.at[k], group.partner())

    both = range(2)
    for k in range(1, group.chips):
        for n in both:
            direct(n, k).start()
    for n in both:
        inner(n, 0).start()
    own[0].wait()
    line.forward(0, 0)
    own[1].wait()
    more.forward(0, 0)
    for k in range(1, group.chips):
        if k < 3:
            line.forward(0, k)
            more.forward(0, k)
        for n in both:
            direct(n, k, True).wait_recv()
            inner(n, k).start()
    for hop in range(min(3, group.chips), 3):
        line.forward(0, hop)
        more.forward(0, hop)
    for k in range(group.chips):
        for n in both:
            inner(n, k, True).wait_recv()
    line.arrived(0)
    more.arrived(0)
    for copy in own[2:]:
        copy.wait()
    for n in both:
        for k in range(1, group.chips):
            direct(n, k).wait_send()
        for k in range(group.chips):
            inner(n, k).wait_send()
    line.finish(1)
    more.finish(1)


def first_gather(a, b, c, ids, devices, ident):
    dma = pltpu.SemaphoreType.DMA((devices // 2,))
    hop = pltpu.SemaphoreType.DMA((3, 1))
    return pl.pallas_call(
        first_gather_kernel,
        out_shape=(
            jax.ShapeDtypeStruct((devices,) + a.shape, a.dtype),
            jax.ShapeDtypeStruct((b.shape[0], 4 * b.shape[1]), b.dtype),
            jax.ShapeDtypeStruct((c.shape[0], 4 * c.shape[1]), c.dtype),
            jax.ShapeDtypeStruct((devices,) + ids.shape, ids.dtype),
        ),
        in_specs=[ANY] * 4,
        out_specs=(ANY,) * 4,
        scratch_shapes=[pltpu.SemaphoreType.DMA((4,))] + [dma] * 8 + [hop] * 8,
        compiler_params=pltpu.CompilerParams(collective_id=ident, has_side_effects=True),
        cost_estimate=cost(20),
        name="first_gather",
    )(a, b, c, ids)


def attention_kernel(groups, size, x_ref, w_ref, gain_ref, gq_ref, gk_ref, cos_ref, sin_ref, qs_ref, ks_ref,
                     q_ref, qhat_ref, qinv_ref, khat_ref, kinv_ref, heads_ref, log_ref, kv_out, all_out,
                     kv, whole, store_kv, store_all, ss1, rs1, ss2, rs2, *sems):
    head = q_ref.shape[1]
    length = kv.shape[1]
    id_rows = size // 128
    blocks = length // (2 * size)
    group = Shared(False)
    rank = group.me
    tile = min(256, size)
    per = size // tile
    line = LineGather(whole, tile, head, sems[:4])
    z = line.z
    group.greet(z)

    def block(g, half, k, own):
        c = rank if own else group.other(-k)
        return kv.at[g], half * (length // 2) + c * size, size

    keys = KeyGather(block, group.chips, sems[4:])

    def place(g, half, c):
        return kv.at[g, pl.ds(pl.multiple_of(half * (length // 2) + c * size, size), size)]

    def straight(t):
        return t == 2 * groups - 1

    def direct(g, half, k, incoming=False):
        at = keys.quarter(g, half, k, z, own=not incoming)
        if straight(2 * g + half):
            at = place(g, half, group.other(-k) if incoming else rank)
        return group.copy(at, at, ss1.at[g, half, k], rs1.at[g, half, k], group.other(k))

    def inner(g, half, k, incoming=False):
        block = group.other(-k)
        at = place(g, half, block + 1 - 2 * group.core if incoming else block)
        return group.copy(at, at, ss2.at[g, half, k], rs2.at[g, half, k], group.partner())

    def project(g, half, u):
        rows = pl.ds((2 * g + half) * size + u * tile, tile)
        spot = pl.ds(half * size + u * tile, tile)
        cosine, sine = cos_ref[spot, :], sin_ref[spot, :]
        hat, _ = norm_parts(x_ref[rows, :].astype(F32))
        raw = dot((hat * (1.0 + gain_ref[0:1, :])).astype(BF16), w_ref[:, : 3 * head])
        hat, inv = norm_parts(raw[:, :head])
        qhat_ref[rows, :] = hat
        qinv_ref[rows, :] = inv
        q_ref[rows, :] = rotate(hat * (1.0 + gq_ref[...]), cosine, sine).astype(BF16)
        hat, inv = norm_parts(raw[:, head : 2 * head])
        khat_ref[rows, :] = hat
        kinv_ref[rows, :] = inv
        at = pl.ds(pl.multiple_of(half * (length // 2) + rank * size + u * tile, tile), tile)
        kv[g, at, :head] = rotate(hat * (1.0 + gk_ref[...]), cosine, sine).astype(BF16)
        kv[g, at, head:] = raw[:, 2 * head :].astype(BF16)

    def attend(g, half):
        row = lax.broadcasted_iota(jnp.int32, (size, size), 0)
        col = lax.broadcasted_iota(jnp.int32, (size, size), 1)
        rows = pl.ds((2 * g + half) * size, size)
        q = q_ref[rows, :] * jnp.asarray(SCALE, BF16)
        qseg = qs_ref[g, half]

        def part(block):
            at = pl.ds(pl.multiple_of(block * size, size), size)
            device = lax.axis_index("dp") * lax.axis_size("ctx") + lax.rem(block, blocks)
            ids = ks_ref[device, pl.ds((2 * g + lax.div(block, blocks)) * id_rows, id_rows), :]
            ids = jnp.concatenate([ids[j : j + 1] for j in range(id_rows)], axis=1)
            same = qseg == jnp.where(ids == 0, -1, ids)
            return dot(q, kv[g, at, :head], NT), kv[g, at, head:], same

        s, v, same = part(rank + half * blocks)
        order = (col <= row) if half == 0 else (col >= row)
        s = jnp.where((same & order) | (col == row), s, NEGATIVE)
        top = jnp.max(s, axis=1, keepdims=True)
        p = jnp.exp(s - top)
        mass = jnp.sum(p, axis=1, keepdims=True)
        acc = dot(p.astype(BF16), v)

        def step(t, carry):
            top, mass, acc = carry
            s, v, same = part(block_starts(half, t, blocks, rank))
            s = jnp.where(same, s, NEGATIVE)
            new = jnp.maximum(top, jnp.max(s, axis=1, keepdims=True))
            keep = jnp.exp(top - new)
            p = jnp.exp(s - new)
            mass = mass * keep + jnp.sum(p, axis=1, keepdims=True)
            return new, mass, acc * keep + dot(p.astype(BF16), v)

        count = rank if half == 0 else 2 * blocks - 1 - rank
        top, mass, acc = lax.fori_loop(0, count, step, (top, mass, acc))
        out = (acc / mass).astype(BF16)
        heads_ref[rows, :] = out
        whole[rows, pl.ds(pl.multiple_of(z * head, head), head)] = out
        log_ref[g, half] = top + jnp.log(mass)

    chips = range(1, group.chips)
    tiles = 2 * groups

    def stage(t, n):
        if not 0 <= t < tiles:
            return
        g, half = divmod(t, 2)
        for k in chips:
            spot = keys.tile_of(g, half, k)
            if n == 0:
                direct(g, half, k).start()
            elif straight(t):
                if n == 4:
                    direct(g, half, k, True).wait_recv()
                    inner(g, half, k).start()
            elif n == 4:
                keys.arrived(spot)
                inner(g, half, k).start()
            else:
                if n == 1:
                    direct(g, half, k, True).wait_recv()
                keys.forward(spot, n - 1)

    def exchange(t):
        for n in (4, 3, 2, 1):
            stage(t - n, n)

    def hops(t):
        for hop in range(3):
            if 0 <= t - hop < tiles:
                for u in range(per):
                    line.forward((t - hop) * per + u, hop)

    def keep(t):
        at = pl.ds(t * tile, tile)
        return pltpu.make_async_copy(whole.at[at], all_out.at[at], store_all.at[t])

    def save(g):
        return pltpu.make_async_copy(kv.at[g], kv_out.at[g], store_kv.at[g])

    def landed(t):
        g, half = divmod(t, 2)
        for k in range(group.chips):
            inner(g, half, k, True).wait_recv()

    for t in range(tiles):
        g, half = divmod(t, 2)
        for u in range(per):
            project(g, half, u)
        stage(t, 0)
        inner(g, half, 0).start()
        exchange(t)
    for t in range(tiles):
        g, half = divmod(t, 2)
        exchange(tiles + t)
        landed(t)
        attend(g, half)
        hops(t)
    for g in range(groups):
        save(g).start()
    for t in range(tiles, tiles + 2):
        hops(t)
    for t in range(tiles * per):
        line.arrived(t)
        keep(t).start()
    for g in range(groups):
        save(g).wait()
        for half in range(2):
            for k in chips:
                direct(g, half, k).wait_send()
            for k in range(group.chips):
                inner(g, half, k).wait_send()
    line.finish(tiles * per)
    keys.finish((tiles - 1) * (group.chips - 1))
    for t in range(tiles * per):
        keep(t).wait()


def attention(x, w, gains, gain_query, gain_key, cosine, sine, qseg, ids, length, ident):
    rows, width = x.shape
    groups, _, size, _ = qseg.shape
    head = gain_query.shape[1]
    chips = length // (4 * size)
    tiles = 2 * groups
    parts = rows // min(256, size)
    vmem = pl.BlockSpec(memory_space=pltpu.VMEM)
    dma = pltpu.SemaphoreType.DMA
    return pl.pallas_call(
        functools.partial(attention_kernel, groups, size),
        out_shape=(
            jax.ShapeDtypeStruct((rows, head), BF16),
            jax.ShapeDtypeStruct((rows, head), F32),
            jax.ShapeDtypeStruct((rows, 1), F32),
            jax.ShapeDtypeStruct((rows, head), F32),
            jax.ShapeDtypeStruct((rows, 1), F32),
            jax.ShapeDtypeStruct((rows, head), BF16),
            jax.ShapeDtypeStruct((groups, 2, size, 1), F32),
            jax.ShapeDtypeStruct((groups, length, 2 * head), BF16),
            jax.ShapeDtypeStruct((rows, 4 * head), BF16),
        ),
        in_specs=[vmem] * 9,
        out_specs=(vmem,) * 7 + (ANY, ANY),
        scratch_shapes=[
            pltpu.VMEM((groups, length, 2 * head), BF16), pltpu.VMEM((rows, 4 * head), BF16),
            dma((groups,)), dma((parts,))] + [dma((groups, 2, chips))] * 4 + [dma((3, parts))] * 4
        + [dma((3, tiles * (chips - 1)))] * 4,
        compiler_params=pltpu.CompilerParams(
            collective_id=ident, has_side_effects=True, vmem_limit_bytes=60 * 2**20),
        cost_estimate=cost(110),
        name="attention",
    )(x, w, gains, gain_query, gain_key, cosine, sine, qseg, ids)


class ResidentSum(LineSum):
    def outwards(self, c):
        return pltpu.make_async_remote_copy(
            self.out.at[self.rows(c)], self.out.at[self.rows(c)], self.sems[4].at[c], self.sems[5].at[c],
            device_id={"tp": self.my_leaf}, device_id_type=MESH)

    def total(self, c):
        @pl.when(self.hub)
        def _():
            self.across(c).wait_recv()
            at = self.rows(c)
            self.out[at, :] = (self.own[at, :].astype(F32) + self.far[at, :].astype(F32)).astype(BF16)
            self.outwards(c).start()

    def arrived(self, c):
        @pl.when(self.leaf)
        def _():
            self.outwards(c).wait_recv()

    def finish(self):
        @pl.when(self.leaf)
        def _():
            for c in range(self.count):
                self.inwards(c).wait_send()

        @pl.when(self.hub)
        def _():
            for c in range(self.count):
                self.across(c).wait_send()
                self.outwards(c).wait_send()


def turned(column, size):
    return jnp.transpose(jnp.broadcast_to(column, (size, 128)))[0:1, :]


def attention_back_kernel(groups, size, q_ref, do_ref, log_ref, delta_ref, qs_ref, ids_ref, hat_ref, inv_ref, cos_ref, sin_ref,
                          x_ref, gain_ref, gq_ref, go_ref, kv_hbm, all_out, dkv_ref, rest_ref, dgain_ref, grad_ref,
                          kv, dk, dv, part, near, pair, far, whole, acc, load, store, ss1, rs1, ss2, rs2, *sems):
    head = q_ref.shape[1]
    length = kv.shape[1]
    blocks = length // (2 * size)
    id_rows = size // 128
    tiles = 2 * groups
    group = Shared(False)
    rank, core = group.me, group.core
    tile = min(256, size)
    per = size // tile
    line = LineGather(whole, tile, head, sems)
    z = line.z
    others = range(1, group.chips)
    order = list(others) + [0]

    def fetch(g):
        return pltpu.make_async_copy(kv_hbm.at[g], kv.at[g], load.at[g])

    for g in range(groups):
        fetch(g).start()
    group.greet(z)
    acc[...] = jnp.zeros_like(acc)
    dgain_ref[...] = jnp.zeros_like(dgain_ref)

    def rows_of(half, device):
        return pl.ds(pl.multiple_of(half * (length // 2) + device * size, size), size)

    def within(g, half, k):
        to = group.other(k) + 1 - 2 * core
        return group.copy(
            part.at[g, rows_of(half, to)], near.at[g, half, k], ss1.at[g, half, k], rs1.at[g, half, k], group.partner())

    def between(g, half, k):
        return group.copy(
            pair.at[g, half, k - 1], far.at[g, half, k - 1], ss2.at[g, half, k], rs2.at[g, half, k], group.other(k))

    def both_cores(g):
        for half in range(2):
            for k in order:
                within(g, half, k).wait_recv()
                total = part[g, rows_of(half, group.other(k)), :].astype(F32) + near[g, half, k].astype(F32)
                if k > 0 and g == groups - 1:
                    rest_ref[half, k - 1] = total.astype(BF16)
                elif k > 0:
                    pair[g, half, k - 1] = total.astype(BF16)
                    between(g, half, k).start()
                else:
                    dkv_ref[pl.ds((2 * g + half) * size, size), :] = total.astype(BF16)

    def all_chips(g):
        for half in range(2):
            at = pl.ds((2 * g + half) * size, size)
            total = dkv_ref[at, :].astype(F32)
            for k in others:
                between(g, half, k).wait_recv()
                total = total + far[g, half, k - 1].astype(F32)
            dkv_ref[at, :] = total.astype(BF16)

    def hops(t):
        for hop in range(3):
            if 0 <= t - hop < tiles:
                for u in range(per):
                    line.forward((t - hop) * per + u, hop)

    def attend(g, half):
        row = lax.broadcasted_iota(jnp.int32, (size, size), 0)
        col = lax.broadcasted_iota(jnp.int32, (size, size), 1)
        own = pl.ds((2 * g + half) * size, size)
        q = q_ref[own, :] * jnp.asarray(SCALE, BF16)
        do = do_ref[own, :]
        qseg = qs_ref[g, half]
        log_mass = turned(log_ref[g, half], size)
        delta = turned(delta_ref[own, :], size)

        def step_of(block, mine):
            at = pl.ds(pl.multiple_of(block * size, size), size)
            k = kv[g, at, :head]
            v = kv[g, at, head:]
            device = lax.axis_index("dp") * lax.axis_size("ctx") + lax.rem(block, blocks)
            ids = ids_ref[device, pl.ds((2 * g + lax.div(block, blocks)) * id_rows, id_rows), :]
            ids = jnp.concatenate([ids[j : j + 1] for j in range(id_rows)], axis=1)
            ids = jnp.transpose(jnp.broadcast_to(jnp.where(ids == 0, -1, ids), (8, size)))[:, 0:1]
            allowed = ids == qseg
            if mine:
                ahead = (row <= col) if half == 0 else (row >= col)
                allowed = (allowed & ahead) | (col == row)
            s = jnp.where(allowed, dot(k, q, NT), NEGATIVE)
            p = jnp.exp(s - log_mass)
            ds = (p * (dot(v, do, NT) - delta)).astype(BF16)
            dv[at, :] += dot(p.astype(BF16), do)
            dk[at, :] += dot(ds, q)
            return dot(ds, k, TN)

        def step(t, dq):
            return dq + step_of(block_starts(half, t, blocks, rank), False)

        dq = step_of(rank + half * blocks, True)
        count = rank if half == 0 else 2 * blocks - 1 - rank
        dq = SCALE * lax.fori_loop(0, count, step, dq)
        spot = pl.ds(half * size, size)
        d_rot = rotate(dq, cos_ref[spot, :], -sin_ref[spot, :])
        d_raw, d_gain = norm_back(d_rot, hat_ref[own, :], inv_ref[own, :], gq_ref[...])
        dgain_ref[...] += d_gain[None]
        whole[own, pl.ds(pl.multiple_of(z * head, head), head)] = d_raw.astype(BF16)

    def weight_gradient(t):
        own = pl.ds(t * size, size)
        hat, _ = norm_parts(x_ref[own, :].astype(F32))
        one = (hat * (1.0 + gain_ref[0:1, :])).astype(BF16)
        acc[...] += dot(one, whole[own, pl.ds(pl.multiple_of(z * head, head), head)], TN)

    def keep(t):
        at = pl.ds(t * tile, tile)
        return pltpu.make_async_copy(whole.at[at], all_out.at[at], store.at[t])

    for g in range(groups):
        fetch(g).wait()
        dk[...] = jnp.zeros_like(dk)
        dv[...] = jnp.zeros_like(dv)
        for half in range(2):
            attend(g, half)
            hops(2 * g + half)
            if half == 0 and g > 0:
                both_cores(g - 1)
        part[g, :, :head] = dk[...].astype(BF16)
        part[g, :, head:] = dv[...].astype(BF16)
        for half in range(2):
            for k in order:
                within(g, half, k).start()
        for half in range(2):
            weight_gradient(2 * g + half)
        if g > 0:
            all_chips(g - 1)
    hops(tiles)
    both_cores(groups - 1)
    hops(tiles + 1)
    grad_ref[:, :head] = acc[...].astype(BF16)
    grad_ref[:, head:] = go_ref[...]
    for t in range(tiles * per):
        line.arrived(t)
        keep(t).start()
    for g in range(groups):
        for half in range(2):
            if g < groups - 1:
                for k in others:
                    between(g, half, k).wait_send()
            for k in order:
                within(g, half, k).wait_send()
    line.finish(tiles * per)
    for t in range(tiles * per):
        keep(t).wait()


def attention_back(q, d_heads, log_mass, delta, qseg, ids, hat, inv, cosine, sine, x, gains, gain_query, grad_o, kv, ident):
    rows, head = q.shape
    width = x.shape[1]
    groups, length, _ = kv.shape
    size = rows // (2 * groups)
    chips = length // (4 * size)
    parts = rows // min(256, size)
    vmem = pl.BlockSpec(memory_space=pltpu.VMEM)
    dma = pltpu.SemaphoreType.DMA
    return pl.pallas_call(
        functools.partial(attention_back_kernel, groups, size),
        out_shape=(
            jax.ShapeDtypeStruct((rows, 4 * head), BF16),
            jax.ShapeDtypeStruct((rows, 2 * head), BF16),
            jax.ShapeDtypeStruct((2, chips - 1, size, 2 * head), BF16),
            jax.ShapeDtypeStruct((1, head), F32),
            jax.ShapeDtypeStruct((width, 2 * head), BF16),
        ),
        in_specs=[vmem] * 14 + [ANY],
        out_specs=(ANY, vmem, vmem, vmem, vmem),
        scratch_shapes=[
            pltpu.VMEM((groups, length, 2 * head), BF16),
            pltpu.VMEM((length, head), F32), pltpu.VMEM((length, head), F32),
            pltpu.VMEM((groups, length, 2 * head), BF16),
            pltpu.VMEM((groups, 2, chips, size, 2 * head), BF16),
            pltpu.VMEM((groups, 2, chips - 1, size, 2 * head), BF16),
            pltpu.VMEM((groups, 2, chips - 1, size, 2 * head), BF16),
            pltpu.VMEM((rows, 4 * head), BF16),
            pltpu.VMEM((width, head), F32),
            dma((groups,)), dma((parts,))] + [dma((groups, 2, chips))] * 4 + [dma((3, parts))] * 4,
        compiler_params=pltpu.CompilerParams(
            collective_id=ident, has_side_effects=True, vmem_limit_bytes=63 * 2**20),
        cost_estimate=cost(80),
        name="attention_back",
    )(q, d_heads, log_mass, delta, qseg, ids, hat, inv, cosine, sine, x, gains, gain_query, grad_o, kv)


class RowScatter:
    def __init__(self, group, own_rows, source, near, pair, far, sems):
        self.group, self.own_rows, self.source = group, own_rows, source
        self.near, self.pair, self.far, self.sems = near, pair, far, sems
        self.others = list(range(1, group.chips))
        self.order = self.others + [0]

    def block(self, device):
        return pl.ds(pl.multiple_of(device * self.own_rows, 16), self.own_rows)

    def within(self, k):
        g = self.group
        return g.copy(self.source.at[self.block(g.other(k) + 1 - 2 * g.core)], self.near.at[k],
                      self.sems[0].at[k], self.sems[1].at[k], g.partner())

    def between(self, k):
        g = self.group
        return g.copy(self.pair.at[k], self.far.at[k], self.sems[2].at[k], self.sems[3].at[k], g.other(k))

    def send(self):
        for k in self.order:
            self.within(k).start()

    def middle(self, out):
        for k in self.order:
            self.within(k).wait_recv()
            both = self.source[self.block(self.group.other(k)), :].astype(F32) + self.near[k].astype(F32)
            if k > 0:
                self.pair[k] = both.astype(BF16)
                self.between(k).start()
            else:
                out[...] = both

    def final(self, out):
        for k in self.others:
            self.between(k).wait_recv()
            out[...] += self.far[k].astype(F32)
        for k in self.others:
            self.between(k).wait_send()
        for k in self.order:
            self.within(k).wait_send()


def row_scatter_scratch(chips, own_rows, cols):
    return [pltpu.VMEM((chips, own_rows, cols), BF16)] * 3 + [pltpu.SemaphoreType.DMA((chips,))] * 4


def key_back_kernel(tiles, tile, chunk, own_rows, scattered, dkv_ref, hat_ref, inv_ref, cos_ref, sin_ref, x_ref, dm_ref, dq_ref,
                    gain_ref, gk_ref, w_ref, wq_ref, dgq_ref, dg_mid_ref, dg_post_ref, qo_ref, rest_ref,
                    dx_ref, last_out, qo_out, acc, acc_in, acc_key, w_kv, w_sem, last_ref, part,
                    add, ss, rs, out, own, near, far, *sems):
    i = pl.program_id(0)
    head = hat_ref.shape[1]
    per = tile // chunk
    count = tiles * per + 1
    line = ResidentSum(count, chunk, count, own, near, far, out, sems[:9])
    group = Shared(True)
    ring = Shared(False)
    size = rest_ref.shape[2]
    first = tiles * per - 2 * size // chunk

    def between(half, k):
        return ring.copy(rest_ref.at[half, k - 1], add.at[half, k - 1], ss.at[half, k], rs.at[half, k], ring.other(k))

    if scattered:
        early = RowScatter(group, own_rows, qo_ref, *sems[9:12], sems[12:16])
        late = RowScatter(group, own_rows, last_ref, *sems[16:19], sems[19:23])

    @pl.when(i == 0)
    def _():
        copy = pltpu.make_async_copy(w_ref.at[:, pl.ds(head, 2 * head)], w_kv, w_sem)
        copy.start()
        if scattered:
            group.greet(line.z)
        else:
            ring.greet(line.z)
            qo_out[...] = qo_ref[...]
        for half in range(2):
            for k in range(1, ring.chips):
                between(half, k).start()
        if scattered:
            early.send()
        for ref in (acc, acc_in, acc_key):
            ref[...] = jnp.zeros_like(ref)
        copy.wait()
        line.put(count - 1, jnp.broadcast_to(
            jnp.concatenate([dgq_ref[...], dgq_ref[...]], axis=1).astype(BF16), (chunk, 2 * head)))

    @pl.when(i < tiles)
    def _():
        for j in range(per):
            c = i * per + j
            mine = dkv_ref[j * chunk : (j + 1) * chunk, :]

            @pl.when(c < first)
            def _():
                line.put(c, mine)

            @pl.when(c >= first)
            def _():
                half = lax.div((c - first) * chunk, size)
                at = lax.rem((c - first) * chunk, size)

                @pl.when(at == 0)
                def _():
                    for k in range(1, ring.chips):
                        between(half, k).wait_recv()

                total = mine.astype(F32)
                for k in range(1, ring.chips):
                    total = total + add[half, k - 1, pl.ds(pl.multiple_of(at, chunk), chunk), :].astype(F32)
                line.put(c, total.astype(BF16))
        part[pl.ds(pl.multiple_of(i * tile, tile), tile), :] = dot(dq_ref[...], wq_ref[...], NT)

    @pl.when((i >= 1) & (i <= tiles))
    def _():
        for j in range(per):
            line.pair((i - 1) * per + j)

    @pl.when((i >= 2) & (i <= tiles + 1))
    def _():
        for j in range(per):
            line.total((i - 2) * per + j)

    @pl.when(i == 1)
    def _():
        line.pair(count - 1)

    @pl.when(i == 2)
    def _():
        line.total(count - 1)
        if scattered:
            early.middle(qo_out)

    if scattered:
        @pl.when(i == tiles)
        def _():
            early.final(qo_out)

    @pl.when(i >= 3)
    def _():
        for j in range(per):
            line.arrived((i - 3) * per + j)
        d_kv = out[pl.ds(pl.multiple_of((i - 3) * tile, tile), tile), :]
        d_rot = rotate(d_kv[:, :head].astype(F32), cos_ref[...], -sin_ref[...])
        d_raw, d_gain = norm_back(d_rot, hat_ref[...], inv_ref[...], gk_ref[...])
        acc_key[...] += d_gain[None]
        d_raw = jnp.concatenate([d_raw.astype(BF16), d_kv[:, head:]], axis=1)
        d_one = part[pl.ds(pl.multiple_of((i - 3) * tile, tile), tile), :] + dot(d_raw, w_kv[...], NT)
        hat, inv = norm_parts(x_ref[...].astype(F32))
        gain = gain_ref[0:1, :]
        d_part, d_gain = norm_back(d_one, hat, inv, gain)
        acc_in[...] += d_gain[None]
        dx_ref[...] = dm_ref[...] + d_part
        acc[...] += dot((hat * (1.0 + gain)).astype(BF16), d_raw, TN)

    @pl.when(i == tiles + 2)
    def _():
        for half in range(2):
            for k in range(1, ring.chips):
                between(half, k).wait_send()
        line.arrived(count - 1)
        width = x_ref.shape[1]
        short = head * own_rows // width
        last_ref[:, : 2 * head] = acc[...].astype(BF16)
        d_query = out[pl.ds((count - 1) * chunk, 16), :head][0:1].astype(F32)
        pair = jnp.concatenate([d_query, acc_key[...], jnp.zeros((14, head), F32)], axis=0).astype(BF16)
        col = lax.broadcasted_iota(jnp.int32, (head, width), 1)
        row = lax.broadcasted_iota(jnp.int32, (head, width), 0)
        shift = short.bit_length() - 1
        spot = lax.shift_right_logical(row, shift) * own_rows + (row & (short - 1))
        spread = dot(pair, jnp.where(col == spot, 1.0, 0.0).astype(BF16))
        gains = jnp.concatenate(
            [acc_in[...], dg_mid_ref[...], dg_post_ref[...], spread[0:2], jnp.zeros((122, width), F32)], axis=0)
        last_ref[:, 2 * head :] = jnp.transpose(gains).astype(BF16)
        if scattered:
            late.send()
            line.finish()
            late.middle(last_out)
            late.final(last_out)
        else:
            last_out[...] = last_ref[...]
            line.finish()


def key_back(d_kv, hat, inv, cosine, sine, x, d_middle, d_query, gains, gain_key, first, w_query, dg_query, dg_mid, dg_post,
             grad_qo, rest, own_rows, ident):
    rows, width = x.shape
    head = hat.shape[1]
    tile, chunk = 128, 128
    tiles = rows // tile
    count = rows // chunk + 1
    dma = pltpu.SemaphoreType.DMA((count,))

    def late(cols):
        return pl.BlockSpec((tile, cols), lambda i: (jnp.maximum(i - 3, 0), 0))

    def fixed(shape):
        return pl.BlockSpec(shape, lambda i: (0, 0))

    turns = cosine.shape[0] // tile
    turn = pl.BlockSpec((tile, head // 2), lambda i: (lax.rem(jnp.maximum(i - 3, 0), turns), 0))
    comm = pltpu.VMEM((count * chunk, 2 * head), BF16)
    scattered = own_rows % 16 == 0
    chips = width // (2 * own_rows)
    last = (width, 2 * head + 128)
    more = []
    if scattered:
        last_out, qo_out, kind = (own_rows, last[1]), (own_rows, 2 * head), F32
        for cols in (2 * head, last[1]):
            more += row_scatter_scratch(chips, own_rows, cols)
    else:
        last_out, qo_out, kind = last, grad_qo.shape, BF16
    return pl.pallas_call(
        functools.partial(key_back_kernel, tiles, tile, chunk, own_rows, scattered),
        grid=(tiles + 3,),
        out_shape=(
            jax.ShapeDtypeStruct((rows, width), F32),
            jax.ShapeDtypeStruct(last_out, kind),
            jax.ShapeDtypeStruct(qo_out, kind),
        ),
        in_specs=[pl.BlockSpec((tile, 2 * head), lambda i: (jnp.minimum(i, tiles - 1), 0)),
                  late(head), late(1), turn, turn, late(width), late(width),
                  pl.BlockSpec((tile, 4 * head), lambda i: (jnp.minimum(i, tiles - 1), 0)),
                  whole_block(gains.shape), whole_block(gain_key.shape), ANY]
        + [whole_block(a.shape) for a in (w_query, dg_query, dg_mid, dg_post, grad_qo, rest)],
        out_specs=(late(width), fixed(last_out), fixed(qo_out)),
        scratch_shapes=[
            pltpu.VMEM((width, 2 * head), F32), pltpu.VMEM((1, width), F32), pltpu.VMEM((1, head), F32),
            pltpu.VMEM((width, 2 * head), BF16), pltpu.SemaphoreType.DMA, pltpu.VMEM(last, BF16),
            pltpu.VMEM((rows, width), F32), pltpu.VMEM(rest.shape, BF16)]
        + [pltpu.SemaphoreType.DMA((2, rest.shape[1] + 1))] * 2 + [comm] * 4 + [dma] * 7
        + [pltpu.SemaphoreType.REGULAR] * 2 + more,
        compiler_params=pltpu.CompilerParams(
            collective_id=ident, has_side_effects=True, vmem_limit_bytes=56 * 2**20),
        cost_estimate=cost(75),
        name="key_back",
    )(d_kv, hat, inv, cosine, sine, x, d_middle, d_query, gains, gain_key, first, w_query, dg_query, dg_mid, dg_post, grad_qo, rest)


def shards(tokens, segments, cotangent, w_query, w_key, w_value, w_out, w_gate, w_up, w_down,
           g_input, g_post_attn, g_pre_ffn, g_post_ffn, g_query, g_key):
    batches, seq_local, _, size, width = tokens.shape
    head = w_key.shape[1]
    groups = batches * seq_local
    per_group = 2 * size
    rows = groups * per_group
    ctx = lax.axis_size("ctx")
    length = per_group * ctx
    rank = lax.axis_index("ctx")
    shared = ("dp", "ctx")
    own_rows = g_input.shape[0]
    hidden = w_gate.shape[1]

    def column(gain):
        return jnp.pad(gain, (0, own_rows - gain.shape[0]))[:, None]

    own_ids = segments.reshape(groups, 2, size)
    id_rows = own_ids.size // 128
    ids = jnp.pad(own_ids.reshape(id_rows, 128), ((0, -id_rows % 16), (0, 0)))
    extra = jnp.concatenate(
        [column(g) for g in (g_input, g_post_attn, g_pre_ffn, g_post_ffn, g_query, g_key)], axis=1)
    extra = jnp.pad(extra, ((0, 0), (0, 128 - extra.shape[1])))

    def rows_of_16(w):
        return jnp.pad(w, ((0, -own_rows % 16), (0, 0)))

    first, line_query, line_out, ids = first_gather(
        rows_of_16(jnp.concatenate([w_query, w_key, w_value, extra], axis=1)),
        rows_of_16(w_query), rows_of_16(w_out.T), ids, width // own_rows, 5)
    first = first[:, :own_rows].reshape(width, -1)
    side = first[:, 3 * head :]
    gain_cols = side[:, :8].astype(F32)
    gain_rows = gain_cols.T
    gain_input = gain_rows[0]
    short = g_query.shape[0]
    gain_query, gain_key = (
        gain_cols[:, i].reshape(-1, own_rows)[:, :short].reshape(-1) for i in (4, 5))

    wide = wide_of(hidden)
    second = jnp.concatenate(
        [line_out[:own_rows]] + [jnp.pad(w, ((0, 0), (0, wide - hidden))) for w in (w_gate, w_up, w_down.T)], axis=1)
    weights = lax.all_gather(second, shared, axis=0, tiled=True)

    offsets = rank * size + jnp.arange(size, dtype=jnp.int32)
    position = jnp.concatenate([offsets, length - 1 - offsets]).astype(F32)
    cosine, sine = angles(position, head // 2, head)

    x_rows = tokens.reshape(rows, width)
    dy_rows = cotangent.reshape(rows, width)
    queries, q_hat, q_scale, k_hat, k_scale, heads_own, log_mass, kv, heads_all = attention(
        x_rows, first, gain_rows, gain_query[None], gain_key[None], cosine, sine, own_ids[..., None], ids, length, 0)

    line_query, heads_all = lax.optimization_barrier((line_query[:own_rows], heads_all))
    query_full = lax.all_gather(line_query, shared, axis=0, tiled=True)
    attn, hidden_two, gate, up, ffn_out = ffn_forward(x_rows, heads_all, gain_rows, weights, hidden, 1)
    ffn_out, query_full = lax.optimization_barrier((ffn_out, query_full))
    d_gain_post_ffn, grad_ffn, d_two = ffn_backward(
        dy_rows, ffn_out, hidden_two, gate, up, gain_rows, weights, 2)
    grad_ffn = lax.psum_scatter(grad_ffn, shared, scatter_dimension=1, tiled=True)
    output, d_middle, d_heads, delta, d_gain_mid, grad_out_t = middle_back(
        x_rows, attn, dy_rows, d_two, ffn_out, heads_own, gain_rows, weights)

    d_q_all, d_kv, rest, d_gain_query, grad_qo = attention_back(
        queries, d_heads, log_mass, delta, own_ids[:, :, None, :], ids, q_hat, q_scale, cosine, sine, x_rows, gain_rows,
        gain_query[None], grad_out_t, kv, 4)
    d_tokens, last, grad_qo = key_back(
        d_kv, k_hat, k_scale, cosine, sine, x_rows, d_middle, d_q_all, gain_rows, gain_key[None],
        first, query_full, d_gain_query, d_gain_mid, d_gain_post_ffn, grad_qo, rest, own_rows, 3)
    grad_ffn = grad_ffn.astype(F32)
    if own_rows % 16:
        last = lax.psum_scatter(last, shared, scatter_dimension=0, tiled=True).astype(F32)
        grad_qo = lax.psum_scatter(grad_qo, shared, scatter_dimension=0, tiled=True).astype(F32)
    g = last[:, 2 * head :]
    return (
        output.reshape(tokens.shape),
        d_tokens.reshape(tokens.shape),
        grad_qo[:, :head],
        last[:, :head],
        last[:, head : 2 * head],
        grad_qo[:, head:].T,
        grad_ffn[0],
        grad_ffn[1],
        grad_ffn[2].T,
        g[:, 0],
        g[:, 1],
        g[:, 2],
        g[:, 3],
        g[:short, 4],
        g[:short, 5],
    )


def solution(mesh):
    shared = ("dp", "ctx")
    rows = P(None, "dp", None, "ctx", None)
    weights = (
        P(shared, "tp"), P(shared, None), P(shared, None), P("tp", shared),
        P(shared, "tp"), P(shared, "tp"), P("tp", shared),
    )
    gains = (P(shared),) * 6
    return jax.shard_map(
        shards,
        mesh=mesh,
        in_specs=(rows, P(None, "dp", None, "ctx"), rows) + weights + gains,
        out_specs=(rows, rows) + weights + gains,
        check_vma=False,
    )
```

```python
import functools

import jax
import jax.numpy as jnp
from jax import lax
from jax.experimental import pallas as pl
from jax.experimental.pallas import tpu as pltpu
from jax.sharding import PartitionSpec as P

EPS = 1e-06
THETA = 1000000.0
SCALE = 0.0625
NEGATIVE = -1e30
BF16 = jnp.bfloat16
F32 = jnp.float32
MESH = pl.DeviceIdType.MESH
NN = (((1,), (0,)), ((), ()))
NT = (((1,), (1,)), ((), ()))
TN = (((0,), (0,)), ((), ()))


def dot(a, b, dims=NN):
    return lax.dot_general(a, b, dims, preferred_element_type=F32)


def cost(us):
    return pl.CostEstimate(flops=int(us * 1.1e9), bytes_accessed=0, transcendentals=0)


def barrier_line(z):
    bar = pltpu.get_barrier_semaphore()

    @pl.when(z > 0)
    def _():
        pl.semaphore_signal(bar, inc=1, device_id={"tp": z - 1}, device_id_type=MESH)

    @pl.when(z < 3)
    def _():
        pl.semaphore_signal(bar, inc=1, device_id={"tp": z + 1}, device_id_type=MESH)

    pl.semaphore_wait(bar, jnp.where((z == 0) | (z == 3), 1, 2))


def block_starts(half, t, blocks, rank):
    if half == 0:
        return t
    return jnp.where(t < blocks, t, t + rank + 1)


def angles(position, half_size, full_size):
    frequency = THETA ** (-2.0 * jnp.arange(half_size, dtype=F32) / full_size)
    turned = position[:, None] * frequency[None, :]
    return (jnp.cos(turned), jnp.sin(turned))


def rotate(tensor, cosine, sine):
    half_size = tensor.shape[-1] // 2
    a = tensor[..., :half_size]
    b = tensor[..., half_size:]
    return jnp.concatenate([a * cosine - b * sine, b * cosine + a * sine], axis=-1)


def norm_parts(values):
    inv = lax.rsqrt(jnp.mean(values * values, axis=-1, keepdims=True) + EPS)
    return (values * inv, inv)


def norm_back(upstream, normalized, inv, gain):
    d_norm = upstream * (1.0 + gain)
    d_values = inv * (d_norm - normalized * jnp.mean(d_norm * normalized, axis=-1, keepdims=True))
    return (d_values, jnp.sum(upstream * normalized, axis=0))


def gelu_tanh(values):
    return jax.nn.gelu(values, approximate=True)


class LineSum:
    def __init__(self, count, chunk, slots, own, near, far, out, sems):
        self.count, self.chunk, self.slots = count, chunk, slots
        self.own, self.near, self.far, self.out = own, near, far, out
        self.sems = sems
        self.z = z = lax.axis_index("tp")
        self.hub = (z == 1) | (z == 2)
        self.leaf = (z == 0) | (z == 3)
        self.other_hub = jnp.where(z == 1, 2, 1)
        self.my_hub = jnp.where(z == 0, 1, 2)
        self.my_leaf = jnp.where(z == 1, 0, 3)

    def slot(self, c):
        return pl.ds(pl.multiple_of(lax.rem(c, self.slots) * self.chunk, self.chunk), self.chunk)

    def rows(self, c):
        return pl.ds(pl.multiple_of(c * self.chunk, self.chunk), self.chunk)

    def inwards(self, c):
        return pltpu.make_async_remote_copy(
            self.own.at[self.slot(c)], self.near.at[self.slot(c)], self.sems[0].at[c], self.sems[1].at[c],
            device_id={"tp": self.my_hub}, device_id_type=MESH)

    def across(self, c):
        return pltpu.make_async_remote_copy(
            self.own.at[self.slot(c)], self.far.at[self.slot(c)], self.sems[2].at[c], self.sems[3].at[c],
            device_id={"tp": self.other_hub}, device_id_type=MESH)

    def outwards(self, c):
        return pltpu.make_async_remote_copy(
            self.far.at[self.slot(c)], self.out.at[self.rows(c)], self.sems[4].at[c], self.sems[5].at[c],
            device_id={"tp": self.my_leaf}, device_id_type=MESH)

    def store(self, c):
        return pltpu.make_async_copy(self.far.at[self.slot(c)], self.out.at[self.rows(c)], self.sems[6].at[c])

    def put(self, c, value):
        ring = self.slots < self.count
        if ring:
            @pl.when(c >= self.slots)
            def _():
                @pl.when(self.leaf)
                def _():
                    self.inwards(c - self.slots).wait_send()

                @pl.when(self.hub)
                def _():
                    self.across(c - self.slots).wait_send()

        self.own[self.slot(c), :] = value

        @pl.when(self.leaf)
        def _():
            if ring:
                @pl.when(c >= self.slots)
                def _():
                    pl.semaphore_wait(self.sems[7], 1)
            self.inwards(c).start()

    def pair(self, c):
        ring = self.slots < self.count

        @pl.when(self.hub)
        def _():
            self.inwards(c).wait_recv()
            at = self.slot(c)
            self.own[at, :] = (self.own[at, :].astype(F32) + self.near[at, :].astype(F32)).astype(BF16)
            if ring:
                @pl.when(c < self.count - self.slots)
                def _():
                    pl.semaphore_signal(self.sems[7], inc=1, device_id={"tp": self.my_leaf}, device_id_type=MESH)

                @pl.when(c >= self.slots)
                def _():
                    pl.semaphore_wait(self.sems[8], 1)
            self.across(c).start()

    def total(self, c):
        @pl.when(self.hub)
        def _():
            self.across(c).wait_recv()
            at = self.slot(c)
            self.far[at, :] = (self.own[at, :].astype(F32) + self.far[at, :].astype(F32)).astype(BF16)
            self.outwards(c).start()
            self.store(c).start()

    def retire(self, c):
        @pl.when(self.hub)
        def _():
            self.outwards(c).wait_send()
            self.store(c).wait()
            if self.slots < self.count:
                @pl.when(c < self.count - self.slots)
                def _():
                    pl.semaphore_signal(self.sems[8], inc=1, device_id={"tp": self.other_hub}, device_id_type=MESH)

    def finish(self):
        first = max(0, self.count - self.slots)

        @pl.when(self.leaf)
        def _():
            for c in range(self.count):
                self.outwards(c).wait_recv()
            for c in range(first, self.count):
                self.inwards(c).wait_send()

        @pl.when(self.hub)
        def _():
            for c in range(first, self.count):
                self.across(c).wait_send()


def line_sum_scratch(count, chunk, slots, cols):
    dma = pltpu.SemaphoreType.DMA((count,))
    regular = pltpu.SemaphoreType.REGULAR
    return [pltpu.VMEM((slots * chunk, cols), BF16)] * 3 + [dma] * 7 + [regular] * 2


def gelu_parts(v):
    c = 0.7978845608028654
    square = v * v
    t = jnp.tanh(v * (c + (c * 0.044715) * square))
    half = 0.5 + 0.5 * t
    value = v * half
    slope = half + (0.5 * v) * (1.0 - t * t) * (c + (3.0 * c * 0.044715) * square)
    return value, slope


def column_parts(cols):
    middle = -(-cols // 256) * 128
    return [(0, middle), (middle, cols)] if middle < cols else [(0, cols)]


def middle_of(x, attn, gain_post_attn):
    hat, inv = norm_parts(attn.astype(F32))
    return x.astype(F32) + hat * (1.0 + gain_post_attn), hat, inv


def load_ffn_weights(weights, refs, sem):
    wide = refs[0].shape[1]
    base = weights.shape[1] - 3 * wide
    return [
        pltpu.make_async_copy(weights.at[:, pl.ds(base + j * wide, wide)], ref, sem.at[j])
        for j, ref in enumerate(refs)
    ]


def ffn_forward_kernel(tiles, tile, chunk, hidden, x_ref, h_ref, gain_ref, w_ref,
                       attn_ref, two_ref, gate_ref, up_ref, out_ref, wo_ref, wg_ref, wu_ref, wd_ref, w_sem, own, near, far, *sems):
    i = pl.program_id(0)
    per = tile // chunk
    line = LineSum(tiles * per, chunk, tiles * per, own, near, far, out_ref, sems)
    head = wo_ref.shape[1] // 4

    copies = [pltpu.make_async_copy(w_ref.at[:, pl.ds(0, 4 * head)], wo_ref, w_sem.at[3])]
    copies += load_ffn_weights(w_ref, (wg_ref, wu_ref, wd_ref), w_sem)

    @pl.when(i == 0)
    def _():
        for copy in copies:
            copy.start()
        barrier_line(line.z)
        copies[0].wait()

    attn = dot(h_ref[...], wo_ref[...], NT).astype(BF16)
    attn_ref[...] = attn
    middle, _, _ = middle_of(x_ref[...], attn, gain_ref[1:2, :])
    hat, _ = norm_parts(middle)
    two = (hat * (1.0 + gain_ref[2:3, :])).astype(BF16)
    two_ref[...] = two
    part = None

    @pl.when(i == 0)
    def _():
        for copy in copies[1:]:
            copy.wait()

    for a, b in column_parts(hidden):
        gate = dot(two, wg_ref[:, a:b])
        up = dot(two, wu_ref[:, a:b])
        gate_ref[:, a:b] = gate.astype(BF16)
        up_ref[:, a:b] = up.astype(BF16)
        value, _ = gelu_parts(gate)
        more = dot((value * up).astype(BF16), wd_ref[:, a:b], NT)
        part = more if part is None else part + more
    for j in range(per):
        line.put(i * per + j, part[j * chunk : (j + 1) * chunk].astype(BF16))

    @pl.when(i >= 1)
    def _():
        for j in range(per):
            line.pair((i - 1) * per + j)

    @pl.when(i >= 2)
    def _():
        for j in range(per):
            line.total((i - 2) * per + j)

    @pl.when(i == tiles - 1)
    def _():
        last = tiles * per
        for j in range(per):
            line.pair(last - per + j)
        for c in range(max(0, last - 2 * per), last):
            line.total(c)
        for c in range(last):
            line.retire(c)
        line.finish()


def whole_block(shape):
    return pl.BlockSpec(shape, lambda i: (0,) * len(shape), pipeline_mode=pl.Buffered(1))


def tile_block(tile, cols):
    return pl.BlockSpec((tile, cols), lambda i: (i, 0))


ANY = pl.BlockSpec(memory_space=pl.ANY)


def wide_of(hidden):
    return -(-hidden // 128) * 128


def ffn_forward(x, heads, gains, weights, hidden, ident):
    rows, width = x.shape
    all_heads = heads.shape[1]
    tile, chunk = 128, 128
    tiles = rows // tile
    count = rows // chunk
    wide = wide_of(hidden)
    return pl.pallas_call(
        functools.partial(ffn_forward_kernel, tiles, tile, chunk, hidden),
        grid=(tiles,),
        out_shape=(
            jax.ShapeDtypeStruct((rows, width), BF16),
            jax.ShapeDtypeStruct((rows, width), BF16),
            jax.ShapeDtypeStruct((rows, hidden), BF16),
            jax.ShapeDtypeStruct((rows, hidden), BF16),
            jax.ShapeDtypeStruct((rows, width), BF16),
        ),
        in_specs=[
            tile_block(tile, width),
            tile_block(tile, all_heads),
            whole_block(gains.shape),
            ANY,
        ],
        out_specs=(tile_block(tile, width), tile_block(tile, width), tile_block(tile, hidden), tile_block(tile, hidden), ANY),
        scratch_shapes=[pltpu.VMEM((width, all_heads), BF16)] + [pltpu.VMEM((width, wide), BF16)] * 3
        + [pltpu.SemaphoreType.DMA((4,))]
        + line_sum_scratch(count, chunk, count, width),
        compiler_params=pltpu.CompilerParams(
            collective_id=ident, has_side_effects=True, vmem_limit_bytes=60 * 2**20),
        cost_estimate=cost(140),
        name="ffn_forward",
    )(x, heads, gains, weights)


def ffn_backward_kernel(tiles, tile, chunk, slots, hidden, dy_ref, ffn_ref, two_ref, gate_ref, up_ref,
                        gain_ref, w_ref,
                        dgain_ref, grad_ref, out_ref, wg_ref, wu_ref, wd_ref, w_sem,
                        acc_g, acc_u, acc_d, keep_g, keep_u, keep_h, stage, stage_sem, own, near, far, *sems):
    i = pl.program_id(0)
    per = tile // chunk
    last = tiles * per
    line = LineSum(last, chunk, slots, own, near, far, out_ref, sems)

    copies = load_ffn_weights(w_ref, (wg_ref, wu_ref, wd_ref), w_sem)

    @pl.when(i == 0)
    def _():
        for copy in copies[::-1]:
            copy.start()
        barrier_line(line.z)
        dgain_ref[...] = jnp.zeros_like(dgain_ref)
        for copy in copies[::-1]:
            copy.wait()

    hat, inv = norm_parts(ffn_ref[...].astype(F32))
    gain = gain_ref[3:4, :]
    d_ffn, d_gain = norm_back(dy_ref[...].astype(F32), hat, inv, gain)
    dgain_ref[...] += d_gain[None]
    d_ffn = d_ffn.astype(BF16)
    part = None
    for a, b in column_parts(hidden):
        d_hidden = dot(d_ffn, wd_ref[:, a:b])
        up = up_ref[:, a:b].astype(F32)
        value, slope = gelu_parts(gate_ref[:, a:b].astype(F32))
        keep_h[:, a:b] = (value * up).astype(BF16)
        d_gate = (d_hidden * up * slope).astype(BF16)
        d_up = (d_hidden * value).astype(BF16)
        keep_g[:, a:b] = d_gate
        keep_u[:, a:b] = d_up
        more = dot(d_gate, wg_ref[:, a:b], NT) + dot(d_up, wu_ref[:, a:b], NT)
        part = more if part is None else part + more
    for j in range(per):
        line.put(i * per + j, part[j * chunk : (j + 1) * chunk].astype(BF16))

    @pl.when(i >= 1)
    def _():
        for j in range(per):
            line.pair((i - 1) * per + j)

    @pl.when(i == 0)
    def _():
        for acc in (acc_g, acc_u, acc_d):
            acc[...] = jnp.zeros_like(acc)

    acc_g[...] += dot(two_ref[...], keep_g[...], TN)
    acc_u[...] += dot(two_ref[...], keep_u[...], TN)
    acc_d[...] += dot(d_ffn, keep_h[...], TN)

    @pl.when(i >= 2)
    def _():
        for j in range(per):
            line.total((i - 2) * per + j)

    @pl.when(i >= 3)
    def _():
        for j in range(per):
            line.retire((i - 3) * per + j)

    @pl.when(i == tiles - 1)
    def _():
        for j in range(per):
            line.pair(last - per + j)
        step = stage.shape[1]
        count = acc_g.shape[0] // step

        def piece(acc, out, k, at):
            @pl.when(k >= 2)
            def _():
                pltpu.make_async_copy(stage.at[at], out.at[pl.ds(0, step)], stage_sem.at[at]).wait()
            rows = pl.ds(pl.multiple_of(k * step, step), step)
            stage[at] = acc[rows, :].astype(BF16)
            pltpu.make_async_copy(stage.at[at], out.at[rows], stage_sem.at[at]).start()

        for acc, out in ((acc_g, grad_ref.at[0]), (acc_u, grad_ref.at[1]), (acc_d, grad_ref.at[2])):
            def pieces(k, _):
                piece(acc, out, k, lax.rem(k, 2))
                return 0

            lax.fori_loop(0, count, pieces, 0)
            for at in range(2):
                pltpu.make_async_copy(stage.at[at], out.at[pl.ds(0, step)], stage_sem.at[at]).wait()
            if acc is acc_g:
                for c in range(max(0, last - 2 * per), last - per):
                    line.total(c)
            if acc is acc_u:
                for c in range(last - per, last):
                    line.total(c)
        for c in range(max(0, last - 3 * per), last):
            line.retire(c)
        line.finish()


def ffn_backward(dy, ffn, two, gate, up, gains, weights, ident):
    rows, width = dy.shape
    hidden = gate.shape[1]
    wide = wide_of(hidden)
    tile, chunk = 256, 128
    tiles = rows // tile
    count = rows // chunk
    slots = min(count, 6)
    step = 144
    acc = pltpu.VMEM((width, hidden), F32)
    keep = pltpu.VMEM((tile, hidden), BF16)
    return pl.pallas_call(
        functools.partial(ffn_backward_kernel, tiles, tile, chunk, slots, hidden),
        grid=(tiles,),
        out_shape=(
            jax.ShapeDtypeStruct((1, width), F32),
            jax.ShapeDtypeStruct((3, width, hidden), BF16),
            jax.ShapeDtypeStruct((rows, width), BF16),
        ),
        in_specs=[tile_block(tile, width)] * 3 + [tile_block(tile, hidden)] * 2
        + [whole_block(gains.shape), ANY],
        out_specs=(pl.BlockSpec((1, width), lambda i: (0, 0)), ANY, ANY),
        scratch_shapes=[pltpu.VMEM((width, wide), BF16)] * 3 + [pltpu.SemaphoreType.DMA((3,))] + [acc] * 3 + [keep] * 3
        + [pltpu.VMEM((2, step, hidden), BF16), pltpu.SemaphoreType.DMA((2,))]
        + line_sum_scratch(count, chunk, slots, width),
        compiler_params=pltpu.CompilerParams(
            collective_id=ident, has_side_effects=True, vmem_limit_bytes=63 * 2**20),
        cost_estimate=cost(145),
        name="ffn_backward",
    )(dy, ffn, two, gate, up, gains, weights)


def middle_back_kernel(x_ref, attn_ref, dy_ref, d2_ref, ffn_ref, h_ref, gain_ref, w_ref,
                       y_ref, dm_ref, dh_ref, delta_ref, dgain_ref, go_ref, acc, wo_ref, w_sem):
    i = pl.program_id(0)

    @pl.when(i == 0)
    def _():
        head = wo_ref.shape[1]
        at = pl.multiple_of(lax.axis_index("tp") * head, head)
        copy = pltpu.make_async_copy(w_ref.at[:, pl.ds(at, head)], wo_ref, w_sem)
        copy.start()
        copy.wait()
        acc[...] = jnp.zeros_like(acc)
        dgain_ref[...] = jnp.zeros_like(dgain_ref)

    middle, attn_hat, attn_inv = middle_of(x_ref[...], attn_ref[...], gain_ref[1:2, :])
    hat, _ = norm_parts(ffn_ref[...].astype(F32))
    y_ref[...] = (middle + hat * (1.0 + gain_ref[3:4, :])).astype(BF16)
    hat, inv = norm_parts(middle)
    d_part, d_gain = norm_back(d2_ref[...].astype(F32), hat, inv, gain_ref[2:3, :])
    dgain_ref[1:2, :] += d_gain[None]
    d_middle = dy_ref[...].astype(F32) + d_part
    dm_ref[...] = d_middle.astype(BF16)
    d_attn, d_gain = norm_back(d_middle, attn_hat, attn_inv, gain_ref[1:2, :])
    dgain_ref[0:1, :] += d_gain[None]
    d_attn = d_attn.astype(BF16)
    d_heads = dot(d_attn, wo_ref[...]).astype(BF16)
    dh_ref[...] = d_heads
    heads = h_ref[...]
    delta_ref[...] = jnp.sum(d_heads.astype(F32) * heads.astype(F32), axis=1, keepdims=True)
    acc[...] += dot(d_attn, heads, TN)

    @pl.when(i == pl.num_programs(0) - 1)
    def _():
        go_ref[...] = acc[...].astype(BF16)


def middle_back(x, attn, dy, d_two, ffn, heads, gains, weights):
    rows, width = x.shape
    head = heads.shape[1]
    tile = 256
    return pl.pallas_call(
        middle_back_kernel,
        grid=(rows // tile,),
        out_shape=(
            jax.ShapeDtypeStruct((rows, width), BF16),
            jax.ShapeDtypeStruct((rows, width), BF16),
            jax.ShapeDtypeStruct((rows, head), BF16),
            jax.ShapeDtypeStruct((rows, 1), F32),
            jax.ShapeDtypeStruct((2, width), F32),
            jax.ShapeDtypeStruct((width, head), BF16),
        ),
        in_specs=[tile_block(tile, width)] * 5 + [tile_block(tile, head)] + [whole_block(gains.shape), ANY],
        out_specs=(
            tile_block(tile, width), tile_block(tile, width), tile_block(tile, head), tile_block(tile, 1),
            pl.BlockSpec((2, width), lambda i: (0, 0)), pl.BlockSpec((width, head), lambda i: (0, 0)),
        ),
        scratch_shapes=[pltpu.VMEM((width, head), F32), pltpu.VMEM((width, head), BF16), pltpu.SemaphoreType.DMA],
        compiler_params=pltpu.CompilerParams(vmem_limit_bytes=48 * 2**20),
        cost_estimate=cost(19),
        name="middle_back",
    )(x, attn, dy, d_two, ffn, heads, gains, weights)


class LineGather:
    def __init__(self, whole, tile, width, sems):
        self.whole, self.tile, self.width, self.sems = whole, tile, width, sems
        self.z = lax.axis_index("tp")

    def place(self, src, t):
        return self.whole.at[
            pl.ds(pl.multiple_of(t * self.tile, self.tile), self.tile),
            pl.ds(pl.multiple_of(src * self.width, self.width), self.width)]

    def send(self, src, t, hop, way):
        ss, rs = self.sems[:2] if way > 0 else self.sems[2:]
        place = self.place(src, t)
        return pltpu.make_async_remote_copy(
            place, place, ss.at[hop, t], rs.at[hop, t],
            device_id={"tp": self.z + way}, device_id_type=MESH)

    def going(self, hop, way):
        src = self.z - way * hop
        return src, (self.z + way >= 0) & (self.z + way <= 3) & (src >= 0) & (src <= 3)

    def coming(self, hop, way):
        src = self.z - way * (hop + 1)
        return src, (src >= 0) & (src <= 3)

    def forward(self, t, hop):
        for way in (1, -1):
            if hop > 0:
                self.wait(t, hop - 1, way)
            src, ok = self.going(hop, way)

            @pl.when(ok)
            def _():
                self.send(src, t, hop, way).start()

    def wait(self, t, hop, way):
        src, ok = self.coming(hop, way)

        @pl.when(ok)
        def _():
            self.send(src, t, hop, way).wait_recv()

    def arrived(self, t):
        for way in (1, -1):
            self.wait(t, 2, way)

    def finish(self, tiles):
        for hop in range(3):
            for way in (1, -1):
                src, ok = self.going(hop, way)

                @pl.when(ok)
                def _():
                    def one(t, _):
                        self.send(src, t, hop, way).wait_send()
                        return 0

                    lax.fori_loop(0, tiles, one, 0)


class KeyGather(LineGather):
    def __init__(self, block, chips, sems):
        self.block, self.chips, self.sems = block, chips, sems
        self.z = lax.axis_index("tp")

    def tile_of(self, g, half, k):
        return (2 * g + half) * (self.chips - 1) + k - 1

    def place(self, src, t):
        pair, k = divmod(t, self.chips - 1)
        return self.quarter(pair // 2, pair % 2, k + 1, src)

    def quarter(self, g, half, k, src, own=False):
        ref, start, size = self.block(g, half, k, own)
        rows = size // 4
        return ref.at[pl.ds(pl.multiple_of(start + src * rows, rows), rows)]

    def finish(self, tiles):
        for hop in range(3):
            for way in (1, -1):
                src, ok = self.going(hop, way)

                @pl.when(ok)
                def _():
                    for t in range(tiles):
                        self.send(src, t, hop, way).wait_send()


class Shared:
    def __init__(self, over_dp):
        self.ctx = ctx = lax.axis_size("ctx")
        me = lax.axis_index("ctx")
        self.devices = ctx
        if over_dp:
            me = me + lax.axis_index("dp") * ctx
            self.devices = ctx * lax.axis_size("dp")
        self.over_dp = over_dp
        self.me = me
        self.chips = self.devices // 2
        self.core = lax.rem(me, 2)
        self.chip = lax.div(me, 2)

    def ident(self, device):
        if self.over_dp:
            return {"dp": lax.div(device, self.ctx), "ctx": lax.rem(device, self.ctx)}
        return {"ctx": device}

    def other(self, k):
        return 2 * lax.rem(self.chip + k + self.chips, self.chips) + self.core

    def partner(self):
        return self.me + 1 - 2 * self.core

    def greet(self, z):
        bar = pltpu.get_barrier_semaphore()
        for device in [self.partner()] + [self.other(k) for k in range(1, self.chips)]:
            pl.semaphore_signal(bar, inc=1, device_id=self.ident(device), device_id_type=MESH)

        @pl.when(z > 0)
        def _():
            pl.semaphore_signal(bar, inc=1, device_id={"tp": z - 1}, device_id_type=MESH)

        @pl.when(z < 3)
        def _():
            pl.semaphore_signal(bar, inc=1, device_id={"tp": z + 1}, device_id_type=MESH)

        pl.semaphore_wait(bar, self.chips + jnp.where((z == 0) | (z == 3), 1, 2))

    def copy(self, source, target, send, recv, device):
        return pltpu.make_async_remote_copy(
            source, target, send, recv, device_id=self.ident(device), device_id_type=MESH)


def first_gather_kernel(a_ref, b_ref, c_ref, i_ref, all_ref, line_ref, more_ref, ids_ref, lsem, ss1, rs1, ss2, rs2, si1, ri1, si2, ri2, *sems):
    group = Shared(True)
    line = LineGather(line_ref, b_ref.shape[0], b_ref.shape[1], sems[:4])
    more = LineGather(more_ref, c_ref.shape[0], c_ref.shape[1], sems[4:])
    width = b_ref.shape[1]
    own = [
        pltpu.make_async_copy(b_ref, line_ref.at[:, pl.ds(pl.multiple_of(line.z * width, width), width)], lsem.at[0]),
        pltpu.make_async_copy(c_ref, more_ref.at[:, pl.ds(pl.multiple_of(line.z * width, width), width)], lsem.at[3]),
        pltpu.make_async_copy(a_ref, all_ref.at[group.me], lsem.at[1]),
        pltpu.make_async_copy(i_ref, ids_ref.at[group.me], lsem.at[2]),
    ]
    for copy in own:
        copy.start()
    group.greet(line.z)
    arrays = ((a_ref, all_ref, ss1, rs1, ss2, rs2), (i_ref, ids_ref, si1, ri1, si2, ri2))

    def direct(n, k, incoming=False):
        ref, whole, ss, rs = arrays[n][:4]
        at = whole.at[group.other(-k)] if incoming else whole.at[group.me]
        return group.copy(ref, at, ss.at[k], rs.at[k], group.other(k))

    def inner(n, k, incoming=False):
        ref, whole, _, _, ss, rs = arrays[n]
        at = whole.at[group.other(-k)]
        if incoming:
            at = whole.at[group.other(-k) + 1 - 2 * group.core]
        return group.copy(ref if k == 0 else at, at, ss.at[k], rs.at[k], group.partner())

    both = range(2)
    for k in range(1, group.chips):
        for n in both:
            direct(n, k).start()
    for n in both:
        inner(n, 0).start()
    own[0].wait()
    line.forward(0, 0)
    own[1].wait()
    more.forward(0, 0)
    for k in range(1, group.chips):
        if k < 3:
            line.forward(0, k)
            more.forward(0, k)
        for n in both:
            direct(n, k, True).wait_recv()
            inner(n, k).start()
    for hop in range(min(3, group.chips), 3):
        line.forward(0, hop)
        more.forward(0, hop)
    for k in range(group.chips):
        for n in both:
            inner(n, k, True).wait_recv()
    line.arrived(0)
    more.arrived(0)
    for copy in own[2:]:
        copy.wait()
    for n in both:
        for k in range(1, group.chips):
            direct(n, k).wait_send()
        for k in range(group.chips):
            inner(n, k).wait_send()
    line.finish(1)
    more.finish(1)


def first_gather(a, b, c, ids, devices, ident):
    dma = pltpu.SemaphoreType.DMA((devices // 2,))
    hop = pltpu.SemaphoreType.DMA((3, 1))
    return pl.pallas_call(
        first_gather_kernel,
        out_shape=(
            jax.ShapeDtypeStruct((devices,) + a.shape, a.dtype),
            jax.ShapeDtypeStruct((b.shape[0], 4 * b.shape[1]), b.dtype),
            jax.ShapeDtypeStruct((c.shape[0], 4 * c.shape[1]), c.dtype),
            jax.ShapeDtypeStruct((devices,) + ids.shape, ids.dtype),
        ),
        in_specs=[ANY] * 4,
        out_specs=(ANY,) * 4,
        scratch_shapes=[pltpu.SemaphoreType.DMA((4,))] + [dma] * 8 + [hop] * 8,
        compiler_params=pltpu.CompilerParams(collective_id=ident, has_side_effects=True),
        cost_estimate=cost(20),
        name="first_gather",
    )(a, b, c, ids)


def attention_kernel(groups, size, x_ref, w_ref, gain_ref, gq_ref, gk_ref, cos_ref, sin_ref, qs_ref, ks_ref,
                     q_ref, qhat_ref, qinv_ref, khat_ref, kinv_ref, heads_ref, log_ref, kv_out, all_out,
                     kv, whole, store_kv, store_all, ss1, rs1, ss2, rs2, *sems):
    head = q_ref.shape[1]
    length = kv.shape[1]
    id_rows = size // 128
    blocks = length // (2 * size)
    group = Shared(False)
    rank = group.me
    tile = min(256, size)
    per = size // tile
    line = LineGather(whole, tile, head, sems[:4])
    z = line.z
    group.greet(z)

    def block(g, half, k, own):
        c = rank if own else group.other(-k)
        return kv.at[g], half * (length // 2) + c * size, size

    keys = KeyGather(block, group.chips, sems[4:])

    def place(g, half, c):
        return kv.at[g, pl.ds(pl.multiple_of(half * (length // 2) + c * size, size), size)]

    def straight(t):
        return t == 2 * groups - 1

    def direct(g, half, k, incoming=False):
        at = keys.quarter(g, half, k, z, own=not incoming)
        if straight(2 * g + half):
            at = place(g, half, group.other(-k) if incoming else rank)
        return group.copy(at, at, ss1.at[g, half, k], rs1.at[g, half, k], group.other(k))

    def inner(g, half, k, incoming=False):
        block = group.other(-k)
        at = place(g, half, block + 1 - 2 * group.core if incoming else block)
        return group.copy(at, at, ss2.at[g, half, k], rs2.at[g, half, k], group.partner())

    def project(g, half, u):
        rows = pl.ds((2 * g + half) * size + u * tile, tile)
        spot = pl.ds(half * size + u * tile, tile)
        cosine, sine = cos_ref[spot, :], sin_ref[spot, :]
        hat, _ = norm_parts(x_ref[rows, :].astype(F32))
        raw = dot((hat * (1.0 + gain_ref[0:1, :])).astype(BF16), w_ref[:, : 3 * head])
        hat, inv = norm_parts(raw[:, :head])
        qhat_ref[rows, :] = hat
        qinv_ref[rows, :] = inv
        q_ref[rows, :] = rotate(hat * (1.0 + gq_ref[...]), cosine, sine).astype(BF16)
        hat, inv = norm_parts(raw[:, head : 2 * head])
        khat_ref[rows, :] = hat
        kinv_ref[rows, :] = inv
        at = pl.ds(pl.multiple_of(half * (length // 2) + rank * size + u * tile, tile), tile)
        kv[g, at, :head] = rotate(hat * (1.0 + gk_ref[...]), cosine, sine).astype(BF16)
        kv[g, at, head:] = raw[:, 2 * head :].astype(BF16)

    def attend(g, half):
        row = lax.broadcasted_iota(jnp.int32, (size, size), 0)
        col = lax.broadcasted_iota(jnp.int32, (size, size), 1)
        rows = pl.ds((2 * g + half) * size, size)
        q = q_ref[rows, :] * jnp.asarray(SCALE, BF16)
        qseg = qs_ref[g, half]

        def part(block):
            at = pl.ds(pl.multiple_of(block * size, size), size)
            device = lax.axis_index("dp") * lax.axis_size("ctx") + lax.rem(block, blocks)
            ids = ks_ref[device, pl.ds((2 * g + lax.div(block, blocks)) * id_rows, id_rows), :]
            ids = jnp.concatenate([ids[j : j + 1] for j in range(id_rows)], axis=1)
            same = qseg == jnp.where(ids == 0, -1, ids)
            return dot(q, kv[g, at, :head], NT), kv[g, at, head:], same

        s, v, same = part(rank + half * blocks)
        order = (col <= row) if half == 0 else (col >= row)
        s = jnp.where((same & order) | (col == row), s, NEGATIVE)
        top = jnp.max(s, axis=1, keepdims=True)
        p = jnp.exp(s - top)
        mass = jnp.sum(p, axis=1, keepdims=True)
        acc = dot(p.astype(BF16), v)

        def step(t, carry):
            top, mass, acc = carry
            s, v, same = part(block_starts(half, t, blocks, rank))
            s = jnp.where(same, s, NEGATIVE)
            new = jnp.maximum(top, jnp.max(s, axis=1, keepdims=True))
            keep = jnp.exp(top - new)
            p = jnp.exp(s - new)
            mass = mass * keep + jnp.sum(p, axis=1, keepdims=True)
            return new, mass, acc * keep + dot(p.astype(BF16), v)

        count = rank if half == 0 else 2 * blocks - 1 - rank
        top, mass, acc = lax.fori_loop(0, count, step, (top, mass, acc))
        out = (acc / mass).astype(BF16)
        heads_ref[rows, :] = out
        whole[rows, pl.ds(pl.multiple_of(z * head, head), head)] = out
        log_ref[g, half] = top + jnp.log(mass)

    chips = range(1, group.chips)
    tiles = 2 * groups

    def stage(t, n):
        if not 0 <= t < tiles:
            return
        g, half = divmod(t, 2)
        for k in chips:
            spot = keys.tile_of(g, half, k)
            if n == 0:
                direct(g, half, k).start()
            elif straight(t):
                if n == 4:
                    direct(g, half, k, True).wait_recv()
                    inner(g, half, k).start()
            elif n == 4:
                keys.arrived(spot)
                inner(g, half, k).start()
            else:
                if n == 1:
                    direct(g, half, k, True).wait_recv()
                keys.forward(spot, n - 1)

    def exchange(t):
        for n in (4, 3, 2, 1):
            stage(t - n, n)

    def hops(t):
        for hop in range(3):
            if 0 <= t - hop < tiles:
                for u in range(per):
                    line.forward((t - hop) * per + u, hop)

    def keep(t):
        at = pl.ds(t * tile, tile)
        return pltpu.make_async_copy(whole.at[at], all_out.at[at], store_all.at[t])

    def save(g):
        return pltpu.make_async_copy(kv.at[g], kv_out.at[g], store_kv.at[g])

    def landed(t):
        g, half = divmod(t, 2)
        for k in range(group.chips):
            inner(g, half, k, True).wait_recv()

    for t in range(tiles):
        g, half = divmod(t, 2)
        for u in range(per):
            project(g, half, u)
        stage(t, 0)
        inner(g, half, 0).start()
        exchange(t)
    for t in range(tiles):
        g, half = divmod(t, 2)
        exchange(tiles + t)
        landed(t)
        attend(g, half)
        hops(t)
    for g in range(groups):
        save(g).start()
    for t in range(tiles, tiles + 2):
        hops(t)
    for t in range(tiles * per):
        line.arrived(t)
        keep(t).start()
    for g in range(groups):
        save(g).wait()
        for half in range(2):
            for k in chips:
                direct(g, half, k).wait_send()
            for k in range(group.chips):
                inner(g, half, k).wait_send()
    line.finish(tiles * per)
    keys.finish((tiles - 1) * (group.chips - 1))
    for t in range(tiles * per):
        keep(t).wait()


def attention(x, w, gains, gain_query, gain_key, cosine, sine, qseg, ids, length, ident):
    rows, width = x.shape
    groups, _, size, _ = qseg.shape
    head = gain_query.shape[1]
    chips = length // (4 * size)
    tiles = 2 * groups
    parts = rows // min(256, size)
    vmem = pl.BlockSpec(memory_space=pltpu.VMEM)
    dma = pltpu.SemaphoreType.DMA
    return pl.pallas_call(
        functools.partial(attention_kernel, groups, size),
        out_shape=(
            jax.ShapeDtypeStruct((rows, head), BF16),
            jax.ShapeDtypeStruct((rows, head), F32),
            jax.ShapeDtypeStruct((rows, 1), F32),
            jax.ShapeDtypeStruct((rows, head), F32),
            jax.ShapeDtypeStruct((rows, 1), F32),
            jax.ShapeDtypeStruct((rows, head), BF16),
            jax.ShapeDtypeStruct((groups, 2, size, 1), F32),
            jax.ShapeDtypeStruct((groups, length, 2 * head), BF16),
            jax.ShapeDtypeStruct((rows, 4 * head), BF16),
        ),
        in_specs=[vmem] * 9,
        out_specs=(vmem,) * 7 + (ANY, ANY),
        scratch_shapes=[
            pltpu.VMEM((groups, length, 2 * head), BF16), pltpu.VMEM((rows, 4 * head), BF16),
            dma((groups,)), dma((parts,))] + [dma((groups, 2, chips))] * 4 + [dma((3, parts))] * 4
        + [dma((3, tiles * (chips - 1)))] * 4,
        compiler_params=pltpu.CompilerParams(
            collective_id=ident, has_side_effects=True, vmem_limit_bytes=60 * 2**20),
        cost_estimate=cost(110),
        name="attention",
    )(x, w, gains, gain_query, gain_key, cosine, sine, qseg, ids)


class ResidentSum(LineSum):
    def outwards(self, c):
        return pltpu.make_async_remote_copy(
            self.out.at[self.rows(c)], self.out.at[self.rows(c)], self.sems[4].at[c], self.sems[5].at[c],
            device_id={"tp": self.my_leaf}, device_id_type=MESH)

    def total(self, c):
        @pl.when(self.hub)
        def _():
            self.across(c).wait_recv()
            at = self.rows(c)
            self.out[at, :] = (self.own[at, :].astype(F32) + self.far[at, :].astype(F32)).astype(BF16)
            self.outwards(c).start()

    def arrived(self, c):
        @pl.when(self.leaf)
        def _():
            self.outwards(c).wait_recv()

    def finish(self):
        @pl.when(self.leaf)
        def _():
            for c in range(self.count):
                self.inwards(c).wait_send()

        @pl.when(self.hub)
        def _():
            for c in range(self.count):
                self.across(c).wait_send()
                self.outwards(c).wait_send()


def turned(column, size):
    return jnp.transpose(jnp.broadcast_to(column, (size, 128)))[0:1, :]


def attention_back_kernel(groups, size, q_ref, do_ref, log_ref, delta_ref, qs_ref, ids_ref, hat_ref, inv_ref, cos_ref, sin_ref,
                          x_ref, gain_ref, gq_ref, go_ref, kv_hbm, all_out, dkv_ref, rest_ref, dgain_ref, grad_ref,
                          kv, dk, dv, part, near, pair, far, whole, acc, load, store, ss1, rs1, ss2, rs2, *sems):
    head = q_ref.shape[1]
    length = kv.shape[1]
    blocks = length // (2 * size)
    id_rows = size // 128
    tiles = 2 * groups
    group = Shared(False)
    rank, core = group.me, group.core
    tile = min(256, size)
    per = size // tile
    line = LineGather(whole, tile, head, sems)
    z = line.z
    others = range(1, group.chips)
    order = list(others) + [0]

    def fetch(g):
        return pltpu.make_async_copy(kv_hbm.at[g], kv.at[g], load.at[g])

    for g in range(groups):
        fetch(g).start()
    group.greet(z)
    acc[...] = jnp.zeros_like(acc)
    dgain_ref[...] = jnp.zeros_like(dgain_ref)

    def rows_of(half, device):
        return pl.ds(pl.multiple_of(half * (length // 2) + device * size, size), size)

    def within(g, half, k):
        to = group.other(k) + 1 - 2 * core
        return group.copy(
            part.at[g, rows_of(half, to)], near.at[g, half, k], ss1.at[g, half, k], rs1.at[g, half, k], group.partner())

    def between(g, half, k):
        return group.copy(
            pair.at[g, half, k - 1], far.at[g, half, k - 1], ss2.at[g, half, k], rs2.at[g, half, k], group.other(k))

    def both_cores(g):
        for half in range(2):
            for k in order:
                within(g, half, k).wait_recv()
                total = part[g, rows_of(half, group.other(k)), :].astype(F32) + near[g, half, k].astype(F32)
                if k > 0 and g == groups - 1:
                    rest_ref[half, k - 1] = total.astype(BF16)
                elif k > 0:
                    pair[g, half, k - 1] = total.astype(BF16)
                    between(g, half, k).start()
                else:
                    dkv_ref[pl.ds((2 * g + half) * size, size), :] = total.astype(BF16)

    def all_chips(g):
        for half in range(2):
            at = pl.ds((2 * g + half) * size, size)
            total = dkv_ref[at, :].astype(F32)
            for k in others:
                between(g, half, k).wait_recv()
                total = total + far[g, half, k - 1].astype(F32)
            dkv_ref[at, :] = total.astype(BF16)

    def hops(t):
        for hop in range(3):
            if 0 <= t - hop < tiles:
                for u in range(per):
                    line.forward((t - hop) * per + u, hop)

    def attend(g, half):
        row = lax.broadcasted_iota(jnp.int32, (size, size), 0)
        col = lax.broadcasted_iota(jnp.int32, (size, size), 1)
        own = pl.ds((2 * g + half) * size, size)
        q = q_ref[own, :] * jnp.asarray(SCALE, BF16)
        do = do_ref[own, :]
        qseg = qs_ref[g, half]
        log_mass = turned(log_ref[g, half], size)
        delta = turned(delta_ref[own, :], size)

        def step_of(block, mine):
            at = pl.ds(pl.multiple_of(block * size, size), size)
            k = kv[g, at, :head]
            v = kv[g, at, head:]
            device = lax.axis_index("dp") * lax.axis_size("ctx") + lax.rem(block, blocks)
            ids = ids_ref[device, pl.ds((2 * g + lax.div(block, blocks)) * id_rows, id_rows), :]
            ids = jnp.concatenate([ids[j : j + 1] for j in range(id_rows)], axis=1)
            ids = jnp.transpose(jnp.broadcast_to(jnp.where(ids == 0, -1, ids), (8, size)))[:, 0:1]
            allowed = ids == qseg
            if mine:
                ahead = (row <= col) if half == 0 else (row >= col)
                allowed = (allowed & ahead) | (col == row)
            s = jnp.where(allowed, dot(k, q, NT), NEGATIVE)
            p = jnp.exp(s - log_mass)
            ds = (p * (dot(v, do, NT) - delta)).astype(BF16)
            dv[at, :] += dot(p.astype(BF16), do)
            dk[at, :] += dot(ds, q)
            return dot(ds, k, TN)

        def step(t, dq):
            return dq + step_of(block_starts(half, t, blocks, rank), False)

        dq = step_of(rank + half * blocks, True)
        count = rank if half == 0 else 2 * blocks - 1 - rank
        dq = SCALE * lax.fori_loop(0, count, step, dq)
        spot = pl.ds(half * size, size)
        d_rot = rotate(dq, cos_ref[spot, :], -sin_ref[spot, :])
        d_raw, d_gain = norm_back(d_rot, hat_ref[own, :], inv_ref[own, :], gq_ref[...])
        dgain_ref[...] += d_gain[None]
        whole[own, pl.ds(pl.multiple_of(z * head, head), head)] = d_raw.astype(BF16)

    def weight_gradient(t):
        own = pl.ds(t * size, size)
        hat, _ = norm_parts(x_ref[own, :].astype(F32))
        one = (hat * (1.0 + gain_ref[0:1, :])).astype(BF16)
        acc[...] += dot(one, whole[own, pl.ds(pl.multiple_of(z * head, head), head)], TN)

    def keep(t):
        at = pl.ds(t * tile, tile)
        return pltpu.make_async_copy(whole.at[at], all_out.at[at], store.at[t])

    for g in range(groups):
        fetch(g).wait()
        dk[...] = jnp.zeros_like(dk)
        dv[...] = jnp.zeros_like(dv)
        for half in range(2):
            attend(g, half)
            hops(2 * g + half)
            if half == 0 and g > 0:
                both_cores(g - 1)
        part[g, :, :head] = dk[...].astype(BF16)
        part[g, :, head:] = dv[...].astype(BF16)
        for half in range(2):
            for k in order:
                within(g, half, k).start()
        for half in range(2):
            weight_gradient(2 * g + half)
        if g > 0:
            all_chips(g - 1)
    hops(tiles)
    both_cores(groups - 1)
    hops(tiles + 1)
    grad_ref[:, :head] = acc[...].astype(BF16)
    grad_ref[:, head:] = go_ref[...]
    for t in range(tiles * per):
        line.arrived(t)
        keep(t).start()
    for g in range(groups):
        for half in range(2):
            if g < groups - 1:
                for k in others:
                    between(g, half, k).wait_send()
            for k in order:
                within(g, half, k).wait_send()
    line.finish(tiles * per)
    for t in range(tiles * per):
        keep(t).wait()


def attention_back(q, d_heads, log_mass, delta, qseg, ids, hat, inv, cosine, sine, x, gains, gain_query, grad_o, kv, ident):
    rows, head = q.shape
    width = x.shape[1]
    groups, length, _ = kv.shape
    size = rows // (2 * groups)
    chips = length // (4 * size)
    parts = rows // min(256, size)
    vmem = pl.BlockSpec(memory_space=pltpu.VMEM)
    dma = pltpu.SemaphoreType.DMA
    return pl.pallas_call(
        functools.partial(attention_back_kernel, groups, size),
        out_shape=(
            jax.ShapeDtypeStruct((rows, 4 * head), BF16),
            jax.ShapeDtypeStruct((rows, 2 * head), BF16),
            jax.ShapeDtypeStruct((2, chips - 1, size, 2 * head), BF16),
            jax.ShapeDtypeStruct((1, head), F32),
            jax.ShapeDtypeStruct((width, 2 * head), BF16),
        ),
        in_specs=[vmem] * 14 + [ANY],
        out_specs=(ANY, vmem, vmem, vmem, vmem),
        scratch_shapes=[
            pltpu.VMEM((groups, length, 2 * head), BF16),
            pltpu.VMEM((length, head), F32), pltpu.VMEM((length, head), F32),
            pltpu.VMEM((groups, length, 2 * head), BF16),
            pltpu.VMEM((groups, 2, chips, size, 2 * head), BF16),
            pltpu.VMEM((groups, 2, chips - 1, size, 2 * head), BF16),
            pltpu.VMEM((groups, 2, chips - 1, size, 2 * head), BF16),
            pltpu.VMEM((rows, 4 * head), BF16),
            pltpu.VMEM((width, head), F32),
            dma((groups,)), dma((parts,))] + [dma((groups, 2, chips))] * 4 + [dma((3, parts))] * 4,
        compiler_params=pltpu.CompilerParams(
            collective_id=ident, has_side_effects=True, vmem_limit_bytes=63 * 2**20),
        cost_estimate=cost(80),
        name="attention_back",
    )(q, d_heads, log_mass, delta, qseg, ids, hat, inv, cosine, sine, x, gains, gain_query, grad_o, kv)


class RowScatter:
    def __init__(self, group, own_rows, source, near, pair, far, sems):
        self.group, self.own_rows, self.source = group, own_rows, source
        self.near, self.pair, self.far, self.sems = near, pair, far, sems
        self.others = list(range(1, group.chips))
        self.order = self.others + [0]

    def block(self, device):
        return pl.ds(pl.multiple_of(device * self.own_rows, 16), self.own_rows)

    def within(self, k):
        g = self.group
        return g.copy(self.source.at[self.block(g.other(k) + 1 - 2 * g.core)], self.near.at[k],
                      self.sems[0].at[k], self.sems[1].at[k], g.partner())

    def between(self, k):
        g = self.group
        return g.copy(self.pair.at[k], self.far.at[k], self.sems[2].at[k], self.sems[3].at[k], g.other(k))

    def send(self):
        for k in self.order:
            self.within(k).start()

    def middle(self, out):
        for k in self.order:
            self.within(k).wait_recv()
            both = self.source[self.block(self.group.other(k)), :].astype(F32) + self.near[k].astype(F32)
            if k > 0:
                self.pair[k] = both.astype(BF16)
                self.between(k).start()
            else:
                out[...] = both

    def final(self, out):
        for k in self.others:
            self.between(k).wait_recv()
            out[...] += self.far[k].astype(F32)
        for k in self.others:
            self.between(k).wait_send()
        for k in self.order:
            self.within(k).wait_send()


def row_scatter_scratch(chips, own_rows, cols):
    return [pltpu.VMEM((chips, own_rows, cols), BF16)] * 3 + [pltpu.SemaphoreType.DMA((chips,))] * 4


def key_back_kernel(tiles, tile, chunk, own_rows, scattered, dkv_ref, hat_ref, inv_ref, cos_ref, sin_ref, x_ref, dq_ref,
                    gain_ref, gk_ref, w_ref, wq_ref, dgq_ref, dg_mid_ref, dg_post_ref, qo_ref, rest_ref,
                    dx_ref, last_out, qo_out, acc, acc_in, acc_key, w_kv, w_sem, last_ref, part,
                    add, ss, rs, out, own, near, far, *sems):
    i = pl.program_id(0)
    head = hat_ref.shape[1]
    per = tile // chunk
    count = tiles * per + 1
    line = ResidentSum(count, chunk, count, own, near, far, out, sems[:9])
    group = Shared(True)
    ring = Shared(False)
    size = rest_ref.shape[2]
    first = tiles * per - 2 * size // chunk

    def between(half, k):
        return ring.copy(rest_ref.at[half, k - 1], add.at[half, k - 1], ss.at[half, k], rs.at[half, k], ring.other(k))

    if scattered:
        early = RowScatter(group, own_rows, qo_ref, *sems[9:12], sems[12:16])
        late = RowScatter(group, own_rows, last_ref, *sems[16:19], sems[19:23])

    @pl.when(i == 0)
    def _():
        copy = pltpu.make_async_copy(w_ref.at[:, pl.ds(head, 2 * head)], w_kv, w_sem)
        copy.start()
        if scattered:
            group.greet(line.z)
        else:
            ring.greet(line.z)
            qo_out[...] = qo_ref[...]
        for half in range(2):
            for k in range(1, ring.chips):
                between(half, k).start()
        if scattered:
            early.send()
        for ref in (acc, acc_in, acc_key):
            ref[...] = jnp.zeros_like(ref)
        copy.wait()
        line.put(count - 1, jnp.broadcast_to(
            jnp.concatenate([dgq_ref[...], dgq_ref[...]], axis=1).astype(BF16), (chunk, 2 * head)))

    def put_rows(c):
        return dkv_ref[pl.ds(pl.multiple_of(c * chunk, chunk), chunk), :]

    @pl.when(i == 0)
    def _():
        def ready(c, _):
            line.put(c, put_rows(c))
            return 0

        lax.fori_loop(0, first, ready, 0)

    for half in range(2):
        @pl.when(i == max(0, (first * chunk + half * size) // tile - 2))
        def _():
            for k in range(1, ring.chips):
                between(half, k).wait_recv()

            def ready(n, _):
                c = first + half * (size // chunk) + n
                total = put_rows(c).astype(F32)
                for k in range(1, ring.chips):
                    total = total + add[half, k - 1, pl.ds(pl.multiple_of(n * chunk, chunk), chunk), :].astype(F32)
                line.put(c, total.astype(BF16))
                return 0

            lax.fori_loop(0, size // chunk, ready, 0)

    @pl.when(i < tiles)
    def _():
        part[pl.ds(pl.multiple_of(i * tile, tile), tile), :] = dot(dq_ref[...], wq_ref[...], NT)

    @pl.when((i >= 1) & (i <= tiles))
    def _():
        for j in range(per):
            line.total((i - 1) * per + j)

    @pl.when(i < tiles)
    def _():
        for j in range(per):
            line.pair(i * per + j)

    @pl.when(i == 1)
    def _():
        line.pair(count - 1)
        if scattered:
            early.middle(qo_out)

    @pl.when(i == 2)
    def _():
        line.total(count - 1)

    if scattered:
        @pl.when(i == tiles)
        def _():
            early.final(qo_out)

    @pl.when(i >= 2)
    def _():
        for j in range(per):
            line.arrived((i - 2) * per + j)
        d_kv = out[pl.ds(pl.multiple_of((i - 2) * tile, tile), tile), :]
        d_rot = rotate(d_kv[:, :head].astype(F32), cos_ref[...], -sin_ref[...])
        d_raw, d_gain = norm_back(d_rot, hat_ref[...], inv_ref[...], gk_ref[...])
        acc_key[...] += d_gain[None]
        d_raw = jnp.concatenate([d_raw.astype(BF16), d_kv[:, head:]], axis=1)
        d_one = part[pl.ds(pl.multiple_of((i - 2) * tile, tile), tile), :] + dot(d_raw, w_kv[...], NT)
        hat, inv = norm_parts(x_ref[...].astype(F32))
        gain = gain_ref[0:1, :]
        d_part, d_gain = norm_back(d_one, hat, inv, gain)
        acc_in[...] += d_gain[None]
        dx_ref[...] = d_part.astype(BF16)
        acc[...] += dot((hat * (1.0 + gain)).astype(BF16), d_raw, TN)

    @pl.when(i == tiles + 1)
    def _():
        for half in range(2):
            for k in range(1, ring.chips):
                between(half, k).wait_send()
        line.arrived(count - 1)
        width = x_ref.shape[1]
        short = head * own_rows // width
        last_ref[:, : 2 * head] = acc[...].astype(BF16)
        d_query = out[pl.ds((count - 1) * chunk, 16), :head][0:1].astype(F32)
        pair = jnp.concatenate([d_query, acc_key[...], jnp.zeros((14, head), F32)], axis=0).astype(BF16)
        col = lax.broadcasted_iota(jnp.int32, (head, width), 1)
        row = lax.broadcasted_iota(jnp.int32, (head, width), 0)
        shift = short.bit_length() - 1
        spot = lax.shift_right_logical(row, shift) * own_rows + (row & (short - 1))
        spread = dot(pair, jnp.where(col == spot, 1.0, 0.0).astype(BF16))
        gains = jnp.concatenate(
            [acc_in[...], dg_mid_ref[...], dg_post_ref[...], spread[0:2], jnp.zeros((122, width), F32)], axis=0)
        last_ref[:, 2 * head :] = jnp.transpose(gains).astype(BF16)
        if scattered:
            late.send()
            line.finish()
            late.middle(last_out)
            late.final(last_out)
        else:
            last_out[...] = last_ref[...]
            line.finish()


def key_back(d_kv, hat, inv, cosine, sine, x, d_query, gains, gain_key, first, w_query, dg_query, dg_mid, dg_post,
             grad_qo, rest, own_rows, ident):
    rows, width = x.shape
    head = hat.shape[1]
    tile, chunk = 256, 128
    tiles = rows // tile
    count = rows // chunk + 1
    dma = pltpu.SemaphoreType.DMA((count,))

    def late(cols):
        return pl.BlockSpec((tile, cols), lambda i: (jnp.maximum(i - 2, 0), 0))

    def fixed(shape):
        return pl.BlockSpec(shape, lambda i: (0, 0))

    turns = cosine.shape[0] // tile
    turn = pl.BlockSpec((tile, head // 2), lambda i: (lax.rem(jnp.maximum(i - 2, 0), turns), 0))
    comm = pltpu.VMEM((count * chunk, 2 * head), BF16)
    scattered = own_rows % 16 == 0
    chips = width // (2 * own_rows)
    last = (width, 2 * head + 128)
    more = []
    if scattered:
        last_out, qo_out, kind = (own_rows, last[1]), (own_rows, 2 * head), F32
        for cols in (2 * head, last[1]):
            more += row_scatter_scratch(chips, own_rows, cols)
    else:
        last_out, qo_out, kind = last, grad_qo.shape, BF16
    return pl.pallas_call(
        functools.partial(key_back_kernel, tiles, tile, chunk, own_rows, scattered),
        grid=(tiles + 2,),
        out_shape=(
            jax.ShapeDtypeStruct((rows, width), BF16),
            jax.ShapeDtypeStruct(last_out, kind),
            jax.ShapeDtypeStruct(qo_out, kind),
        ),
        in_specs=[whole_block(d_kv.shape),
                  late(head), late(1), turn, turn, late(width),
                  pl.BlockSpec((tile, 4 * head), lambda i: (jnp.minimum(i, tiles - 1), 0)),
                  whole_block(gains.shape), whole_block(gain_key.shape), ANY]
        + [whole_block(a.shape) for a in (w_query, dg_query, dg_mid, dg_post, grad_qo, rest)],
        out_specs=(late(width), fixed(last_out), fixed(qo_out)),
        scratch_shapes=[
            pltpu.VMEM((width, 2 * head), F32), pltpu.VMEM((1, width), F32), pltpu.VMEM((1, head), F32),
            pltpu.VMEM((width, 2 * head), BF16), pltpu.SemaphoreType.DMA, pltpu.VMEM(last, BF16),
            pltpu.VMEM((rows, width), F32), pltpu.VMEM(rest.shape, BF16)]
        + [pltpu.SemaphoreType.DMA((2, rest.shape[1] + 1))] * 2 + [comm] * 4 + [dma] * 7
        + [pltpu.SemaphoreType.REGULAR] * 2 + more,
        compiler_params=pltpu.CompilerParams(
            collective_id=ident, has_side_effects=True, vmem_limit_bytes=56 * 2**20),
        cost_estimate=cost(75),
        name="key_back",
    )(d_kv, hat, inv, cosine, sine, x, d_query, gains, gain_key, first, w_query, dg_query, dg_mid, dg_post, grad_qo, rest)


def shards(tokens, segments, cotangent, w_query, w_key, w_value, w_out, w_gate, w_up, w_down,
           g_input, g_post_attn, g_pre_ffn, g_post_ffn, g_query, g_key):
    batches, seq_local, _, size, width = tokens.shape
    head = w_key.shape[1]
    groups = batches * seq_local
    per_group = 2 * size
    rows = groups * per_group
    ctx = lax.axis_size("ctx")
    length = per_group * ctx
    rank = lax.axis_index("ctx")
    shared = ("dp", "ctx")
    own_rows = g_input.shape[0]
    hidden = w_gate.shape[1]

    def column(gain):
        return jnp.pad(gain, (0, own_rows - gain.shape[0]))[:, None]

    own_ids = segments.reshape(groups, 2, size)
    id_rows = own_ids.size // 128
    ids = jnp.pad(own_ids.reshape(id_rows, 128), ((0, -id_rows % 16), (0, 0)))
    extra = jnp.concatenate(
        [column(g) for g in (g_input, g_post_attn, g_pre_ffn, g_post_ffn, g_query, g_key)], axis=1)
    extra = jnp.pad(extra, ((0, 0), (0, 128 - extra.shape[1])))

    def rows_of_16(w):
        return jnp.pad(w, ((0, -own_rows % 16), (0, 0)))

    first, line_query, line_out, ids = first_gather(
        rows_of_16(jnp.concatenate([w_query, w_key, w_value, extra], axis=1)),
        rows_of_16(w_query), rows_of_16(w_out.T), ids, width // own_rows, 5)
    first = first[:, :own_rows].reshape(width, -1)
    side = first[:, 3 * head :]
    gain_cols = side[:, :8].astype(F32)
    gain_rows = gain_cols.T
    gain_input = gain_rows[0]
    short = g_query.shape[0]
    gain_query, gain_key = (
        gain_cols[:, i].reshape(-1, own_rows)[:, :short].reshape(-1) for i in (4, 5))

    wide = wide_of(hidden)
    second = jnp.concatenate(
        [line_out[:own_rows]] + [jnp.pad(w, ((0, 0), (0, wide - hidden))) for w in (w_gate, w_up, w_down.T)], axis=1)
    weights = lax.all_gather(second, shared, axis=0, tiled=True)

    offsets = rank * size + jnp.arange(size, dtype=jnp.int32)
    position = jnp.concatenate([offsets, length - 1 - offsets]).astype(F32)
    cosine, sine = angles(position, head // 2, head)

    x_rows = tokens.reshape(rows, width)
    dy_rows = cotangent.reshape(rows, width)
    queries, q_hat, q_scale, k_hat, k_scale, heads_own, log_mass, kv, heads_all = attention(
        x_rows, first, gain_rows, gain_query[None], gain_key[None], cosine, sine, own_ids[..., None], ids, length, 0)

    line_query, heads_all = lax.optimization_barrier((line_query[:own_rows], heads_all))
    query_full = lax.all_gather(line_query, shared, axis=0, tiled=True)
    attn, hidden_two, gate, up, ffn_out = ffn_forward(x_rows, heads_all, gain_rows, weights, hidden, 1)
    ffn_out, query_full = lax.optimization_barrier((ffn_out, query_full))
    d_gain_post_ffn, grad_ffn, d_two = ffn_backward(
        dy_rows, ffn_out, hidden_two, gate, up, gain_rows, weights, 2)
    grad_ffn = lax.psum_scatter(grad_ffn, shared, scatter_dimension=1, tiled=True)
    output, d_middle, d_heads, delta, d_gain_mid, grad_out_t = middle_back(
        x_rows, attn, dy_rows, d_two, ffn_out, heads_own, gain_rows, weights)

    d_q_all, d_kv, rest, d_gain_query, grad_qo = attention_back(
        queries, d_heads, log_mass, delta, own_ids[:, :, None, :], ids, q_hat, q_scale, cosine, sine, x_rows, gain_rows,
        gain_query[None], grad_out_t, kv, 4)
    d_part, last, grad_qo = key_back(
        d_kv, k_hat, k_scale, cosine, sine, x_rows, d_q_all, gain_rows, gain_key[None],
        first, query_full, d_gain_query, d_gain_mid, d_gain_post_ffn, grad_qo, rest, own_rows, 3)
    d_tokens = d_middle.astype(F32) + d_part.astype(F32)
    if own_rows % 16:
        last = lax.psum_scatter(last, shared, scatter_dimension=0, tiled=True).astype(F32)
        grad_qo = lax.psum_scatter(grad_qo, shared, scatter_dimension=0, tiled=True).astype(F32)
    g = last[:, 2 * head :]
    return (
        output.reshape(tokens.shape),
        d_tokens.reshape(tokens.shape),
        grad_qo[:, :head],
        last[:, :head],
        last[:, head : 2 * head],
        grad_qo[:, head:].T,
        grad_ffn[0].astype(F32),
        grad_ffn[1].astype(F32),
        grad_ffn[2].astype(F32).T,
        g[:, 0],
        g[:, 1],
        g[:, 2],
        g[:, 3],
        g[:short, 4],
        g[:short, 5],
    )


def solution(mesh):
    shared = ("dp", "ctx")
    rows = P(None, "dp", None, "ctx", None)
    weights = (
        P(shared, "tp"), P(shared, None), P(shared, None), P("tp", shared),
        P(shared, "tp"), P(shared, "tp"), P("tp", shared),
    )
    gains = (P(shared),) * 6
    return jax.shard_map(
        shards,
        mesh=mesh,
        in_specs=(rows, P(None, "dp", None, "ctx"), rows) + weights + gains,
        out_specs=(rows, rows) + weights + gains,
        check_vma=False,
    )
```

```python
import functools

import jax
import jax.numpy as jnp
from jax import lax
from jax.experimental import pallas as pl
from jax.experimental.pallas import tpu as pltpu
from jax.sharding import PartitionSpec as P

EPS = 1e-06
THETA = 1000000.0
SCALE = 0.0625
NEGATIVE = -1e30
BF16 = jnp.bfloat16
F32 = jnp.float32
MESH = pl.DeviceIdType.MESH
NN = (((1,), (0,)), ((), ()))
NT = (((1,), (1,)), ((), ()))
TN = (((0,), (0,)), ((), ()))


def dot(a, b, dims=NN):
    return lax.dot_general(a, b, dims, preferred_element_type=F32)


def cost(us):
    return pl.CostEstimate(flops=int(us * 1.1e9), bytes_accessed=0, transcendentals=0)


def barrier_line(z):
    bar = pltpu.get_barrier_semaphore()

    @pl.when(z > 0)
    def _():
        pl.semaphore_signal(bar, inc=1, device_id={"tp": z - 1}, device_id_type=MESH)

    @pl.when(z < 3)
    def _():
        pl.semaphore_signal(bar, inc=1, device_id={"tp": z + 1}, device_id_type=MESH)

    pl.semaphore_wait(bar, jnp.where((z == 0) | (z == 3), 1, 2))


def block_starts(half, t, blocks, rank):
    if half == 0:
        return t
    return jnp.where(t < blocks, t, t + rank + 1)


def angles(position, half_size, full_size):
    frequency = THETA ** (-2.0 * jnp.arange(half_size, dtype=F32) / full_size)
    turned = position[:, None] * frequency[None, :]
    return (jnp.cos(turned), jnp.sin(turned))


def rotate(tensor, cosine, sine):
    half_size = tensor.shape[-1] // 2
    a = tensor[..., :half_size]
    b = tensor[..., half_size:]
    return jnp.concatenate([a * cosine - b * sine, b * cosine + a * sine], axis=-1)


def norm_parts(values):
    inv = lax.rsqrt(jnp.mean(values * values, axis=-1, keepdims=True) + EPS)
    return (values * inv, inv)


def norm_back(upstream, normalized, inv, gain):
    d_norm = upstream * (1.0 + gain)
    d_values = inv * (d_norm - normalized * jnp.mean(d_norm * normalized, axis=-1, keepdims=True))
    return (d_values, jnp.sum(upstream * normalized, axis=0))


def gelu_tanh(values):
    return jax.nn.gelu(values, approximate=True)


class LineSum:
    def __init__(self, count, chunk, slots, own, near, far, out, sems):
        self.count, self.chunk, self.slots = count, chunk, slots
        self.own, self.near, self.far, self.out = own, near, far, out
        self.sems = sems
        self.z = z = lax.axis_index("tp")
        self.hub = (z == 1) | (z == 2)
        self.leaf = (z == 0) | (z == 3)
        self.other_hub = jnp.where(z == 1, 2, 1)
        self.my_hub = jnp.where(z == 0, 1, 2)
        self.my_leaf = jnp.where(z == 1, 0, 3)

    def slot(self, c):
        return pl.ds(pl.multiple_of(lax.rem(c, self.slots) * self.chunk, self.chunk), self.chunk)

    def rows(self, c):
        return pl.ds(pl.multiple_of(c * self.chunk, self.chunk), self.chunk)

    def inwards(self, c):
        return pltpu.make_async_remote_copy(
            self.own.at[self.slot(c)], self.near.at[self.slot(c)], self.sems[0].at[c], self.sems[1].at[c],
            device_id={"tp": self.my_hub}, device_id_type=MESH)

    def across(self, c):
        return pltpu.make_async_remote_copy(
            self.own.at[self.slot(c)], self.far.at[self.slot(c)], self.sems[2].at[c], self.sems[3].at[c],
            device_id={"tp": self.other_hub}, device_id_type=MESH)

    def outwards(self, c):
        return pltpu.make_async_remote_copy(
            self.far.at[self.slot(c)], self.out.at[self.rows(c)], self.sems[4].at[c], self.sems[5].at[c],
            device_id={"tp": self.my_leaf}, device_id_type=MESH)

    def store(self, c):
        return pltpu.make_async_copy(self.far.at[self.slot(c)], self.out.at[self.rows(c)], self.sems[6].at[c])

    def put(self, c, value):
        ring = self.slots < self.count
        if ring:
            @pl.when(c >= self.slots)
            def _():
                @pl.when(self.leaf)
                def _():
                    self.inwards(c - self.slots).wait_send()

                @pl.when(self.hub)
                def _():
                    self.across(c - self.slots).wait_send()

        self.own[self.slot(c), :] = value

        @pl.when(self.leaf)
        def _():
            if ring:
                @pl.when(c >= self.slots)
                def _():
                    pl.semaphore_wait(self.sems[7], 1)
            self.inwards(c).start()

    def pair(self, c):
        ring = self.slots < self.count

        @pl.when(self.hub)
        def _():
            self.inwards(c).wait_recv()
            at = self.slot(c)
            self.own[at, :] = (self.own[at, :].astype(F32) + self.near[at, :].astype(F32)).astype(BF16)
            if ring:
                @pl.when(c < self.count - self.slots)
                def _():
                    pl.semaphore_signal(self.sems[7], inc=1, device_id={"tp": self.my_leaf}, device_id_type=MESH)

                @pl.when(c >= self.slots)
                def _():
                    pl.semaphore_wait(self.sems[8], 1)
            self.across(c).start()

    def total(self, c):
        @pl.when(self.hub)
        def _():
            self.across(c).wait_recv()
            at = self.slot(c)
            self.far[at, :] = (self.own[at, :].astype(F32) + self.far[at, :].astype(F32)).astype(BF16)
            self.outwards(c).start()
            self.store(c).start()

    def retire(self, c):
        @pl.when(self.hub)
        def _():
            self.outwards(c).wait_send()
            self.store(c).wait()
            if self.slots < self.count:
                @pl.when(c < self.count - self.slots)
                def _():
                    pl.semaphore_signal(self.sems[8], inc=1, device_id={"tp": self.other_hub}, device_id_type=MESH)

    def finish(self):
        first = max(0, self.count - self.slots)

        @pl.when(self.leaf)
        def _():
            for c in range(self.count):
                self.outwards(c).wait_recv()
            for c in range(first, self.count):
                self.inwards(c).wait_send()

        @pl.when(self.hub)
        def _():
            for c in range(first, self.count):
                self.across(c).wait_send()


def line_sum_scratch(count, chunk, slots, cols):
    dma = pltpu.SemaphoreType.DMA((count,))
    regular = pltpu.SemaphoreType.REGULAR
    return [pltpu.VMEM((slots * chunk, cols), BF16)] * 3 + [dma] * 7 + [regular] * 2


def gelu_parts(v):
    c = 0.7978845608028654
    square = v * v
    t = jnp.tanh(v * (c + (c * 0.044715) * square))
    half = 0.5 + 0.5 * t
    value = v * half
    slope = half + (0.5 * v) * (1.0 - t * t) * (c + (3.0 * c * 0.044715) * square)
    return value, slope


def column_parts(cols, step):
    return [(a, min(a + step, cols)) for a in range(0, cols, step)]


def middle_of(x, attn, gain_post_attn):
    hat, inv = norm_parts(attn.astype(F32))
    return x.astype(F32) + hat * (1.0 + gain_post_attn), hat, inv


def load_ffn_weights(weights, refs, sem):
    wide = refs[0].shape[1]
    base = weights.shape[1] - 3 * wide
    return [
        pltpu.make_async_copy(weights.at[:, pl.ds(base + j * wide, wide)], ref, sem.at[j])
        for j, ref in enumerate(refs)
    ]


def ffn_forward_kernel(tiles, tile, chunk, hidden, x_ref, h_ref, gain_ref, w_ref,
                       attn_ref, two_ref, gate_ref, up_ref, out_ref, wo_ref, wg_ref, wu_ref, wd_ref, w_sem, own, near, far, *sems):
    i = pl.program_id(0)
    per = tile // chunk
    line = LineSum(tiles * per, chunk, tiles * per, own, near, far, out_ref, sems)
    head = wo_ref.shape[1] // 4

    copies = [pltpu.make_async_copy(w_ref.at[:, pl.ds(0, 4 * head)], wo_ref, w_sem.at[3])]
    copies += load_ffn_weights(w_ref, (wg_ref, wu_ref, wd_ref), w_sem)

    @pl.when(i == 0)
    def _():
        for copy in copies:
            copy.start()
        barrier_line(line.z)
        copies[0].wait()

    attn = dot(h_ref[...], wo_ref[...], NT).astype(BF16)
    attn_ref[...] = attn
    middle, _, _ = middle_of(x_ref[...], attn, gain_ref[1:2, :])
    hat, _ = norm_parts(middle)
    two = (hat * (1.0 + gain_ref[2:3, :])).astype(BF16)
    two_ref[...] = two
    part = None

    @pl.when(i == 0)
    def _():
        for copy in copies[1:]:
            copy.wait()

    for a, b in column_parts(hidden, 896):
        gate = dot(two, wg_ref[:, a:b])
        up = dot(two, wu_ref[:, a:b])
        gate_ref[:, a:b] = gate.astype(BF16)
        up_ref[:, a:b] = up.astype(BF16)
        value, _ = gelu_parts(gate)
        more = dot((value * up).astype(BF16), wd_ref[:, a:b], NT)
        part = more if part is None else part + more
    for j in range(per):
        line.put(i * per + j, part[j * chunk : (j + 1) * chunk].astype(BF16))

    @pl.when(i >= 1)
    def _():
        for j in range(per):
            line.pair((i - 1) * per + j)

    @pl.when(i >= 2)
    def _():
        for j in range(per):
            line.total((i - 2) * per + j)

    @pl.when(i == tiles - 1)
    def _():
        last = tiles * per
        for c in range(max(0, last - 2 * per), last - per):
            line.total(c)
        for c in range(last - per, last):
            line.pair(c)
        for c in range(last - per, last):
            line.total(c)
        for c in range(last):
            line.retire(c)
        line.finish()


def whole_block(shape):
    return pl.BlockSpec(shape, lambda i: (0,) * len(shape), pipeline_mode=pl.Buffered(1))


def tile_block(tile, cols):
    return pl.BlockSpec((tile, cols), lambda i: (i, 0))


ANY = pl.BlockSpec(memory_space=pl.ANY)


def wide_of(hidden):
    return -(-hidden // 128) * 128


def ffn_forward(x, heads, gains, weights, hidden, ident):
    rows, width = x.shape
    all_heads = heads.shape[1]
    tile, chunk = 128, 128
    tiles = rows // tile
    count = rows // chunk
    wide = wide_of(hidden)
    return pl.pallas_call(
        functools.partial(ffn_forward_kernel, tiles, tile, chunk, hidden),
        grid=(tiles,),
        out_shape=(
            jax.ShapeDtypeStruct((rows, width), BF16),
            jax.ShapeDtypeStruct((rows, width), BF16),
            jax.ShapeDtypeStruct((rows, hidden), BF16),
            jax.ShapeDtypeStruct((rows, hidden), BF16),
            jax.ShapeDtypeStruct((rows, width), BF16),
        ),
        in_specs=[
            tile_block(tile, width),
            tile_block(tile, all_heads),
            whole_block(gains.shape),
            ANY,
        ],
        out_specs=(tile_block(tile, width), tile_block(tile, width), tile_block(tile, hidden), tile_block(tile, hidden), ANY),
        scratch_shapes=[pltpu.VMEM((width, all_heads), BF16)] + [pltpu.VMEM((width, wide), BF16)] * 3
        + [pltpu.SemaphoreType.DMA((4,))]
        + line_sum_scratch(count, chunk, count, width),
        compiler_params=pltpu.CompilerParams(
            collective_id=ident, has_side_effects=True, vmem_limit_bytes=60 * 2**20),
        cost_estimate=cost(140),
        name="ffn_forward",
    )(x, heads, gains, weights)


def ffn_backward_kernel(tiles, tile, chunk, slots, hidden, dy_ref, ffn_ref, two_ref, gate_ref, up_ref,
                        gain_ref, w_ref,
                        dgain_ref, grad_ref, out_ref, wg_ref, wu_ref, wd_ref, w_sem,
                        acc_g, acc_u, acc_d, keep_g, keep_u, keep_h, stage, stage_sem, own, near, far, *sems):
    i = pl.program_id(0)
    per = tile // chunk
    last = tiles * per
    line = LineSum(last, chunk, slots, own, near, far, out_ref, sems)

    copies = load_ffn_weights(w_ref, (wg_ref, wu_ref, wd_ref), w_sem)

    @pl.when(i == 0)
    def _():
        for copy in copies[::-1]:
            copy.start()
        barrier_line(line.z)
        dgain_ref[...] = jnp.zeros_like(dgain_ref)
        for copy in copies[::-1]:
            copy.wait()

    hat, inv = norm_parts(ffn_ref[...].astype(F32))
    gain = gain_ref[3:4, :]
    d_ffn, d_gain = norm_back(dy_ref[...].astype(F32), hat, inv, gain)
    dgain_ref[...] += d_gain[None]
    d_ffn = d_ffn.astype(BF16)
    part = None

    def handle(j):
        @pl.when(i >= 1)
        def _():
            line.pair((i - 1) * per + j)

        @pl.when(i >= 2)
        def _():
            line.total((i - 2) * per + j)

    for a, b in column_parts(hidden, 512):
        d_hidden = dot(d_ffn, wd_ref[:, a:b])
        up = up_ref[:, a:b].astype(F32)
        value, slope = gelu_parts(gate_ref[:, a:b].astype(F32))
        keep_h[:, a:b] = (value * up).astype(BF16)
        d_gate = (d_hidden * up * slope).astype(BF16)
        d_up = (d_hidden * value).astype(BF16)
        keep_g[:, a:b] = d_gate
        keep_u[:, a:b] = d_up
        more = dot(d_gate, wg_ref[:, a:b], NT) + dot(d_up, wu_ref[:, a:b], NT)
        part = more if part is None else part + more
        if a == 0:
            handle(0)
    for j in range(per):
        line.put(i * per + j, part[j * chunk : (j + 1) * chunk].astype(BF16))

    @pl.when(i == 0)
    def _():
        for acc in (acc_g, acc_u, acc_d):
            acc[...] = jnp.zeros_like(acc)

    acc_g[...] += dot(two_ref[...], keep_g[...], TN)
    acc_u[...] += dot(two_ref[...], keep_u[...], TN)
    for j in range(1, per):
        handle(j)
    acc_d[...] += dot(d_ffn, keep_h[...], TN)

    @pl.when(i >= 3)
    def _():
        for j in range(per):
            line.retire((i - 3) * per + j)

    @pl.when(i == tiles - 1)
    def _():
        step = stage.shape[1]
        count = acc_g.shape[0] // step

        def write(acc, out):
            def pieces(k, _):
                at = lax.rem(k, 2)
                rows = pl.ds(pl.multiple_of(k * step, step), step)

                @pl.when(k >= 2)
                def _():
                    pltpu.make_async_copy(stage.at[at], out.at[pl.ds(0, step)], stage_sem.at[at]).wait()
                stage[at] = acc[rows, :].astype(BF16)
                pltpu.make_async_copy(stage.at[at], out.at[rows], stage_sem.at[at]).start()
                return 0

            lax.fori_loop(0, count, pieces, 0)
            for at in range(2):
                pltpu.make_async_copy(stage.at[at], out.at[pl.ds(0, step)], stage_sem.at[at]).wait()

        for c in range(max(0, last - 2 * per), last - per):
            line.total(c)
        write(acc_g, grad_ref.at[0])
        line.pair(last - per)
        write(acc_u, grad_ref.at[1])
        for c in range(last - per + 1, last):
            line.pair(c)
            line.total(c - 1)
        write(acc_d, grad_ref.at[2])
        line.total(last - 1)
        for c in range(max(0, last - 3 * per), last):
            line.retire(c)
        line.finish()


def ffn_backward(dy, ffn, two, gate, up, gains, weights, ident):
    rows, width = dy.shape
    hidden = gate.shape[1]
    wide = wide_of(hidden)
    tile, chunk = 256, 128
    tiles = rows // tile
    count = rows // chunk
    slots = min(count, 6)
    step = 144
    acc = pltpu.VMEM((width, hidden), F32)
    keep = pltpu.VMEM((tile, hidden), BF16)
    return pl.pallas_call(
        functools.partial(ffn_backward_kernel, tiles, tile, chunk, slots, hidden),
        grid=(tiles,),
        out_shape=(
            jax.ShapeDtypeStruct((1, width), F32),
            jax.ShapeDtypeStruct((3, width, hidden), BF16),
            jax.ShapeDtypeStruct((rows, width), BF16),
        ),
        in_specs=[tile_block(tile, width)] * 3 + [tile_block(tile, hidden)] * 2
        + [whole_block(gains.shape), ANY],
        out_specs=(pl.BlockSpec((1, width), lambda i: (0, 0)), ANY, ANY),
        scratch_shapes=[pltpu.VMEM((width, wide), BF16)] * 3 + [pltpu.SemaphoreType.DMA((3,))] + [acc] * 3 + [keep] * 3
        + [pltpu.VMEM((2, step, hidden), BF16), pltpu.SemaphoreType.DMA((2,))]
        + line_sum_scratch(count, chunk, slots, width),
        compiler_params=pltpu.CompilerParams(
            collective_id=ident, has_side_effects=True, vmem_limit_bytes=63 * 2**20),
        cost_estimate=cost(145),
        name="ffn_backward",
    )(dy, ffn, two, gate, up, gains, weights)


def middle_back_kernel(x_ref, attn_ref, dy_ref, d2_ref, ffn_ref, h_ref, gain_ref, w_ref,
                       y_ref, dm_ref, dh_ref, delta_ref, dgain_ref, go_ref, acc, wo_ref, w_sem):
    i = pl.program_id(0)

    @pl.when(i == 0)
    def _():
        head = wo_ref.shape[1]
        at = pl.multiple_of(lax.axis_index("tp") * head, head)
        copy = pltpu.make_async_copy(w_ref.at[:, pl.ds(at, head)], wo_ref, w_sem)
        copy.start()
        copy.wait()
        acc[...] = jnp.zeros_like(acc)
        dgain_ref[...] = jnp.zeros_like(dgain_ref)

    middle, attn_hat, attn_inv = middle_of(x_ref[...], attn_ref[...], gain_ref[1:2, :])
    hat, _ = norm_parts(ffn_ref[...].astype(F32))
    y_ref[...] = (middle + hat * (1.0 + gain_ref[3:4, :])).astype(BF16)
    hat, inv = norm_parts(middle)
    d_part, d_gain = norm_back(d2_ref[...].astype(F32), hat, inv, gain_ref[2:3, :])
    dgain_ref[1:2, :] += d_gain[None]
    d_middle = dy_ref[...].astype(F32) + d_part
    dm_ref[...] = d_middle.astype(BF16)
    d_attn, d_gain = norm_back(d_middle, attn_hat, attn_inv, gain_ref[1:2, :])
    dgain_ref[0:1, :] += d_gain[None]
    d_attn = d_attn.astype(BF16)
    d_heads = dot(d_attn, wo_ref[...]).astype(BF16)
    dh_ref[...] = d_heads
    heads = h_ref[...]
    delta_ref[...] = jnp.sum(d_heads.astype(F32) * heads.astype(F32), axis=1, keepdims=True)
    acc[...] += dot(d_attn, heads, TN)

    @pl.when(i == pl.num_programs(0) - 1)
    def _():
        go_ref[...] = acc[...].astype(BF16)


def middle_back(x, attn, dy, d_two, ffn, heads, gains, weights):
    rows, width = x.shape
    head = heads.shape[1]
    tile = 256
    return pl.pallas_call(
        middle_back_kernel,
        grid=(rows // tile,),
        out_shape=(
            jax.ShapeDtypeStruct((rows, width), BF16),
            jax.ShapeDtypeStruct((rows, width), BF16),
            jax.ShapeDtypeStruct((rows, head), BF16),
            jax.ShapeDtypeStruct((rows, 1), F32),
            jax.ShapeDtypeStruct((2, width), F32),
            jax.ShapeDtypeStruct((width, head), BF16),
        ),
        in_specs=[tile_block(tile, width)] * 5 + [tile_block(tile, head)] + [whole_block(gains.shape), ANY],
        out_specs=(
            tile_block(tile, width), tile_block(tile, width), tile_block(tile, head), tile_block(tile, 1),
            pl.BlockSpec((2, width), lambda i: (0, 0)), pl.BlockSpec((width, head), lambda i: (0, 0)),
        ),
        scratch_shapes=[pltpu.VMEM((width, head), F32), pltpu.VMEM((width, head), BF16), pltpu.SemaphoreType.DMA],
        compiler_params=pltpu.CompilerParams(vmem_limit_bytes=48 * 2**20),
        cost_estimate=cost(19),
        name="middle_back",
    )(x, attn, dy, d_two, ffn, heads, gains, weights)


class LineGather:
    def __init__(self, whole, tile, width, sems):
        self.whole, self.tile, self.width, self.sems = whole, tile, width, sems
        self.z = lax.axis_index("tp")

    def place(self, src, t):
        return self.whole.at[
            pl.ds(pl.multiple_of(t * self.tile, self.tile), self.tile),
            pl.ds(pl.multiple_of(src * self.width, self.width), self.width)]

    def send(self, src, t, hop, way):
        ss, rs = self.sems[:2] if way > 0 else self.sems[2:]
        place = self.place(src, t)
        return pltpu.make_async_remote_copy(
            place, place, ss.at[hop, t], rs.at[hop, t],
            device_id={"tp": self.z + way}, device_id_type=MESH)

    def going(self, hop, way):
        src = self.z - way * hop
        return src, (self.z + way >= 0) & (self.z + way <= 3) & (src >= 0) & (src <= 3)

    def coming(self, hop, way):
        src = self.z - way * (hop + 1)
        return src, (src >= 0) & (src <= 3)

    def forward(self, t, hop):
        for way in (1, -1):
            if hop > 0:
                self.wait(t, hop - 1, way)
            src, ok = self.going(hop, way)

            @pl.when(ok)
            def _():
                self.send(src, t, hop, way).start()

    def wait(self, t, hop, way):
        src, ok = self.coming(hop, way)

        @pl.when(ok)
        def _():
            self.send(src, t, hop, way).wait_recv()

    def arrived(self, t):
        for way in (1, -1):
            self.wait(t, 2, way)

    def finish(self, tiles):
        for hop in range(3):
            for way in (1, -1):
                src, ok = self.going(hop, way)

                @pl.when(ok)
                def _():
                    def one(t, _):
                        self.send(src, t, hop, way).wait_send()
                        return 0

                    lax.fori_loop(0, tiles, one, 0)


class KeyGather(LineGather):
    def __init__(self, block, chips, sems):
        self.block, self.chips, self.sems = block, chips, sems
        self.z = lax.axis_index("tp")

    def tile_of(self, g, half, k):
        return (2 * g + half) * (self.chips - 1) + k - 1

    def place(self, src, t):
        pair, k = divmod(t, self.chips - 1)
        return self.quarter(pair // 2, pair % 2, k + 1, src)

    def quarter(self, g, half, k, src, own=False):
        ref, start, size = self.block(g, half, k, own)
        rows = size // 4
        return ref.at[pl.ds(pl.multiple_of(start + src * rows, rows), rows)]

    def finish(self, tiles):
        for hop in range(3):
            for way in (1, -1):
                src, ok = self.going(hop, way)

                @pl.when(ok)
                def _():
                    for t in range(tiles):
                        self.send(src, t, hop, way).wait_send()


class Shared:
    def __init__(self, over_dp):
        self.ctx = ctx = lax.axis_size("ctx")
        me = lax.axis_index("ctx")
        self.devices = ctx
        if over_dp:
            me = me + lax.axis_index("dp") * ctx
            self.devices = ctx * lax.axis_size("dp")
        self.over_dp = over_dp
        self.me = me
        self.chips = self.devices // 2
        self.core = lax.rem(me, 2)
        self.chip = lax.div(me, 2)

    def ident(self, device):
        if self.over_dp:
            return {"dp": lax.div(device, self.ctx), "ctx": lax.rem(device, self.ctx)}
        return {"ctx": device}

    def other(self, k):
        return 2 * lax.rem(self.chip + k + self.chips, self.chips) + self.core

    def partner(self):
        return self.me + 1 - 2 * self.core

    def greet(self, z):
        bar = pltpu.get_barrier_semaphore()
        for device in [self.partner()] + [self.other(k) for k in range(1, self.chips)]:
            pl.semaphore_signal(bar, inc=1, device_id=self.ident(device), device_id_type=MESH)

        @pl.when(z > 0)
        def _():
            pl.semaphore_signal(bar, inc=1, device_id={"tp": z - 1}, device_id_type=MESH)

        @pl.when(z < 3)
        def _():
            pl.semaphore_signal(bar, inc=1, device_id={"tp": z + 1}, device_id_type=MESH)

        pl.semaphore_wait(bar, self.chips + jnp.where((z == 0) | (z == 3), 1, 2))

    def copy(self, source, target, send, recv, device):
        return pltpu.make_async_remote_copy(
            source, target, send, recv, device_id=self.ident(device), device_id_type=MESH)


def first_gather_kernel(a_ref, b_ref, c_ref, i_ref, all_ref, line_ref, more_ref, ids_ref, lsem, ss1, rs1, ss2, rs2, si1, ri1, si2, ri2, *sems):
    group = Shared(True)
    line = LineGather(line_ref, b_ref.shape[0], b_ref.shape[1], sems[:4])
    more = LineGather(more_ref, c_ref.shape[0], c_ref.shape[1], sems[4:])
    width = b_ref.shape[1]
    own = [
        pltpu.make_async_copy(b_ref, line_ref.at[:, pl.ds(pl.multiple_of(line.z * width, width), width)], lsem.at[0]),
        pltpu.make_async_copy(c_ref, more_ref.at[:, pl.ds(pl.multiple_of(line.z * width, width), width)], lsem.at[3]),
        pltpu.make_async_copy(a_ref, all_ref.at[group.me], lsem.at[1]),
        pltpu.make_async_copy(i_ref, ids_ref.at[group.me], lsem.at[2]),
    ]
    for copy in own:
        copy.start()
    group.greet(line.z)
    arrays = ((a_ref, all_ref, ss1, rs1, ss2, rs2), (i_ref, ids_ref, si1, ri1, si2, ri2))

    def direct(n, k, incoming=False):
        ref, whole, ss, rs = arrays[n][:4]
        at = whole.at[group.other(-k)] if incoming else whole.at[group.me]
        return group.copy(ref, at, ss.at[k], rs.at[k], group.other(k))

    def inner(n, k, incoming=False):
        ref, whole, _, _, ss, rs = arrays[n]
        at = whole.at[group.other(-k)]
        if incoming:
            at = whole.at[group.other(-k) + 1 - 2 * group.core]
        return group.copy(ref if k == 0 else at, at, ss.at[k], rs.at[k], group.partner())

    both = range(2)
    for k in range(1, group.chips):
        for n in both:
            direct(n, k).start()
    for n in both:
        inner(n, 0).start()
    own[0].wait()
    line.forward(0, 0)
    own[1].wait()
    more.forward(0, 0)
    for k in range(1, group.chips):
        if k < 3:
            line.forward(0, k)
            more.forward(0, k)
        for n in both:
            direct(n, k, True).wait_recv()
            inner(n, k).start()
    for hop in range(min(3, group.chips), 3):
        line.forward(0, hop)
        more.forward(0, hop)
    for k in range(group.chips):
        for n in both:
            inner(n, k, True).wait_recv()
    line.arrived(0)
    more.arrived(0)
    for copy in own[2:]:
        copy.wait()
    for n in both:
        for k in range(1, group.chips):
            direct(n, k).wait_send()
        for k in range(group.chips):
            inner(n, k).wait_send()
    line.finish(1)
    more.finish(1)


def first_gather(a, b, c, ids, devices, ident):
    dma = pltpu.SemaphoreType.DMA((devices // 2,))
    hop = pltpu.SemaphoreType.DMA((3, 1))
    return pl.pallas_call(
        first_gather_kernel,
        out_shape=(
            jax.ShapeDtypeStruct((devices,) + a.shape, a.dtype),
            jax.ShapeDtypeStruct((b.shape[0], 4 * b.shape[1]), b.dtype),
            jax.ShapeDtypeStruct((c.shape[0], 4 * c.shape[1]), c.dtype),
            jax.ShapeDtypeStruct((devices,) + ids.shape, ids.dtype),
        ),
        in_specs=[ANY] * 4,
        out_specs=(ANY,) * 4,
        scratch_shapes=[pltpu.SemaphoreType.DMA((4,))] + [dma] * 8 + [hop] * 8,
        compiler_params=pltpu.CompilerParams(collective_id=ident, has_side_effects=True),
        cost_estimate=cost(20),
        name="first_gather",
    )(a, b, c, ids)


def attention_kernel(groups, size, x_ref, w_ref, gain_ref, gq_ref, gk_ref, cos_ref, sin_ref, qs_ref, ks_ref,
                     q_ref, qhat_ref, qinv_ref, khat_ref, kinv_ref, heads_ref, log_ref, kv_out, all_out,
                     kv, whole, store_kv, store_all, ss1, rs1, ss2, rs2, *sems):
    head = q_ref.shape[1]
    length = kv.shape[1]
    id_rows = size // 128
    blocks = length // (2 * size)
    group = Shared(False)
    rank = group.me
    tile = min(256, size)
    per = size // tile
    line = LineGather(whole, tile, head, sems[:4])
    z = line.z
    group.greet(z)

    def block(g, half, k, own):
        c = rank if own else group.other(-k)
        return kv.at[g], half * (length // 2) + c * size, size

    keys = KeyGather(block, group.chips, sems[4:])

    def place(g, half, c):
        return kv.at[g, pl.ds(pl.multiple_of(half * (length // 2) + c * size, size), size)]

    def straight(t):
        return t == 2 * groups - 1

    def direct(g, half, k, incoming=False):
        at = keys.quarter(g, half, k, z, own=not incoming)
        if straight(2 * g + half):
            at = place(g, half, group.other(-k) if incoming else rank)
        return group.copy(at, at, ss1.at[g, half, k], rs1.at[g, half, k], group.other(k))

    def inner(g, half, k, incoming=False):
        block = group.other(-k)
        at = place(g, half, block + 1 - 2 * group.core if incoming else block)
        return group.copy(at, at, ss2.at[g, half, k], rs2.at[g, half, k], group.partner())

    def project(g, half, u):
        rows = pl.ds((2 * g + half) * size + u * tile, tile)
        spot = pl.ds(half * size + u * tile, tile)
        cosine, sine = cos_ref[spot, :], sin_ref[spot, :]
        hat, _ = norm_parts(x_ref[rows, :].astype(F32))
        raw = dot((hat * (1.0 + gain_ref[0:1, :])).astype(BF16), w_ref[:, : 3 * head])
        hat, inv = norm_parts(raw[:, :head])
        qhat_ref[rows, :] = hat
        qinv_ref[rows, :] = inv
        q_ref[rows, :] = rotate(hat * (1.0 + gq_ref[...]), cosine, sine).astype(BF16)
        hat, inv = norm_parts(raw[:, head : 2 * head])
        khat_ref[rows, :] = hat
        kinv_ref[rows, :] = inv
        at = pl.ds(pl.multiple_of(half * (length // 2) + rank * size + u * tile, tile), tile)
        kv[g, at, :head] = rotate(hat * (1.0 + gk_ref[...]), cosine, sine).astype(BF16)
        kv[g, at, head:] = raw[:, 2 * head :].astype(BF16)

    def attend(g, half):
        row = lax.broadcasted_iota(jnp.int32, (size, size), 0)
        col = lax.broadcasted_iota(jnp.int32, (size, size), 1)
        rows = pl.ds((2 * g + half) * size, size)
        q = q_ref[rows, :] * jnp.asarray(SCALE, BF16)
        qseg = qs_ref[g, half]

        def part(block):
            at = pl.ds(pl.multiple_of(block * size, size), size)
            device = lax.axis_index("dp") * lax.axis_size("ctx") + lax.rem(block, blocks)
            ids = ks_ref[device, pl.ds((2 * g + lax.div(block, blocks)) * id_rows, id_rows), :]
            ids = jnp.concatenate([ids[j : j + 1] for j in range(id_rows)], axis=1)
            same = qseg == jnp.where(ids == 0, -1, ids)
            return dot(q, kv[g, at, :head], NT), kv[g, at, head:], same

        s, v, same = part(rank + half * blocks)
        order = (col <= row) if half == 0 else (col >= row)
        s = jnp.where((same & order) | (col == row), s, NEGATIVE)
        top = jnp.max(s, axis=1, keepdims=True)
        p = jnp.exp(s - top)
        mass = jnp.sum(p, axis=1, keepdims=True)
        acc = dot(p.astype(BF16), v)

        def step(t, carry):
            top, mass, acc = carry
            s, v, same = part(block_starts(half, t, blocks, rank))
            s = jnp.where(same, s, NEGATIVE)
            new = jnp.maximum(top, jnp.max(s, axis=1, keepdims=True))
            keep = jnp.exp(top - new)
            p = jnp.exp(s - new)
            mass = mass * keep + jnp.sum(p, axis=1, keepdims=True)
            return new, mass, acc * keep + dot(p.astype(BF16), v)

        count = rank if half == 0 else 2 * blocks - 1 - rank
        top, mass, acc = lax.fori_loop(0, count, step, (top, mass, acc))
        out = (acc / mass).astype(BF16)
        heads_ref[rows, :] = out
        whole[rows, pl.ds(pl.multiple_of(z * head, head), head)] = out
        log_ref[g, half] = top + jnp.log(mass)

    chips = range(1, group.chips)
    tiles = 2 * groups

    def stage(t, n):
        if not 0 <= t < tiles:
            return
        g, half = divmod(t, 2)
        for k in chips:
            spot = keys.tile_of(g, half, k)
            if n == 0:
                direct(g, half, k).start()
            elif straight(t):
                if n == 4:
                    direct(g, half, k, True).wait_recv()
                    inner(g, half, k).start()
            elif n == 4:
                keys.arrived(spot)
                inner(g, half, k).start()
            else:
                if n == 1:
                    direct(g, half, k, True).wait_recv()
                keys.forward(spot, n - 1)

    def exchange(t):
        for n in (4, 3, 2, 1):
            stage(t - n, n)

    def hops(t):
        for hop in range(3):
            if 0 <= t - hop < tiles:
                for u in range(per):
                    line.forward((t - hop) * per + u, hop)

    def keep(t):
        at = pl.ds(t * tile, tile)
        return pltpu.make_async_copy(whole.at[at], all_out.at[at], store_all.at[t])

    def save(g):
        return pltpu.make_async_copy(kv.at[g], kv_out.at[g], store_kv.at[g])

    def landed(t):
        g, half = divmod(t, 2)
        for k in range(group.chips):
            inner(g, half, k, True).wait_recv()

    for t in range(tiles):
        g, half = divmod(t, 2)
        for u in range(per):
            project(g, half, u)
        stage(t, 0)
        inner(g, half, 0).start()
        exchange(t)
    for t in range(tiles):
        g, half = divmod(t, 2)
        exchange(tiles + t)
        landed(t)
        attend(g, half)
        hops(t)
    for g in range(groups):
        save(g).start()
    for t in range(tiles, tiles + 2):
        hops(t)
    for t in range(tiles * per):
        line.arrived(t)
        keep(t).start()
    for g in range(groups):
        save(g).wait()
        for half in range(2):
            for k in chips:
                direct(g, half, k).wait_send()
            for k in range(group.chips):
                inner(g, half, k).wait_send()
    line.finish(tiles * per)
    keys.finish((tiles - 1) * (group.chips - 1))
    for t in range(tiles * per):
        keep(t).wait()


def attention(x, w, gains, gain_query, gain_key, cosine, sine, qseg, ids, length, ident):
    rows, width = x.shape
    groups, _, size, _ = qseg.shape
    head = gain_query.shape[1]
    chips = length // (4 * size)
    tiles = 2 * groups
    parts = rows // min(256, size)
    vmem = pl.BlockSpec(memory_space=pltpu.VMEM)
    dma = pltpu.SemaphoreType.DMA
    return pl.pallas_call(
        functools.partial(attention_kernel, groups, size),
        out_shape=(
            jax.ShapeDtypeStruct((rows, head), BF16),
            jax.ShapeDtypeStruct((rows, head), F32),
            jax.ShapeDtypeStruct((rows, 1), F32),
            jax.ShapeDtypeStruct((rows, head), F32),
            jax.ShapeDtypeStruct((rows, 1), F32),
            jax.ShapeDtypeStruct((rows, head), BF16),
            jax.ShapeDtypeStruct((groups, 2, size, 1), F32),
            jax.ShapeDtypeStruct((groups, length, 2 * head), BF16),
            jax.ShapeDtypeStruct((rows, 4 * head), BF16),
        ),
        in_specs=[vmem] * 9,
        out_specs=(vmem,) * 7 + (ANY, ANY),
        scratch_shapes=[
            pltpu.VMEM((groups, length, 2 * head), BF16), pltpu.VMEM((rows, 4 * head), BF16),
            dma((groups,)), dma((parts,))] + [dma((groups, 2, chips))] * 4 + [dma((3, parts))] * 4
        + [dma((3, tiles * (chips - 1)))] * 4,
        compiler_params=pltpu.CompilerParams(
            collective_id=ident, has_side_effects=True, vmem_limit_bytes=60 * 2**20),
        cost_estimate=cost(110),
        name="attention",
    )(x, w, gains, gain_query, gain_key, cosine, sine, qseg, ids)


class ResidentSum(LineSum):
    def outwards(self, c):
        return pltpu.make_async_remote_copy(
            self.out.at[self.rows(c)], self.out.at[self.rows(c)], self.sems[4].at[c], self.sems[5].at[c],
            device_id={"tp": self.my_leaf}, device_id_type=MESH)

    def total(self, c):
        @pl.when(self.hub)
        def _():
            self.across(c).wait_recv()
            at = self.rows(c)
            self.out[at, :] = (self.own[at, :].astype(F32) + self.far[at, :].astype(F32)).astype(BF16)
            self.outwards(c).start()

    def arrived(self, c):
        @pl.when(self.leaf)
        def _():
            self.outwards(c).wait_recv()

    def finish(self):
        @pl.when(self.leaf)
        def _():
            for c in range(self.count):
                self.inwards(c).wait_send()

        @pl.when(self.hub)
        def _():
            for c in range(self.count):
                self.across(c).wait_send()
                self.outwards(c).wait_send()


def turned(column, size):
    return jnp.transpose(jnp.broadcast_to(column, (size, 128)))[0:1, :]


def attention_back_kernel(groups, size, q_ref, do_ref, log_ref, delta_ref, qs_ref, ids_ref, hat_ref, inv_ref, cos_ref, sin_ref,
                          x_ref, gain_ref, gq_ref, go_ref, kv_hbm, all_out, dkv_ref, rest_ref, dgain_ref, grad_ref,
                          kv, dk, dv, part, near, pair, far, whole, acc, load, store, ss1, rs1, ss2, rs2, *sems):
    head = q_ref.shape[1]
    length = kv.shape[1]
    blocks = length // (2 * size)
    id_rows = size // 128
    tiles = 2 * groups
    group = Shared(False)
    rank, core = group.me, group.core
    tile = min(256, size)
    per = size // tile
    line = LineGather(whole, tile, head, sems)
    z = line.z
    others = range(1, group.chips)
    order = list(others) + [0]

    def fetch(g):
        return pltpu.make_async_copy(kv_hbm.at[g], kv.at[g], load.at[g])

    for g in range(groups):
        fetch(g).start()
    group.greet(z)
    acc[...] = jnp.zeros_like(acc)
    dgain_ref[...] = jnp.zeros_like(dgain_ref)

    def rows_of(half, device):
        return pl.ds(pl.multiple_of(half * (length // 2) + device * size, size), size)

    def within(g, half, k):
        to = group.other(k) + 1 - 2 * core
        return group.copy(
            part.at[g, rows_of(half, to)], near.at[g, half, k], ss1.at[g, half, k], rs1.at[g, half, k], group.partner())

    def between(g, half, k):
        return group.copy(
            pair.at[g, half, k - 1], far.at[g, half, k - 1], ss2.at[g, half, k], rs2.at[g, half, k], group.other(k))

    def both_cores(g):
        for half in range(2):
            for k in order:
                within(g, half, k).wait_recv()
                total = part[g, rows_of(half, group.other(k)), :].astype(F32) + near[g, half, k].astype(F32)
                if k > 0 and g == groups - 1:
                    rest_ref[half, k - 1] = total.astype(BF16)
                elif k > 0:
                    pair[g, half, k - 1] = total.astype(BF16)
                    between(g, half, k).start()
                else:
                    dkv_ref[pl.ds((2 * g + half) * size, size), :] = total.astype(BF16)

    def all_chips(g):
        for half in range(2):
            at = pl.ds((2 * g + half) * size, size)
            total = dkv_ref[at, :].astype(F32)
            for k in others:
                between(g, half, k).wait_recv()
                total = total + far[g, half, k - 1].astype(F32)
            dkv_ref[at, :] = total.astype(BF16)

    def hops(t):
        for hop in range(3):
            if 0 <= t - hop < tiles:
                for u in range(per):
                    line.forward((t - hop) * per + u, hop)

    def attend(g, half):
        row = lax.broadcasted_iota(jnp.int32, (size, size), 0)
        col = lax.broadcasted_iota(jnp.int32, (size, size), 1)
        own = pl.ds((2 * g + half) * size, size)
        q = q_ref[own, :] * jnp.asarray(SCALE, BF16)
        do = do_ref[own, :]
        qseg = qs_ref[g, half]
        log_mass = turned(log_ref[g, half], size)
        delta = turned(delta_ref[own, :], size)

        def step_of(block, mine):
            at = pl.ds(pl.multiple_of(block * size, size), size)
            k = kv[g, at, :head]
            v = kv[g, at, head:]
            device = lax.axis_index("dp") * lax.axis_size("ctx") + lax.rem(block, blocks)
            ids = ids_ref[device, pl.ds((2 * g + lax.div(block, blocks)) * id_rows, id_rows), :]
            ids = jnp.concatenate([ids[j : j + 1] for j in range(id_rows)], axis=1)
            ids = jnp.transpose(jnp.broadcast_to(jnp.where(ids == 0, -1, ids), (8, size)))[:, 0:1]
            allowed = ids == qseg
            if mine:
                ahead = (row <= col) if half == 0 else (row >= col)
                allowed = (allowed & ahead) | (col == row)
            s = jnp.where(allowed, dot(k, q, NT), NEGATIVE)
            p = jnp.exp(s - log_mass)
            ds = (p * (dot(v, do, NT) - delta)).astype(BF16)
            dv[at, :] += dot(p.astype(BF16), do)
            dk[at, :] += dot(ds, q)
            return dot(ds, k, TN)

        def step(t, dq):
            return dq + step_of(block_starts(half, t, blocks, rank), False)

        dq = step_of(rank + half * blocks, True)
        count = rank if half == 0 else 2 * blocks - 1 - rank
        dq = SCALE * lax.fori_loop(0, count, step, dq)
        spot = pl.ds(half * size, size)
        d_rot = rotate(dq, cos_ref[spot, :], -sin_ref[spot, :])
        d_raw, d_gain = norm_back(d_rot, hat_ref[own, :], inv_ref[own, :], gq_ref[...])
        dgain_ref[...] += d_gain[None]
        whole[own, pl.ds(pl.multiple_of(z * head, head), head)] = d_raw.astype(BF16)

    def weight_gradient(t):
        own = pl.ds(t * size, size)
        hat, _ = norm_parts(x_ref[own, :].astype(F32))
        one = (hat * (1.0 + gain_ref[0:1, :])).astype(BF16)
        acc[...] += dot(one, whole[own, pl.ds(pl.multiple_of(z * head, head), head)], TN)

    def keep(t):
        at = pl.ds(t * tile, tile)
        return pltpu.make_async_copy(whole.at[at], all_out.at[at], store.at[t])

    for g in range(groups):
        fetch(g).wait()
        dk[...] = jnp.zeros_like(dk)
        dv[...] = jnp.zeros_like(dv)
        for half in range(2):
            attend(g, half)
            hops(2 * g + half)
            if half == 0 and g > 0:
                both_cores(g - 1)
        part[g, :, :head] = dk[...].astype(BF16)
        part[g, :, head:] = dv[...].astype(BF16)
        for half in range(2):
            for k in order:
                within(g, half, k).start()
        for half in range(2):
            weight_gradient(2 * g + half)
        if g > 0:
            all_chips(g - 1)
    hops(tiles)
    both_cores(groups - 1)
    hops(tiles + 1)
    grad_ref[:, :head] = acc[...].astype(BF16)
    grad_ref[:, head:] = go_ref[...]
    for t in range(tiles * per):
        line.arrived(t)
        keep(t).start()
    for g in range(groups):
        for half in range(2):
            if g < groups - 1:
                for k in others:
                    between(g, half, k).wait_send()
            for k in order:
                within(g, half, k).wait_send()
    line.finish(tiles * per)
    for t in range(tiles * per):
        keep(t).wait()


def attention_back(q, d_heads, log_mass, delta, qseg, ids, hat, inv, cosine, sine, x, gains, gain_query, grad_o, kv, ident):
    rows, head = q.shape
    width = x.shape[1]
    groups, length, _ = kv.shape
    size = rows // (2 * groups)
    chips = length // (4 * size)
    parts = rows // min(256, size)
    vmem = pl.BlockSpec(memory_space=pltpu.VMEM)
    dma = pltpu.SemaphoreType.DMA
    return pl.pallas_call(
        functools.partial(attention_back_kernel, groups, size),
        out_shape=(
            jax.ShapeDtypeStruct((rows, 4 * head), BF16),
            jax.ShapeDtypeStruct((rows, 2 * head), BF16),
            jax.ShapeDtypeStruct((2, chips - 1, size, 2 * head), BF16),
            jax.ShapeDtypeStruct((1, head), F32),
            jax.ShapeDtypeStruct((width, 2 * head), BF16),
        ),
        in_specs=[vmem] * 14 + [ANY],
        out_specs=(ANY, vmem, vmem, vmem, vmem),
        scratch_shapes=[
            pltpu.VMEM((groups, length, 2 * head), BF16),
            pltpu.VMEM((length, head), F32), pltpu.VMEM((length, head), F32),
            pltpu.VMEM((groups, length, 2 * head), BF16),
            pltpu.VMEM((groups, 2, chips, size, 2 * head), BF16),
            pltpu.VMEM((groups, 2, chips - 1, size, 2 * head), BF16),
            pltpu.VMEM((groups, 2, chips - 1, size, 2 * head), BF16),
            pltpu.VMEM((rows, 4 * head), BF16),
            pltpu.VMEM((width, head), F32),
            dma((groups,)), dma((parts,))] + [dma((groups, 2, chips))] * 4 + [dma((3, parts))] * 4,
        compiler_params=pltpu.CompilerParams(
            collective_id=ident, has_side_effects=True, vmem_limit_bytes=63 * 2**20),
        cost_estimate=cost(80),
        name="attention_back",
    )(q, d_heads, log_mass, delta, qseg, ids, hat, inv, cosine, sine, x, gains, gain_query, grad_o, kv)


class RowScatter:
    def __init__(self, group, own_rows, source, near, pair, far, sems):
        self.group, self.own_rows, self.source = group, own_rows, source
        self.near, self.pair, self.far, self.sems = near, pair, far, sems
        self.others = list(range(1, group.chips))
        self.order = self.others + [0]

    def block(self, device):
        return pl.ds(pl.multiple_of(device * self.own_rows, 16), self.own_rows)

    def within(self, k):
        g = self.group
        return g.copy(self.source.at[self.block(g.other(k) + 1 - 2 * g.core)], self.near.at[k],
                      self.sems[0].at[k], self.sems[1].at[k], g.partner())

    def between(self, k):
        g = self.group
        return g.copy(self.pair.at[k], self.far.at[k], self.sems[2].at[k], self.sems[3].at[k], g.other(k))

    def send(self):
        for k in self.order:
            self.within(k).start()

    def middle(self, out):
        for k in self.order:
            self.within(k).wait_recv()
            both = self.source[self.block(self.group.other(k)), :].astype(F32) + self.near[k].astype(F32)
            if k > 0:
                self.pair[k] = both.astype(BF16)
                self.between(k).start()
            else:
                out[...] = both

    def final(self, out):
        for k in self.others:
            self.between(k).wait_recv()
            out[...] += self.far[k].astype(F32)
        for k in self.others:
            self.between(k).wait_send()
        for k in self.order:
            self.within(k).wait_send()


def row_scatter_scratch(chips, own_rows, cols):
    return [pltpu.VMEM((chips, own_rows, cols), BF16)] * 3 + [pltpu.SemaphoreType.DMA((chips,))] * 4


def key_back_kernel(tiles, tile, chunk, own_rows, scattered, dkv_ref, hat_ref, inv_ref, cos_ref, sin_ref, x_ref, dq_ref,
                    gain_ref, gk_ref, w_ref, wq_ref, dgq_ref, dg_mid_ref, dg_post_ref, qo_ref, rest_ref,
                    dx_ref, last_out, qo_out, acc, acc_in, acc_key, w_kv, w_sem, last_ref, part,
                    add, ss, rs, out, own, near, far, *sems):
    i = pl.program_id(0)
    head = hat_ref.shape[1]
    per = tile // chunk
    count = tiles * per + 1
    line = ResidentSum(count, chunk, count, own, near, far, out, sems[:9])
    group = Shared(True)
    ring = Shared(False)
    size = rest_ref.shape[2]
    first = tiles * per - 2 * size // chunk

    def between(half, k):
        return ring.copy(rest_ref.at[half, k - 1], add.at[half, k - 1], ss.at[half, k], rs.at[half, k], ring.other(k))

    if scattered:
        early = RowScatter(group, own_rows, qo_ref, *sems[9:12], sems[12:16])
        late = RowScatter(group, own_rows, last_ref, *sems[16:19], sems[19:23])

    @pl.when(i == 0)
    def _():
        copy = pltpu.make_async_copy(w_ref.at[:, pl.ds(head, 2 * head)], w_kv, w_sem)
        copy.start()
        if scattered:
            group.greet(line.z)
        else:
            ring.greet(line.z)
            qo_out[...] = qo_ref[...]
        for half in range(2):
            for k in range(1, ring.chips):
                between(half, k).start()
        if scattered:
            early.send()
        for ref in (acc, acc_in, acc_key):
            ref[...] = jnp.zeros_like(ref)
        copy.wait()
        line.put(count - 1, jnp.broadcast_to(
            jnp.concatenate([dgq_ref[...], dgq_ref[...]], axis=1).astype(BF16), (chunk, 2 * head)))

    def put_rows(c):
        return dkv_ref[pl.ds(pl.multiple_of(c * chunk, chunk), chunk), :]

    @pl.when(i == 0)
    def _():
        def ready(c, _):
            line.put(c, put_rows(c))
            return 0

        lax.fori_loop(0, first, ready, 0)

    for half in range(2):
        @pl.when(i == max(0, (first * chunk + half * size) // tile - 2))
        def _():
            for k in range(1, ring.chips):
                between(half, k).wait_recv()

            def ready(n, _):
                c = first + half * (size // chunk) + n
                total = put_rows(c).astype(F32)
                for k in range(1, ring.chips):
                    total = total + add[half, k - 1, pl.ds(pl.multiple_of(n * chunk, chunk), chunk), :].astype(F32)
                line.put(c, total.astype(BF16))
                return 0

            lax.fori_loop(0, size // chunk, ready, 0)

    @pl.when(i < tiles)
    def _():
        part[pl.ds(pl.multiple_of(i * tile, tile), tile), :] = dot(dq_ref[...], wq_ref[...], NT)

    @pl.when((i >= 1) & (i <= tiles))
    def _():
        for j in range(per):
            line.total((i - 1) * per + j)

    @pl.when(i < tiles)
    def _():
        for j in range(per):
            line.pair(i * per + j)

    @pl.when(i == 1)
    def _():
        line.pair(count - 1)
        if scattered:
            early.middle(qo_out)

    @pl.when(i == 2)
    def _():
        line.total(count - 1)

    if scattered:
        @pl.when(i == tiles)
        def _():
            early.final(qo_out)

    @pl.when(i >= 2)
    def _():
        for j in range(per):
            line.arrived((i - 2) * per + j)
        d_kv = out[pl.ds(pl.multiple_of((i - 2) * tile, tile), tile), :]
        d_rot = rotate(d_kv[:, :head].astype(F32), cos_ref[...], -sin_ref[...])
        d_raw, d_gain = norm_back(d_rot, hat_ref[...], inv_ref[...], gk_ref[...])
        acc_key[...] += d_gain[None]
        d_raw = jnp.concatenate([d_raw.astype(BF16), d_kv[:, head:]], axis=1)
        d_one = part[pl.ds(pl.multiple_of((i - 2) * tile, tile), tile), :] + dot(d_raw, w_kv[...], NT)
        hat, inv = norm_parts(x_ref[...].astype(F32))
        gain = gain_ref[0:1, :]
        d_part, d_gain = norm_back(d_one, hat, inv, gain)
        acc_in[...] += d_gain[None]
        dx_ref[...] = d_part.astype(BF16)
        acc[...] += dot((hat * (1.0 + gain)).astype(BF16), d_raw, TN)

    @pl.when(i == tiles + 1)
    def _():
        for half in range(2):
            for k in range(1, ring.chips):
                between(half, k).wait_send()
        line.arrived(count - 1)
        width = x_ref.shape[1]
        short = head * own_rows // width
        last_ref[:, : 2 * head] = acc[...].astype(BF16)
        d_query = out[pl.ds((count - 1) * chunk, 16), :head][0:1].astype(F32)
        pair = jnp.concatenate([d_query, acc_key[...], jnp.zeros((14, head), F32)], axis=0).astype(BF16)
        col = lax.broadcasted_iota(jnp.int32, (head, width), 1)
        row = lax.broadcasted_iota(jnp.int32, (head, width), 0)
        shift = short.bit_length() - 1
        spot = lax.shift_right_logical(row, shift) * own_rows + (row & (short - 1))
        spread = dot(pair, jnp.where(col == spot, 1.0, 0.0).astype(BF16))
        gains = jnp.concatenate(
            [acc_in[...], dg_mid_ref[...], dg_post_ref[...], spread[0:2], jnp.zeros((122, width), F32)], axis=0)
        last_ref[:, 2 * head :] = jnp.transpose(gains).astype(BF16)
        if scattered:
            late.send()
            line.finish()
            late.middle(last_out)
            late.final(last_out)
        else:
            last_out[...] = last_ref[...]
            line.finish()


def key_back(d_kv, hat, inv, cosine, sine, x, d_query, gains, gain_key, first, w_query, dg_query, dg_mid, dg_post,
             grad_qo, rest, own_rows, ident):
    rows, width = x.shape
    head = hat.shape[1]
    tile, chunk = 256, 128
    tiles = rows // tile
    count = rows // chunk + 1
    dma = pltpu.SemaphoreType.DMA((count,))

    def late(cols):
        return pl.BlockSpec((tile, cols), lambda i: (jnp.maximum(i - 2, 0), 0))

    def fixed(shape):
        return pl.BlockSpec(shape, lambda i: (0, 0))

    turns = cosine.shape[0] // tile
    turn = pl.BlockSpec((tile, head // 2), lambda i: (lax.rem(jnp.maximum(i - 2, 0), turns), 0))
    comm = pltpu.VMEM((count * chunk, 2 * head), BF16)
    scattered = own_rows % 16 == 0
    chips = width // (2 * own_rows)
    last = (width, 2 * head + 128)
    more = []
    if scattered:
        last_out, qo_out, kind = (own_rows, last[1]), (own_rows, 2 * head), F32
        for cols in (2 * head, last[1]):
            more += row_scatter_scratch(chips, own_rows, cols)
    else:
        last_out, qo_out, kind = last, grad_qo.shape, BF16
    return pl.pallas_call(
        functools.partial(key_back_kernel, tiles, tile, chunk, own_rows, scattered),
        grid=(tiles + 2,),
        out_shape=(
            jax.ShapeDtypeStruct((rows, width), BF16),
            jax.ShapeDtypeStruct(last_out, kind),
            jax.ShapeDtypeStruct(qo_out, kind),
        ),
        in_specs=[whole_block(d_kv.shape),
                  late(head), late(1), turn, turn, late(width),
                  pl.BlockSpec((tile, 4 * head), lambda i: (jnp.minimum(i, tiles - 1), 0)),
                  whole_block(gains.shape), whole_block(gain_key.shape), ANY]
        + [whole_block(a.shape) for a in (w_query, dg_query, dg_mid, dg_post, grad_qo, rest)],
        out_specs=(late(width), fixed(last_out), fixed(qo_out)),
        scratch_shapes=[
            pltpu.VMEM((width, 2 * head), F32), pltpu.VMEM((1, width), F32), pltpu.VMEM((1, head), F32),
            pltpu.VMEM((width, 2 * head), BF16), pltpu.SemaphoreType.DMA, pltpu.VMEM(last, BF16),
            pltpu.VMEM((rows, width), F32), pltpu.VMEM(rest.shape, BF16)]
        + [pltpu.SemaphoreType.DMA((2, rest.shape[1] + 1))] * 2 + [comm] * 4 + [dma] * 7
        + [pltpu.SemaphoreType.REGULAR] * 2 + more,
        compiler_params=pltpu.CompilerParams(
            collective_id=ident, has_side_effects=True, vmem_limit_bytes=56 * 2**20),
        cost_estimate=cost(75),
        name="key_back",
    )(d_kv, hat, inv, cosine, sine, x, d_query, gains, gain_key, first, w_query, dg_query, dg_mid, dg_post, grad_qo, rest)


def shards(tokens, segments, cotangent, w_query, w_key, w_value, w_out, w_gate, w_up, w_down,
           g_input, g_post_attn, g_pre_ffn, g_post_ffn, g_query, g_key):
    batches, seq_local, _, size, width = tokens.shape
    head = w_key.shape[1]
    groups = batches * seq_local
    per_group = 2 * size
    rows = groups * per_group
    ctx = lax.axis_size("ctx")
    length = per_group * ctx
    rank = lax.axis_index("ctx")
    shared = ("dp", "ctx")
    own_rows = g_input.shape[0]
    hidden = w_gate.shape[1]

    def column(gain):
        return jnp.pad(gain, (0, own_rows - gain.shape[0]))[:, None]

    own_ids = segments.reshape(groups, 2, size)
    id_rows = own_ids.size // 128
    ids = jnp.pad(own_ids.reshape(id_rows, 128), ((0, -id_rows % 16), (0, 0)))
    extra = jnp.concatenate(
        [column(g) for g in (g_input, g_post_attn, g_pre_ffn, g_post_ffn, g_query, g_key)], axis=1)
    extra = jnp.pad(extra, ((0, 0), (0, 128 - extra.shape[1])))

    def rows_of_16(w):
        return jnp.pad(w, ((0, -own_rows % 16), (0, 0)))

    first, line_query, line_out, ids = first_gather(
        rows_of_16(jnp.concatenate([w_query, w_key, w_value, extra], axis=1)),
        rows_of_16(w_query), rows_of_16(w_out.T), ids, width // own_rows, 5)
    first = first[:, :own_rows].reshape(width, -1)
    side = first[:, 3 * head :]
    gain_cols = side[:, :8].astype(F32)
    gain_rows = gain_cols.T
    gain_input = gain_rows[0]
    short = g_query.shape[0]
    gain_query, gain_key = (
        gain_cols[:, i].reshape(-1, own_rows)[:, :short].reshape(-1) for i in (4, 5))

    wide = wide_of(hidden)
    second = jnp.concatenate(
        [line_out[:own_rows]] + [jnp.pad(w, ((0, 0), (0, wide - hidden))) for w in (w_gate, w_up, w_down.T)], axis=1)
    weights = lax.all_gather(second, shared, axis=0, tiled=True)

    offsets = rank * size + jnp.arange(size, dtype=jnp.int32)
    position = jnp.concatenate([offsets, length - 1 - offsets]).astype(F32)
    cosine, sine = angles(position, head // 2, head)

    x_rows = tokens.reshape(rows, width)
    dy_rows = cotangent.reshape(rows, width)
    queries, q_hat, q_scale, k_hat, k_scale, heads_own, log_mass, kv, heads_all = attention(
        x_rows, first, gain_rows, gain_query[None], gain_key[None], cosine, sine, own_ids[..., None], ids, length, 0)

    line_query, heads_all = lax.optimization_barrier((line_query[:own_rows], heads_all))
    query_full = lax.all_gather(line_query, shared, axis=0, tiled=True)
    attn, hidden_two, gate, up, ffn_out = ffn_forward(x_rows, heads_all, gain_rows, weights, hidden, 1)
    ffn_out, query_full = lax.optimization_barrier((ffn_out, query_full))
    d_gain_post_ffn, grad_ffn, d_two = ffn_backward(
        dy_rows, ffn_out, hidden_two, gate, up, gain_rows, weights, 2)
    grad_ffn = lax.psum_scatter(grad_ffn, shared, scatter_dimension=1, tiled=True)
    output, d_middle, d_heads, delta, d_gain_mid, grad_out_t = middle_back(
        x_rows, attn, dy_rows, d_two, ffn_out, heads_own, gain_rows, weights)

    d_q_all, d_kv, rest, d_gain_query, grad_qo = attention_back(
        queries, d_heads, log_mass, delta, own_ids[:, :, None, :], ids, q_hat, q_scale, cosine, sine, x_rows, gain_rows,
        gain_query[None], grad_out_t, kv, 4)
    d_part, last, grad_qo = key_back(
        d_kv, k_hat, k_scale, cosine, sine, x_rows, d_q_all, gain_rows, gain_key[None],
        first, query_full, d_gain_query, d_gain_mid, d_gain_post_ffn, grad_qo, rest, own_rows, 3)
    d_tokens = d_middle.astype(F32) + d_part.astype(F32)
    if own_rows % 16:
        last = lax.psum_scatter(last, shared, scatter_dimension=0, tiled=True).astype(F32)
        grad_qo = lax.psum_scatter(grad_qo, shared, scatter_dimension=0, tiled=True).astype(F32)
    g = last[:, 2 * head :]
    return (
        output.reshape(tokens.shape),
        d_tokens.reshape(tokens.shape),
        grad_qo[:, :head],
        last[:, :head],
        last[:, head : 2 * head],
        grad_qo[:, head:].T,
        grad_ffn[0].astype(F32),
        grad_ffn[1].astype(F32),
        grad_ffn[2].astype(F32).T,
        g[:, 0],
        g[:, 1],
        g[:, 2],
        g[:, 3],
        g[:short, 4],
        g[:short, 5],
    )


def solution(mesh):
    shared = ("dp", "ctx")
    rows = P(None, "dp", None, "ctx", None)
    weights = (
        P(shared, "tp"), P(shared, None), P(shared, None), P("tp", shared),
        P(shared, "tp"), P(shared, "tp"), P("tp", shared),
    )
    gains = (P(shared),) * 6
    return jax.shard_map(
        shards,
        mesh=mesh,
        in_specs=(rows, P(None, "dp", None, "ctx"), rows) + weights + gains,
        out_specs=(rows, rows) + weights + gains,
        check_vma=False,
    )
```

```python
import functools

import jax
import jax.numpy as jnp
from jax import lax
from jax.experimental import pallas as pl
from jax.experimental.pallas import tpu as pltpu
from jax.sharding import PartitionSpec as P

EPS = 1e-06
THETA = 1000000.0
SCALE = 0.0625
NEGATIVE = -1e30
BF16 = jnp.bfloat16
F32 = jnp.float32
MESH = pl.DeviceIdType.MESH
NN = (((1,), (0,)), ((), ()))
NT = (((1,), (1,)), ((), ()))
TN = (((0,), (0,)), ((), ()))


def dot(a, b, dims=NN):
    return lax.dot_general(a, b, dims, preferred_element_type=F32)


def cost(us):
    return pl.CostEstimate(flops=int(us * 1.1e9), bytes_accessed=0, transcendentals=0)


def barrier_line(z):
    bar = pltpu.get_barrier_semaphore()

    @pl.when(z > 0)
    def _():
        pl.semaphore_signal(bar, inc=1, device_id={"tp": z - 1}, device_id_type=MESH)

    @pl.when(z < 3)
    def _():
        pl.semaphore_signal(bar, inc=1, device_id={"tp": z + 1}, device_id_type=MESH)

    pl.semaphore_wait(bar, jnp.where((z == 0) | (z == 3), 1, 2))


def block_starts(half, t, blocks, rank):
    if half == 0:
        return t
    return jnp.where(t < blocks, t, t + rank + 1)


def angles(position, half_size, full_size):
    frequency = THETA ** (-2.0 * jnp.arange(half_size, dtype=F32) / full_size)
    turned = position[:, None] * frequency[None, :]
    return (jnp.cos(turned), jnp.sin(turned))


def rotate(tensor, cosine, sine):
    half_size = tensor.shape[-1] // 2
    a = tensor[..., :half_size]
    b = tensor[..., half_size:]
    return jnp.concatenate([a * cosine - b * sine, b * cosine + a * sine], axis=-1)


def norm_parts(values):
    inv = lax.rsqrt(jnp.mean(values * values, axis=-1, keepdims=True) + EPS)
    return (values * inv, inv)


def norm_back(upstream, normalized, inv, gain):
    d_norm = upstream * (1.0 + gain)
    d_values = inv * (d_norm - normalized * jnp.mean(d_norm * normalized, axis=-1, keepdims=True))
    return (d_values, jnp.sum(upstream * normalized, axis=0))


def gelu_tanh(values):
    return jax.nn.gelu(values, approximate=True)


class LineSum:
    def __init__(self, count, chunk, slots, own, near, far, out, sems):
        self.count, self.chunk, self.slots = count, chunk, slots
        self.own, self.near, self.far, self.out = own, near, far, out
        self.sems = sems
        self.z = z = lax.axis_index("tp")
        self.hub = (z == 1) | (z == 2)
        self.leaf = (z == 0) | (z == 3)
        self.other_hub = jnp.where(z == 1, 2, 1)
        self.my_hub = jnp.where(z == 0, 1, 2)
        self.my_leaf = jnp.where(z == 1, 0, 3)

    def slot(self, c):
        return pl.ds(pl.multiple_of(lax.rem(c, self.slots) * self.chunk, self.chunk), self.chunk)

    def rows(self, c):
        return pl.ds(pl.multiple_of(c * self.chunk, self.chunk), self.chunk)

    def inwards(self, c):
        return pltpu.make_async_remote_copy(
            self.own.at[self.slot(c)], self.near.at[self.slot(c)], self.sems[0].at[c], self.sems[1].at[c],
            device_id={"tp": self.my_hub}, device_id_type=MESH)

    def across(self, c):
        return pltpu.make_async_remote_copy(
            self.own.at[self.slot(c)], self.far.at[self.slot(c)], self.sems[2].at[c], self.sems[3].at[c],
            device_id={"tp": self.other_hub}, device_id_type=MESH)

    def outwards(self, c):
        return pltpu.make_async_remote_copy(
            self.far.at[self.slot(c)], self.out.at[self.rows(c)], self.sems[4].at[c], self.sems[5].at[c],
            device_id={"tp": self.my_leaf}, device_id_type=MESH)

    def store(self, c):
        return pltpu.make_async_copy(self.far.at[self.slot(c)], self.out.at[self.rows(c)], self.sems[6].at[c])

    def put(self, c, value):
        ring = self.slots < self.count
        if ring:
            @pl.when(c >= self.slots)
            def _():
                @pl.when(self.leaf)
                def _():
                    self.inwards(c - self.slots).wait_send()

                @pl.when(self.hub)
                def _():
                    self.across(c - self.slots).wait_send()

        self.own[self.slot(c), :] = value

        @pl.when(self.leaf)
        def _():
            if ring:
                @pl.when(c >= self.slots)
                def _():
                    pl.semaphore_wait(self.sems[7], 1)
            self.inwards(c).start()

    def pair(self, c):
        ring = self.slots < self.count

        @pl.when(self.hub)
        def _():
            self.inwards(c).wait_recv()
            at = self.slot(c)
            self.own[at, :] = (self.own[at, :].astype(F32) + self.near[at, :].astype(F32)).astype(BF16)
            if ring:
                @pl.when(c < self.count - self.slots)
                def _():
                    pl.semaphore_signal(self.sems[7], inc=1, device_id={"tp": self.my_leaf}, device_id_type=MESH)

                @pl.when(c >= self.slots)
                def _():
                    pl.semaphore_wait(self.sems[8], 1)
            self.across(c).start()

    def total(self, c):
        @pl.when(self.hub)
        def _():
            self.across(c).wait_recv()
            at = self.slot(c)
            self.far[at, :] = (self.own[at, :].astype(F32) + self.far[at, :].astype(F32)).astype(BF16)
            self.outwards(c).start()
            self.store(c).start()

    def retire(self, c):
        @pl.when(self.hub)
        def _():
            self.outwards(c).wait_send()
            self.store(c).wait()
            if self.slots < self.count:
                @pl.when(c < self.count - self.slots)
                def _():
                    pl.semaphore_signal(self.sems[8], inc=1, device_id={"tp": self.other_hub}, device_id_type=MESH)

    def finish(self):
        first = max(0, self.count - self.slots)

        @pl.when(self.leaf)
        def _():
            for c in range(self.count):
                self.outwards(c).wait_recv()
            for c in range(first, self.count):
                self.inwards(c).wait_send()

        @pl.when(self.hub)
        def _():
            for c in range(first, self.count):
                self.across(c).wait_send()


def line_sum_scratch(count, chunk, slots, cols):
    dma = pltpu.SemaphoreType.DMA((count,))
    regular = pltpu.SemaphoreType.REGULAR
    return [pltpu.VMEM((slots * chunk, cols), BF16)] * 3 + [dma] * 7 + [regular] * 2


def gelu_parts(v):
    c = 0.7978845608028654
    square = v * v
    t = jnp.tanh(v * (c + (c * 0.044715) * square))
    half = 0.5 + 0.5 * t
    value = v * half
    slope = half + (0.5 * v) * (1.0 - t * t) * (c + (3.0 * c * 0.044715) * square)
    return value, slope


def column_parts(cols, step):
    return [(a, min(a + step, cols)) for a in range(0, cols, step)]


def middle_of(x, attn, gain_post_attn):
    hat, inv = norm_parts(attn.astype(F32))
    return x.astype(F32) + hat * (1.0 + gain_post_attn), hat, inv


def load_ffn_weights(weights, refs, sem):
    wide = refs[0].shape[1]
    base = weights.shape[1] - 3 * wide
    return [
        pltpu.make_async_copy(weights.at[:, pl.ds(base + j * wide, wide)], ref, sem.at[j])
        for j, ref in enumerate(refs)
    ]


def ffn_forward_kernel(tiles, tile, chunk, hidden, x_ref, h_ref, gain_ref, w_ref,
                       attn_ref, two_ref, gate_ref, up_ref, out_ref, wo_ref, wg_ref, wu_ref, wd_ref, w_sem, own, near, far, *sems):
    i = pl.program_id(0)
    per = tile // chunk
    line = LineSum(tiles * per, chunk, tiles * per, own, near, far, out_ref, sems)
    head = wo_ref.shape[1] // 4

    copies = [pltpu.make_async_copy(w_ref.at[:, pl.ds(0, 4 * head)], wo_ref, w_sem.at[3])]
    copies += load_ffn_weights(w_ref, (wg_ref, wu_ref, wd_ref), w_sem)

    @pl.when(i == 0)
    def _():
        for copy in copies:
            copy.start()
        barrier_line(line.z)
        copies[0].wait()

    attn = dot(h_ref[...], wo_ref[...], NT).astype(BF16)
    attn_ref[...] = attn
    middle, _, _ = middle_of(x_ref[...], attn, gain_ref[1:2, :])
    hat, _ = norm_parts(middle)
    two = (hat * (1.0 + gain_ref[2:3, :])).astype(BF16)
    two_ref[...] = two
    part = None

    @pl.when(i == 0)
    def _():
        for copy in copies[1:]:
            copy.wait()

    for a, b in column_parts(hidden, 896):
        gate = dot(two, wg_ref[:, a:b])
        up = dot(two, wu_ref[:, a:b])
        gate_ref[:, a:b] = gate.astype(BF16)
        up_ref[:, a:b] = up.astype(BF16)
        value, _ = gelu_parts(gate)
        more = dot((value * up).astype(BF16), wd_ref[:, a:b], NT)
        part = more if part is None else part + more
    for j in range(per):
        line.put(i * per + j, part[j * chunk : (j + 1) * chunk].astype(BF16))

    @pl.when(i >= 1)
    def _():
        for j in range(per):
            line.pair((i - 1) * per + j)

    @pl.when(i >= 2)
    def _():
        for j in range(per):
            line.total((i - 2) * per + j)

    @pl.when(i == tiles - 1)
    def _():
        last = tiles * per
        for c in range(max(0, last - 2 * per), last - per):
            line.total(c)
        for c in range(last - per, last):
            line.pair(c)
        for c in range(last - per, last):
            line.total(c)
        for c in range(last):
            line.retire(c)
        line.finish()


def whole_block(shape):
    return pl.BlockSpec(shape, lambda i: (0,) * len(shape), pipeline_mode=pl.Buffered(1))


def tile_block(tile, cols):
    return pl.BlockSpec((tile, cols), lambda i: (i, 0))


ANY = pl.BlockSpec(memory_space=pl.ANY)


def wide_of(hidden):
    return -(-hidden // 128) * 128


def ffn_forward(x, heads, gains, weights, hidden, ident):
    rows, width = x.shape
    all_heads = heads.shape[1]
    tile, chunk = 128, 128
    tiles = rows // tile
    count = rows // chunk
    wide = wide_of(hidden)
    return pl.pallas_call(
        functools.partial(ffn_forward_kernel, tiles, tile, chunk, hidden),
        grid=(tiles,),
        out_shape=(
            jax.ShapeDtypeStruct((rows, width), BF16),
            jax.ShapeDtypeStruct((rows, width), BF16),
            jax.ShapeDtypeStruct((rows, hidden), BF16),
            jax.ShapeDtypeStruct((rows, hidden), BF16),
            jax.ShapeDtypeStruct((rows, width), BF16),
        ),
        in_specs=[
            tile_block(tile, width),
            tile_block(tile, all_heads),
            whole_block(gains.shape),
            ANY,
        ],
        out_specs=(tile_block(tile, width), tile_block(tile, width), tile_block(tile, hidden), tile_block(tile, hidden), ANY),
        scratch_shapes=[pltpu.VMEM((width, all_heads), BF16)] + [pltpu.VMEM((width, wide), BF16)] * 3
        + [pltpu.SemaphoreType.DMA((4,))]
        + line_sum_scratch(count, chunk, count, width),
        compiler_params=pltpu.CompilerParams(
            collective_id=ident, has_side_effects=True, vmem_limit_bytes=60 * 2**20),
        cost_estimate=cost(140),
        name="ffn_forward",
    )(x, heads, gains, weights)


def ffn_backward_kernel(tiles, tile, chunk, slots, hidden, dy_ref, ffn_ref, two_ref, gate_ref, up_ref,
                        gain_ref, w_ref,
                        dgain_ref, grad_ref, out_ref, wg_ref, wu_ref, wd_ref, w_sem,
                        acc_g, acc_u, acc_d, keep_g, keep_u, keep_h, stage, stage_sem, own, near, far, *sems):
    i = pl.program_id(0)
    per = tile // chunk
    last = tiles * per
    line = LineSum(last, chunk, slots, own, near, far, out_ref, sems)

    copies = load_ffn_weights(w_ref, (wg_ref, wu_ref, wd_ref), w_sem)

    @pl.when(i == 0)
    def _():
        for copy in copies[::-1]:
            copy.start()
        barrier_line(line.z)
        dgain_ref[...] = jnp.zeros_like(dgain_ref)
        for copy in copies[::-1]:
            copy.wait()

    hat, inv = norm_parts(ffn_ref[...].astype(F32))
    gain = gain_ref[3:4, :]
    d_ffn, d_gain = norm_back(dy_ref[...].astype(F32), hat, inv, gain)
    dgain_ref[...] += d_gain[None]
    d_ffn = d_ffn.astype(BF16)
    part = None

    def handle(j):
        @pl.when(i >= 1)
        def _():
            line.pair((i - 1) * per + j)

        @pl.when(i >= 2)
        def _():
            line.total((i - 2) * per + j)

    for a, b in column_parts(hidden, 512):
        d_hidden = dot(d_ffn, wd_ref[:, a:b])
        up = up_ref[:, a:b].astype(F32)
        value, slope = gelu_parts(gate_ref[:, a:b].astype(F32))
        keep_h[:, a:b] = (value * up).astype(BF16)
        d_gate = (d_hidden * up * slope).astype(BF16)
        d_up = (d_hidden * value).astype(BF16)
        keep_g[:, a:b] = d_gate
        keep_u[:, a:b] = d_up
        more = dot(d_gate, wg_ref[:, a:b], NT) + dot(d_up, wu_ref[:, a:b], NT)
        part = more if part is None else part + more
        if a == 0:
            handle(0)
    for j in range(per):
        line.put(i * per + j, part[j * chunk : (j + 1) * chunk].astype(BF16))

    @pl.when(i == 0)
    def _():
        for acc in (acc_g, acc_u, acc_d):
            acc[...] = jnp.zeros_like(acc)

    acc_g[...] += dot(two_ref[...], keep_g[...], TN)
    acc_u[...] += dot(two_ref[...], keep_u[...], TN)
    for j in range(1, per):
        handle(j)
    acc_d[...] += dot(d_ffn, keep_h[...], TN)

    @pl.when(i >= 3)
    def _():
        for j in range(per):
            line.retire((i - 3) * per + j)

    @pl.when(i == tiles - 1)
    def _():
        step = stage.shape[1]
        count = acc_g.shape[0] // step

        def write(acc, out):
            def pieces(k, _):
                at = lax.rem(k, 2)
                rows = pl.ds(pl.multiple_of(k * step, step), step)

                @pl.when(k >= 2)
                def _():
                    pltpu.make_async_copy(stage.at[at], out.at[pl.ds(0, step)], stage_sem.at[at]).wait()
                stage[at] = acc[rows, :].astype(BF16)
                pltpu.make_async_copy(stage.at[at], out.at[rows], stage_sem.at[at]).start()
                return 0

            lax.fori_loop(0, count, pieces, 0)
            for at in range(2):
                pltpu.make_async_copy(stage.at[at], out.at[pl.ds(0, step)], stage_sem.at[at]).wait()

        for c in range(max(0, last - 2 * per), last - per):
            line.total(c)
        write(acc_g, grad_ref.at[0])
        line.pair(last - per)
        write(acc_u, grad_ref.at[1])
        for c in range(last - per + 1, last):
            line.pair(c)
            line.total(c - 1)
        write(acc_d, grad_ref.at[2])
        line.total(last - 1)
        for c in range(max(0, last - 3 * per), last):
            line.retire(c)
        line.finish()


def ffn_backward(dy, ffn, two, gate, up, gains, weights, ident):
    rows, width = dy.shape
    hidden = gate.shape[1]
    wide = wide_of(hidden)
    tile, chunk = 256, 128
    tiles = rows // tile
    count = rows // chunk
    slots = min(count, 6)
    step = 144
    acc = pltpu.VMEM((width, hidden), F32)
    keep = pltpu.VMEM((tile, hidden), BF16)
    return pl.pallas_call(
        functools.partial(ffn_backward_kernel, tiles, tile, chunk, slots, hidden),
        grid=(tiles,),
        out_shape=(
            jax.ShapeDtypeStruct((1, width), F32),
            jax.ShapeDtypeStruct((3, width, hidden), BF16),
            jax.ShapeDtypeStruct((rows, width), BF16),
        ),
        in_specs=[tile_block(tile, width)] * 3 + [tile_block(tile, hidden)] * 2
        + [whole_block(gains.shape), ANY],
        out_specs=(pl.BlockSpec((1, width), lambda i: (0, 0)), ANY, ANY),
        scratch_shapes=[pltpu.VMEM((width, wide), BF16)] * 3 + [pltpu.SemaphoreType.DMA((3,))] + [acc] * 3 + [keep] * 3
        + [pltpu.VMEM((2, step, hidden), BF16), pltpu.SemaphoreType.DMA((2,))]
        + line_sum_scratch(count, chunk, slots, width),
        compiler_params=pltpu.CompilerParams(
            collective_id=ident, has_side_effects=True, vmem_limit_bytes=63 * 2**20),
        cost_estimate=cost(145),
        name="ffn_backward",
    )(dy, ffn, two, gate, up, gains, weights)


def middle_back_kernel(x_ref, attn_ref, dy_ref, d2_ref, ffn_ref, h_ref, gain_ref, w_ref,
                       y_ref, dm_ref, dh_ref, delta_ref, dgain_ref, go_ref, acc, wo_ref, w_sem):
    i = pl.program_id(0)

    @pl.when(i == 0)
    def _():
        head = wo_ref.shape[1]
        at = pl.multiple_of(lax.axis_index("tp") * head, head)
        copy = pltpu.make_async_copy(w_ref.at[:, pl.ds(at, head)], wo_ref, w_sem)
        copy.start()
        copy.wait()
        acc[...] = jnp.zeros_like(acc)
        dgain_ref[...] = jnp.zeros_like(dgain_ref)

    middle, attn_hat, attn_inv = middle_of(x_ref[...], attn_ref[...], gain_ref[1:2, :])
    hat, _ = norm_parts(ffn_ref[...].astype(F32))
    y_ref[...] = (middle + hat * (1.0 + gain_ref[3:4, :])).astype(BF16)
    hat, inv = norm_parts(middle)
    d_part, d_gain = norm_back(d2_ref[...].astype(F32), hat, inv, gain_ref[2:3, :])
    dgain_ref[1:2, :] += d_gain[None]
    d_middle = dy_ref[...].astype(F32) + d_part
    dm_ref[...] = d_middle.astype(BF16)
    d_attn, d_gain = norm_back(d_middle, attn_hat, attn_inv, gain_ref[1:2, :])
    dgain_ref[0:1, :] += d_gain[None]
    d_attn = d_attn.astype(BF16)
    d_heads = dot(d_attn, wo_ref[...]).astype(BF16)
    dh_ref[...] = d_heads
    heads = h_ref[...]
    delta_ref[...] = jnp.sum(d_heads.astype(F32) * heads.astype(F32), axis=1, keepdims=True)
    acc[...] += dot(d_attn, heads, TN)

    @pl.when(i == pl.num_programs(0) - 1)
    def _():
        go_ref[...] = acc[...].astype(BF16)


def middle_back(x, attn, dy, d_two, ffn, heads, gains, weights):
    rows, width = x.shape
    head = heads.shape[1]
    tile = 256
    return pl.pallas_call(
        middle_back_kernel,
        grid=(rows // tile,),
        out_shape=(
            jax.ShapeDtypeStruct((rows, width), BF16),
            jax.ShapeDtypeStruct((rows, width), BF16),
            jax.ShapeDtypeStruct((rows, head), BF16),
            jax.ShapeDtypeStruct((rows, 1), F32),
            jax.ShapeDtypeStruct((2, width), F32),
            jax.ShapeDtypeStruct((width, head), BF16),
        ),
        in_specs=[tile_block(tile, width)] * 5 + [tile_block(tile, head)] + [whole_block(gains.shape), ANY],
        out_specs=(
            tile_block(tile, width), tile_block(tile, width), tile_block(tile, head), tile_block(tile, 1),
            pl.BlockSpec((2, width), lambda i: (0, 0)), pl.BlockSpec((width, head), lambda i: (0, 0)),
        ),
        scratch_shapes=[pltpu.VMEM((width, head), F32), pltpu.VMEM((width, head), BF16), pltpu.SemaphoreType.DMA],
        compiler_params=pltpu.CompilerParams(vmem_limit_bytes=48 * 2**20),
        cost_estimate=cost(19),
        name="middle_back",
    )(x, attn, dy, d_two, ffn, heads, gains, weights)


class LineGather:
    def __init__(self, whole, tile, width, sems):
        self.whole, self.tile, self.width, self.sems = whole, tile, width, sems
        self.z = lax.axis_index("tp")

    def place(self, src, t):
        return self.whole.at[
            pl.ds(pl.multiple_of(t * self.tile, self.tile), self.tile),
            pl.ds(pl.multiple_of(src * self.width, self.width), self.width)]

    def send(self, src, t, hop, way):
        ss, rs = self.sems[:2] if way > 0 else self.sems[2:]
        place = self.place(src, t)
        return pltpu.make_async_remote_copy(
            place, place, ss.at[hop, t], rs.at[hop, t],
            device_id={"tp": self.z + way}, device_id_type=MESH)

    def going(self, hop, way):
        src = self.z - way * hop
        return src, (self.z + way >= 0) & (self.z + way <= 3) & (src >= 0) & (src <= 3)

    def coming(self, hop, way):
        src = self.z - way * (hop + 1)
        return src, (src >= 0) & (src <= 3)

    def forward(self, t, hop):
        for way in (1, -1):
            if hop > 0:
                self.wait(t, hop - 1, way)
            src, ok = self.going(hop, way)

            @pl.when(ok)
            def _():
                self.send(src, t, hop, way).start()

    def wait(self, t, hop, way):
        src, ok = self.coming(hop, way)

        @pl.when(ok)
        def _():
            self.send(src, t, hop, way).wait_recv()

    def arrived(self, t):
        for way in (1, -1):
            self.wait(t, 2, way)

    def finish(self, tiles):
        for hop in range(3):
            for way in (1, -1):
                src, ok = self.going(hop, way)

                @pl.when(ok)
                def _():
                    def one(t, _):
                        self.send(src, t, hop, way).wait_send()
                        return 0

                    lax.fori_loop(0, tiles, one, 0)


class KeyGather(LineGather):
    def __init__(self, block, chips, sems):
        self.block, self.chips, self.sems = block, chips, sems
        self.z = lax.axis_index("tp")

    def tile_of(self, g, half, k):
        return (2 * g + half) * (self.chips - 1) + k - 1

    def place(self, src, t):
        pair, k = divmod(t, self.chips - 1)
        return self.quarter(pair // 2, pair % 2, k + 1, src)

    def quarter(self, g, half, k, src, own=False):
        ref, start, size = self.block(g, half, k, own)
        rows = size // 4
        return ref.at[pl.ds(pl.multiple_of(start + src * rows, rows), rows)]

    def finish(self, tiles):
        for hop in range(3):
            for way in (1, -1):
                src, ok = self.going(hop, way)

                @pl.when(ok)
                def _():
                    for t in range(tiles):
                        self.send(src, t, hop, way).wait_send()


class Shared:
    def __init__(self, over_dp):
        self.ctx = ctx = lax.axis_size("ctx")
        me = lax.axis_index("ctx")
        self.devices = ctx
        if over_dp:
            me = me + lax.axis_index("dp") * ctx
            self.devices = ctx * lax.axis_size("dp")
        self.over_dp = over_dp
        self.me = me
        self.chips = self.devices // 2
        self.core = lax.rem(me, 2)
        self.chip = lax.div(me, 2)

    def ident(self, device):
        if self.over_dp:
            return {"dp": lax.div(device, self.ctx), "ctx": lax.rem(device, self.ctx)}
        return {"ctx": device}

    def other(self, k):
        return 2 * lax.rem(self.chip + k + self.chips, self.chips) + self.core

    def partner(self):
        return self.me + 1 - 2 * self.core

    def greet(self, z):
        bar = pltpu.get_barrier_semaphore()
        for device in [self.partner()] + [self.other(k) for k in range(1, self.chips)]:
            pl.semaphore_signal(bar, inc=1, device_id=self.ident(device), device_id_type=MESH)

        @pl.when(z > 0)
        def _():
            pl.semaphore_signal(bar, inc=1, device_id={"tp": z - 1}, device_id_type=MESH)

        @pl.when(z < 3)
        def _():
            pl.semaphore_signal(bar, inc=1, device_id={"tp": z + 1}, device_id_type=MESH)

        pl.semaphore_wait(bar, self.chips + jnp.where((z == 0) | (z == 3), 1, 2))

    def copy(self, source, target, send, recv, device):
        return pltpu.make_async_remote_copy(
            source, target, send, recv, device_id=self.ident(device), device_id_type=MESH)


def first_gather_kernel(a_ref, b_ref, c_ref, i_ref, all_ref, line_ref, more_ref, ids_ref, lsem, ss1, rs1, ss2, rs2, si1, ri1, si2, ri2, *sems):
    group = Shared(True)
    line = LineGather(line_ref, b_ref.shape[0], b_ref.shape[1], sems[:4])
    more = LineGather(more_ref, c_ref.shape[0], c_ref.shape[1], sems[4:])
    width = b_ref.shape[1]
    own = [
        pltpu.make_async_copy(b_ref, line_ref.at[:, pl.ds(pl.multiple_of(line.z * width, width), width)], lsem.at[0]),
        pltpu.make_async_copy(c_ref, more_ref.at[:, pl.ds(pl.multiple_of(line.z * width, width), width)], lsem.at[3]),
        pltpu.make_async_copy(a_ref, all_ref.at[group.me], lsem.at[1]),
        pltpu.make_async_copy(i_ref, ids_ref.at[group.me], lsem.at[2]),
    ]
    for copy in own:
        copy.start()
    group.greet(line.z)
    arrays = ((a_ref, all_ref, ss1, rs1, ss2, rs2), (i_ref, ids_ref, si1, ri1, si2, ri2))

    def direct(n, k, incoming=False):
        ref, whole, ss, rs = arrays[n][:4]
        at = whole.at[group.other(-k)] if incoming else whole.at[group.me]
        return group.copy(ref, at, ss.at[k], rs.at[k], group.other(k))

    def inner(n, k, incoming=False):
        ref, whole, _, _, ss, rs = arrays[n]
        at = whole.at[group.other(-k)]
        if incoming:
            at = whole.at[group.other(-k) + 1 - 2 * group.core]
        return group.copy(ref if k == 0 else at, at, ss.at[k], rs.at[k], group.partner())

    both = range(2)
    for k in range(1, group.chips):
        for n in both:
            direct(n, k).start()
    for n in both:
        inner(n, 0).start()
    own[0].wait()
    line.forward(0, 0)
    own[1].wait()
    more.forward(0, 0)
    for k in range(1, group.chips):
        if k < 3:
            line.forward(0, k)
            more.forward(0, k)
        for n in both:
            direct(n, k, True).wait_recv()
            inner(n, k).start()
    for hop in range(min(3, group.chips), 3):
        line.forward(0, hop)
        more.forward(0, hop)
    for k in range(group.chips):
        for n in both:
            inner(n, k, True).wait_recv()
    line.arrived(0)
    more.arrived(0)
    for copy in own[2:]:
        copy.wait()
    for n in both:
        for k in range(1, group.chips):
            direct(n, k).wait_send()
        for k in range(group.chips):
            inner(n, k).wait_send()
    line.finish(1)
    more.finish(1)


def first_gather(a, b, c, ids, devices, ident):
    dma = pltpu.SemaphoreType.DMA((devices // 2,))
    hop = pltpu.SemaphoreType.DMA((3, 1))
    return pl.pallas_call(
        first_gather_kernel,
        out_shape=(
            jax.ShapeDtypeStruct((devices,) + a.shape, a.dtype),
            jax.ShapeDtypeStruct((b.shape[0], 4 * b.shape[1]), b.dtype),
            jax.ShapeDtypeStruct((c.shape[0], 4 * c.shape[1]), c.dtype),
            jax.ShapeDtypeStruct((devices,) + ids.shape, ids.dtype),
        ),
        in_specs=[ANY] * 4,
        out_specs=(ANY,) * 4,
        scratch_shapes=[pltpu.SemaphoreType.DMA((4,))] + [dma] * 8 + [hop] * 8,
        compiler_params=pltpu.CompilerParams(collective_id=ident, has_side_effects=True),
        cost_estimate=cost(20),
        name="first_gather",
    )(a, b, c, ids)


def attention_kernel(groups, size, x_ref, w_ref, gain_ref, gq_ref, gk_ref, cos_ref, sin_ref, qs_ref, ks_ref,
                     q_ref, qhat_ref, qinv_ref, khat_ref, kinv_ref, heads_ref, log_ref, kv_out, all_out,
                     kv, whole, store_kv, store_all, ss1, rs1, ss2, rs2, *sems):
    head = q_ref.shape[1]
    length = kv.shape[1]
    id_rows = size // 128
    blocks = length // (2 * size)
    group = Shared(False)
    rank = group.me
    tile = min(256, size)
    per = size // tile
    line = LineGather(whole, tile, head, sems[:4])
    z = line.z
    group.greet(z)

    def block(g, half, k, own):
        c = rank if own else group.other(-k)
        return kv.at[g], half * (length // 2) + c * size, size

    keys = KeyGather(block, group.chips, sems[4:])

    def place(g, half, c):
        return kv.at[g, pl.ds(pl.multiple_of(half * (length // 2) + c * size, size), size)]

    def straight(t):
        return t == 2 * groups - 1

    def direct(g, half, k, incoming=False):
        at = keys.quarter(g, half, k, z, own=not incoming)
        if straight(2 * g + half):
            at = place(g, half, group.other(-k) if incoming else rank)
        return group.copy(at, at, ss1.at[g, half, k], rs1.at[g, half, k], group.other(k))

    def inner(g, half, k, incoming=False):
        block = group.other(-k)
        at = place(g, half, block + 1 - 2 * group.core if incoming else block)
        return group.copy(at, at, ss2.at[g, half, k], rs2.at[g, half, k], group.partner())

    def project(g, half, u):
        rows = pl.ds((2 * g + half) * size + u * tile, tile)
        spot = pl.ds(half * size + u * tile, tile)
        cosine, sine = cos_ref[spot, :], sin_ref[spot, :]
        hat, _ = norm_parts(x_ref[rows, :].astype(F32))
        raw = dot((hat * (1.0 + gain_ref[0:1, :])).astype(BF16), w_ref[:, : 3 * head])
        hat, inv = norm_parts(raw[:, :head])
        qhat_ref[rows, :] = hat
        qinv_ref[rows, :] = inv
        q_ref[rows, :] = rotate(hat * (1.0 + gq_ref[...]), cosine, sine).astype(BF16)
        hat, inv = norm_parts(raw[:, head : 2 * head])
        khat_ref[rows, :] = hat
        kinv_ref[rows, :] = inv
        at = pl.ds(pl.multiple_of(half * (length // 2) + rank * size + u * tile, tile), tile)
        kv[g, at, :head] = rotate(hat * (1.0 + gk_ref[...]), cosine, sine).astype(BF16)
        kv[g, at, head:] = raw[:, 2 * head :].astype(BF16)

    def attend(g, half):
        row = lax.broadcasted_iota(jnp.int32, (size, size), 0)
        col = lax.broadcasted_iota(jnp.int32, (size, size), 1)
        rows = pl.ds((2 * g + half) * size, size)
        q = q_ref[rows, :] * jnp.asarray(SCALE, BF16)
        qseg = qs_ref[g, half]

        def part(block):
            at = pl.ds(pl.multiple_of(block * size, size), size)
            device = lax.axis_index("dp") * lax.axis_size("ctx") + lax.rem(block, blocks)
            ids = ks_ref[device, pl.ds((2 * g + lax.div(block, blocks)) * id_rows, id_rows), :]
            ids = jnp.concatenate([ids[j : j + 1] for j in range(id_rows)], axis=1)
            same = qseg == jnp.where(ids == 0, -1, ids)
            return dot(q, kv[g, at, :head], NT), kv[g, at, head:], same

        s, v, same = part(rank + half * blocks)
        order = (col <= row) if half == 0 else (col >= row)
        s = jnp.where((same & order) | (col == row), s, NEGATIVE)
        top = jnp.max(s, axis=1, keepdims=True)
        p = jnp.exp(s - top)
        mass = jnp.sum(p, axis=1, keepdims=True)
        acc = dot(p.astype(BF16), v)

        def step(t, carry):
            top, mass, acc = carry
            s, v, same = part(block_starts(half, t, blocks, rank))
            s = jnp.where(same, s, NEGATIVE)
            new = jnp.maximum(top, jnp.max(s, axis=1, keepdims=True))
            keep = jnp.exp(top - new)
            p = jnp.exp(s - new)
            mass = mass * keep + jnp.sum(p, axis=1, keepdims=True)
            return new, mass, acc * keep + dot(p.astype(BF16), v)

        count = rank if half == 0 else 2 * blocks - 1 - rank
        top, mass, acc = lax.fori_loop(0, count, step, (top, mass, acc))
        out = (acc / mass).astype(BF16)
        heads_ref[rows, :] = out
        whole[rows, pl.ds(pl.multiple_of(z * head, head), head)] = out
        log_ref[g, half] = top + jnp.log(mass)

    chips = range(1, group.chips)
    tiles = 2 * groups

    def stage(t, n):
        if not 0 <= t < tiles:
            return
        g, half = divmod(t, 2)
        for k in chips:
            spot = keys.tile_of(g, half, k)
            if n == 0:
                direct(g, half, k).start()
            elif straight(t):
                if n == 4:
                    direct(g, half, k, True).wait_recv()
                    inner(g, half, k).start()
            elif n == 4:
                keys.arrived(spot)
                inner(g, half, k).start()
            else:
                if n == 1:
                    direct(g, half, k, True).wait_recv()
                keys.forward(spot, n - 1)

    def exchange(t):
        for n in (4, 3, 2, 1):
            stage(t - n, n)

    def hops(t):
        for hop in range(3):
            if 0 <= t - hop < tiles:
                for u in range(per):
                    line.forward((t - hop) * per + u, hop)

    def keep(t):
        at = pl.ds(t * tile, tile)
        return pltpu.make_async_copy(whole.at[at], all_out.at[at], store_all.at[t])

    def save(g):
        return pltpu.make_async_copy(kv.at[g], kv_out.at[g], store_kv.at[g])

    def landed(t):
        g, half = divmod(t, 2)
        for k in range(group.chips):
            inner(g, half, k, True).wait_recv()

    for t in range(tiles):
        g, half = divmod(t, 2)
        for u in range(per):
            project(g, half, u)
        stage(t, 0)
        inner(g, half, 0).start()
        exchange(t)
    for t in range(tiles):
        g, half = divmod(t, 2)
        exchange(tiles + t)
        landed(t)
        attend(g, half)
        hops(t)
    for g in range(groups):
        save(g).start()
    for t in range(tiles, tiles + 2):
        hops(t)
    for t in range(tiles * per):
        line.arrived(t)
        keep(t).start()
    for g in range(groups):
        save(g).wait()
        for half in range(2):
            for k in chips:
                direct(g, half, k).wait_send()
            for k in range(group.chips):
                inner(g, half, k).wait_send()
    line.finish(tiles * per)
    keys.finish((tiles - 1) * (group.chips - 1))
    for t in range(tiles * per):
        keep(t).wait()


def attention(x, w, gains, gain_query, gain_key, cosine, sine, qseg, ids, length, ident):
    rows, width = x.shape
    groups, _, size, _ = qseg.shape
    head = gain_query.shape[1]
    chips = length // (4 * size)
    tiles = 2 * groups
    parts = rows // min(256, size)
    vmem = pl.BlockSpec(memory_space=pltpu.VMEM)
    dma = pltpu.SemaphoreType.DMA
    return pl.pallas_call(
        functools.partial(attention_kernel, groups, size),
        out_shape=(
            jax.ShapeDtypeStruct((rows, head), BF16),
            jax.ShapeDtypeStruct((rows, head), F32),
            jax.ShapeDtypeStruct((rows, 1), F32),
            jax.ShapeDtypeStruct((rows, head), F32),
            jax.ShapeDtypeStruct((rows, 1), F32),
            jax.ShapeDtypeStruct((rows, head), BF16),
            jax.ShapeDtypeStruct((groups, 2, size, 1), F32),
            jax.ShapeDtypeStruct((groups, length, 2 * head), BF16),
            jax.ShapeDtypeStruct((rows, 4 * head), BF16),
        ),
        in_specs=[vmem] * 9,
        out_specs=(vmem,) * 7 + (ANY, ANY),
        scratch_shapes=[
            pltpu.VMEM((groups, length, 2 * head), BF16), pltpu.VMEM((rows, 4 * head), BF16),
            dma((groups,)), dma((parts,))] + [dma((groups, 2, chips))] * 4 + [dma((3, parts))] * 4
        + [dma((3, tiles * (chips - 1)))] * 4,
        compiler_params=pltpu.CompilerParams(
            collective_id=ident, has_side_effects=True, vmem_limit_bytes=60 * 2**20),
        cost_estimate=cost(110),
        name="attention",
    )(x, w, gains, gain_query, gain_key, cosine, sine, qseg, ids)


class ResidentSum(LineSum):
    def outwards(self, c):
        return pltpu.make_async_remote_copy(
            self.out.at[self.rows(c)], self.out.at[self.rows(c)], self.sems[4].at[c], self.sems[5].at[c],
            device_id={"tp": self.my_leaf}, device_id_type=MESH)

    def total(self, c):
        @pl.when(self.hub)
        def _():
            self.across(c).wait_recv()
            at = self.rows(c)
            self.out[at, :] = (self.own[at, :].astype(F32) + self.far[at, :].astype(F32)).astype(BF16)
            self.outwards(c).start()

    def arrived(self, c):
        @pl.when(self.leaf)
        def _():
            self.outwards(c).wait_recv()

    def finish(self):
        @pl.when(self.leaf)
        def _():
            for c in range(self.count):
                self.inwards(c).wait_send()

        @pl.when(self.hub)
        def _():
            for c in range(self.count):
                self.across(c).wait_send()
                self.outwards(c).wait_send()


def turned(column, size):
    return jnp.transpose(jnp.broadcast_to(column, (size, 128)))[0:1, :]


def attention_back_kernel(groups, size, q_ref, do_ref, log_ref, delta_ref, qs_ref, ids_ref, hat_ref, inv_ref, cos_ref, sin_ref,
                          x_ref, gain_ref, gq_ref, go_ref, kv_hbm, all_out, dkv_ref, rest_ref, dgain_ref, grad_ref,
                          kv, dk, dv, part, near, pair, far, whole, acc, load, store, ss1, rs1, ss2, rs2, *sems):
    head = q_ref.shape[1]
    length = kv.shape[1]
    blocks = length // (2 * size)
    id_rows = size // 128
    tiles = 2 * groups
    group = Shared(False)
    rank, core = group.me, group.core
    tile = min(256, size)
    per = size // tile
    line = LineGather(whole, tile, head, sems)
    z = line.z
    others = range(1, group.chips)
    order = list(others) + [0]

    def fetch(g):
        return pltpu.make_async_copy(kv_hbm.at[g], kv.at[g], load.at[g])

    for g in range(groups):
        fetch(g).start()
    group.greet(z)
    acc[...] = jnp.zeros_like(acc)
    dgain_ref[...] = jnp.zeros_like(dgain_ref)

    def rows_of(half, device):
        return pl.ds(pl.multiple_of(half * (length // 2) + device * size, size), size)

    def within(g, half, k):
        to = group.other(k) + 1 - 2 * core
        return group.copy(
            part.at[g, rows_of(half, to)], near.at[g, half, k], ss1.at[g, half, k], rs1.at[g, half, k], group.partner())

    def between(g, half, k):
        return group.copy(
            pair.at[g, half, k - 1], far.at[g, half, k - 1], ss2.at[g, half, k], rs2.at[g, half, k], group.other(k))

    def both_cores(g):
        for half in range(2):
            for k in order:
                within(g, half, k).wait_recv()
                total = part[g, rows_of(half, group.other(k)), :].astype(F32) + near[g, half, k].astype(F32)
                if k > 0 and g == groups - 1:
                    rest_ref[half, k - 1] = total.astype(BF16)
                elif k > 0:
                    pair[g, half, k - 1] = total.astype(BF16)
                    between(g, half, k).start()
                else:
                    dkv_ref[pl.ds((2 * g + half) * size, size), :] = total.astype(BF16)

    def all_chips(g):
        for half in range(2):
            at = pl.ds((2 * g + half) * size, size)
            total = dkv_ref[at, :].astype(F32)
            for k in others:
                between(g, half, k).wait_recv()
                total = total + far[g, half, k - 1].astype(F32)
            dkv_ref[at, :] = total.astype(BF16)

    def hops(t):
        for hop in range(3):
            if 0 <= t - hop < tiles:
                for u in range(per):
                    line.forward((t - hop) * per + u, hop)

    def attend(g, half):
        row = lax.broadcasted_iota(jnp.int32, (size, size), 0)
        col = lax.broadcasted_iota(jnp.int32, (size, size), 1)
        own = pl.ds((2 * g + half) * size, size)
        q = q_ref[own, :] * jnp.asarray(SCALE, BF16)
        do = do_ref[own, :]
        qseg = qs_ref[g, half]
        log_mass = turned(log_ref[g, half], size)
        delta = turned(delta_ref[own, :], size)

        def step_of(block, mine):
            at = pl.ds(pl.multiple_of(block * size, size), size)
            k = kv[g, at, :head]
            v = kv[g, at, head:]
            device = lax.axis_index("dp") * lax.axis_size("ctx") + lax.rem(block, blocks)
            ids = ids_ref[device, pl.ds((2 * g + lax.div(block, blocks)) * id_rows, id_rows), :]
            ids = jnp.concatenate([ids[j : j + 1] for j in range(id_rows)], axis=1)
            ids = jnp.transpose(jnp.broadcast_to(jnp.where(ids == 0, -1, ids), (8, size)))[:, 0:1]
            allowed = ids == qseg
            if mine:
                ahead = (row <= col) if half == 0 else (row >= col)
                allowed = (allowed & ahead) | (col == row)
            s = jnp.where(allowed, dot(k, q, NT), NEGATIVE)
            p = jnp.exp(s - log_mass)
            ds = (p * (dot(v, do, NT) - delta)).astype(BF16)
            dv[at, :] += dot(p.astype(BF16), do)
            dk[at, :] += dot(ds, q)
            return dot(ds, k, TN)

        def step(t, dq):
            return dq + step_of(block_starts(half, t, blocks, rank), False)

        dq = step_of(rank + half * blocks, True)
        count = rank if half == 0 else 2 * blocks - 1 - rank
        dq = SCALE * lax.fori_loop(0, count, step, dq)
        spot = pl.ds(half * size, size)
        d_rot = rotate(dq, cos_ref[spot, :], -sin_ref[spot, :])
        d_raw, d_gain = norm_back(d_rot, hat_ref[own, :], inv_ref[own, :], gq_ref[...])
        dgain_ref[...] += d_gain[None]
        whole[own, pl.ds(pl.multiple_of(z * head, head), head)] = d_raw.astype(BF16)

    def weight_gradient(t):
        own = pl.ds(t * size, size)
        hat, _ = norm_parts(x_ref[own, :].astype(F32))
        one = (hat * (1.0 + gain_ref[0:1, :])).astype(BF16)
        acc[...] += dot(one, whole[own, pl.ds(pl.multiple_of(z * head, head), head)], TN)

    def keep(t):
        at = pl.ds(t * tile, tile)
        return pltpu.make_async_copy(whole.at[at], all_out.at[at], store.at[t])

    for g in range(groups):
        fetch(g).wait()
        dk[...] = jnp.zeros_like(dk)
        dv[...] = jnp.zeros_like(dv)
        for half in range(2):
            attend(g, half)
            hops(2 * g + half)
            if half == 0 and g > 0:
                both_cores(g - 1)
        part[g, :, :head] = dk[...].astype(BF16)
        part[g, :, head:] = dv[...].astype(BF16)
        for half in range(2):
            for k in order:
                within(g, half, k).start()
        for half in range(2):
            weight_gradient(2 * g + half)
        if g > 0:
            all_chips(g - 1)
    hops(tiles)
    both_cores(groups - 1)
    hops(tiles + 1)
    grad_ref[:, :head] = acc[...].astype(BF16)
    grad_ref[:, head:] = go_ref[...]
    for t in range(tiles * per):
        line.arrived(t)
        keep(t).start()
    for g in range(groups):
        for half in range(2):
            if g < groups - 1:
                for k in others:
                    between(g, half, k).wait_send()
            for k in order:
                within(g, half, k).wait_send()
    line.finish(tiles * per)
    for t in range(tiles * per):
        keep(t).wait()


def attention_back(q, d_heads, log_mass, delta, qseg, ids, hat, inv, cosine, sine, x, gains, gain_query, grad_o, kv, ident):
    rows, head = q.shape
    width = x.shape[1]
    groups, length, _ = kv.shape
    size = rows // (2 * groups)
    chips = length // (4 * size)
    parts = rows // min(256, size)
    vmem = pl.BlockSpec(memory_space=pltpu.VMEM)
    dma = pltpu.SemaphoreType.DMA
    return pl.pallas_call(
        functools.partial(attention_back_kernel, groups, size),
        out_shape=(
            jax.ShapeDtypeStruct((rows, 4 * head), BF16),
            jax.ShapeDtypeStruct((rows, 2 * head), BF16),
            jax.ShapeDtypeStruct((2, chips - 1, size, 2 * head), BF16),
            jax.ShapeDtypeStruct((1, head), F32),
            jax.ShapeDtypeStruct((width, 2 * head), BF16),
        ),
        in_specs=[vmem] * 14 + [ANY],
        out_specs=(ANY, vmem, vmem, vmem, vmem),
        scratch_shapes=[
            pltpu.VMEM((groups, length, 2 * head), BF16),
            pltpu.VMEM((length, head), F32), pltpu.VMEM((length, head), F32),
            pltpu.VMEM((groups, length, 2 * head), BF16),
            pltpu.VMEM((groups, 2, chips, size, 2 * head), BF16),
            pltpu.VMEM((groups, 2, chips - 1, size, 2 * head), BF16),
            pltpu.VMEM((groups, 2, chips - 1, size, 2 * head), BF16),
            pltpu.VMEM((rows, 4 * head), BF16),
            pltpu.VMEM((width, head), F32),
            dma((groups,)), dma((parts,))] + [dma((groups, 2, chips))] * 4 + [dma((3, parts))] * 4,
        compiler_params=pltpu.CompilerParams(
            collective_id=ident, has_side_effects=True, vmem_limit_bytes=63 * 2**20),
        cost_estimate=cost(80),
        name="attention_back",
    )(q, d_heads, log_mass, delta, qseg, ids, hat, inv, cosine, sine, x, gains, gain_query, grad_o, kv)


class RowScatter:
    def __init__(self, group, own_rows, source, near, pair, far, sems):
        self.group, self.own_rows, self.source = group, own_rows, source
        self.near, self.pair, self.far, self.sems = near, pair, far, sems
        self.others = list(range(1, group.chips))
        self.order = self.others + [0]

    def block(self, device):
        return pl.ds(pl.multiple_of(device * self.own_rows, 16), self.own_rows)

    def within(self, k):
        g = self.group
        return g.copy(self.source.at[self.block(g.other(k) + 1 - 2 * g.core)], self.near.at[k],
                      self.sems[0].at[k], self.sems[1].at[k], g.partner())

    def between(self, k):
        g = self.group
        return g.copy(self.pair.at[k], self.far.at[k], self.sems[2].at[k], self.sems[3].at[k], g.other(k))

    def send(self):
        for k in self.order:
            self.within(k).start()

    def middle(self, out):
        for k in self.order:
            self.within(k).wait_recv()
            both = self.source[self.block(self.group.other(k)), :].astype(F32) + self.near[k].astype(F32)
            if k > 0:
                self.pair[k] = both.astype(BF16)
                self.between(k).start()
            else:
                out[...] = both

    def final(self, out):
        for k in self.others:
            self.between(k).wait_recv()
            out[...] += self.far[k].astype(F32)
        for k in self.others:
            self.between(k).wait_send()
        for k in self.order:
            self.within(k).wait_send()


def row_scatter_scratch(chips, own_rows, cols):
    return [pltpu.VMEM((chips, own_rows, cols), BF16)] * 3 + [pltpu.SemaphoreType.DMA((chips,))] * 4


def key_back_kernel(tiles, tile, chunk, own_rows, scattered, dkv_ref, hat_ref, inv_ref, cos_ref, sin_ref, x_ref, dq_ref,
                    gain_ref, gk_ref, w_ref, wq_ref, dgq_ref, dg_mid_ref, dg_post_ref, qo_ref, rest_ref,
                    dx_ref, last_out, qo_out, acc, acc_in, acc_key, w_kv, w_sem, last_ref, part,
                    add, ss, rs, out, own, near, far, *sems):
    i = pl.program_id(0)
    head = hat_ref.shape[1]
    per = tile // chunk
    count = tiles * per + 1
    line = ResidentSum(count, chunk, count, own, near, far, out, sems[:9])
    group = Shared(True)
    ring = Shared(False)
    size = rest_ref.shape[2]
    first = tiles * per - 2 * size // chunk

    def between(half, k):
        return ring.copy(rest_ref.at[half, k - 1], add.at[half, k - 1], ss.at[half, k], rs.at[half, k], ring.other(k))

    if scattered:
        early = RowScatter(group, own_rows, qo_ref, *sems[9:12], sems[12:16])
        late = RowScatter(group, own_rows, last_ref, *sems[16:19], sems[19:23])

    @pl.when(i == 0)
    def _():
        copy = pltpu.make_async_copy(w_ref.at[:, pl.ds(head, 2 * head)], w_kv, w_sem)
        copy.start()
        if scattered:
            group.greet(line.z)
        else:
            ring.greet(line.z)
            qo_out[...] = qo_ref[...]
        for half in range(2):
            for k in range(1, ring.chips):
                between(half, k).start()
        if scattered:
            early.send()
        for ref in (acc, acc_in, acc_key):
            ref[...] = jnp.zeros_like(ref)
        copy.wait()
        line.put(count - 1, jnp.broadcast_to(
            jnp.concatenate([dgq_ref[...], dgq_ref[...]], axis=1).astype(BF16), (chunk, 2 * head)))

    def put_rows(c):
        return dkv_ref[pl.ds(pl.multiple_of(c * chunk, chunk), chunk), :]

    @pl.when(i == 0)
    def _():
        def ready(c, _):
            line.put(c, put_rows(c))
            return 0

        lax.fori_loop(0, first, ready, 0)

    for half in range(2):
        @pl.when(i == max(0, (first * chunk + half * size) // tile - 2))
        def _():
            for k in range(1, ring.chips):
                between(half, k).wait_recv()

            def ready(n, _):
                c = first + half * (size // chunk) + n
                total = put_rows(c).astype(F32)
                for k in range(1, ring.chips):
                    total = total + add[half, k - 1, pl.ds(pl.multiple_of(n * chunk, chunk), chunk), :].astype(F32)
                line.put(c, total.astype(BF16))
                return 0

            lax.fori_loop(0, size // chunk, ready, 0)

    @pl.when(i < tiles)
    def _():
        part[pl.ds(pl.multiple_of(i * tile, tile), tile), :] = dot(dq_ref[...], wq_ref[...], NT)

    def handle(j):
        @pl.when((i >= 1) & (i <= tiles))
        def _():
            line.total((i - 1) * per + j)

        @pl.when(i < tiles)
        def _():
            line.pair(i * per + j)

    for j in range(per // 2):
        handle(j)

    @pl.when(i == 1)
    def _():
        line.pair(count - 1)
        if scattered:
            early.middle(qo_out)

    @pl.when(i == 2)
    def _():
        line.total(count - 1)

    if scattered:
        @pl.when(i == tiles)
        def _():
            early.final(qo_out)

    @pl.when(i >= 2)
    def _():
        for j in range(per):
            line.arrived((i - 2) * per + j)
        d_kv = out[pl.ds(pl.multiple_of((i - 2) * tile, tile), tile), :]
        d_rot = rotate(d_kv[:, :head].astype(F32), cos_ref[...], -sin_ref[...])
        d_raw, d_gain = norm_back(d_rot, hat_ref[...], inv_ref[...], gk_ref[...])
        acc_key[...] += d_gain[None]
        d_raw = jnp.concatenate([d_raw.astype(BF16), d_kv[:, head:]], axis=1)
        d_one = part[pl.ds(pl.multiple_of((i - 2) * tile, tile), tile), :] + dot(d_raw, w_kv[...], NT)
        hat, inv = norm_parts(x_ref[...].astype(F32))
        gain = gain_ref[0:1, :]
        d_part, d_gain = norm_back(d_one, hat, inv, gain)
        acc_in[...] += d_gain[None]
        dx_ref[...] = d_part.astype(BF16)
        acc[...] += dot((hat * (1.0 + gain)).astype(BF16), d_raw, TN)

    for j in range(per // 2, per):
        handle(j)

    @pl.when(i == tiles + 1)
    def _():
        for half in range(2):
            for k in range(1, ring.chips):
                between(half, k).wait_send()
        line.arrived(count - 1)
        width = x_ref.shape[1]
        short = head * own_rows // width
        last_ref[:, : 2 * head] = acc[...].astype(BF16)
        d_query = out[pl.ds((count - 1) * chunk, 16), :head][0:1].astype(F32)
        pair = jnp.concatenate([d_query, acc_key[...], jnp.zeros((14, head), F32)], axis=0).astype(BF16)
        col = lax.broadcasted_iota(jnp.int32, (head, width), 1)
        row = lax.broadcasted_iota(jnp.int32, (head, width), 0)
        shift = short.bit_length() - 1
        spot = lax.shift_right_logical(row, shift) * own_rows + (row & (short - 1))
        spread = dot(pair, jnp.where(col == spot, 1.0, 0.0).astype(BF16))
        gains = jnp.concatenate(
            [acc_in[...], dg_mid_ref[...], dg_post_ref[...], spread[0:2], jnp.zeros((122, width), F32)], axis=0)
        last_ref[:, 2 * head :] = jnp.transpose(gains).astype(BF16)
        if scattered:
            late.send()
            line.finish()
            late.middle(last_out)
            late.final(last_out)
        else:
            last_out[...] = last_ref[...]
            line.finish()


def key_back(d_kv, hat, inv, cosine, sine, x, d_query, gains, gain_key, first, w_query, dg_query, dg_mid, dg_post,
             grad_qo, rest, own_rows, ident):
    rows, width = x.shape
    head = hat.shape[1]
    tile, chunk = 256, 64
    tiles = rows // tile
    count = rows // chunk + 1
    dma = pltpu.SemaphoreType.DMA((count,))

    def late(cols):
        return pl.BlockSpec((tile, cols), lambda i: (jnp.maximum(i - 2, 0), 0))

    def fixed(shape):
        return pl.BlockSpec(shape, lambda i: (0, 0))

    turns = cosine.shape[0] // tile
    turn = pl.BlockSpec((tile, head // 2), lambda i: (lax.rem(jnp.maximum(i - 2, 0), turns), 0))
    comm = pltpu.VMEM((count * chunk, 2 * head), BF16)
    scattered = own_rows % 16 == 0
    chips = width // (2 * own_rows)
    last = (width, 2 * head + 128)
    more = []
    if scattered:
        last_out, qo_out, kind = (own_rows, last[1]), (own_rows, 2 * head), F32
        for cols in (2 * head, last[1]):
            more += row_scatter_scratch(chips, own_rows, cols)
    else:
        last_out, qo_out, kind = last, grad_qo.shape, BF16
    return pl.pallas_call(
        functools.partial(key_back_kernel, tiles, tile, chunk, own_rows, scattered),
        grid=(tiles + 2,),
        out_shape=(
            jax.ShapeDtypeStruct((rows, width), BF16),
            jax.ShapeDtypeStruct(last_out, kind),
            jax.ShapeDtypeStruct(qo_out, kind),
        ),
        in_specs=[whole_block(d_kv.shape),
                  late(head), late(1), turn, turn, late(width),
                  pl.BlockSpec((tile, 4 * head), lambda i: (jnp.minimum(i, tiles - 1), 0)),
                  whole_block(gains.shape), whole_block(gain_key.shape), ANY]
        + [whole_block(a.shape) for a in (w_query, dg_query, dg_mid, dg_post, grad_qo, rest)],
        out_specs=(late(width), fixed(last_out), fixed(qo_out)),
        scratch_shapes=[
            pltpu.VMEM((width, 2 * head), F32), pltpu.VMEM((1, width), F32), pltpu.VMEM((1, head), F32),
            pltpu.VMEM((width, 2 * head), BF16), pltpu.SemaphoreType.DMA, pltpu.VMEM(last, BF16),
            pltpu.VMEM((rows, width), F32), pltpu.VMEM(rest.shape, BF16)]
        + [pltpu.SemaphoreType.DMA((2, rest.shape[1] + 1))] * 2 + [comm] * 4 + [dma] * 7
        + [pltpu.SemaphoreType.REGULAR] * 2 + more,
        compiler_params=pltpu.CompilerParams(
            collective_id=ident, has_side_effects=True, vmem_limit_bytes=56 * 2**20),
        cost_estimate=cost(75),
        name="key_back",
    )(d_kv, hat, inv, cosine, sine, x, d_query, gains, gain_key, first, w_query, dg_query, dg_mid, dg_post, grad_qo, rest)


def shards(tokens, segments, cotangent, w_query, w_key, w_value, w_out, w_gate, w_up, w_down,
           g_input, g_post_attn, g_pre_ffn, g_post_ffn, g_query, g_key):
    batches, seq_local, _, size, width = tokens.shape
    head = w_key.shape[1]
    groups = batches * seq_local
    per_group = 2 * size
    rows = groups * per_group
    ctx = lax.axis_size("ctx")
    length = per_group * ctx
    rank = lax.axis_index("ctx")
    shared = ("dp", "ctx")
    own_rows = g_input.shape[0]
    hidden = w_gate.shape[1]

    def column(gain):
        return jnp.pad(gain, (0, own_rows - gain.shape[0]))[:, None]

    own_ids = segments.reshape(groups, 2, size)
    id_rows = own_ids.size // 128
    ids = jnp.pad(own_ids.reshape(id_rows, 128), ((0, -id_rows % 16), (0, 0)))
    extra = jnp.concatenate(
        [column(g) for g in (g_input, g_post_attn, g_pre_ffn, g_post_ffn, g_query, g_key)], axis=1)
    extra = jnp.pad(extra, ((0, 0), (0, 128 - extra.shape[1])))

    def rows_of_16(w):
        return jnp.pad(w, ((0, -own_rows % 16), (0, 0)))

    first, line_query, line_out, ids = first_gather(
        rows_of_16(jnp.concatenate([w_query, w_key, w_value, extra], axis=1)),
        rows_of_16(w_query), rows_of_16(w_out.T), ids, width // own_rows, 5)
    first = first[:, :own_rows].reshape(width, -1)
    side = first[:, 3 * head :]
    gain_cols = side[:, :8].astype(F32)
    gain_rows = gain_cols.T
    gain_input = gain_rows[0]
    short = g_query.shape[0]
    gain_query, gain_key = (
        gain_cols[:, i].reshape(-1, own_rows)[:, :short].reshape(-1) for i in (4, 5))

    wide = wide_of(hidden)
    second = jnp.concatenate(
        [line_out[:own_rows]] + [jnp.pad(w, ((0, 0), (0, wide - hidden))) for w in (w_gate, w_up, w_down.T)], axis=1)
    weights = lax.all_gather(second, shared, axis=0, tiled=True)

    offsets = rank * size + jnp.arange(size, dtype=jnp.int32)
    position = jnp.concatenate([offsets, length - 1 - offsets]).astype(F32)
    cosine, sine = angles(position, head // 2, head)

    x_rows = tokens.reshape(rows, width)
    dy_rows = cotangent.reshape(rows, width)
    queries, q_hat, q_scale, k_hat, k_scale, heads_own, log_mass, kv, heads_all = attention(
        x_rows, first, gain_rows, gain_query[None], gain_key[None], cosine, sine, own_ids[..., None], ids, length, 0)

    line_query, heads_all = lax.optimization_barrier((line_query[:own_rows], heads_all))
    query_full = lax.all_gather(line_query, shared, axis=0, tiled=True)
    attn, hidden_two, gate, up, ffn_out = ffn_forward(x_rows, heads_all, gain_rows, weights, hidden, 1)
    ffn_out, query_full = lax.optimization_barrier((ffn_out, query_full))
    d_gain_post_ffn, grad_ffn, d_two = ffn_backward(
        dy_rows, ffn_out, hidden_two, gate, up, gain_rows, weights, 2)
    grad_ffn = lax.psum_scatter(grad_ffn, shared, scatter_dimension=1, tiled=True)
    output, d_middle, d_heads, delta, d_gain_mid, grad_out_t = middle_back(
        x_rows, attn, dy_rows, d_two, ffn_out, heads_own, gain_rows, weights)

    d_q_all, d_kv, rest, d_gain_query, grad_qo = attention_back(
        queries, d_heads, log_mass, delta, own_ids[:, :, None, :], ids, q_hat, q_scale, cosine, sine, x_rows, gain_rows,
        gain_query[None], grad_out_t, kv, 4)
    d_part, last, grad_qo = key_back(
        d_kv, k_hat, k_scale, cosine, sine, x_rows, d_q_all, gain_rows, gain_key[None],
        first, query_full, d_gain_query, d_gain_mid, d_gain_post_ffn, grad_qo, rest, own_rows, 3)
    d_tokens = d_middle.astype(F32) + d_part.astype(F32)
    if own_rows % 16:
        last = lax.psum_scatter(last, shared, scatter_dimension=0, tiled=True).astype(F32)
        grad_qo = lax.psum_scatter(grad_qo, shared, scatter_dimension=0, tiled=True).astype(F32)
    g = last[:, 2 * head :]
    return (
        output.reshape(tokens.shape),
        d_tokens.reshape(tokens.shape),
        grad_qo[:, :head],
        last[:, :head],
        last[:, head : 2 * head],
        grad_qo[:, head:].T,
        grad_ffn[0].astype(F32),
        grad_ffn[1].astype(F32),
        grad_ffn[2].astype(F32).T,
        g[:, 0],
        g[:, 1],
        g[:, 2],
        g[:, 3],
        g[:short, 4],
        g[:short, 5],
    )


def solution(mesh):
    shared = ("dp", "ctx")
    rows = P(None, "dp", None, "ctx", None)
    weights = (
        P(shared, "tp"), P(shared, None), P(shared, None), P("tp", shared),
        P(shared, "tp"), P(shared, "tp"), P("tp", shared),
    )
    gains = (P(shared),) * 6
    return jax.shard_map(
        shards,
        mesh=mesh,
        in_specs=(rows, P(None, "dp", None, "ctx"), rows) + weights + gains,
        out_specs=(rows, rows) + weights + gains,
        check_vma=False,
    )
```

```python
import functools

import jax
import jax.numpy as jnp
from jax import lax
from jax.experimental import pallas as pl
from jax.experimental.pallas import tpu as pltpu
from jax.sharding import PartitionSpec as P

EPS = 1e-06
THETA = 1000000.0
SCALE = 0.0625
NEGATIVE = -1e30
BF16 = jnp.bfloat16
F32 = jnp.float32
MESH = pl.DeviceIdType.MESH
NN = (((1,), (0,)), ((), ()))
NT = (((1,), (1,)), ((), ()))
TN = (((0,), (0,)), ((), ()))


def dot(a, b, dims=NN):
    return lax.dot_general(a, b, dims, preferred_element_type=F32)


def cost(us):
    return pl.CostEstimate(flops=int(us * 1.1e9), bytes_accessed=0, transcendentals=0)


def barrier_line(z):
    bar = pltpu.get_barrier_semaphore()

    @pl.when(z > 0)
    def _():
        pl.semaphore_signal(bar, inc=1, device_id={"tp": z - 1}, device_id_type=MESH)

    @pl.when(z < 3)
    def _():
        pl.semaphore_signal(bar, inc=1, device_id={"tp": z + 1}, device_id_type=MESH)

    pl.semaphore_wait(bar, jnp.where((z == 0) | (z == 3), 1, 2))


def block_starts(half, t, blocks, rank):
    if half == 0:
        return t
    return jnp.where(t < blocks, t, t + rank + 1)


def angles(position, half_size, full_size):
    frequency = THETA ** (-2.0 * jnp.arange(half_size, dtype=F32) / full_size)
    turned = position[:, None] * frequency[None, :]
    return (jnp.cos(turned), jnp.sin(turned))


def rotate(tensor, cosine, sine):
    half_size = tensor.shape[-1] // 2
    a = tensor[..., :half_size]
    b = tensor[..., half_size:]
    return jnp.concatenate([a * cosine - b * sine, b * cosine + a * sine], axis=-1)


def norm_parts(values):
    inv = lax.rsqrt(jnp.mean(values * values, axis=-1, keepdims=True) + EPS)
    return (values * inv, inv)


def norm_back(upstream, normalized, inv, gain):
    d_norm = upstream * (1.0 + gain)
    d_values = inv * (d_norm - normalized * jnp.mean(d_norm * normalized, axis=-1, keepdims=True))
    return (d_values, jnp.sum(upstream * normalized, axis=0))


def gelu_tanh(values):
    return jax.nn.gelu(values, approximate=True)


class LineSum:
    def __init__(self, count, chunk, slots, own, near, far, out, sems):
        self.count, self.chunk, self.slots = count, chunk, slots
        self.own, self.near, self.far, self.out = own, near, far, out
        self.sems = sems
        self.z = z = lax.axis_index("tp")
        self.hub = (z == 1) | (z == 2)
        self.leaf = (z == 0) | (z == 3)
        self.other_hub = jnp.where(z == 1, 2, 1)
        self.my_hub = jnp.where(z == 0, 1, 2)
        self.my_leaf = jnp.where(z == 1, 0, 3)

    def slot(self, c):
        return pl.ds(pl.multiple_of(lax.rem(c, self.slots) * self.chunk, self.chunk), self.chunk)

    def rows(self, c):
        return pl.ds(pl.multiple_of(c * self.chunk, self.chunk), self.chunk)

    def inwards(self, c):
        return pltpu.make_async_remote_copy(
            self.own.at[self.slot(c)], self.near.at[self.slot(c)], self.sems[0].at[c], self.sems[1].at[c],
            device_id={"tp": self.my_hub}, device_id_type=MESH)

    def across(self, c):
        return pltpu.make_async_remote_copy(
            self.own.at[self.slot(c)], self.far.at[self.slot(c)], self.sems[2].at[c], self.sems[3].at[c],
            device_id={"tp": self.other_hub}, device_id_type=MESH)

    def outwards(self, c):
        return pltpu.make_async_remote_copy(
            self.far.at[self.slot(c)], self.out.at[self.rows(c)], self.sems[4].at[c], self.sems[5].at[c],
            device_id={"tp": self.my_leaf}, device_id_type=MESH)

    def store(self, c):
        return pltpu.make_async_copy(self.far.at[self.slot(c)], self.out.at[self.rows(c)], self.sems[6].at[c])

    def put(self, c, value):
        ring = self.slots < self.count
        if ring:
            @pl.when(c >= self.slots)
            def _():
                @pl.when(self.leaf)
                def _():
                    self.inwards(c - self.slots).wait_send()

                @pl.when(self.hub)
                def _():
                    self.across(c - self.slots).wait_send()

        self.own[self.slot(c), :] = value

        @pl.when(self.leaf)
        def _():
            if ring:
                @pl.when(c >= self.slots)
                def _():
                    pl.semaphore_wait(self.sems[7], 1)
            self.inwards(c).start()

    def pair(self, c):
        ring = self.slots < self.count

        @pl.when(self.hub)
        def _():
            self.inwards(c).wait_recv()
            at = self.slot(c)
            self.own[at, :] = (self.own[at, :].astype(F32) + self.near[at, :].astype(F32)).astype(BF16)
            if ring:
                @pl.when(c < self.count - self.slots)
                def _():
                    pl.semaphore_signal(self.sems[7], inc=1, device_id={"tp": self.my_leaf}, device_id_type=MESH)

                @pl.when(c >= self.slots)
                def _():
                    pl.semaphore_wait(self.sems[8], 1)
            self.across(c).start()

    def total(self, c):
        @pl.when(self.hub)
        def _():
            self.across(c).wait_recv()
            at = self.slot(c)
            self.far[at, :] = (self.own[at, :].astype(F32) + self.far[at, :].astype(F32)).astype(BF16)
            self.outwards(c).start()
            self.store(c).start()

    def retire(self, c):
        @pl.when(self.hub)
        def _():
            self.outwards(c).wait_send()
            self.store(c).wait()
            if self.slots < self.count:
                @pl.when(c < self.count - self.slots)
                def _():
                    pl.semaphore_signal(self.sems[8], inc=1, device_id={"tp": self.other_hub}, device_id_type=MESH)

    def finish(self):
        first = max(0, self.count - self.slots)

        @pl.when(self.leaf)
        def _():
            for c in range(self.count):
                self.outwards(c).wait_recv()
            for c in range(first, self.count):
                self.inwards(c).wait_send()

        @pl.when(self.hub)
        def _():
            for c in range(first, self.count):
                self.across(c).wait_send()


def line_sum_scratch(count, chunk, slots, cols):
    dma = pltpu.SemaphoreType.DMA((count,))
    regular = pltpu.SemaphoreType.REGULAR
    return [pltpu.VMEM((slots * chunk, cols), BF16)] * 3 + [dma] * 7 + [regular] * 2


def gelu_parts(v):
    c = 0.7978845608028654
    square = v * v
    t = jnp.tanh(v * (c + (c * 0.044715) * square))
    half = 0.5 + 0.5 * t
    value = v * half
    slope = half + (0.5 * v) * (1.0 - t * t) * (c + (3.0 * c * 0.044715) * square)
    return value, slope


def column_parts(cols, step):
    return [(a, min(a + step, cols)) for a in range(0, cols, step)]


def middle_of(x, attn, gain_post_attn):
    hat, inv = norm_parts(attn.astype(F32))
    return x.astype(F32) + hat * (1.0 + gain_post_attn), hat, inv


def load_ffn_weights(weights, refs, sem):
    wide = refs[0].shape[1]
    base = weights.shape[1] - 3 * wide
    return [
        pltpu.make_async_copy(weights.at[:, pl.ds(base + j * wide, wide)], ref, sem.at[j])
        for j, ref in enumerate(refs)
    ]


def ffn_forward_kernel(tiles, tile, chunk, hidden, x_ref, h_ref, gain_ref, w_ref,
                       attn_ref, two_ref, gate_ref, up_ref, out_ref, wo_ref, wg_ref, wu_ref, wd_ref, w_sem, own, near, far, *sems):
    i = pl.program_id(0)
    per = tile // chunk
    line = LineSum(tiles * per, chunk, tiles * per, own, near, far, out_ref, sems)
    head = wo_ref.shape[1] // 4

    copies = [pltpu.make_async_copy(w_ref.at[:, pl.ds(0, 4 * head)], wo_ref, w_sem.at[3])]
    copies += load_ffn_weights(w_ref, (wg_ref, wu_ref, wd_ref), w_sem)

    @pl.when(i == 0)
    def _():
        for copy in copies:
            copy.start()
        barrier_line(line.z)
        copies[0].wait()

    attn = dot(h_ref[...], wo_ref[...], NT).astype(BF16)
    attn_ref[...] = attn
    middle, _, _ = middle_of(x_ref[...], attn, gain_ref[1:2, :])
    hat, _ = norm_parts(middle)
    two = (hat * (1.0 + gain_ref[2:3, :])).astype(BF16)
    two_ref[...] = two
    part = None

    def handle(j):
        @pl.when(i >= 1)
        def _():
            line.pair((i - 1) * per + j)

        @pl.when(i >= 2)
        def _():
            line.total((i - 2) * per + j)

    @pl.when(i == 0)
    def _():
        for copy in copies[1:]:
            copy.wait()

    for a, b in column_parts(hidden, 896):
        gate = dot(two, wg_ref[:, a:b])
        up = dot(two, wu_ref[:, a:b])
        gate_ref[:, a:b] = gate.astype(BF16)
        up_ref[:, a:b] = up.astype(BF16)
        value, _ = gelu_parts(gate)
        more = dot((value * up).astype(BF16), wd_ref[:, a:b], NT)
        part = more if part is None else part + more
        if a == 0:
            for j in range(per // 2):
                handle(j)
    for j in range(per):
        line.put(i * per + j, part[j * chunk : (j + 1) * chunk].astype(BF16))

    for j in range(per // 2, per):
        handle(j)

    @pl.when(i == tiles - 1)
    def _():
        last = tiles * per
        for c in range(max(0, last - 2 * per), last - per):
            line.total(c)
        for c in range(last - per, last):
            line.pair(c)
        for c in range(last - per, last):
            line.total(c)
        for c in range(last):
            line.retire(c)
        line.finish()


def whole_block(shape):
    return pl.BlockSpec(shape, lambda i: (0,) * len(shape), pipeline_mode=pl.Buffered(1))


def tile_block(tile, cols):
    return pl.BlockSpec((tile, cols), lambda i: (i, 0))


ANY = pl.BlockSpec(memory_space=pl.ANY)


def wide_of(hidden):
    return -(-hidden // 128) * 128


def ffn_forward(x, heads, gains, weights, hidden, ident):
    rows, width = x.shape
    all_heads = heads.shape[1]
    tile, chunk = 128, 64
    tiles = rows // tile
    count = rows // chunk
    wide = wide_of(hidden)
    return pl.pallas_call(
        functools.partial(ffn_forward_kernel, tiles, tile, chunk, hidden),
        grid=(tiles,),
        out_shape=(
            jax.ShapeDtypeStruct((rows, width), BF16),
            jax.ShapeDtypeStruct((rows, width), BF16),
            jax.ShapeDtypeStruct((rows, hidden), BF16),
            jax.ShapeDtypeStruct((rows, hidden), BF16),
            jax.ShapeDtypeStruct((rows, width), BF16),
        ),
        in_specs=[
            tile_block(tile, width),
            tile_block(tile, all_heads),
            whole_block(gains.shape),
            ANY,
        ],
        out_specs=(tile_block(tile, width), tile_block(tile, width), tile_block(tile, hidden), tile_block(tile, hidden), ANY),
        scratch_shapes=[pltpu.VMEM((width, all_heads), BF16)] + [pltpu.VMEM((width, wide), BF16)] * 3
        + [pltpu.SemaphoreType.DMA((4,))]
        + line_sum_scratch(count, chunk, count, width),
        compiler_params=pltpu.CompilerParams(
            collective_id=ident, has_side_effects=True, vmem_limit_bytes=60 * 2**20),
        cost_estimate=cost(140),
        name="ffn_forward",
    )(x, heads, gains, weights)


def ffn_backward_kernel(tiles, tile, chunk, slots, hidden, dy_ref, ffn_ref, two_ref, gate_ref, up_ref,
                        gain_ref, w_ref,
                        dgain_ref, grad_ref, out_ref, wg_ref, wu_ref, wd_ref, w_sem,
                        acc_g, acc_u, acc_d, keep_g, keep_u, keep_h, stage, stage_sem, own, near, far, *sems):
    i = pl.program_id(0)
    per = tile // chunk
    last = tiles * per
    line = LineSum(last, chunk, slots, own, near, far, out_ref, sems)

    copies = load_ffn_weights(w_ref, (wg_ref, wu_ref, wd_ref), w_sem)

    @pl.when(i == 0)
    def _():
        for copy in copies[::-1]:
            copy.start()
        barrier_line(line.z)
        dgain_ref[...] = jnp.zeros_like(dgain_ref)
        for copy in copies[::-1]:
            copy.wait()

    hat, inv = norm_parts(ffn_ref[...].astype(F32))
    gain = gain_ref[3:4, :]
    d_ffn, d_gain = norm_back(dy_ref[...].astype(F32), hat, inv, gain)
    dgain_ref[...] += d_gain[None]
    d_ffn = d_ffn.astype(BF16)
    part = None

    def handle(j):
        @pl.when(i >= 1)
        def _():
            line.pair((i - 1) * per + j)

        @pl.when(i >= 2)
        def _():
            line.total((i - 2) * per + j)

    for a, b in column_parts(hidden, 512):
        d_hidden = dot(d_ffn, wd_ref[:, a:b])
        up = up_ref[:, a:b].astype(F32)
        value, slope = gelu_parts(gate_ref[:, a:b].astype(F32))
        keep_h[:, a:b] = (value * up).astype(BF16)
        d_gate = (d_hidden * up * slope).astype(BF16)
        d_up = (d_hidden * value).astype(BF16)
        keep_g[:, a:b] = d_gate
        keep_u[:, a:b] = d_up
        more = dot(d_gate, wg_ref[:, a:b], NT) + dot(d_up, wu_ref[:, a:b], NT)
        part = more if part is None else part + more
        if a == 0:
            handle(0)
    for j in range(per):
        line.put(i * per + j, part[j * chunk : (j + 1) * chunk].astype(BF16))

    @pl.when(i == 0)
    def _():
        for acc in (acc_g, acc_u, acc_d):
            acc[...] = jnp.zeros_like(acc)

    acc_g[...] += dot(two_ref[...], keep_g[...], TN)
    acc_u[...] += dot(two_ref[...], keep_u[...], TN)
    for j in range(1, per):
        handle(j)
    acc_d[...] += dot(d_ffn, keep_h[...], TN)

    @pl.when(i >= 3)
    def _():
        for j in range(per):
            line.retire((i - 3) * per + j)

    @pl.when(i == tiles - 1)
    def _():
        step = stage.shape[1]
        count = acc_g.shape[0] // step

        def write(acc, out):
            def pieces(k, _):
                at = lax.rem(k, 2)
                rows = pl.ds(pl.multiple_of(k * step, step), step)

                @pl.when(k >= 2)
                def _():
                    pltpu.make_async_copy(stage.at[at], out.at[pl.ds(0, step)], stage_sem.at[at]).wait()
                stage[at] = acc[rows, :].astype(BF16)
                pltpu.make_async_copy(stage.at[at], out.at[rows], stage_sem.at[at]).start()
                return 0

            lax.fori_loop(0, count, pieces, 0)
            for at in range(2):
                pltpu.make_async_copy(stage.at[at], out.at[pl.ds(0, step)], stage_sem.at[at]).wait()

        for c in range(max(0, last - 2 * per), last - per):
            line.total(c)
        write(acc_g, grad_ref.at[0])
        line.pair(last - per)
        write(acc_u, grad_ref.at[1])
        for c in range(last - per + 1, last):
            line.pair(c)
            line.total(c - 1)
        write(acc_d, grad_ref.at[2])
        line.total(last - 1)
        for c in range(max(0, last - 3 * per), last):
            line.retire(c)
        line.finish()


def ffn_backward(dy, ffn, two, gate, up, gains, weights, ident):
    rows, width = dy.shape
    hidden = gate.shape[1]
    wide = wide_of(hidden)
    tile, chunk = 256, 128
    tiles = rows // tile
    count = rows // chunk
    slots = min(count, 6)
    step = 144
    acc = pltpu.VMEM((width, hidden), F32)
    keep = pltpu.VMEM((tile, hidden), BF16)
    return pl.pallas_call(
        functools.partial(ffn_backward_kernel, tiles, tile, chunk, slots, hidden),
        grid=(tiles,),
        out_shape=(
            jax.ShapeDtypeStruct((1, width), F32),
            jax.ShapeDtypeStruct((3, width, hidden), BF16),
            jax.ShapeDtypeStruct((rows, width), BF16),
        ),
        in_specs=[tile_block(tile, width)] * 3 + [tile_block(tile, hidden)] * 2
        + [whole_block(gains.shape), ANY],
        out_specs=(pl.BlockSpec((1, width), lambda i: (0, 0)), ANY, ANY),
        scratch_shapes=[pltpu.VMEM((width, wide), BF16)] * 3 + [pltpu.SemaphoreType.DMA((3,))] + [acc] * 3 + [keep] * 3
        + [pltpu.VMEM((2, step, hidden), BF16), pltpu.SemaphoreType.DMA((2,))]
        + line_sum_scratch(count, chunk, slots, width),
        compiler_params=pltpu.CompilerParams(
            collective_id=ident, has_side_effects=True, vmem_limit_bytes=63 * 2**20),
        cost_estimate=cost(145),
        name="ffn_backward",
    )(dy, ffn, two, gate, up, gains, weights)


def middle_back_kernel(x_ref, attn_ref, dy_ref, d2_ref, ffn_ref, h_ref, gain_ref, w_ref,
                       y_ref, dm_ref, dh_ref, delta_ref, dgain_ref, go_ref, acc, wo_ref, w_sem):
    i = pl.program_id(0)

    @pl.when(i == 0)
    def _():
        head = wo_ref.shape[1]
        at = pl.multiple_of(lax.axis_index("tp") * head, head)
        copy = pltpu.make_async_copy(w_ref.at[:, pl.ds(at, head)], wo_ref, w_sem)
        copy.start()
        copy.wait()
        acc[...] = jnp.zeros_like(acc)
        dgain_ref[...] = jnp.zeros_like(dgain_ref)

    middle, attn_hat, attn_inv = middle_of(x_ref[...], attn_ref[...], gain_ref[1:2, :])
    hat, _ = norm_parts(ffn_ref[...].astype(F32))
    y_ref[...] = (middle + hat * (1.0 + gain_ref[3:4, :])).astype(BF16)
    hat, inv = norm_parts(middle)
    d_part, d_gain = norm_back(d2_ref[...].astype(F32), hat, inv, gain_ref[2:3, :])
    dgain_ref[1:2, :] += d_gain[None]
    d_middle = dy_ref[...].astype(F32) + d_part
    dm_ref[...] = d_middle.astype(BF16)
    d_attn, d_gain = norm_back(d_middle, attn_hat, attn_inv, gain_ref[1:2, :])
    dgain_ref[0:1, :] += d_gain[None]
    d_attn = d_attn.astype(BF16)
    d_heads = dot(d_attn, wo_ref[...]).astype(BF16)
    dh_ref[...] = d_heads
    heads = h_ref[...]
    delta_ref[...] = jnp.sum(d_heads.astype(F32) * heads.astype(F32), axis=1, keepdims=True)
    acc[...] += dot(d_attn, heads, TN)

    @pl.when(i == pl.num_programs(0) - 1)
    def _():
        go_ref[...] = acc[...].astype(BF16)


def middle_back(x, attn, dy, d_two, ffn, heads, gains, weights):
    rows, width = x.shape
    head = heads.shape[1]
    tile = 256
    return pl.pallas_call(
        middle_back_kernel,
        grid=(rows // tile,),
        out_shape=(
            jax.ShapeDtypeStruct((rows, width), BF16),
            jax.ShapeDtypeStruct((rows, width), BF16),
            jax.ShapeDtypeStruct((rows, head), BF16),
            jax.ShapeDtypeStruct((rows, 1), F32),
            jax.ShapeDtypeStruct((2, width), F32),
            jax.ShapeDtypeStruct((width, head), BF16),
        ),
        in_specs=[tile_block(tile, width)] * 5 + [tile_block(tile, head)] + [whole_block(gains.shape), ANY],
        out_specs=(
            tile_block(tile, width), tile_block(tile, width), tile_block(tile, head), tile_block(tile, 1),
            pl.BlockSpec((2, width), lambda i: (0, 0)), pl.BlockSpec((width, head), lambda i: (0, 0)),
        ),
        scratch_shapes=[pltpu.VMEM((width, head), F32), pltpu.VMEM((width, head), BF16), pltpu.SemaphoreType.DMA],
        compiler_params=pltpu.CompilerParams(vmem_limit_bytes=48 * 2**20),
        cost_estimate=cost(19),
        name="middle_back",
    )(x, attn, dy, d_two, ffn, heads, gains, weights)


class LineGather:
    def __init__(self, whole, tile, width, sems):
        self.whole, self.tile, self.width, self.sems = whole, tile, width, sems
        self.z = lax.axis_index("tp")

    def place(self, src, t):
        return self.whole.at[
            pl.ds(pl.multiple_of(t * self.tile, self.tile), self.tile),
            pl.ds(pl.multiple_of(src * self.width, self.width), self.width)]

    def send(self, src, t, hop, way):
        ss, rs = self.sems[:2] if way > 0 else self.sems[2:]
        place = self.place(src, t)
        return pltpu.make_async_remote_copy(
            place, place, ss.at[hop, t], rs.at[hop, t],
            device_id={"tp": self.z + way}, device_id_type=MESH)

    def going(self, hop, way):
        src = self.z - way * hop
        return src, (self.z + way >= 0) & (self.z + way <= 3) & (src >= 0) & (src <= 3)

    def coming(self, hop, way):
        src = self.z - way * (hop + 1)
        return src, (src >= 0) & (src <= 3)

    def forward(self, t, hop):
        for way in (1, -1):
            if hop > 0:
                self.wait(t, hop - 1, way)
            src, ok = self.going(hop, way)

            @pl.when(ok)
            def _():
                self.send(src, t, hop, way).start()

    def wait(self, t, hop, way):
        src, ok = self.coming(hop, way)

        @pl.when(ok)
        def _():
            self.send(src, t, hop, way).wait_recv()

    def arrived(self, t):
        for way in (1, -1):
            self.wait(t, 2, way)

    def finish(self, tiles):
        for hop in range(3):
            for way in (1, -1):
                src, ok = self.going(hop, way)

                @pl.when(ok)
                def _():
                    def one(t, _):
                        self.send(src, t, hop, way).wait_send()
                        return 0

                    lax.fori_loop(0, tiles, one, 0)


class KeyGather(LineGather):
    def __init__(self, block, chips, sems):
        self.block, self.chips, self.sems = block, chips, sems
        self.z = lax.axis_index("tp")

    def tile_of(self, g, half, k):
        return (2 * g + half) * (self.chips - 1) + k - 1

    def place(self, src, t):
        pair, k = divmod(t, self.chips - 1)
        return self.quarter(pair // 2, pair % 2, k + 1, src)

    def quarter(self, g, half, k, src, own=False):
        ref, start, size = self.block(g, half, k, own)
        rows = size // 4
        return ref.at[pl.ds(pl.multiple_of(start + src * rows, rows), rows)]

    def finish(self, tiles):
        for hop in range(3):
            for way in (1, -1):
                src, ok = self.going(hop, way)

                @pl.when(ok)
                def _():
                    for t in range(tiles):
                        self.send(src, t, hop, way).wait_send()


class Shared:
    def __init__(self, over_dp):
        self.ctx = ctx = lax.axis_size("ctx")
        me = lax.axis_index("ctx")
        self.devices = ctx
        if over_dp:
            me = me + lax.axis_index("dp") * ctx
            self.devices = ctx * lax.axis_size("dp")
        self.over_dp = over_dp
        self.me = me
        self.chips = self.devices // 2
        self.core = lax.rem(me, 2)
        self.chip = lax.div(me, 2)

    def ident(self, device):
        if self.over_dp:
            return {"dp": lax.div(device, self.ctx), "ctx": lax.rem(device, self.ctx)}
        return {"ctx": device}

    def other(self, k):
        return 2 * lax.rem(self.chip + k + self.chips, self.chips) + self.core

    def partner(self):
        return self.me + 1 - 2 * self.core

    def greet(self, z):
        bar = pltpu.get_barrier_semaphore()
        for device in [self.partner()] + [self.other(k) for k in range(1, self.chips)]:
            pl.semaphore_signal(bar, inc=1, device_id=self.ident(device), device_id_type=MESH)

        @pl.when(z > 0)
        def _():
            pl.semaphore_signal(bar, inc=1, device_id={"tp": z - 1}, device_id_type=MESH)

        @pl.when(z < 3)
        def _():
            pl.semaphore_signal(bar, inc=1, device_id={"tp": z + 1}, device_id_type=MESH)

        pl.semaphore_wait(bar, self.chips + jnp.where((z == 0) | (z == 3), 1, 2))

    def copy(self, source, target, send, recv, device):
        return pltpu.make_async_remote_copy(
            source, target, send, recv, device_id=self.ident(device), device_id_type=MESH)


def first_gather_kernel(a_ref, b_ref, c_ref, i_ref, all_ref, line_ref, more_ref, ids_ref, lsem, ss1, rs1, ss2, rs2, si1, ri1, si2, ri2, *sems):
    group = Shared(True)
    line = LineGather(line_ref, b_ref.shape[0], b_ref.shape[1], sems[:4])
    more = LineGather(more_ref, c_ref.shape[0], c_ref.shape[1], sems[4:])
    width = b_ref.shape[1]
    own = [
        pltpu.make_async_copy(b_ref, line_ref.at[:, pl.ds(pl.multiple_of(line.z * width, width), width)], lsem.at[0]),
        pltpu.make_async_copy(c_ref, more_ref.at[:, pl.ds(pl.multiple_of(line.z * width, width), width)], lsem.at[3]),
        pltpu.make_async_copy(a_ref, all_ref.at[group.me], lsem.at[1]),
        pltpu.make_async_copy(i_ref, ids_ref.at[group.me], lsem.at[2]),
    ]
    for copy in own:
        copy.start()
    group.greet(line.z)
    arrays = ((a_ref, all_ref, ss1, rs1, ss2, rs2), (i_ref, ids_ref, si1, ri1, si2, ri2))

    def direct(n, k, incoming=False):
        ref, whole, ss, rs = arrays[n][:4]
        at = whole.at[group.other(-k)] if incoming else whole.at[group.me]
        return group.copy(ref, at, ss.at[k], rs.at[k], group.other(k))

    def inner(n, k, incoming=False):
        ref, whole, _, _, ss, rs = arrays[n]
        at = whole.at[group.other(-k)]
        if incoming:
            at = whole.at[group.other(-k) + 1 - 2 * group.core]
        return group.copy(ref if k == 0 else at, at, ss.at[k], rs.at[k], group.partner())

    both = range(2)
    for k in range(1, group.chips):
        for n in both:
            direct(n, k).start()
    for n in both:
        inner(n, 0).start()
    own[0].wait()
    line.forward(0, 0)
    own[1].wait()
    more.forward(0, 0)
    for k in range(1, group.chips):
        if k < 3:
            line.forward(0, k)
            more.forward(0, k)
        for n in both:
            direct(n, k, True).wait_recv()
            inner(n, k).start()
    for hop in range(min(3, group.chips), 3):
        line.forward(0, hop)
        more.forward(0, hop)
    for k in range(group.chips):
        for n in both:
            inner(n, k, True).wait_recv()
    line.arrived(0)
    more.arrived(0)
    for copy in own[2:]:
        copy.wait()
    for n in both:
        for k in range(1, group.chips):
            direct(n, k).wait_send()
        for k in range(group.chips):
            inner(n, k).wait_send()
    line.finish(1)
    more.finish(1)


def first_gather(a, b, c, ids, devices, ident):
    dma = pltpu.SemaphoreType.DMA((devices // 2,))
    hop = pltpu.SemaphoreType.DMA((3, 1))
    return pl.pallas_call(
        first_gather_kernel,
        out_shape=(
            jax.ShapeDtypeStruct((devices,) + a.shape, a.dtype),
            jax.ShapeDtypeStruct((b.shape[0], 4 * b.shape[1]), b.dtype),
            jax.ShapeDtypeStruct((c.shape[0], 4 * c.shape[1]), c.dtype),
            jax.ShapeDtypeStruct((devices,) + ids.shape, ids.dtype),
        ),
        in_specs=[ANY] * 4,
        out_specs=(ANY,) * 4,
        scratch_shapes=[pltpu.SemaphoreType.DMA((4,))] + [dma] * 8 + [hop] * 8,
        compiler_params=pltpu.CompilerParams(collective_id=ident, has_side_effects=True),
        cost_estimate=cost(20),
        name="first_gather",
    )(a, b, c, ids)


def attention_kernel(groups, size, x_ref, w_ref, gain_ref, gq_ref, gk_ref, cos_ref, sin_ref, qs_ref, ks_ref,
                     q_ref, qhat_ref, qinv_ref, khat_ref, kinv_ref, heads_ref, log_ref, kv_out, all_out,
                     kv, whole, store_kv, store_all, ss1, rs1, ss2, rs2, *sems):
    head = q_ref.shape[1]
    length = kv.shape[1]
    id_rows = size // 128
    blocks = length // (2 * size)
    group = Shared(False)
    rank = group.me
    tile = min(256, size)
    per = size // tile
    line = LineGather(whole, tile, head, sems[:4])
    z = line.z
    group.greet(z)

    def block(g, half, k, own):
        c = rank if own else group.other(-k)
        return kv.at[g], half * (length // 2) + c * size, size

    keys = KeyGather(block, group.chips, sems[4:])

    def place(g, half, c):
        return kv.at[g, pl.ds(pl.multiple_of(half * (length // 2) + c * size, size), size)]

    def straight(t):
        return t == 2 * groups - 1

    def direct(g, half, k, incoming=False):
        at = keys.quarter(g, half, k, z, own=not incoming)
        if straight(2 * g + half):
            at = place(g, half, group.other(-k) if incoming else rank)
        return group.copy(at, at, ss1.at[g, half, k], rs1.at[g, half, k], group.other(k))

    def inner(g, half, k, incoming=False):
        block = group.other(-k)
        at = place(g, half, block + 1 - 2 * group.core if incoming else block)
        return group.copy(at, at, ss2.at[g, half, k], rs2.at[g, half, k], group.partner())

    def project(g, half, u):
        rows = pl.ds((2 * g + half) * size + u * tile, tile)
        spot = pl.ds(half * size + u * tile, tile)
        cosine, sine = cos_ref[spot, :], sin_ref[spot, :]
        hat, _ = norm_parts(x_ref[rows, :].astype(F32))
        raw = dot((hat * (1.0 + gain_ref[0:1, :])).astype(BF16), w_ref[:, : 3 * head])
        hat, inv = norm_parts(raw[:, :head])
        qhat_ref[rows, :] = hat
        qinv_ref[rows, :] = inv
        q_ref[rows, :] = rotate(hat * (1.0 + gq_ref[...]), cosine, sine).astype(BF16)
        hat, inv = norm_parts(raw[:, head : 2 * head])
        khat_ref[rows, :] = hat
        kinv_ref[rows, :] = inv
        at = pl.ds(pl.multiple_of(half * (length // 2) + rank * size + u * tile, tile), tile)
        kv[g, at, :head] = rotate(hat * (1.0 + gk_ref[...]), cosine, sine).astype(BF16)
        kv[g, at, head:] = raw[:, 2 * head :].astype(BF16)

    def attend(g, half):
        row = lax.broadcasted_iota(jnp.int32, (size, size), 0)
        col = lax.broadcasted_iota(jnp.int32, (size, size), 1)
        rows = pl.ds((2 * g + half) * size, size)
        q = q_ref[rows, :] * jnp.asarray(SCALE, BF16)
        qseg = qs_ref[g, half]

        def part(block):
            at = pl.ds(pl.multiple_of(block * size, size), size)
            device = lax.axis_index("dp") * lax.axis_size("ctx") + lax.rem(block, blocks)
            ids = ks_ref[device, pl.ds((2 * g + lax.div(block, blocks)) * id_rows, id_rows), :]
            ids = jnp.concatenate([ids[j : j + 1] for j in range(id_rows)], axis=1)
            same = qseg == jnp.where(ids == 0, -1, ids)
            return dot(q, kv[g, at, :head], NT), kv[g, at, head:], same

        s, v, same = part(rank + half * blocks)
        order = (col <= row) if half == 0 else (col >= row)
        s = jnp.where((same & order) | (col == row), s, NEGATIVE)
        top = jnp.max(s, axis=1, keepdims=True)
        p = jnp.exp(s - top)
        mass = jnp.sum(p, axis=1, keepdims=True)
        acc = dot(p.astype(BF16), v)

        def step(t, carry):
            top, mass, acc = carry
            s, v, same = part(block_starts(half, t, blocks, rank))
            s = jnp.where(same, s, NEGATIVE)
            new = jnp.maximum(top, jnp.max(s, axis=1, keepdims=True))
            keep = jnp.exp(top - new)
            p = jnp.exp(s - new)
            mass = mass * keep + jnp.sum(p, axis=1, keepdims=True)
            return new, mass, acc * keep + dot(p.astype(BF16), v)

        count = rank if half == 0 else 2 * blocks - 1 - rank
        top, mass, acc = lax.fori_loop(0, count, step, (top, mass, acc))
        out = (acc / mass).astype(BF16)
        heads_ref[rows, :] = out
        whole[rows, pl.ds(pl.multiple_of(z * head, head), head)] = out
        log_ref[g, half] = top + jnp.log(mass)

    chips = range(1, group.chips)
    tiles = 2 * groups

    def stage(t, n):
        if not 0 <= t < tiles:
            return
        g, half = divmod(t, 2)
        for k in chips:
            spot = keys.tile_of(g, half, k)
            if n == 0:
                direct(g, half, k).start()
            elif straight(t):
                if n == 4:
                    direct(g, half, k, True).wait_recv()
                    inner(g, half, k).start()
            elif n == 4:
                keys.arrived(spot)
                inner(g, half, k).start()
            else:
                if n == 1:
                    direct(g, half, k, True).wait_recv()
                keys.forward(spot, n - 1)

    def exchange(t):
        for n in (4, 3, 2, 1):
            stage(t - n, n)

    def hops(t):
        for hop in range(3):
            if 0 <= t - hop < tiles:
                for u in range(per):
                    line.forward((t - hop) * per + u, hop)

    def keep(t):
        at = pl.ds(t * tile, tile)
        return pltpu.make_async_copy(whole.at[at], all_out.at[at], store_all.at[t])

    def save(g):
        return pltpu.make_async_copy(kv.at[g], kv_out.at[g], store_kv.at[g])

    def landed(t):
        g, half = divmod(t, 2)
        for k in range(group.chips):
            inner(g, half, k, True).wait_recv()

    for t in range(tiles):
        g, half = divmod(t, 2)
        for u in range(per):
            project(g, half, u)
        stage(t, 0)
        inner(g, half, 0).start()
        exchange(t)
    for t in range(tiles):
        g, half = divmod(t, 2)
        exchange(tiles + t)
        landed(t)
        attend(g, half)
        hops(t)
    for g in range(groups):
        save(g).start()
    for t in range(tiles, tiles + 2):
        hops(t)
    for t in range(tiles * per):
        line.arrived(t)
        keep(t).start()
    for g in range(groups):
        save(g).wait()
        for half in range(2):
            for k in chips:
                direct(g, half, k).wait_send()
            for k in range(group.chips):
                inner(g, half, k).wait_send()
    line.finish(tiles * per)
    keys.finish((tiles - 1) * (group.chips - 1))
    for t in range(tiles * per):
        keep(t).wait()


def attention(x, w, gains, gain_query, gain_key, cosine, sine, qseg, ids, length, ident):
    rows, width = x.shape
    groups, _, size, _ = qseg.shape
    head = gain_query.shape[1]
    chips = length // (4 * size)
    tiles = 2 * groups
    parts = rows // min(256, size)
    vmem = pl.BlockSpec(memory_space=pltpu.VMEM)
    dma = pltpu.SemaphoreType.DMA
    return pl.pallas_call(
        functools.partial(attention_kernel, groups, size),
        out_shape=(
            jax.ShapeDtypeStruct((rows, head), BF16),
            jax.ShapeDtypeStruct((rows, head), F32),
            jax.ShapeDtypeStruct((rows, 1), F32),
            jax.ShapeDtypeStruct((rows, head), F32),
            jax.ShapeDtypeStruct((rows, 1), F32),
            jax.ShapeDtypeStruct((rows, head), BF16),
            jax.ShapeDtypeStruct((groups, 2, size, 1), F32),
            jax.ShapeDtypeStruct((groups, length, 2 * head), BF16),
            jax.ShapeDtypeStruct((rows, 4 * head), BF16),
        ),
        in_specs=[vmem] * 9,
        out_specs=(vmem,) * 7 + (ANY, ANY),
        scratch_shapes=[
            pltpu.VMEM((groups, length, 2 * head), BF16), pltpu.VMEM((rows, 4 * head), BF16),
            dma((groups,)), dma((parts,))] + [dma((groups, 2, chips))] * 4 + [dma((3, parts))] * 4
        + [dma((3, tiles * (chips - 1)))] * 4,
        compiler_params=pltpu.CompilerParams(
            collective_id=ident, has_side_effects=True, vmem_limit_bytes=60 * 2**20),
        cost_estimate=cost(110),
        name="attention",
    )(x, w, gains, gain_query, gain_key, cosine, sine, qseg, ids)


class ResidentSum(LineSum):
    def outwards(self, c):
        return pltpu.make_async_remote_copy(
            self.out.at[self.rows(c)], self.out.at[self.rows(c)], self.sems[4].at[c], self.sems[5].at[c],
            device_id={"tp": self.my_leaf}, device_id_type=MESH)

    def total(self, c):
        @pl.when(self.hub)
        def _():
            self.across(c).wait_recv()
            at = self.rows(c)
            self.out[at, :] = (self.own[at, :].astype(F32) + self.far[at, :].astype(F32)).astype(BF16)
            self.outwards(c).start()

    def arrived(self, c):
        @pl.when(self.leaf)
        def _():
            self.outwards(c).wait_recv()

    def finish(self):
        @pl.when(self.leaf)
        def _():
            for c in range(self.count):
                self.inwards(c).wait_send()

        @pl.when(self.hub)
        def _():
            for c in range(self.count):
                self.across(c).wait_send()
                self.outwards(c).wait_send()


def turned(column, size):
    return jnp.transpose(jnp.broadcast_to(column, (size, 128)))[0:1, :]


def attention_back_kernel(groups, size, q_ref, do_ref, log_ref, delta_ref, qs_ref, ids_ref, hat_ref, inv_ref, cos_ref, sin_ref,
                          x_ref, gain_ref, gq_ref, go_ref, kv_hbm, all_out, dkv_ref, rest_ref, dgain_ref, grad_ref,
                          kv, dk, dv, part, near, pair, far, whole, acc, load, store, ss1, rs1, ss2, rs2, *sems):
    head = q_ref.shape[1]
    length = kv.shape[1]
    blocks = length // (2 * size)
    id_rows = size // 128
    tiles = 2 * groups
    group = Shared(False)
    rank, core = group.me, group.core
    tile = min(128, size)
    per = size // tile
    line = LineGather(whole, tile, head, sems)
    z = line.z
    others = range(1, group.chips)
    order = list(others) + [0]

    def fetch(g):
        return pltpu.make_async_copy(kv_hbm.at[g], kv.at[g], load.at[g])

    for g in range(groups):
        fetch(g).start()
    group.greet(z)
    acc[...] = jnp.zeros_like(acc)
    dgain_ref[...] = jnp.zeros_like(dgain_ref)

    def rows_of(half, device):
        return pl.ds(pl.multiple_of(half * (length // 2) + device * size, size), size)

    def within(g, half, k):
        to = group.other(k) + 1 - 2 * core
        return group.copy(
            part.at[g, rows_of(half, to)], near.at[g, half, k], ss1.at[g, half, k], rs1.at[g, half, k], group.partner())

    def between(g, half, k):
        return group.copy(
            pair.at[g, half, k - 1], far.at[g, half, k - 1], ss2.at[g, half, k], rs2.at[g, half, k], group.other(k))

    def both_cores(g):
        for half in range(2):
            for k in order:
                within(g, half, k).wait_recv()
                total = part[g, rows_of(half, group.other(k)), :].astype(F32) + near[g, half, k].astype(F32)
                if k > 0 and g == groups - 1:
                    rest_ref[half, k - 1] = total.astype(BF16)
                elif k > 0:
                    pair[g, half, k - 1] = total.astype(BF16)
                    between(g, half, k).start()
                else:
                    dkv_ref[pl.ds((2 * g + half) * size, size), :] = total.astype(BF16)

    def all_chips(g):
        for half in range(2):
            at = pl.ds((2 * g + half) * size, size)
            total = dkv_ref[at, :].astype(F32)
            for k in others:
                between(g, half, k).wait_recv()
                total = total + far[g, half, k - 1].astype(F32)
            dkv_ref[at, :] = total.astype(BF16)

    def hops(t):
        for hop in range(3):
            if 0 <= t - hop < tiles:
                for u in range(per):
                    line.forward((t - hop) * per + u, hop)

    def attend(g, half):
        row = lax.broadcasted_iota(jnp.int32, (size, size), 0)
        col = lax.broadcasted_iota(jnp.int32, (size, size), 1)
        own = pl.ds((2 * g + half) * size, size)
        q = q_ref[own, :] * jnp.asarray(SCALE, BF16)
        do = do_ref[own, :]
        qseg = qs_ref[g, half]
        log_mass = turned(log_ref[g, half], size)
        delta = turned(delta_ref[own, :], size)

        def step_of(block, mine):
            at = pl.ds(pl.multiple_of(block * size, size), size)
            k = kv[g, at, :head]
            v = kv[g, at, head:]
            device = lax.axis_index("dp") * lax.axis_size("ctx") + lax.rem(block, blocks)
            ids = ids_ref[device, pl.ds((2 * g + lax.div(block, blocks)) * id_rows, id_rows), :]
            ids = jnp.concatenate([ids[j : j + 1] for j in range(id_rows)], axis=1)
            ids = jnp.transpose(jnp.broadcast_to(jnp.where(ids == 0, -1, ids), (8, size)))[:, 0:1]
            allowed = ids == qseg
            if mine:
                ahead = (row <= col) if half == 0 else (row >= col)
                allowed = (allowed & ahead) | (col == row)
            s = jnp.where(allowed, dot(k, q, NT), NEGATIVE)
            p = jnp.exp(s - log_mass)
            ds = (p * (dot(v, do, NT) - delta)).astype(BF16)
            dv[at, :] += dot(p.astype(BF16), do)
            dk[at, :] += dot(ds, q)
            return dot(ds, k, TN)

        def step(t, dq):
            return dq + step_of(block_starts(half, t, blocks, rank), False)

        dq = step_of(rank + half * blocks, True)
        count = rank if half == 0 else 2 * blocks - 1 - rank
        dq = SCALE * lax.fori_loop(0, count, step, dq)
        spot = pl.ds(half * size, size)
        d_rot = rotate(dq, cos_ref[spot, :], -sin_ref[spot, :])
        d_raw, d_gain = norm_back(d_rot, hat_ref[own, :], inv_ref[own, :], gq_ref[...])
        dgain_ref[...] += d_gain[None]
        whole[own, pl.ds(pl.multiple_of(z * head, head), head)] = d_raw.astype(BF16)

    def weight_gradient(t):
        own = pl.ds(t * size, size)
        hat, _ = norm_parts(x_ref[own, :].astype(F32))
        one = (hat * (1.0 + gain_ref[0:1, :])).astype(BF16)
        acc[...] += dot(one, whole[own, pl.ds(pl.multiple_of(z * head, head), head)], TN)

    def keep(t):
        at = pl.ds(t * tile, tile)
        return pltpu.make_async_copy(whole.at[at], all_out.at[at], store.at[t])

    for g in range(groups):
        fetch(g).wait()
        dk[...] = jnp.zeros_like(dk)
        dv[...] = jnp.zeros_like(dv)
        for half in range(2):
            attend(g, half)
            hops(2 * g + half)
            if half == 0 and g > 0:
                both_cores(g - 1)
        part[g, :, :head] = dk[...].astype(BF16)
        part[g, :, head:] = dv[...].astype(BF16)
        for half in range(2):
            for k in order:
                within(g, half, k).start()
        for half in range(2):
            weight_gradient(2 * g + half)
        if g > 0:
            all_chips(g - 1)
    hops(tiles)
    both_cores(groups - 1)
    hops(tiles + 1)
    grad_ref[:, :head] = acc[...].astype(BF16)
    grad_ref[:, head:] = go_ref[...]
    for t in range(tiles * per):
        line.arrived(t)
        keep(t).start()
    for g in range(groups):
        for half in range(2):
            if g < groups - 1:
                for k in others:
                    between(g, half, k).wait_send()
            for k in order:
                within(g, half, k).wait_send()
    line.finish(tiles * per)
    for t in range(tiles * per):
        keep(t).wait()


def attention_back(q, d_heads, log_mass, delta, qseg, ids, hat, inv, cosine, sine, x, gains, gain_query, grad_o, kv, ident):
    rows, head = q.shape
    width = x.shape[1]
    groups, length, _ = kv.shape
    size = rows // (2 * groups)
    chips = length // (4 * size)
    parts = rows // min(128, size)
    vmem = pl.BlockSpec(memory_space=pltpu.VMEM)
    dma = pltpu.SemaphoreType.DMA
    return pl.pallas_call(
        functools.partial(attention_back_kernel, groups, size),
        out_shape=(
            jax.ShapeDtypeStruct((rows, 4 * head), BF16),
            jax.ShapeDtypeStruct((rows, 2 * head), BF16),
            jax.ShapeDtypeStruct((2, chips - 1, size, 2 * head), BF16),
            jax.ShapeDtypeStruct((1, head), F32),
            jax.ShapeDtypeStruct((width, 2 * head), BF16),
        ),
        in_specs=[vmem] * 14 + [ANY],
        out_specs=(ANY, vmem, vmem, vmem, vmem),
        scratch_shapes=[
            pltpu.VMEM((groups, length, 2 * head), BF16),
            pltpu.VMEM((length, head), F32), pltpu.VMEM((length, head), F32),
            pltpu.VMEM((groups, length, 2 * head), BF16),
            pltpu.VMEM((groups, 2, chips, size, 2 * head), BF16),
            pltpu.VMEM((groups, 2, chips - 1, size, 2 * head), BF16),
            pltpu.VMEM((groups, 2, chips - 1, size, 2 * head), BF16),
            pltpu.VMEM((rows, 4 * head), BF16),
            pltpu.VMEM((width, head), F32),
            dma((groups,)), dma((parts,))] + [dma((groups, 2, chips))] * 4 + [dma((3, parts))] * 4,
        compiler_params=pltpu.CompilerParams(
            collective_id=ident, has_side_effects=True, vmem_limit_bytes=63 * 2**20),
        cost_estimate=cost(80),
        name="attention_back",
    )(q, d_heads, log_mass, delta, qseg, ids, hat, inv, cosine, sine, x, gains, gain_query, grad_o, kv)


class RowScatter:
    def __init__(self, group, own_rows, source, near, pair, far, sems):
        self.group, self.own_rows, self.source = group, own_rows, source
        self.near, self.pair, self.far, self.sems = near, pair, far, sems
        self.others = list(range(1, group.chips))
        self.order = self.others + [0]

    def block(self, device):
        return pl.ds(pl.multiple_of(device * self.own_rows, 16), self.own_rows)

    def within(self, k):
        g = self.group
        return g.copy(self.source.at[self.block(g.other(k) + 1 - 2 * g.core)], self.near.at[k],
                      self.sems[0].at[k], self.sems[1].at[k], g.partner())

    def between(self, k):
        g = self.group
        return g.copy(self.pair.at[k], self.far.at[k], self.sems[2].at[k], self.sems[3].at[k], g.other(k))

    def send(self):
        for k in self.order:
            self.within(k).start()

    def middle(self, out):
        for k in self.order:
            self.within(k).wait_recv()
            both = self.source[self.block(self.group.other(k)), :].astype(F32) + self.near[k].astype(F32)
            if k > 0:
                self.pair[k] = both.astype(BF16)
                self.between(k).start()
            else:
                out[...] = both

    def final(self, out):
        for k in self.others:
            self.between(k).wait_recv()
            out[...] += self.far[k].astype(F32)
        for k in self.others:
            self.between(k).wait_send()
        for k in self.order:
            self.within(k).wait_send()


def row_scatter_scratch(chips, own_rows, cols):
    return [pltpu.VMEM((chips, own_rows, cols), BF16)] * 3 + [pltpu.SemaphoreType.DMA((chips,))] * 4


def key_back_kernel(tiles, tile, chunk, own_rows, scattered, dkv_ref, hat_ref, inv_ref, cos_ref, sin_ref, x_ref, dq_ref,
                    gain_ref, gk_ref, w_ref, wq_ref, dgq_ref, dg_mid_ref, dg_post_ref, qo_ref, rest_ref,
                    dx_ref, last_out, qo_out, acc, acc_in, acc_key, w_kv, w_sem, last_ref, part,
                    add, ss, rs, out, own, near, far, *sems):
    i = pl.program_id(0)
    head = hat_ref.shape[1]
    per = tile // chunk
    count = tiles * per + 1
    line = ResidentSum(count, chunk, count, own, near, far, out, sems[:9])
    group = Shared(True)
    ring = Shared(False)
    size = rest_ref.shape[2]
    first = tiles * per - 2 * size // chunk

    def between(half, k):
        return ring.copy(rest_ref.at[half, k - 1], add.at[half, k - 1], ss.at[half, k], rs.at[half, k], ring.other(k))

    if scattered:
        early = RowScatter(group, own_rows, qo_ref, *sems[9:12], sems[12:16])
        late = RowScatter(group, own_rows, last_ref, *sems[16:19], sems[19:23])

    @pl.when(i == 0)
    def _():
        copy = pltpu.make_async_copy(w_ref.at[:, pl.ds(head, 2 * head)], w_kv, w_sem)
        copy.start()
        if scattered:
            group.greet(line.z)
        else:
            ring.greet(line.z)
            qo_out[...] = qo_ref[...]
        for half in range(2):
            for k in range(1, ring.chips):
                between(half, k).start()
        if scattered:
            early.send()
        for ref in (acc, acc_in, acc_key):
            ref[...] = jnp.zeros_like(ref)
        copy.wait()
        line.put(count - 1, jnp.broadcast_to(
            jnp.concatenate([dgq_ref[...], dgq_ref[...]], axis=1).astype(BF16), (chunk, 2 * head)))

    def put_rows(c):
        return dkv_ref[pl.ds(pl.multiple_of(c * chunk, chunk), chunk), :]

    @pl.when(i == 0)
    def _():
        def ready(c, _):
            line.put(c, put_rows(c))
            return 0

        lax.fori_loop(0, first, ready, 0)

    for half in range(2):
        @pl.when(i == max(0, (first * chunk + half * size) // tile - 2))
        def _():
            for k in range(1, ring.chips):
                between(half, k).wait_recv()

            def ready(n, _):
                c = first + half * (size // chunk) + n
                total = put_rows(c).astype(F32)
                for k in range(1, ring.chips):
                    total = total + add[half, k - 1, pl.ds(pl.multiple_of(n * chunk, chunk), chunk), :].astype(F32)
                line.put(c, total.astype(BF16))
                return 0

            lax.fori_loop(0, size // chunk, ready, 0)

    @pl.when(i < tiles)
    def _():
        part[pl.ds(pl.multiple_of(i * tile, tile), tile), :] = dot(dq_ref[...], wq_ref[...], NT)

    def handle(j):
        @pl.when((i >= 1) & (i <= tiles))
        def _():
            line.total((i - 1) * per + j)

        @pl.when(i < tiles)
        def _():
            line.pair(i * per + j)

    for j in range(per // 2):
        handle(j)

    @pl.when(i == 1)
    def _():
        line.pair(count - 1)
        if scattered:
            early.middle(qo_out)

    @pl.when(i == 2)
    def _():
        line.total(count - 1)

    if scattered:
        @pl.when(i == tiles)
        def _():
            early.final(qo_out)

    @pl.when(i >= 2)
    def _():
        for j in range(per):
            line.arrived((i - 2) * per + j)
        d_kv = out[pl.ds(pl.multiple_of((i - 2) * tile, tile), tile), :]
        d_rot = rotate(d_kv[:, :head].astype(F32), cos_ref[...], -sin_ref[...])
        d_raw, d_gain = norm_back(d_rot, hat_ref[...], inv_ref[...], gk_ref[...])
        acc_key[...] += d_gain[None]
        d_raw = jnp.concatenate([d_raw.astype(BF16), d_kv[:, head:]], axis=1)
        d_one = part[pl.ds(pl.multiple_of((i - 2) * tile, tile), tile), :] + dot(d_raw, w_kv[...], NT)
        hat, inv = norm_parts(x_ref[...].astype(F32))
        gain = gain_ref[0:1, :]
        d_part, d_gain = norm_back(d_one, hat, inv, gain)
        acc_in[...] += d_gain[None]
        dx_ref[...] = d_part.astype(BF16)
        acc[...] += dot((hat * (1.0 + gain)).astype(BF16), d_raw, TN)

    for j in range(per // 2, per):
        handle(j)

    @pl.when(i == tiles + 1)
    def _():
        for half in range(2):
            for k in range(1, ring.chips):
                between(half, k).wait_send()
        line.arrived(count - 1)
        width = x_ref.shape[1]
        short = head * own_rows // width
        last_ref[:, : 2 * head] = acc[...].astype(BF16)
        d_query = out[pl.ds((count - 1) * chunk, 16), :head][0:1].astype(F32)
        pair = jnp.concatenate([d_query, acc_key[...], jnp.zeros((14, head), F32)], axis=0).astype(BF16)
        col = lax.broadcasted_iota(jnp.int32, (head, width), 1)
        row = lax.broadcasted_iota(jnp.int32, (head, width), 0)
        shift = short.bit_length() - 1
        spot = lax.shift_right_logical(row, shift) * own_rows + (row & (short - 1))
        spread = dot(pair, jnp.where(col == spot, 1.0, 0.0).astype(BF16))
        gains = jnp.concatenate(
            [acc_in[...], dg_mid_ref[...], dg_post_ref[...], spread[0:2], jnp.zeros((122, width), F32)], axis=0)
        last_ref[:, 2 * head :] = jnp.transpose(gains).astype(BF16)
        if scattered:
            late.send()
            line.finish()
            late.middle(last_out)
            late.final(last_out)
        else:
            last_out[...] = last_ref[...]
            line.finish()


def key_back(d_kv, hat, inv, cosine, sine, x, d_query, gains, gain_key, first, w_query, dg_query, dg_mid, dg_post,
             grad_qo, rest, own_rows, ident):
    rows, width = x.shape
    head = hat.shape[1]
    tile, chunk = 256, 64
    tiles = rows // tile
    count = rows // chunk + 1
    dma = pltpu.SemaphoreType.DMA((count,))

    def late(cols):
        return pl.BlockSpec((tile, cols), lambda i: (jnp.maximum(i - 2, 0), 0))

    def fixed(shape):
        return pl.BlockSpec(shape, lambda i: (0, 0))

    turns = cosine.shape[0] // tile
    turn = pl.BlockSpec((tile, head // 2), lambda i: (lax.rem(jnp.maximum(i - 2, 0), turns), 0))
    comm = pltpu.VMEM((count * chunk, 2 * head), BF16)
    scattered = own_rows % 16 == 0
    chips = width // (2 * own_rows)
    last = (width, 2 * head + 128)
    more = []
    if scattered:
        last_out, qo_out, kind = (own_rows, last[1]), (own_rows, 2 * head), F32
        for cols in (2 * head, last[1]):
            more += row_scatter_scratch(chips, own_rows, cols)
    else:
        last_out, qo_out, kind = last, grad_qo.shape, BF16
    return pl.pallas_call(
        functools.partial(key_back_kernel, tiles, tile, chunk, own_rows, scattered),
        grid=(tiles + 2,),
        out_shape=(
            jax.ShapeDtypeStruct((rows, width), BF16),
            jax.ShapeDtypeStruct(last_out, kind),
            jax.ShapeDtypeStruct(qo_out, kind),
        ),
        in_specs=[whole_block(d_kv.shape),
                  late(head), late(1), turn, turn, late(width),
                  pl.BlockSpec((tile, 4 * head), lambda i: (jnp.minimum(i, tiles - 1), 0)),
                  whole_block(gains.shape), whole_block(gain_key.shape), ANY]
        + [whole_block(a.shape) for a in (w_query, dg_query, dg_mid, dg_post, grad_qo, rest)],
        out_specs=(late(width), fixed(last_out), fixed(qo_out)),
        scratch_shapes=[
            pltpu.VMEM((width, 2 * head), F32), pltpu.VMEM((1, width), F32), pltpu.VMEM((1, head), F32),
            pltpu.VMEM((width, 2 * head), BF16), pltpu.SemaphoreType.DMA, pltpu.VMEM(last, BF16),
            pltpu.VMEM((rows, width), F32), pltpu.VMEM(rest.shape, BF16)]
        + [pltpu.SemaphoreType.DMA((2, rest.shape[1] + 1))] * 2 + [comm] * 4 + [dma] * 7
        + [pltpu.SemaphoreType.REGULAR] * 2 + more,
        compiler_params=pltpu.CompilerParams(
            collective_id=ident, has_side_effects=True, vmem_limit_bytes=56 * 2**20),
        cost_estimate=cost(75),
        name="key_back",
    )(d_kv, hat, inv, cosine, sine, x, d_query, gains, gain_key, first, w_query, dg_query, dg_mid, dg_post, grad_qo, rest)


def shards(tokens, segments, cotangent, w_query, w_key, w_value, w_out, w_gate, w_up, w_down,
           g_input, g_post_attn, g_pre_ffn, g_post_ffn, g_query, g_key):
    batches, seq_local, _, size, width = tokens.shape
    head = w_key.shape[1]
    groups = batches * seq_local
    per_group = 2 * size
    rows = groups * per_group
    ctx = lax.axis_size("ctx")
    length = per_group * ctx
    rank = lax.axis_index("ctx")
    shared = ("dp", "ctx")
    own_rows = g_input.shape[0]
    hidden = w_gate.shape[1]

    def column(gain):
        return jnp.pad(gain, (0, own_rows - gain.shape[0]))[:, None]

    own_ids = segments.reshape(groups, 2, size)
    id_rows = own_ids.size // 128
    ids = jnp.pad(own_ids.reshape(id_rows, 128), ((0, -id_rows % 16), (0, 0)))
    extra = jnp.concatenate(
        [column(g) for g in (g_input, g_post_attn, g_pre_ffn, g_post_ffn, g_query, g_key)], axis=1)
    extra = jnp.pad(extra, ((0, 0), (0, 128 - extra.shape[1])))

    def rows_of_16(w):
        return jnp.pad(w, ((0, -own_rows % 16), (0, 0)))

    first, line_query, line_out, ids = first_gather(
        rows_of_16(jnp.concatenate([w_query, w_key, w_value, extra], axis=1)),
        rows_of_16(w_query), rows_of_16(w_out.T), ids, width // own_rows, 5)
    first = first[:, :own_rows].reshape(width, -1)
    side = first[:, 3 * head :]
    gain_cols = side[:, :8].astype(F32)
    gain_rows = gain_cols.T
    gain_input = gain_rows[0]
    short = g_query.shape[0]
    gain_query, gain_key = (
        gain_cols[:, i].reshape(-1, own_rows)[:, :short].reshape(-1) for i in (4, 5))

    wide = wide_of(hidden)
    second = jnp.concatenate(
        [line_out[:own_rows]] + [jnp.pad(w, ((0, 0), (0, wide - hidden))) for w in (w_gate, w_up, w_down.T)], axis=1)
    weights = lax.all_gather(second, shared, axis=0, tiled=True)

    offsets = rank * size + jnp.arange(size, dtype=jnp.int32)
    position = jnp.concatenate([offsets, length - 1 - offsets]).astype(F32)
    cosine, sine = angles(position, head // 2, head)

    x_rows = tokens.reshape(rows, width)
    dy_rows = cotangent.reshape(rows, width)
    queries, q_hat, q_scale, k_hat, k_scale, heads_own, log_mass, kv, heads_all = attention(
        x_rows, first, gain_rows, gain_query[None], gain_key[None], cosine, sine, own_ids[..., None], ids, length, 0)

    line_query, heads_all = lax.optimization_barrier((line_query[:own_rows], heads_all))
    query_full = lax.all_gather(line_query, shared, axis=0, tiled=True)
    attn, hidden_two, gate, up, ffn_out = ffn_forward(x_rows, heads_all, gain_rows, weights, hidden, 1)
    ffn_out, query_full = lax.optimization_barrier((ffn_out, query_full))
    d_gain_post_ffn, grad_ffn, d_two = ffn_backward(
        dy_rows, ffn_out, hidden_two, gate, up, gain_rows, weights, 2)
    grad_ffn = lax.psum_scatter(grad_ffn, shared, scatter_dimension=1, tiled=True)
    output, d_middle, d_heads, delta, d_gain_mid, grad_out_t = middle_back(
        x_rows, attn, dy_rows, d_two, ffn_out, heads_own, gain_rows, weights)

    d_q_all, d_kv, rest, d_gain_query, grad_qo = attention_back(
        queries, d_heads, log_mass, delta, own_ids[:, :, None, :], ids, q_hat, q_scale, cosine, sine, x_rows, gain_rows,
        gain_query[None], grad_out_t, kv, 4)
    d_part, last, grad_qo = key_back(
        d_kv, k_hat, k_scale, cosine, sine, x_rows, d_q_all, gain_rows, gain_key[None],
        first, query_full, d_gain_query, d_gain_mid, d_gain_post_ffn, grad_qo, rest, own_rows, 3)
    d_tokens = d_middle.astype(F32) + d_part.astype(F32)
    if own_rows % 16:
        last = lax.psum_scatter(last, shared, scatter_dimension=0, tiled=True).astype(F32)
        grad_qo = lax.psum_scatter(grad_qo, shared, scatter_dimension=0, tiled=True).astype(F32)
    g = last[:, 2 * head :]
    return (
        output.reshape(tokens.shape),
        d_tokens.reshape(tokens.shape),
        grad_qo[:, :head],
        last[:, :head],
        last[:, head : 2 * head],
        grad_qo[:, head:].T,
        grad_ffn[0].astype(F32),
        grad_ffn[1].astype(F32),
        grad_ffn[2].astype(F32).T,
        g[:, 0],
        g[:, 1],
        g[:, 2],
        g[:, 3],
        g[:short, 4],
        g[:short, 5],
    )


def solution(mesh):
    shared = ("dp", "ctx")
    rows = P(None, "dp", None, "ctx", None)
    weights = (
        P(shared, "tp"), P(shared, None), P(shared, None), P("tp", shared),
        P(shared, "tp"), P(shared, "tp"), P("tp", shared),
    )
    gains = (P(shared),) * 6
    return jax.shard_map(
        shards,
        mesh=mesh,
        in_specs=(rows, P(None, "dp", None, "ctx"), rows) + weights + gains,
        out_specs=(rows, rows) + weights + gains,
        check_vma=False,
    )
```
